32 devices in a mesh: dp: 4 (over y, x), ctx: 4 (over z), expert: 2 (over core).
Axes of the slice: x: 2, y: 2, z: 4, core: 2. Of those that a mesh axis runs over, the one named last changes fastest.
Arguments:
- inputs: bfloat16 [8, 2048, 768], P(('dp', 'expert'), 'ctx'), may hold values from -6 to 6
- cotangent: bfloat16 [8, 2048, 768], P(('dp', 'expert'), 'ctx'), may hold values from -6 to 6
- route: int32 [8, 2048, 1], P(('dp', 'expert'), 'ctx'), may hold values from 0 to 7
- arrival: int32 [8, 4, 512], P(('dp', 'expert'), 'ctx'), may hold values from 0 to 511, each once within a row
- branch: int32 [8, 4], P(('dp', 'expert'), 'ctx'), may hold values from 256 to 1024, as said below
- attn_gain: bfloat16 [768], replicated, may hold values from 0.5 to 1.5
- query_weight: bfloat16 [768, 768], replicated, may hold values from -0.0546875 to 0.0546875
- key_weight: bfloat16 [768, 768], replicated, may hold values from -0.21875 to 0.21875
- value_weight: bfloat16 [768, 768], replicated, may hold values from -0.21875 to 0.21875
- output_weight: bfloat16 [768, 768], replicated, may hold values from -0.875 to 0.875
- rel_table: bfloat16 [32, 12], replicated, may hold values from -3 to 3
- moe_gain: bfloat16 [768], replicated, may hold values from 0.5 to 1.5
- router_weight: bfloat16 [768, 8], replicated, may hold values from -0.15625 to 0.15625
- expert_in: bfloat16 [8, 768, 3072], P(('ctx', 'expert')), may hold values from -0.21875 to 0.21875
- expert_out: bfloat16 [8, 3072, 768], P(('ctx', 'expert')), may hold values from -0.875 to 0.875
Outputs:
- layer_out: bfloat16 [8, 2048, 768], P(('dp', 'expert'), 'ctx')
- input_grad: float32 [8, 2048, 768], P(('dp', 'expert'), 'ctx')
- attn_gain_grad: float32 [768], replicated
- query_weight_grad: float32 [768, 768], replicated
- key_weight_grad: float32 [768, 768], replicated
- value_weight_grad: float32 [768, 768], replicated
- output_weight_grad: float32 [768, 768], replicated
- table_grad: float32 [32, 12], replicated
- moe_gain_grad: float32 [768], replicated
- router_grad: float32 [768, 8], replicated
- expert_in_grad: float32 [8, 768, 3072], P(('ctx', 'expert'), None, 'dp')
- expert_out_grad: float32 [8, 3072, 768], P(('ctx', 'expert'), 'dp')
The draws below stay inside these ranges and needn't reach their ends.
Inputs may be any that keep to these rules, and one draw needn't show every extreme that they name: `route`: every expert is named by some token. `arrival`: the 512 entries of one device block are a permutation; a smaller entry arrives earlier at its expert. Continuation c of group g follows the first branch[g, c] tokens of its prompt; in every group some continuation follows all 1024.
All inputs are finite; a program needn't handle non-finite values.
Results may differ from the reference program's by a relative error of at most 0.02.
Values may be sent and summed in bfloat16 or wider, within the bound.
A program may use at most 192 MiB of HBM per device.

```python
from functools import partial
import jax
import jax.numpy as jnp
from jax import lax

D = 768
H = 12
HD = 64
FF = 3072
NB = 32
PB = 256
CLEN = 256
TOK = 512
PLEN = 1024
CONTS = 4
GROUPS = 8
EXPERTS = 8
CAP = 72
N_CTX = 4
DEVICES = 32


def draw_branch(key, part):
    key = jax.random.fold_in(key, 11)
    key_lengths, key_chosen = jax.random.split(key)
    lengths = jax.random.randint(key_lengths, (GROUPS, CONTS), PB, PLEN + 1, dtype=jnp.int32)
    chosen = jax.random.randint(key_chosen, (GROUPS,), 0, CONTS, dtype=jnp.int32)
    full_view = jnp.arange(CONTS, dtype=jnp.int32)[None, :] == chosen[:, None]
    return jnp.where(full_view, PLEN, lengths).astype(jnp.int32)


def steps_of(rng, shape, cuts, smallest, largest):
    gain = 1.0
    for position, blocks in cuts:
        steps = jax.random.uniform(jax.random.fold_in(jax.random.fold_in(rng, 6), position), (blocks,), jnp.float32, smallest / len(cuts), largest / len(cuts))
        gain = gain * jnp.repeat(jnp.exp(steps), shape[position] // blocks).reshape((-1,) + (1,) * (len(shape) - 1 - position))
    return gain


def picks_of(rng, rows, count, top, lift):
    sequence = jax.random.permutation(jax.random.fold_in(rng, 1), count)
    boost = sequence
    for power in range(3):
        boost = boost * boost // count
    boost = boost * lift // count
    chance = jax.random.randint(jax.random.fold_in(rng, 2), (rows, count), 0, 4096) + boost
    fixed_rows = jax.random.permutation(jax.random.fold_in(rng, 3), rows)[jnp.arange(count) % rows]
    chance = jnp.where(jnp.arange(rows)[:, None] == fixed_rows[None, :], 1 << 14, chance)
    merit = chance * count + jnp.arange(count)
    return lax.top_k(merit.astype(jnp.int32), top)[1].astype(jnp.int32)


def noise(own_key, dims, deviation, limit, cuts=(), kind=jnp.bfloat16):
    level = steps_of(own_key, dims, cuts, -0.22, 0.18) if cuts else 1.0
    values = jax.random.normal(own_key, dims, jnp.float32) * deviation * level
    return jnp.minimum(jnp.maximum(values, -limit), limit).astype(kind)


def setup_inputs(seed: int = 0) -> dict:
    splits = jax.random.split(jax.random.key(seed), 16)
    return {
        "inputs": noise(splits[0], (GROUPS, N_CTX * TOK, D), 1.0, 6.0, ((0, 8), (1, 4))),
        "cotangent": noise(splits[1], (GROUPS, N_CTX * TOK, D), 1.0, 6.0, ((0, 8), (1, 4))),
        "route": picks_of(splits[2], GROUPS * (N_CTX * TOK), EXPERTS, 1, 1024).reshape((GROUPS, N_CTX * TOK, 1)),
        "arrival": jax.vmap(lambda own: jax.random.permutation(own, TOK))(jax.random.split(splits[3], GROUPS * N_CTX)).reshape((GROUPS, N_CTX, TOK)).astype(jnp.int32),
        "branch": draw_branch(jax.random.fold_in(splits[15], 71), 0),
        "attn_gain": jnp.clip(1.0 + 0.1 * jax.random.normal(splits[5], (D,), jnp.float32), 0.5, 1.5).astype(jnp.bfloat16),
        "query_weight": noise(splits[6], (D, D), (D * HD // 4) ** -0.5, 0.0546875),
        "key_weight": noise(splits[7], (D, D), D ** -0.5, 0.21875),
        "value_weight": noise(splits[8], (D, D), D ** -0.5, 0.21875),
        "output_weight": noise(splits[9], (D, D), (D // 16) ** -0.5, 0.875),
        "rel_table": noise(splits[10], (NB, H), 0.5, 3.0),
        "moe_gain": jnp.clip(1.0 + 0.1 * jax.random.normal(splits[11], (D,), jnp.float32), 0.5, 1.5).astype(jnp.bfloat16),
        "router_weight": noise(splits[12], (D, EXPERTS), (2 * D) ** -0.5, 0.15625),
        "expert_in": noise(splits[13], (EXPERTS, D, FF), D ** -0.5, 0.21875, ((0, 8),)),
        "expert_out": noise(splits[14], (EXPERTS, FF, D), (max(FF // (EXPERTS * EXPERTS), 1)) ** -0.5, 0.875, ((0, 8),)),
    }


bucket_edges = (19, 21, 24, 27, 31, 35, 40, 46, 52, 59, 67, 77, 87, 99, 113)
norm_eps = 1e-06
masked_score = -1e+30

@jax.custom_vjp
def low(v):
    return lax.optimization_barrier(v.astype(jnp.bfloat16)).astype(jnp.float32)

@jax.custom_vjp
def low_back(v):
    return v

def low_keep(v):
    return (low(v), None)

def low_pass(kept, grad):
    return (grad,)

def back_keep(v):
    return (v, None)

def back_low(kept, grad):
    return (low(grad),)
low.defvjp(low_keep, low_pass)
low_back.defvjp(back_keep, back_low)

def exact(pattern, operand_a, operand_b):
    return jnp.einsum(pattern, operand_a, operand_b, precision=lax.Precision.HIGHEST)

def rms_norm(values, norm_gain):
    return values * lax.rsqrt(lax.optimization_barrier(jnp.mean(values * values, axis=-1, keepdims=True)) + norm_eps) * norm_gain

def bucket_of(distance):
    distance = jnp.maximum(distance, 0)
    bucket_ids = jnp.minimum(distance, 16)
    for boundary in bucket_edges:
        bucket_ids = bucket_ids + (distance >= boundary).astype(jnp.int32)
    return bucket_ids

def attend(queries, key_heads, value_heads, allowed, distance, rel_table):
    rel_bias = jnp.transpose(rel_table[bucket_of(distance)], (2, 0, 1))
    scores = low_back(exact('qhd,khd->hqk', queries, key_heads) + rel_bias)
    scores = jnp.where(allowed[None], scores, masked_score)
    weights = jnp.exp(scores - jax.nn.logsumexp(scores, axis=-1, keepdims=True))
    return exact('hqk,khd->qhd', low(weights), value_heads)

def split_heads(row_block):
    return row_block.reshape(row_block.shape[0], H, HD)

def group_attention(group_items, rel_table):
    queries, key_rows, value_rows, branch_row = group_items
    prompt_queries = split_heads(queries[:, :PB].reshape(PLEN, D))
    prompt_keys = split_heads(key_rows[:, :PB].reshape(PLEN, D))
    prompt_values = split_heads(value_rows[:, :PB].reshape(PLEN, D))
    prompt_places = jnp.arange(PLEN, dtype=jnp.int32)
    distance = prompt_places[:, None] - prompt_places[None, :]
    prompt_out = attend(prompt_queries, prompt_keys, prompt_values, distance >= 0, distance, rel_table)

    def continuation(pieces):
        cont_queries, cont_keys, cont_values, branch_at = pieces
        cont_steps = jnp.arange(CLEN, dtype=jnp.int32)
        key_places = jnp.concatenate([prompt_places, branch_at + cont_steps])
        query_places = branch_at + cont_steps
        allowed = jnp.concatenate([jnp.broadcast_to(prompt_places[None, :] < branch_at, (CLEN, PLEN)), cont_steps[None, :] <= cont_steps[:, None]], axis=1)
        all_keys = jnp.concatenate([prompt_keys, split_heads(cont_keys)])
        all_values = jnp.concatenate([prompt_values, split_heads(cont_values)])
        result = attend(split_heads(cont_queries), all_keys, all_values, allowed, query_places[:, None] - key_places[None, :], rel_table)
        return result.reshape(CLEN, D)
    cont_out = lax.map(jax.checkpoint(continuation), (queries[:, PB:], key_rows[:, PB:], value_rows[:, PB:], branch_row))
    return jnp.concatenate([prompt_out.reshape(N_CTX, PB, D), cont_out], axis=1)

def layer_forward(tokens, attn_gain, query_weight, key_weight, value_weight, output_weight, rel_table, moe_gain, router_weight, expert_in, expert_out, branch, chosen, slot_place, kept_mask):
    token_grid = tokens.reshape(GROUPS, N_CTX, TOK, D)
    normed = low(rms_norm(token_grid, attn_gain))
    queries = low_back(low(exact('gctd,de->gcte', normed, query_weight)))
    key_rows = low_back(low(exact('gctd,de->gcte', normed, key_weight)))
    value_rows = low_back(low(exact('gctd,de->gcte', normed, value_weight)))
    attended = lax.map(jax.checkpoint(partial(group_attention, rel_table=rel_table)), (queries, key_rows, value_rows, branch))
    attended = low_back(low(attended))
    hidden = token_grid + low_back(exact('gctd,de->gcte', attended, output_weight))
    moe_in = low(rms_norm(hidden, moe_gain))
    router_probs = jax.nn.softmax(exact('gctd,de->gcte', moe_in, router_weight), axis=-1)
    gate_value = lax.optimization_barrier(jnp.sum(jnp.where(chosen, router_probs, 0.0), axis=-1))
    sent_rows = low_back(moe_in).reshape(DEVICES * TOK, D)
    slot_total = EXPERTS * DEVICES * CAP
    buffer = jnp.zeros((slot_total, D), jnp.float32).at[slot_place].add(sent_rows, mode='drop')
    buffer = buffer.reshape(EXPERTS, DEVICES * CAP, D)
    pre_act = low_back(exact('erd,edf->erf', buffer, expert_in))
    activation = low(jax.nn.gelu(pre_act))
    expert_rows = low_back(low(exact('erf,efd->erd', activation, expert_out))).reshape(slot_total, D)
    returned = jnp.where(kept_mask[:, None], expert_rows[jnp.minimum(slot_place, slot_total - 1)], 0.0)
    layer_value = hidden + gate_value[..., None] * returned.reshape(GROUPS, N_CTX, TOK, D)
    return layer_value.reshape(GROUPS, N_CTX * TOK, D)

def reference(inputs, cotangent, route, arrival, branch, attn_gain, query_weight, key_weight, value_weight, output_weight, rel_table, moe_gain, router_weight, expert_in, expert_out):
    expert_ids = route.reshape(DEVICES, TOK)
    orders = arrival.reshape(DEVICES, TOK)

    def slot_count(pieces):
        ids_row, order_row = pieces
        same_expert = ids_row[:, None] == ids_row[None, :]
        earlier = order_row[None, :] < order_row[:, None]
        return lax.optimization_barrier(jnp.sum((same_expert & earlier).astype(jnp.int32), axis=1))
    slot_rank = lax.map(slot_count, (expert_ids, orders))
    kept_grid = slot_rank < CAP
    owners = jnp.arange(DEVICES, dtype=jnp.int32)[:, None]
    slot_index = expert_ids * (DEVICES * CAP) + owners * CAP + slot_rank
    slot_place = jnp.where(kept_grid, slot_index, EXPERTS * DEVICES * CAP).reshape(DEVICES * TOK).astype(jnp.int32)
    kept_mask = kept_grid.reshape(DEVICES * TOK)
    chosen = route.reshape(GROUPS, N_CTX, TOK)[..., None] == jnp.arange(EXPERTS, dtype=jnp.int32)
    floats = tuple((array_in.astype(jnp.float32) for array_in in (inputs, attn_gain, query_weight, key_weight, value_weight, output_weight, rel_table, moe_gain, router_weight, expert_in, expert_out)))

    def forward_of(*params):
        return layer_forward(*params, branch, chosen, slot_place, kept_mask)
    layer_value, pullback = jax.vjp(forward_of, *floats)
    gradients = pullback(cotangent.astype(jnp.float32))
    return (layer_value.astype(jnp.bfloat16), gradients[0], gradients[1], gradients[2], gradients[3], gradients[4], gradients[5], gradients[6], gradients[7], gradients[8], gradients[9], gradients[10])
```

```python
import functools

import jax
import jax.numpy as jnp
from jax import lax
from jax.experimental import pallas as pl
from jax.experimental.pallas import tpu as pltpu
from jax.sharding import PartitionSpec as P

PB = 256
TILE = 128

bucket_edges = (19, 21, 24, 27, 31, 35, 40, 46, 52, 59, 67, 77, 87, 99, 113)
norm_eps = 1e-06
masked_score = -1e30
gelu_scale = 0.7978845608
gelu_cube = 0.044715

bf16 = jnp.bfloat16
f32 = jnp.float32
VMEM_LIMIT = 56 * 1024 * 1024


def dot_nn(a, b):
    return jnp.dot(a, b, preferred_element_type=f32)


def dot_nt(a, b):
    return lax.dot_general(a, b, (((1,), (1,)), ((), ())), preferred_element_type=f32)


def dot_tn(a, b):
    return lax.dot_general(a, b, (((0,), (0,)), ((), ())), preferred_element_type=f32)


def two_parts(a):
    high = a.astype(bf16)
    return high, (a - high.astype(f32)).astype(bf16)


def vmem():
    return pl.BlockSpec(memory_space=pltpu.VMEM)


def smem():
    return pl.BlockSpec(memory_space=pltpu.SMEM)


def params():
    return pltpu.CompilerParams(vmem_limit_bytes=VMEM_LIMIT)


def cost(flops, nbytes):
    return pl.CostEstimate(flops=int(flops), bytes_accessed=int(nbytes), transcendentals=0)


def shape(dims, kind):
    return jax.ShapeDtypeStruct(dims, kind)


def inverse_rms(x):
    return lax.rsqrt(jnp.mean(x * x, axis=-1, keepdims=True) + norm_eps)


def bucket_onehot(buckets):
    distance = jnp.arange(TILE, dtype=jnp.int32)
    ids = jnp.minimum(distance, 16)
    for edge in bucket_edges:
        ids = ids + (distance >= edge).astype(jnp.int32)
    return (ids[:, None] == jnp.arange(buckets, dtype=jnp.int32)[None, :]).astype(f32)


def slot_kernel(capacity, route_col, route_row, arrive_col, arrive_row, cot_ref, slot_out, rows_out):
    slots = rows_out.shape[0]
    tokens = cot_ref.shape[0]
    same = route_col[...] == route_row[...]
    earlier = arrive_col[...] < arrive_row[...]
    rank = jnp.sum(jnp.where(same & earlier, 1.0, 0.0), axis=0, keepdims=True).astype(jnp.int32)
    slot = jnp.where(rank < capacity, route_row[...] * capacity + rank, slots)
    slot_out[...] = slot
    place = lax.broadcasted_iota(jnp.int32, (slots, tokens), 0) == slot
    rows_out[...] = dot_nn(place.astype(bf16), cot_ref[...]).astype(bf16)


def own_kernel(x_ref, gain_ref, wq_ref, wk_ref, wv_ref, normed_out, q_out, k_out, v_out):
    x = x_ref[...].astype(f32)
    normed = (x * inverse_rms(x) * gain_ref[...].astype(f32)).astype(bf16)
    normed_out[...] = normed
    width = x_ref.shape[1]

    def column(i, _):
        cols = pl.ds(pl.multiple_of(i * 256, 256), 256)
        q_out[:, cols] = dot_nn(normed_out[...], wq_ref[:, cols]).astype(bf16)
        k_out[:, cols] = dot_nn(normed_out[PB:, :], wk_ref[:, cols]).astype(bf16)
        v_out[:, cols] = dot_nn(normed_out[PB:, :], wv_ref[:, cols]).astype(bf16)
        return 0

    lax.fori_loop(0, width // 256, column, 0)


def near_index(first):
    rows = lax.broadcasted_iota(jnp.int32, (TILE, TILE), 0)
    lanes = lax.broadcasted_iota(jnp.int32, (TILE, TILE), 1)
    return first + lanes - rows


def near_tiles(ctx_at, branch, plen):
    start = ctx_at * PB
    window = jnp.minimum((branch - (bucket_edges[-1] - 1)) // 16 * 16, plen - TILE)
    return (
        (start, 0, 0, False),
        (start, TILE, TILE, False),
        (start + TILE, TILE, 0, False),
        (plen, PB, 0, False),
        (plen, PB + TILE, TILE, False),
        (plen + TILE, PB + TILE, 0, False),
        (window, PB, branch - window, False),
        (start - TILE, 0, TILE, True),
    )


def add_near(s_ref, bias_row, ctx_at, branch, plen):
    source = jnp.broadcast_to(bias_row, (TILE, TILE))
    for first_row, first_lane, gap, guarded in near_tiles(ctx_at, branch, plen):
        def work(first_row=first_row, first_lane=first_lane, gap=gap):
            rows = pl.ds(first_row if isinstance(first_row, int) else pl.multiple_of(first_row, 16), TILE)
            lanes = slice(first_lane, first_lane + TILE)
            index = jnp.clip(near_index(gap), 0, TILE - 1)
            s_ref[rows, lanes] = s_ref[rows, lanes] + jnp.take_along_axis(source, index, axis=1)

        if guarded:
            pl.when(ctx_at > 0)(work)
        else:
            work()


def scores_to(s_ref, keys, queries, plen):
    s_ref[:plen, :] = dot_nt(keys[:plen], queries)
    s_ref[plen:, PB:] = dot_nt(keys[plen:], queries[PB:])


def limits(ctx_at, branch, tokens):
    lane = lax.broadcasted_iota(jnp.int32, (1, tokens), 1)
    return jnp.where(lane < PB, ctx_at * PB + lane + 1, branch)


def row_steps(first, count, lanes):
    return first + lax.broadcasted_iota(jnp.int32, (count, lanes), 0)


def own_allowed(first, count, lanes):
    return row_steps(first, count, lanes) <= lax.broadcasted_iota(jnp.int32, (count, lanes), 1)


def head_lanes(half):
    return lax.broadcasted_iota(jnp.int32, (1, TILE), 1) // (TILE // 2) == half


def pick_rows(pieces, lanes):
    row = lax.broadcasted_iota(jnp.int32, (8, lanes), 0)
    return jnp.where(row == 0, pieces[0], jnp.where(row == 1, pieces[1], 0.0))


def fold8(x, op):
    return op(x.reshape(x.shape[0] // 8, 8, x.shape[1]), axis=0)


def attend_kernel(
    meta_ref, bias_ref, x_ref, gain_ref, q_ref, kc_ref, vc_ref, wk_ref, wv_ref,
    normed_out, k_out, v_out, att_out, lse_out,
    s_ref, p_ref,
):
    ctx_at, branch = meta_ref[0], meta_ref[1]
    plen, width = x_ref.shape
    tokens = q_ref.shape[0]
    own = tokens - PB
    gain = gain_ref[...].astype(f32)

    def norm_block(i, _):
        rows = pl.ds(pl.multiple_of(i * PB, PB), PB)
        x = x_ref[rows, :].astype(f32)
        normed_out[rows, :] = (x * inverse_rms(x) * gain).astype(bf16)
        return 0

    lax.fori_loop(0, plen // PB, norm_block, 0)

    def column(i, _):
        cols = pl.ds(pl.multiple_of(i * 256, 256), 256)
        k_out[:plen, cols] = dot_nn(normed_out[...], wk_ref[:, cols]).astype(bf16)
        v_out[:plen, cols] = dot_nn(normed_out[...], wv_ref[:, cols]).astype(bf16)
        return 0

    lax.fori_loop(0, width // 256, column, 0)
    k_out[plen:, :] = kc_ref[...]
    v_out[plen:, :] = vc_ref[...]
    p_ref[plen:, :PB] = jnp.zeros((own, PB), bf16)
    limit = limits(ctx_at, branch, tokens)

    def pair(g, _):
        lanes = pl.ds(pl.multiple_of(g * TILE, TILE), TILE)
        queries = q_ref[:, lanes]
        keys = k_out[:, lanes]
        values_t = v_out[:, lanes].T
        bias = bias_ref[g]
        lse_rows, att_rows = [], []
        for half in range(2):
            scores_to(s_ref, jnp.where(head_lanes(half), keys, jnp.zeros_like(keys)), queries, plen)
            add_near(s_ref, bias[half : half + 1, :], ctx_at, branch, plen)

            def top_of(i, top):
                rows = pl.ds(pl.multiple_of(i * TILE, TILE), TILE)
                s = jnp.where(row_steps(i * TILE, TILE, tokens) < limit, s_ref[rows, :], masked_score)
                s_ref[rows, :] = s
                return jnp.maximum(top, fold8(s, jnp.max))

            top = lax.fori_loop(0, plen // TILE, top_of, jnp.full((8, tokens), masked_score, f32))
            own_top = jnp.full((8, own), masked_score, f32)
            for i in range(own // TILE):
                rows = slice(plen + i * TILE, plen + (i + 1) * TILE)
                s = jnp.where(own_allowed(i * TILE, TILE, own), s_ref[rows, PB:], masked_score)
                s_ref[rows, PB:] = s
                own_top = jnp.maximum(own_top, fold8(s, jnp.max))
            top = jnp.concatenate([top[:, :PB], jnp.maximum(top[:, PB:], own_top)], axis=1)
            top = jnp.max(top, axis=0, keepdims=True)

            def weigh(i, total):
                rows = pl.ds(pl.multiple_of(i * TILE, TILE), TILE)
                p = jnp.exp(s_ref[rows, :] - top)
                p_ref[rows, :] = p.astype(bf16)
                return total + fold8(p, jnp.sum)

            total = lax.fori_loop(0, plen // TILE, weigh, jnp.zeros((8, tokens), f32))
            own_total = jnp.zeros((8, own), f32)
            for i in range(own // TILE):
                rows = slice(plen + i * TILE, plen + (i + 1) * TILE)
                p = jnp.exp(s_ref[rows, PB:] - top[:, PB:])
                p_ref[rows, PB:] = p.astype(bf16)
                own_total = own_total + fold8(p, jnp.sum)
            total = jnp.concatenate([total[:, :PB], total[:, PB:] + own_total], axis=1)
            total = jnp.sum(total, axis=0, keepdims=True)
            rows = slice(half * 64, half * 64 + 64)
            att_rows.append((dot_nn(values_t[rows, :], p_ref[...]) / total).astype(bf16))
            lse_rows.append(top + jnp.log(total))
        att_out[lanes, :] = jnp.concatenate(att_rows, axis=0)
        lse_out[g] = pick_rows(lse_rows, tokens)
        return 0

    lax.fori_loop(0, width // TILE, pair, 0)


def route_kernel(
    att_ref, x_ref, wo_ref, gain_ref, router_ref, route_col, slot_row, experts,
    hidden_out, rows_out, gate_out,
):
    slots = rows_out.shape[0]
    tokens, width = x_ref.shape

    def column(i, _):
        cols = pl.ds(pl.multiple_of(i * 256, 256), 256)
        hidden_out[:, cols] = x_ref[:, cols].astype(f32) + dot_tn(att_ref[...], wo_ref[:, cols])
        return 0

    lax.fori_loop(0, width // 256, column, 0)
    hidden = hidden_out[...]
    moe_in = (hidden * inverse_rms(hidden) * gain_ref[...].astype(f32)).astype(bf16)
    lane = lax.broadcasted_iota(jnp.int32, (tokens, TILE), 1)
    probs = router_probs(dot_nn(moe_in, router_ref[...]), lane, experts)
    gate_out[...] = jnp.sum(jnp.where(lane == route_col[...], probs, 0.0), axis=1, keepdims=True)
    place = lax.broadcasted_iota(jnp.int32, (slots, tokens), 0) == slot_row[...]
    rows_out[...] = dot_nn(place.astype(bf16), moe_in).astype(bf16)


def router_probs(logits, lane, experts):
    logits = jnp.where(lane < experts, logits, masked_score)
    logits = jnp.exp(logits - jnp.max(logits, axis=1, keepdims=True))
    return logits / jnp.sum(logits, axis=1, keepdims=True)


def gelu_parts(v):
    t = jnp.tanh(gelu_scale * (v + gelu_cube * (v * v * v)))
    half = 0.5 * (1.0 + t)
    slope = half + 0.5 * v * (1.0 - t * t) * (gelu_scale + (3.0 * gelu_scale * gelu_cube) * (v * v))
    return v * half, slope


def expert_kernel(
    experts, meta_ref, rows_ref, cot_ref, win_ref, wout_ref, router_ref,
    result_out, grad_out, router_out,
    probs_ref, sent_ref, result_acc, grad_acc,
):
    step = pl.program_id(0)
    slots = rows_ref.shape[0]
    lane = lax.broadcasted_iota(jnp.int32, (slots, TILE), 1)

    @pl.when(step == 0)
    def _():
        probs = router_probs(dot_nn(rows_ref[...], router_ref[...]), lane, experts)
        probs_ref[...] = probs
        gate = jnp.sum(jnp.where(lane == meta_ref[2], probs, 0.0), axis=1, keepdims=True)
        sent_ref[...] = (gate * cot_ref[...].astype(f32)).astype(bf16)
        result_acc[...] = jnp.zeros_like(result_acc)
        grad_acc[...] = jnp.zeros_like(grad_acc)

    act, slope = gelu_parts(dot_nn(rows_ref[...], win_ref[...]))
    result_acc[...] += dot_nn(act.astype(bf16), wout_ref[...])
    pre_grad = (dot_nt(sent_ref[...], wout_ref[...]) * slope).astype(bf16)
    grad_acc[...] += dot_nt(pre_grad, win_ref[...])

    @pl.when(step == pl.num_programs(0) - 1)
    def _():
        result = result_acc[...].astype(bf16)
        result_out[...] = result
        probs = probs_ref[...]
        mine = lane == meta_ref[2]
        gate = jnp.sum(jnp.where(mine, probs, 0.0), axis=1, keepdims=True)
        gate_grad = jnp.sum(cot_ref[...].astype(f32) * result.astype(f32), axis=1, keepdims=True)
        logit_grad = (gate_grad * gate) * (jnp.where(mine, 1.0, 0.0) - probs)
        high, low = two_parts(logit_grad)
        router_t = router_ref[...]
        grad = grad_acc[...] + (dot_nt(high, router_t) + dot_nt(low, router_t))
        grad_out[...] = grad.astype(bf16)
        router_out[...] = dot_tn(high, rows_ref[...]) + dot_tn(low, rows_ref[...])


def expert_grad_kernel(
    experts, meta_ref, rows_ref, cot_ref, win_ref, wout_ref, router_ref, in_out, out_out,
):
    step = pl.program_id(0)
    slots = rows_ref.shape[0]
    lane = lax.broadcasted_iota(jnp.int32, (slots, TILE), 1)

    @pl.when(step == 0)
    def _():
        in_out[...] = jnp.zeros_like(in_out)
        out_out[...] = jnp.zeros_like(out_out)

    rows = rows_ref[...]
    probs = router_probs(dot_nn(rows, router_ref[...]), lane, experts)
    gate = jnp.sum(jnp.where(lane == meta_ref[2], probs, 0.0), axis=1, keepdims=True)
    sent = (gate * cot_ref[...].astype(f32)).astype(bf16)
    act, slope = gelu_parts(dot_nn(rows, win_ref[...]))
    out_out[...] += dot_tn(act.astype(bf16), sent)
    pre_grad = (dot_nt(sent, wout_ref[...]) * slope).astype(bf16)
    in_out[...] += dot_tn(rows, pre_grad)


def hidden_kernel(
    grad_ref, slot_row, hidden_ref, cot_ref, gain_ref, att_ref, wo_ref,
    hidden_grad_out, wo_grad_out, att_grad_out, delta_out, gain_grad_out,
    low_ref, att_t_ref,
):
    slots = grad_ref.shape[0]
    tokens, width = hidden_ref.shape
    place = lax.broadcasted_iota(jnp.int32, (slots, tokens), 0) == slot_row[...]
    moe_grad = dot_tn(place.astype(bf16), grad_ref[...])
    hidden = hidden_ref[...]
    inverse = inverse_rms(hidden)
    scaled = hidden * inverse
    gain_grad_out[...] = jnp.sum(moe_grad * scaled, axis=0, keepdims=True)
    through = moe_grad * gain_ref[...].astype(f32)
    shared = jnp.mean(through * scaled, axis=1, keepdims=True)
    hidden_grad = cot_ref[...].astype(f32) + inverse * (through - scaled * shared)
    hidden_grad_out[...] = hidden_grad
    low_ref[...] = hidden_grad.astype(bf16)

    def column(i, _):
        cols = pl.ds(pl.multiple_of(i * 256, 256), 256)
        wo_grad_out[:, cols] = dot_nn(att_ref[...], low_ref[:, cols]).astype(wo_grad_out.dtype)
        att_grad_out[:, cols] = dot_nt(low_ref[...], wo_ref[cols, :]).astype(bf16)
        att_t_ref[cols, :] = dot_nt(wo_ref[cols, :], low_ref[...]).astype(bf16)
        return 0

    lax.fori_loop(0, width // 256, column, 0)

    def pair(g, _):
        rows = pl.ds(pl.multiple_of(g * TILE, TILE), TILE)
        both = att_ref[rows, :].astype(f32) * att_t_ref[rows, :].astype(f32)
        delta_out[g] = pick_rows(
            [jnp.sum(both[:64], axis=0, keepdims=True), jnp.sum(both[64:], axis=0, keepdims=True)],
            tokens,
        )
        return 0

    lax.fori_loop(0, width // TILE, pair, 0)


def back_kernel(
    meta_ref, bias_ref, q_ref, k_ref, v_ref, att_grad_ref, lse_ref, delta_ref,
    normed_ref, normed_own_ref, gain_ref, wq_ref, wk_ref, wv_ref,
    wq_out, wk_out, wv_out, shared_out, local_out, gain_out, hist_out,
    s_ref, dp_ref, p_ref, ds_ref, dq_ref, dk_ref, dv_ref, nt_ref,
):
    ctx_at, branch = meta_ref[0], meta_ref[1]
    keys_total, width = k_ref.shape
    tokens = q_ref.shape[0]
    own = tokens - PB
    plen = keys_total - own
    limit = limits(ctx_at, branch, tokens)
    p_ref[plen:, :PB] = jnp.zeros((own, PB), bf16)
    ds_ref[plen:, :PB] = jnp.zeros((own, PB), bf16)

    def pair(g, _):
        lanes = pl.ds(pl.multiple_of(g * TILE, TILE), TILE)
        queries = q_ref[:, lanes]
        keys = k_ref[:, lanes]
        values = v_ref[:, lanes]
        grads = att_grad_ref[:, lanes]
        keys_t = keys.T
        bias = bias_ref[g]
        lse_rows = lse_ref[g]
        delta_rows = delta_ref[g]
        dq_rows, dk_parts, dv_parts, hist_rows = [], [], [], []
        for half in range(2):
            mine = head_lanes(half)
            lse = lse_rows[half : half + 1, :]
            delta = delta_rows[half : half + 1, :]
            scores_to(s_ref, jnp.where(mine, keys, jnp.zeros_like(keys)), queries, plen)
            scores_to(dp_ref, jnp.where(mine, values, jnp.zeros_like(values)), grads, plen)
            add_near(s_ref, bias[half : half + 1, :], ctx_at, branch, plen)

            def block(i, _):
                rows = pl.ds(pl.multiple_of(i * TILE, TILE), TILE)
                allowed = row_steps(i * TILE, TILE, tokens) < limit
                p = jnp.where(allowed, jnp.exp(s_ref[rows, :] - lse), 0.0)
                p_ref[rows, :] = p.astype(bf16)
                ds_ref[rows, :] = (p * (dp_ref[rows, :] - delta)).astype(bf16)
                return 0

            lax.fori_loop(0, plen // TILE, block, 0)
            for i in range(own // TILE):
                rows = slice(plen + i * TILE, plen + (i + 1) * TILE)
                allowed = own_allowed(i * TILE, TILE, own)
                p = jnp.where(allowed, jnp.exp(s_ref[rows, PB:] - lse[:, PB:]), 0.0)
                p_ref[rows, PB:] = p.astype(bf16)
                ds_ref[rows, PB:] = (p * (dp_ref[rows, PB:] - delta[:, PB:])).astype(bf16)

            hist_out[g * 2 + half] = jnp.zeros((8, TILE), f32)
            for first_row, first_lane, gap, guarded in near_tiles(ctx_at, branch, plen):
                def work(first_row=first_row, first_lane=first_lane, gap=gap):
                    rows = pl.ds(first_row if isinstance(first_row, int) else pl.multiple_of(first_row, 16), TILE)
                    tile = ds_ref[rows, first_lane : first_lane + TILE].astype(f32)
                    tile = jnp.where(near_index(gap) < TILE, tile, 0.0)
                    back = lax.broadcasted_iota(jnp.int32, (TILE, TILE), 1) + lax.broadcasted_iota(
                        jnp.int32, (TILE, TILE), 0
                    )
                    index = (back - gap) & (TILE - 1)
                    tile = jnp.take_along_axis(tile, index, axis=1)
                    hist_out[g * 2 + half] += fold8(tile, jnp.sum)

                if guarded:
                    pl.when(ctx_at > 0)(work)
                else:
                    work()

            ds = ds_ref[...]
            dv_parts.append(dot_nn(p_ref[...], grads))
            dk_parts.append(dot_nn(ds, queries))
            dq_rows.append(dot_nn(keys_t[half * 64 : half * 64 + 64, :], ds))
        first = head_lanes(0)
        dv_ref[:, lanes] = jnp.where(first, dv_parts[0], dv_parts[1]).astype(bf16)
        dk_ref[:, lanes] = jnp.where(first, dk_parts[0], dk_parts[1]).astype(bf16)
        dq_ref[:, lanes] = jnp.concatenate(dq_rows, axis=0).T.astype(bf16)
        return 0

    lax.fori_loop(0, width // TILE, pair, 0)

    nt_ref[:, :plen] = normed_ref[...].T
    nt_ref[:, plen:] = normed_own_ref[PB:, :].T
    gain = gain_ref[...].astype(f32)

    def column(i, _):
        cols = pl.ds(pl.multiple_of(i * 256, 256), 256)
        wk_out[:, cols] = dot_nn(nt_ref[...], dk_ref[:, cols]).astype(wk_out.dtype)
        wv_out[:, cols] = dot_nn(nt_ref[...], dv_ref[:, cols]).astype(wv_out.dtype)
        wq_out[:, cols] = dot_tn(normed_own_ref[...], dq_ref[:, cols]).astype(wq_out.dtype)
        part = dot_nt(dk_ref[...], wk_ref[cols, :]) + dot_nt(dv_ref[...], wv_ref[cols, :])
        query_part = dot_nt(dq_ref[...], wq_ref[cols, :])
        shared_out[:, cols] = part[:plen].astype(bf16)
        local_out[:PB, cols] = query_part[:PB]
        local = query_part[PB:] + part[plen:]
        local_out[PB:, cols] = local
        gain_sum = jnp.sum(part[:plen] * normed_ref[:, cols].astype(f32), axis=0, keepdims=True)
        gain_sum += jnp.sum(query_part[:PB] * normed_own_ref[:PB, cols].astype(f32), axis=0, keepdims=True)
        gain_sum += jnp.sum(local * normed_own_ref[PB:, cols].astype(f32), axis=0, keepdims=True)
        gain_out[:, cols] = gain_sum / gain_ref[:, cols].astype(f32)
        return 0

    lax.fori_loop(0, width // 256, column, 0)


def input_kernel(x_ref, gain_ref, shared_ref, local_ref, hidden_grad_ref, out_ref):
    for first, extra in ((0, True), (PB, False)):
        rows = slice(first, PB if extra else x_ref.shape[0])
        x = x_ref[rows, :].astype(f32)
        inverse = inverse_rms(x)
        grad = local_ref[rows, :]
        if extra:
            grad = grad + shared_ref[...].astype(f32)
        through = grad * gain_ref[...].astype(f32)
        scaled = x * inverse
        shared = jnp.mean(through * scaled, axis=1, keepdims=True)
        out_ref[rows, :] = hidden_grad_ref[rows, :] + inverse * (through - scaled * shared)


def layer_kernel(result_ref, slot_row, hidden_ref, gate_ref, out_ref):
    slots = result_ref.shape[0]
    tokens = hidden_ref.shape[0]
    place = lax.broadcasted_iota(jnp.int32, (slots, tokens), 0) == slot_row[...]
    returned = dot_tn(place.astype(bf16), result_ref[...])
    out_ref[...] = (hidden_ref[...] + gate_ref[...] * returned).astype(bf16)


def exchange(rows, experts):
    slots, width = rows.shape
    arrived = lax.all_to_all(
        rows.reshape(experts, slots // experts, width),
        ("ctx", "expert"), split_axis=0, concat_axis=0, tiled=True,
    )
    return arrived.reshape(slots, width)


def body(
    inputs, cotangent, route, arrival, branch, attn_gain, query_weight, key_weight, value_weight,
    output_weight, rel_table, moe_gain, router_weight, expert_in, expert_out,
):
    x = inputs[0]
    cot = cotangent[0]
    tokens, width = x.shape
    own = tokens - PB
    buckets, heads = rel_table.shape
    experts = router_weight.shape[1]
    capacity = 9 * tokens // (8 * experts)
    slots = experts * capacity
    ctx_count = lax.axis_size("ctx")
    dp_count = lax.axis_size("dp")
    ctx_at = lax.axis_index("ctx")
    plen = PB * ctx_count
    keys_total = plen + own
    hidden_units = expert_in.shape[2]
    pairs = width // TILE
    meta = jnp.stack(
        [
            ctx_at,
            branch[0, 0],
            ctx_at * lax.axis_size("expert") + lax.axis_index("expert"),
            lax.axis_index("dp"),
        ]
    ).astype(jnp.int32)
    attn_gain_row = attn_gain.reshape(1, width)
    moe_gain_row = moe_gain.reshape(1, width)
    onehot = bucket_onehot(buckets)
    by_distance = jnp.dot(onehot, rel_table.astype(f32), precision=lax.Precision.HIGHEST).T
    by_distance = by_distance - by_distance[:, TILE - 1 :]
    bias = jnp.pad(by_distance.reshape(pairs, 2, TILE), ((0, 0), (0, 6), (0, 0)))
    router_wide = jnp.pad(router_weight, ((0, 0), (0, TILE - experts)))
    route_col = route[0]
    route_row = route_col.reshape(1, tokens)
    arrive_row = arrival[0]
    arrive_col = arrive_row.reshape(tokens, 1)

    prompt_x = lax.all_gather(x[:PB], "ctx", axis=0, tiled=True)

    slot_row, cot_rows = pl.pallas_call(
        functools.partial(slot_kernel, capacity),
        out_shape=[shape((1, tokens), jnp.int32), shape((slots, width), bf16)],
        in_specs=[vmem()] * 5,
        out_specs=[vmem()] * 2,
        compiler_params=params(),
        cost_estimate=cost(2 * slots * tokens * width, 2 * (slots + tokens) * width),
        name="slots",
    )(route_col, route_row, arrive_col, arrive_row, cot)
    cot_sent = exchange(cot_rows, experts)

    normed_own, queries, own_keys, own_values = pl.pallas_call(
        own_kernel,
        out_shape=[
            shape((tokens, width), bf16), shape((tokens, width), bf16),
            shape((own, width), bf16), shape((own, width), bf16),
        ],
        in_specs=[vmem()] * 5,
        out_specs=[vmem()] * 4,
        compiler_params=params(),
        cost_estimate=cost(4 * tokens * width * width, 6 * width * width),
        name="own_rows",
    )(x, attn_gain_row, query_weight, key_weight, value_weight)

    cot_all = lax.all_gather(cot_sent, "dp", axis=0, tiled=True)

    normed_all, keys, values, att, lse = pl.pallas_call(
        attend_kernel,
        out_shape=[
            shape((plen, width), bf16),
            shape((keys_total, width), bf16),
            shape((keys_total, width), bf16),
            shape((width, tokens), bf16),
            shape((pairs, 8, tokens), f32),
        ],
        in_specs=[smem()] + [vmem()] * 8,
        out_specs=[vmem()] * 5,
        scratch_shapes=[
            pltpu.VMEM((keys_total, tokens), f32),
            pltpu.VMEM((keys_total, tokens), bf16),
        ],
        compiler_params=params(),
        cost_estimate=cost(30 * keys_total * tokens * width, 10 * width * width),
        name="attend",
    )(meta, bias, prompt_x, attn_gain_row, queries, own_keys, own_values, key_weight, value_weight)

    hidden, moe_rows, gate = pl.pallas_call(
        lambda *refs: route_kernel(*refs[:7], experts, *refs[7:]),
        out_shape=[
            shape((tokens, width), f32), shape((slots, width), bf16), shape((tokens, 1), f32),
        ],
        in_specs=[vmem()] * 7,
        out_specs=[vmem()] * 3,
        compiler_params=params(),
        cost_estimate=cost(2 * tokens * width * (width + slots), 8 * tokens * width),
        name="route",
    )(att, x, output_weight, moe_gain_row, router_wide, route_col, slot_row)
    rows_sent = exchange(moe_rows, experts)
    rows_all = lax.all_gather(rows_sent, "dp", axis=0, tiled=True)

    steps = hidden_units // width
    whole_rows = pl.BlockSpec((slots, width), lambda i: (0, 0))
    result, row_grad, router_part = pl.pallas_call(
        functools.partial(expert_kernel, experts),
        grid=(steps,),
        out_shape=[shape((slots, width), bf16), shape((slots, width), bf16), shape((TILE, width), f32)],
        in_specs=[
            smem(), whole_rows, whole_rows,
            pl.BlockSpec((width, width), lambda i: (0, i)),
            pl.BlockSpec((width, width), lambda i: (i, 0)),
            pl.BlockSpec((width, TILE), lambda i: (0, 0)),
        ],
        out_specs=[whole_rows, whole_rows, pl.BlockSpec((TILE, width), lambda i: (0, 0))],
        scratch_shapes=[
            pltpu.VMEM((slots, TILE), f32), pltpu.VMEM((slots, width), bf16),
            pltpu.VMEM((slots, width), f32), pltpu.VMEM((slots, width), f32),
        ],
        compiler_params=params(),
        cost_estimate=cost(8 * slots * width * hidden_units, 4 * width * hidden_units),
        name="expert",
    )(meta, rows_sent, cot_sent, expert_in[0], expert_out[0], router_wide)

    grad_back = exchange(row_grad, experts)
    result_back = exchange(result, experts)

    hidden_grad, wo_part, att_grad, delta, moe_gain_part = pl.pallas_call(
        hidden_kernel,
        out_shape=[
            shape((tokens, width), f32), shape((width, width), bf16), shape((tokens, width), bf16),
            shape((pairs, 8, tokens), f32), shape((1, width), f32),
        ],
        in_specs=[vmem()] * 7,
        out_specs=[vmem()] * 5,
        scratch_shapes=[pltpu.VMEM((tokens, width), bf16), pltpu.VMEM((width, tokens), bf16)],
        compiler_params=params(),
        cost_estimate=cost(8 * tokens * width * width, 12 * tokens * width),
        name="hidden_back",
    )(grad_back, slot_row, hidden, cot, moe_gain_row, att, output_weight)

    wq_part, wk_part, wv_part, shared_part, local_grad, attn_gain_part, hist = pl.pallas_call(
        back_kernel,
        out_shape=[
            shape((width, width), bf16), shape((width, width), bf16), shape((width, width), bf16),
            shape((plen, width), bf16), shape((tokens, width), f32), shape((1, width), f32),
            shape((heads, 8, TILE), f32),
        ],
        in_specs=[smem()] + [vmem()] * 13,
        out_specs=[vmem()] * 7,
        scratch_shapes=[
            pltpu.VMEM((keys_total, tokens), f32),
            pltpu.VMEM((keys_total, tokens), f32),
            pltpu.VMEM((keys_total, tokens), bf16),
            pltpu.VMEM((keys_total, tokens), bf16),
            pltpu.VMEM((tokens, width), bf16),
            pltpu.VMEM((keys_total, width), bf16),
            pltpu.VMEM((keys_total, width), bf16),
            pltpu.VMEM((width, keys_total), bf16),
        ],
        compiler_params=params(),
        cost_estimate=cost(60 * keys_total * tokens * width, 20 * width * width),
        name="attend_back",
    )(
        meta, bias, queries, keys, values, att_grad, lse, delta,
        normed_all, normed_own, attn_gain_row, query_weight, key_weight, value_weight,
    )

    shared_grad = lax.psum_scatter(shared_part, "ctx", scatter_dimension=0, tiled=True)
    weights = lax.psum(
        jnp.concatenate([wq_part, wk_part, wv_part, wo_part], axis=0), ("dp", "ctx", "expert")
    )
    small = lax.psum(
        jnp.concatenate(
            [
                attn_gain_part,
                moe_gain_part,
                router_part[:experts],
                jnp.sum(hist, axis=1).reshape(heads * TILE // width, width),
            ]
        ),
        ("dp", "ctx", "expert"),
    )

    slice_width = hidden_units // dp_count
    rows_step = pl.BlockSpec((slots, width), lambda i, meta: (i, 0))
    in_grad, out_grad = pl.pallas_call(
        functools.partial(expert_grad_kernel, experts),
        grid_spec=pltpu.PrefetchScalarGridSpec(
            num_scalar_prefetch=1,
            grid=(dp_count,),
            in_specs=[
                rows_step, rows_step,
                pl.BlockSpec((width, slice_width), lambda i, meta: (0, meta[3])),
                pl.BlockSpec((slice_width, width), lambda i, meta: (meta[3], 0)),
                pl.BlockSpec((width, TILE), lambda i, meta: (0, 0)),
            ],
            out_specs=[
                pl.BlockSpec((width, slice_width), lambda i, meta: (0, 0)),
                pl.BlockSpec((slice_width, width), lambda i, meta: (0, 0)),
            ],
        ),
        out_shape=[shape((width, slice_width), f32), shape((slice_width, width), f32)],
        compiler_params=params(),
        cost_estimate=cost(8 * dp_count * slots * width * slice_width, 8 * width * slice_width),
        name="expert_grads",
    )(meta, rows_all, cot_all, expert_in[0], expert_out[0], router_wide)

    layer_out = pl.pallas_call(
        layer_kernel,
        out_shape=shape((tokens, width), bf16),
        in_specs=[vmem()] * 4,
        out_specs=vmem(),
        compiler_params=params(),
        cost_estimate=cost(2 * tokens * width * slots, 8 * tokens * width),
        name="layer_out",
    )(result_back, slot_row, hidden, gate)

    input_grad = pl.pallas_call(
        input_kernel,
        out_shape=shape((tokens, width), f32),
        in_specs=[vmem()] * 5,
        out_specs=vmem(),
        compiler_params=params(),
        cost_estimate=cost(20 * tokens * width, 14 * tokens * width),
        name="input_back",
    )(x, attn_gain_row, shared_grad, local_grad, hidden_grad)

    weights = weights.astype(f32).reshape(4, width, width)
    router_grad = small[2 : 2 + experts].T
    hist_sum = small[2 + experts :].reshape(heads, TILE)
    last = onehot[:, buckets - 1 :]
    spread = jnp.concatenate([onehot[:, : buckets - 1], last - 1.0], axis=1)
    table_grad = jnp.dot(spread.T, hist_sum.T, precision=lax.Precision.HIGHEST)
    return (
        layer_out[None],
        input_grad[None],
        small[0],
        weights[0],
        weights[1],
        weights[2],
        weights[3],
        table_grad,
        small[1],
        router_grad,
        in_grad[None],
        out_grad[None],
    )


def solution(mesh):
    grouped = P(("dp", "expert"), "ctx", None)
    placed = (
        grouped, grouped, grouped, grouped, P(("dp", "expert"), "ctx"),
        P(), P(), P(), P(), P(), P(), P(), P(),
        P(("ctx", "expert"), None, None),
        P(("ctx", "expert"), None, None),
    )
    return jax.shard_map(
        body,
        mesh=mesh,
        in_specs=placed,
        out_specs=(
            grouped, grouped, P(), P(), P(), P(), P(), P(), P(), P(),
            P(("ctx", "expert"), None, "dp"),
            P(("ctx", "expert"), "dp", None),
        ),
        check_vma=False,
    )
```

```python
import functools

import jax
import jax.numpy as jnp
from jax import lax
from jax.experimental import pallas as pl
from jax.experimental.pallas import tpu as pltpu
from jax.sharding import PartitionSpec as P

PB = 256
TILE = 128

bucket_edges = (19, 21, 24, 27, 31, 35, 40, 46, 52, 59, 67, 77, 87, 99, 113)
norm_eps = 1e-06
masked_score = -1e30
gelu_scale = 0.7978845608
gelu_cube = 0.044715

bf16 = jnp.bfloat16
f32 = jnp.float32
VMEM_LIMIT = 121 * 512 * 1024


def dot_nn(a, b):
    return jnp.dot(a, b, preferred_element_type=f32)


def dot_nt(a, b):
    return lax.dot_general(a, b, (((1,), (1,)), ((), ())), preferred_element_type=f32)


def dot_tn(a, b):
    return lax.dot_general(a, b, (((0,), (0,)), ((), ())), preferred_element_type=f32)


def two_parts(a):
    high = a.astype(bf16)
    return high, (a - high.astype(f32)).astype(bf16)


def vmem():
    return pl.BlockSpec(memory_space=pltpu.VMEM)


def smem():
    return pl.BlockSpec(memory_space=pltpu.SMEM)


def params():
    return pltpu.CompilerParams(vmem_limit_bytes=VMEM_LIMIT)


def remote_params(number):
    return pltpu.CompilerParams(
        vmem_limit_bytes=VMEM_LIMIT, collective_id=number, has_side_effects=True
    )


def cost(flops, nbytes):
    return pl.CostEstimate(flops=int(flops), bytes_accessed=int(nbytes), transcendentals=0)


def shape(dims, kind):
    return jax.ShapeDtypeStruct(dims, kind)


def inverse_rms(x):
    return lax.rsqrt(jnp.mean(x * x, axis=-1, keepdims=True) + norm_eps)


def bucket_onehot(buckets):
    distance = jnp.arange(TILE, dtype=jnp.int32)
    ids = jnp.minimum(distance, 16)
    for edge in bucket_edges:
        ids = ids + (distance >= edge).astype(jnp.int32)
    return (ids[:, None] == jnp.arange(buckets, dtype=jnp.int32)[None, :]).astype(f32)


def near_index(first):
    rows = lax.broadcasted_iota(jnp.int32, (TILE, TILE), 0)
    lanes = lax.broadcasted_iota(jnp.int32, (TILE, TILE), 1)
    return first + lanes - rows


def near_tiles(ctx_at, plen):
    start = ctx_at * PB
    return (
        (start, 0, 0, False),
        (start, TILE, TILE, False),
        (start + TILE, TILE, 0, False),
        (plen, PB, 0, False),
        (plen, PB + TILE, TILE, False),
        (plen + TILE, PB + TILE, 0, False),
        (start - TILE, 0, TILE, True),
    )


def add_near(s_ref, bias_row, ctx_at, branch, plen):
    source = jnp.broadcast_to(bias_row, (TILE, TILE))
    add_tiles(s_ref, source, ctx_at, near_tiles(ctx_at, plen))

    def window(i, _):
        rows = pl.ds(pl.multiple_of(i * TILE, TILE), TILE)
        lanes = slice(PB, PB + TILE)
        index = jnp.clip(near_index(branch - i * TILE), 0, TILE - 1)
        s_ref[rows, lanes] = s_ref[rows, lanes] + jnp.take_along_axis(source, index, axis=1)
        return 0

    lax.fori_loop(1, plen // TILE, window, 0)


def add_tiles(s_ref, source, ctx_at, tiles):
    for first_row, first_lane, gap, guarded in tiles:
        def work(first_row=first_row, first_lane=first_lane, gap=gap):
            rows = pl.ds(first_row if isinstance(first_row, int) else pl.multiple_of(first_row, 16), TILE)
            lanes = slice(first_lane, first_lane + TILE)
            index = jnp.clip(near_index(gap), 0, TILE - 1)
            s_ref[rows, lanes] = s_ref[rows, lanes] + jnp.take_along_axis(source, index, axis=1)

        if guarded:
            pl.when(ctx_at > 0)(work)
        else:
            work()


def scores_to(s_ref, keys, queries, plen):
    s_ref[:plen, :] = dot_nt(keys[:plen], queries)
    s_ref[plen:, PB:] = dot_nt(keys[plen:], queries[PB:])


def limits(ctx_at, branch, tokens):
    lane = lax.broadcasted_iota(jnp.int32, (1, tokens), 1)
    return jnp.where(lane < PB, ctx_at * PB + lane + 1, branch)


def row_steps(first, count, lanes):
    return first + lax.broadcasted_iota(jnp.int32, (count, lanes), 0)


def own_allowed(first, count, lanes):
    return row_steps(first, count, lanes) <= lax.broadcasted_iota(jnp.int32, (count, lanes), 1)


def head_lanes(half):
    return lax.broadcasted_iota(jnp.int32, (1, TILE), 1) // (TILE // 2) == half


def pick_rows(pieces, lanes):
    row = lax.broadcasted_iota(jnp.int32, (8, lanes), 0)
    return jnp.where(row == 0, pieces[0], jnp.where(row == 1, pieces[1], 0.0))


def fold8(x, op):
    return op(x.reshape(x.shape[0] // 8, 8, x.shape[1]), axis=0)


def owner_device(index):
    cores = lax.axis_size("expert")
    return {"ctx": index // cores, "expert": lax.rem(index, cores)}


def owners():
    cores = lax.axis_size("expert")
    count = cores * lax.axis_size("ctx")
    return count, lax.axis_index("ctx") * cores + lax.axis_index("expert")


def greet_owners():
    count, me = owners()
    barrier = pltpu.get_barrier_semaphore()

    def greet(ahead, _):
        pl.semaphore_signal(
            barrier, inc=1, device_id=owner_device(lax.rem(me + ahead, count)),
            device_id_type=pl.DeviceIdType.MESH,
        )
        return 0

    lax.fori_loop(1, count, greet, 0)
    pl.semaphore_wait(barrier, count - 1)


def block_copy(source, target, sems, ahead):
    count, me = owners()
    peer = lax.rem(me + ahead, count)
    return pltpu.make_async_remote_copy(
        src_ref=source.at[peer], dst_ref=target.at[me],
        send_sem=sems.at[0, ahead - 1], recv_sem=sems.at[1, ahead - 1],
        device_id=owner_device(peer), device_id_type=pl.DeviceIdType.MESH,
    )


def await_blocks(source, target, sems, sent, received):
    def one(ahead, _):
        copy = block_copy(source, target, sems, ahead)
        if received:
            copy.wait_recv()
        if sent:
            copy.wait_send()
        return 0

    lax.fori_loop(1, owners()[0], one, 0)


def place_rows(slot_row, index, block_rows, tokens):
    rows = lax.broadcasted_iota(jnp.int32, (block_rows, tokens), 0) + index * block_rows
    return (rows == slot_row).astype(bf16)


def front_kernel(
    capacity,
    branch_ref, bias_ref, x_ref, cot_ref, gain_ref, route_col, route_row, arrive_col, arrive_row,
    wq_ref, wk_ref, wv_ref,
    slot_out, cot_out, normed_own_out, normed_out, q_ref, k_out, v_out, att_out, lse_out,
    prompt_ref, send_ref, s_ref, p_ref, prompt_sems, cot_sems,
):
    branch = branch_ref[0, 0]
    ctx_at, ctx_count = lax.axis_index("ctx"), lax.axis_size("ctx")
    plen = PB * ctx_count
    tokens, width = x_ref.shape
    own = tokens - PB
    gain = gain_ref[...].astype(f32)
    count, me = owners()
    block_rows = send_ref.shape[1]
    greet_owners()

    def pass_on(step, up):
        block = ctx_at - step if up else ctx_at + step
        ahead = ctx_at + 1 if up else ctx_at - 1
        fits = (block >= 0) & (ahead < ctx_count) if up else (block < ctx_count) & (ahead >= 0)
        source = x_ref.at[pl.ds(0, PB)] if step == 0 else prompt_ref.at[block]
        copy = pltpu.make_async_remote_copy(
            src_ref=source, dst_ref=prompt_ref.at[block],
            send_sem=prompt_sems.at[0, int(up), step], recv_sem=prompt_sems.at[1, int(up), step],
            device_id={"ctx": ahead}, device_id_type=pl.DeviceIdType.MESH,
        )
        return fits, copy

    def arrival(step, up):
        block = ctx_at - step - 1 if up else ctx_at + step + 1
        fits = block >= 0 if up else block < ctx_count
        place = prompt_ref.at[block]
        copy = pltpu.make_async_remote_copy(
            src_ref=place, dst_ref=place,
            send_sem=prompt_sems.at[0, int(up), step], recv_sem=prompt_sems.at[1, int(up), step],
            device_id={"ctx": ctx_at}, device_id_type=pl.DeviceIdType.MESH,
        )
        return fits, block, copy

    for up in (True, False):
        fits, copy = pass_on(0, up)
        pl.when(fits)(copy.start)

    same = route_col[...] == route_row[...]
    earlier = arrive_col[...] < arrive_row[...]
    rank = jnp.sum(jnp.where(same & earlier, 1.0, 0.0), axis=0, keepdims=True).astype(jnp.int32)
    slot = jnp.where(rank < capacity, route_row[...] * block_rows + rank, count * block_rows)
    slot_out[...] = slot

    x = x_ref[...].astype(f32)
    normed_own_out[...] = (x * inverse_rms(x) * gain).astype(bf16)

    def column(i, _):
        cols = pl.ds(pl.multiple_of(i * 256, 256), 256)
        q_ref[:, cols] = dot_nn(normed_own_out[...], wq_ref[:, cols]).astype(bf16)
        k_out[plen:, cols] = dot_nn(normed_own_out[PB:, :], wk_ref[:, cols]).astype(bf16)
        v_out[plen:, cols] = dot_nn(normed_own_out[PB:, :], wv_ref[:, cols]).astype(bf16)
        return 0

    lax.fori_loop(0, width // 256, column, 0)

    def project(block):
        rows = pl.ds(pl.multiple_of(block * PB, PB), PB)

        def prompt_column(i, _):
            cols = pl.ds(pl.multiple_of(i * 256, 256), 256)
            k_out[rows, cols] = dot_nn(normed_out[rows, :], wk_ref[:, cols]).astype(bf16)
            v_out[rows, cols] = dot_nn(normed_out[rows, :], wv_ref[:, cols]).astype(bf16)
            return 0

        lax.fori_loop(0, width // 256, prompt_column, 0)

    normed_out[pl.ds(pl.multiple_of(ctx_at * PB, PB), PB), :] = normed_own_out[:PB, :]
    project(ctx_at)

    def take(block):
        x = prompt_ref[block].astype(f32)
        rows = pl.ds(pl.multiple_of(block * PB, PB), PB)
        normed_out[rows, :] = (x * inverse_rms(x) * gain).astype(bf16)
        project(block)

    for step in range(ctx_count - 1):
        for up in (True, False):
            fits, block, copy = arrival(step, up)
            pl.when(fits)(copy.wait_recv)
            if step < ctx_count - 2:
                fits, copy = pass_on(step + 1, up)
                pl.when(fits)(copy.start)
        if step == ctx_count - 2:
            def send_cot(ahead, _):
                peer = lax.rem(me + ahead, count)
                place = place_rows(slot_out[...], peer, block_rows, tokens)
                send_ref[peer] = dot_nn(place, cot_ref[...]).astype(bf16)
                block_copy(send_ref, cot_out, cot_sems, ahead).start()
                return 0

            lax.fori_loop(1, count, send_cot, 0)
            cot_out[me] = dot_nn(place_rows(slot, me, block_rows, tokens), cot_ref[...]).astype(bf16)
        for up in (True, False):
            fits, block, copy = arrival(step, up)
            pl.when(fits)(functools.partial(take, block))

    p_ref[plen:, :PB] = jnp.zeros((own, PB), bf16)
    limit = limits(ctx_at, branch, tokens)

    def pair(g, _):
        lanes = pl.ds(pl.multiple_of(g * TILE, TILE), TILE)
        queries = q_ref[:, lanes]
        keys = k_out[:, lanes]
        values_t = v_out[:, lanes].T
        bias = bias_ref[g]
        lse_rows, att_rows = [], []
        for half in range(2):
            scores_to(s_ref, jnp.where(head_lanes(half), keys, jnp.zeros_like(keys)), queries, plen)
            add_near(s_ref, bias[half : half + 1, :], ctx_at, branch, plen)

            def top_of(i, top):
                rows = pl.ds(pl.multiple_of(i * TILE, TILE), TILE)
                s = jnp.where(row_steps(i * TILE, TILE, tokens) < limit, s_ref[rows, :], masked_score)
                s_ref[rows, :] = s
                return jnp.maximum(top, fold8(s, jnp.max))

            top = lax.fori_loop(0, plen // TILE, top_of, jnp.full((8, tokens), masked_score, f32))
            own_top = jnp.full((8, own), masked_score, f32)
            for i in range(own // TILE):
                rows = slice(plen + i * TILE, plen + (i + 1) * TILE)
                s = jnp.where(own_allowed(i * TILE, TILE, own), s_ref[rows, PB:], masked_score)
                s_ref[rows, PB:] = s
                own_top = jnp.maximum(own_top, fold8(s, jnp.max))
            top = jnp.concatenate([top[:, :PB], jnp.maximum(top[:, PB:], own_top)], axis=1)
            top = jnp.max(top, axis=0, keepdims=True)

            def weigh(i, total):
                rows = pl.ds(pl.multiple_of(i * TILE, TILE), TILE)
                p = jnp.exp(s_ref[rows, :] - top)
                p_ref[rows, :] = p.astype(bf16)
                return total + fold8(p, jnp.sum)

            total = lax.fori_loop(0, plen // TILE, weigh, jnp.zeros((8, tokens), f32))
            own_total = jnp.zeros((8, own), f32)
            for i in range(own // TILE):
                rows = slice(plen + i * TILE, plen + (i + 1) * TILE)
                p = jnp.exp(s_ref[rows, PB:] - top[:, PB:])
                p_ref[rows, PB:] = p.astype(bf16)
                own_total = own_total + fold8(p, jnp.sum)
            total = jnp.concatenate([total[:, :PB], total[:, PB:] + own_total], axis=1)
            total = jnp.sum(total, axis=0, keepdims=True)
            rows = slice(half * 64, half * 64 + 64)
            att_rows.append((dot_nn(values_t[rows, :], p_ref[...]) / total).astype(bf16))
            lse_rows.append(top + jnp.log(total))
        att_out[lanes, :] = jnp.concatenate(att_rows, axis=0)
        lse_out[g] = pick_rows(lse_rows, tokens)
        return 0

    lax.fori_loop(0, width // TILE, pair, 0)
    await_blocks(send_ref, cot_out, cot_sems, True, True)
    for step in range(ctx_count - 1):
        for up in (True, False):
            fits, copy = pass_on(step, up)
            pl.when(fits)(copy.wait_send)


def router_probs(logits, lane, experts):
    logits = jnp.where(lane < experts, logits, masked_score)
    logits = jnp.exp(logits - jnp.max(logits, axis=1, keepdims=True))
    return logits / jnp.sum(logits, axis=1, keepdims=True)


def gelu_parts(v):
    t = jnp.tanh(gelu_scale * (v + gelu_cube * (v * v * v)))
    half = 0.5 * (1.0 + t)
    slope = half + 0.5 * v * (1.0 - t * t) * (gelu_scale + (3.0 * gelu_scale * gelu_cube) * (v * v))
    return v * half, slope


def expert_kernel(
    experts,
    att_ref, x_ref, wo_ref, gain_ref, router_ref, slot_row, cot_ref, cot_rows, win_hbm, wout_hbm,
    rows_out, router_out, hidden_grad_out, wo_grad_out, att_grad_out, delta_out, gain_grad_out,
    result_out, hidden_ref,
    moe_ref, send_ref, win_ref, wout_ref, group_rows, sent_ref, result_acc, grad_acc,
    grad_send, grad_recv, low_ref, att_t_ref, rows_sems, grad_sems, load_sems,
):
    tokens, width = x_ref.shape
    count, me = owners()
    block_rows = send_ref.shape[1]
    hidden_units = win_ref.shape[1]
    loads = [
        pltpu.make_async_copy(win_hbm, win_ref, load_sems.at[0]),
        pltpu.make_async_copy(wout_hbm, wout_ref, load_sems.at[1]),
    ]
    for copy in loads:
        copy.start()
    greet_owners()

    def column(i, _):
        cols = pl.ds(pl.multiple_of(i * 256, 256), 256)
        hidden_ref[:, cols] = x_ref[:, cols].astype(f32) + dot_tn(att_ref[...], wo_ref[:, cols])
        return 0

    lax.fori_loop(0, width // 256, column, 0)
    hidden = hidden_ref[...]
    moe_ref[...] = (hidden * inverse_rms(hidden) * gain_ref[...].astype(f32)).astype(bf16)

    members = 2 * lax.axis_size("expert") if lax.axis_size("ctx") % 2 == 0 else count
    groups = count // members
    my_group = me // members

    def send_rows(ahead, _):
        peer = lax.rem(me + ahead, count)
        place = place_rows(slot_row[...], peer, block_rows, tokens)
        send_ref[peer] = dot_nn(place, moe_ref[...]).astype(bf16)
        block_copy(send_ref, rows_out, rows_sems, ahead).start()
        return 0

    def send_group(g, _):
        base = lax.rem(my_group + g, groups) * members

        def member(i, _):
            ahead = lax.rem(base + i - me + count, count)
            pl.when(ahead > 0)(lambda: (send_rows(ahead, 0), None)[1])
            return 0

        return lax.fori_loop(0, members, member, 0)

    lax.fori_loop(0, groups, send_group, 0)
    rows_out[me] = dot_nn(place_rows(slot_row[...], me, block_rows, tokens), moe_ref[...]).astype(bf16)

    router_out[...] = jnp.zeros_like(router_out)
    for copy in loads:
        copy.wait()

    def group(g, _):
        base = lax.rem(my_group + g, groups) * members

        def arrive(i, _):
            behind = lax.rem(me - base - i + count, count)
            pl.when(behind > 0)(lambda: block_copy(send_ref, rows_out, rows_sems, behind).wait_recv())
            return 0

        lax.fori_loop(0, members, arrive, 0)
        blocks = pl.ds(base, members)
        size = members * block_rows
        group_rows[...] = rows_out[blocks].reshape(size, width)
        slot_lane = lax.broadcasted_iota(jnp.int32, (size, TILE), 1)
        mine = slot_lane == me
        probs = router_probs(dot_nn(group_rows[...], router_ref[...]), slot_lane, experts)
        gate = jnp.sum(jnp.where(mine, probs, 0.0), axis=1, keepdims=True)
        cot_group = cot_rows[blocks].reshape(size, width).astype(f32)
        sent_ref[...] = (gate * cot_group).astype(bf16)
        result_acc[...] = jnp.zeros_like(result_acc)
        grad_acc[...] = jnp.zeros_like(grad_acc)

        def units(i, _):
            cols = pl.ds(pl.multiple_of(i * width, width), width)
            act, slope = gelu_parts(dot_nn(group_rows[...], win_ref[:, cols]))
            result_acc[...] += dot_nn(act.astype(bf16), wout_ref[cols, :])
            pre_grad = (dot_nt(sent_ref[...], wout_ref[cols, :]) * slope).astype(bf16)
            grad_acc[...] += dot_nt(pre_grad, win_ref[:, cols])
            return 0

        lax.fori_loop(0, hidden_units // width, units, 0)
        result = result_acc[...].astype(bf16)
        gate_grad = jnp.sum(cot_group * result.astype(f32), axis=1, keepdims=True)
        logit_grad = (gate_grad * gate) * (jnp.where(mine, 1.0, 0.0) - probs)
        high, low = two_parts(logit_grad)
        grad = grad_acc[...] + (dot_nt(high, router_ref[...]) + dot_nt(low, router_ref[...]))
        grad_send[blocks] = grad.astype(bf16).reshape(members, block_rows, width)
        gated = (gate * result.astype(f32)).astype(bf16)
        result_out[blocks] = gated.reshape(members, block_rows, width)

        def give(i, _):
            ahead = lax.rem(base + i - me + count, count)

            @pl.when(ahead > 0)
            def _():
                block_copy(grad_send, grad_recv, grad_sems, ahead).start()

            return 0

        lax.fori_loop(0, members, give, 0)
        router_out[...] += dot_tn(high, group_rows[...]) + dot_tn(low, group_rows[...])
        return 0

    lax.fori_loop(0, groups, group, 0)
    grad_recv[me] = grad_send[me]

    slots = count * block_rows
    place = place_rows(slot_row[...], 0, slots, tokens)
    await_blocks(grad_send, grad_recv, grad_sems, False, True)
    moe_grad = dot_tn(place, grad_recv[...].reshape(slots, width))
    hidden = hidden_ref[...]
    inverse = inverse_rms(hidden)
    scaled = hidden * inverse
    gain_grad_out[...] = jnp.sum(moe_grad * scaled, axis=0, keepdims=True)
    through = moe_grad * gain_ref[...].astype(f32)
    shared = jnp.mean(through * scaled, axis=1, keepdims=True)
    hidden_grad = cot_ref[...].astype(f32) + inverse * (through - scaled * shared)
    hidden_grad_out[...] = hidden_grad
    low_ref[...] = hidden_grad.astype(bf16)

    def back_column(i, _):
        cols = pl.ds(pl.multiple_of(i * 256, 256), 256)
        wo_grad = dot_nn(att_ref[...], low_ref[:, cols]).astype(bf16)
        wo_grad_out[:, :, cols] = wo_grad.reshape(width // 16, 16, 256)
        att_grad_out[:, cols] = dot_nt(low_ref[...], wo_ref[cols, :]).astype(bf16)
        att_t_ref[cols, :] = dot_nt(wo_ref[cols, :], low_ref[...]).astype(bf16)
        return 0

    lax.fori_loop(0, width // 256, back_column, 0)

    def pair(g, _):
        rows = pl.ds(pl.multiple_of(g * TILE, TILE), TILE)
        both = att_ref[rows, :].astype(f32) * att_t_ref[rows, :].astype(f32)
        delta_out[g] = pick_rows(
            [jnp.sum(both[:64], axis=0, keepdims=True), jnp.sum(both[64:], axis=0, keepdims=True)],
            tokens,
        )
        return 0

    lax.fori_loop(0, width // TILE, pair, 0)
    await_blocks(send_ref, rows_out, rows_sems, True, False)
    await_blocks(grad_send, grad_recv, grad_sems, True, False)


class Axis:
    def __init__(self, name, size, step=1):
        place = lax.axis_index(name)
        self.name, self.size, self.step, self.place = name, size, step, place
        self.index = lax.rem(place // step, size)

    def at(self, ahead):
        return lax.rem(self.index + ahead, self.size)

    def peer(self, ahead):
        return {self.name: self.place + (self.at(ahead) - self.index) * self.step}


def mesh_axes():
    dp, ctx, expert = lax.axis_size("dp"), lax.axis_size("ctx"), lax.axis_size("expert")
    cores, lines = Axis("expert", expert), Axis("ctx", ctx)
    if dp == 4:
        near, far = Axis("dp", 2, 1), Axis("dp", 2, 2)
        return [[cores, near, far, lines], [cores, far, near, lines]]
    return [[cores, Axis("dp", dp), lines]] * 2


def push(source, target, sems, slot, device):
    copy = pltpu.make_async_remote_copy(
        src_ref=source, dst_ref=target, send_sem=sems.at[0, slot], recv_sem=sems.at[1, slot],
        device_id=device, device_id_type=pl.DeviceIdType.MESH,
    )
    copy.start()
    return copy


def back_kernel(
    experts, plan,
    branch_ref, bias_ref, q_ref, k_hbm, v_hbm, att_grad_ref, lse_ref, delta_ref, normed_hbm, normed_own_ref,
    gain_ref, wq_ref, wk_ref, wv_ref, wo_part_hbm, moe_gain_ref, router_part_hbm, x_hbm, hidden_grad_hbm,
    hidden_hbm, slot_row, result_hbm, rows_hbm, cot_hbm, win_hbm, wout_hbm, router_ref,
    full_ref, small_out, input_out, in_out, out_out, layer_out,
    k_ref, v_ref, normed_ref, s_ref, dp_ref, p_ref, ds_ref, dq_ref, dk_ref, dv_ref, hist_ref, gain_sum,
    local_ref, shared_send, shared_recv, parts_ref, acc_refs, recv_refs, small_ref, small_recv,
    result_recv, win_ref, wout_ref, rows_ref, cot_ref, rows_t,
    block_sems, load_sems, sems, small_sems, shared_sems, result_sems,
):
    group, pieces, lengths = plan
    flows = mesh_axes()
    branch = branch_ref[0, 0]
    ctx_at = lax.axis_index("ctx")
    ctx_count, dp_count = lax.axis_size("ctx"), lax.axis_size("dp")
    tokens, width = q_ref.shape
    own = tokens - PB
    plen = PB * ctx_count
    count, me = owners()
    lines, columns_dp = Axis("ctx", ctx_count), Axis("dp", dp_count)
    whole_axes = [Axis("expert", lax.axis_size("expert")), columns_dp, lines]
    gain = gain_ref[...].astype(f32)
    limit = limits(ctx_at, branch, tokens)
    blocks = ctx_count + 1
    rows_16 = width // 16

    def block_loads(i):
        rows = plen if i == blocks - 1 else pl.multiple_of(lines.at(i + 1) * PB, PB)
        sources = [(k_hbm, k_ref, 0), (v_hbm, v_ref, 1)]
        if i < blocks - 2:
            sources.append((normed_hbm, normed_ref, 2))
        return [
            pltpu.make_async_copy(source.at[pl.ds(rows, PB)], target.at[i % 2], block_sems.at[i, n])
            for source, target, n in sources
        ]

    for copy in block_loads(0):
        copy.start()
    slice_width = win_ref.shape[1]
    part = pl.ds(pl.multiple_of(lax.axis_index("dp") * slice_width, slice_width), slice_width)
    weight_loads = [
        pltpu.make_async_copy(win_hbm.at[:, part], win_ref, load_sems.at[0]),
        pltpu.make_async_copy(wout_hbm.at[part], wout_ref, load_sems.at[1]),
    ]
    own_result = pltpu.make_async_copy(result_hbm.at[me], result_recv.at[me], load_sems.at[2])
    wo_load = pltpu.make_async_copy(wo_part_hbm, parts_ref.at[pl.ds(0, rows_16)], load_sems.at[5 + 2 * dp_count])
    router_load = pltpu.make_async_copy(
        router_part_hbm.at[pl.ds(0, experts)], small_ref.at[pl.ds(0, experts)], load_sems.at[7 + 2 * dp_count]
    )
    for copy in [wo_load, *weight_loads, own_result, router_load]:
        copy.start()

    barrier = pltpu.get_barrier_semaphore()

    def greet(ahead, _):
        pl.semaphore_signal(
            barrier, inc=1, device_id=owner_device(lax.rem(me + ahead, count)),
            device_id_type=pl.DeviceIdType.MESH,
        )
        return 0

    lax.fori_loop(1, count, greet, 0)
    for ahead in range(1, dp_count):
        pl.semaphore_signal(
            barrier, inc=1, device_id=columns_dp.peer(ahead), device_id_type=pl.DeviceIdType.MESH
        )
    pl.semaphore_wait(barrier, count - 1 + dp_count - 1)

    slots_of = {}

    def slot(*key):
        return slots_of.setdefault(key, len(slots_of))

    started = []

    def reduce_start(j, s):
        axis, length = flows[j % 2][s], lengths[s]
        copies = []
        for ahead in range(1, axis.size):
            target = axis.at(ahead)
            if s == 0:
                source = parts_ref.at[pl.ds(j * group + target * length, length)]
            else:
                source = acc_refs[s - 1].at[j, pl.ds(target * length, length)]
            copies.append(
                push(source, recv_refs[s].at[j, ahead - 1], sems, slot("r", j, s, ahead), axis.peer(ahead))
            )
        started.extend(copies)
        return copies

    def base_of(j, s):
        base = j * group
        for t in range(s + 1):
            base = base + flows[j % 2][t].index * lengths[t]
        return base

    def reduce_finish(j, s, copies):
        axis, length = flows[j % 2][s], lengths[s]
        for copy in copies:
            copy.wait_recv()
        last = s == len(lengths) - 1

        def unit(u, _):
            if s == 0:
                total = parts_ref[base_of(j, 0) + u].astype(f32)
            else:
                total = acc_refs[s - 1][j, axis.index * length + u].astype(f32)
            for ahead in range(1, axis.size):
                total = total + recv_refs[s][j, ahead - 1, u].astype(f32)
            if last:
                full_ref[base_of(j, s) + u] = total.astype(bf16)
            else:
                acc_refs[s][j, u] = total.astype(bf16)
            return 0

        lax.fori_loop(0, length, unit, 0)

    def spread_start(j, s):
        axis, length = flows[j % 2][s], lengths[s]
        here = full_ref.at[pl.ds(base_of(j, s), length)]
        copies = [
            push(here, here, sems, slot("s", j, s, ahead), axis.peer(ahead))
            for ahead in range(1, axis.size)
        ]
        started.extend(copies)
        return copies

    def small_slot(s, ahead):
        return sum(axis.size - 1 for axis in whole_axes[:s]) + ahead - 1

    def small_start(s):
        axis = whole_axes[s]
        copies = [
            push(small_ref, small_recv[s].at[ahead - 1], small_sems, small_slot(s, ahead), axis.peer(ahead))
            for ahead in range(1, axis.size)
        ]
        return copies

    def small_finish(s, copies):
        axis = whole_axes[s]
        for copy in copies:
            copy.wait()
        mine = small_ref[...]
        total = jnp.zeros_like(mine)
        for index in range(axis.size):
            piece = mine
            for ahead in range(1, axis.size):
                piece = jnp.where(axis.at(axis.size - ahead) == index, small_recv[s][ahead - 1], piece)
            total = total + piece
        if s == len(whole_axes) - 1:
            small_out[...] = total
        else:
            small_ref[...] = total

    stages = len(lengths)
    early = pieces > 1 and group <= rows_16
    begin = [blocks + j for j in range(pieces)]
    if early:
        begin = [0] + [blocks + j - 1 for j in range(1, pieces)]
    pending = {}

    def advance(time):
        for j in sorted(range(pieces), key=lambda j: begin[j]):
            s = time - begin[j]
            if not 0 <= s < 2 * stages:
                continue
            if s < stages:
                reduce_finish(j, s, pending[j, s])
                if s + 1 < stages:
                    pending[j, s + 1] = reduce_start(j, s + 1)
                else:
                    pending[j, s + 1] = spread_start(j, s)
            else:
                for copy in pending[j, s]:
                    copy.wait_recv()
                if s + 1 < 2 * stages:
                    pending[j, s + 1] = spread_start(j, 2 * stages - 1 - (s + 1))

    def put(first, cols, value):
        rows = value.shape[0]
        parts_ref[first // 16 : (first + rows) // 16, :, cols] = value.astype(bf16).reshape(
            rows // 16, 16, value.shape[1]
        )

    def columns(work):
        def column(i, _):
            work(pl.ds(pl.multiple_of(i * 256, 256), 256))
            return 0

        lax.fori_loop(0, width // 256, column, 0)

    if parts_ref.shape[0] > 4 * rows_16:
        extra = parts_ref.shape[0] - 4 * rows_16
        parts_ref[4 * rows_16 :] = jnp.zeros((extra, 16, width), bf16)
    wo_load.wait()
    if early:
        pending[0, 0] = reduce_start(0, 0)

    def give_result(ahead, _):
        block_copy(result_hbm, result_recv, result_sems, ahead).start()
        return 0

    lax.fori_loop(1, count, give_result, 0)

    shared_copies = []
    shared_slots = shared_send.shape[0]
    hist_ref[...] = jnp.zeros_like(hist_ref)
    gain_sum[...] = jnp.zeros_like(gain_sum)
    for i in range(blocks):
        cont = i == blocks - 1
        at_home = i == blocks - 2
        for copy in block_loads(i):
            copy.wait()
        if i + 1 < blocks:
            for copy in block_loads(i + 1):
                copy.start()
        block = lines.at(i + 1)
        lanes_from = PB if cont else 0
        lanes_used = slice(lanes_from, tokens)
        near = []
        if cont or at_home:
            near = [
                (0, lanes_from, 0, None),
                (0, lanes_from + TILE, TILE, None),
                (TILE, lanes_from + TILE, 0, None),
            ]
        else:
            near = [(TILE, 0, TILE, block == ctx_at - 1)]
        if not cont:
            near += [(first, PB, branch - block * PB - first, None) for first in range(0, PB, TILE)]

        def pair(g, _, i=i, cont=cont, block=block, lanes_used=lanes_used, near=near):
            lanes = pl.ds(pl.multiple_of(g * TILE, TILE), TILE)
            queries = q_ref[lanes_used, lanes]
            grads = att_grad_ref[lanes_used, lanes]
            keys = k_ref[i % 2, :, lanes]
            values = v_ref[i % 2, :, lanes]
            keys_t = keys.T
            bias = bias_ref[g]
            dk_parts, dv_parts, dq_parts = [], [], []
            for half in range(2):
                mine = head_lanes(half)
                lse = lse_ref[g][half : half + 1, lanes_used]
                delta = delta_ref[g][half : half + 1, lanes_used]
                s_ref[:, lanes_used] = dot_nt(jnp.where(mine, keys, jnp.zeros_like(keys)), queries)
                dp_ref[:, lanes_used] = dot_nt(jnp.where(mine, values, jnp.zeros_like(values)), grads)
                source = jnp.broadcast_to(bias[half : half + 1, :], (TILE, TILE))
                for first, lane, gap, when in near:
                    def add(first=first, lane=lane, gap=gap):
                        there = (slice(first, first + TILE), slice(lane, lane + TILE))
                        index = jnp.clip(near_index(gap), 0, TILE - 1)
                        s_ref[there] = s_ref[there] + jnp.take_along_axis(source, index, axis=1)

                    add() if when is None else pl.when(when)(add)
                step = 32
                for first in range(0, PB, step):
                    rows = slice(first, first + step)
                    if cont:
                        allowed = own_allowed(first, step, own)
                    else:
                        allowed = row_steps(block * PB + first, step, tokens) < limit
                    p = jnp.where(allowed, jnp.exp(s_ref[rows, lanes_used] - lse), 0.0)
                    p_ref[rows, lanes_used] = p.astype(bf16)
                    ds_ref[rows, lanes_used] = (p * (dp_ref[rows, lanes_used] - delta)).astype(bf16)
                for first, lane, gap, when in near:
                    def collect(first=first, lane=lane, gap=gap):
                        tile = ds_ref[first : first + TILE, lane : lane + TILE].astype(f32)
                        if not isinstance(gap, int) or gap > 0:
                            tile = jnp.where(near_index(gap) < TILE, tile, 0.0)
                        turn = lax.broadcasted_iota(jnp.int32, (TILE, TILE), 1) + lax.broadcasted_iota(
                            jnp.int32, (TILE, TILE), 0
                        )
                        tile = jnp.take_along_axis(tile, (turn - gap) & (TILE - 1), axis=1)
                        hist_ref[g * 2 + half] += fold8(tile, jnp.sum)

                    collect() if when is None else pl.when(when)(collect)
                ds = ds_ref[:, lanes_used]
                dv_parts.append(dot_nn(p_ref[:, lanes_used], grads))
                dk_parts.append(dot_nn(ds, queries))
                dq_parts.append(dot_nn(keys_t[half * 64 : half * 64 + 64, :], ds))
            dq = jnp.concatenate(dq_parts, axis=0)
            if i == 0:
                dq_ref[lanes, :] = dq
            else:
                dq_ref[lanes, lanes_used] += dq
            mine = head_lanes(0)
            dv_ref[:, lanes] = jnp.where(mine, dv_parts[0], dv_parts[1]).astype(bf16)
            dk_ref[:, lanes] = jnp.where(mine, dk_parts[0], dk_parts[1]).astype(bf16)
            return 0

        lax.fori_loop(0, width // TILE, pair, 0)

        def block_column(cols, i=i, cont=cont, at_home=at_home):
            if cont:
                normed, whole = normed_own_ref[PB:, cols], normed_own_ref[PB:, :]
            elif at_home:
                normed, whole = normed_own_ref[:PB, cols], normed_own_ref[:PB, :]
            else:
                normed, whole = normed_ref[i % 2, :, cols], normed_ref[i % 2]
            wk_part, wv_part = dot_tn(whole, dk_ref[:, cols]), dot_tn(whole, dv_ref[:, cols])
            if i == 0:
                in_out[:, cols] = wk_part
                out_out[:, cols] = wv_part
            elif not cont:
                in_out[:, cols] += wk_part
                out_out[:, cols] += wv_part
            else:
                put(width, cols, out_out[:, cols] + wv_part)
                put(2 * width, cols, in_out[:, cols] + wk_part)
            grad = dot_nt(dk_ref[...], wk_ref[cols, :]) + dot_nt(dv_ref[...], wv_ref[cols, :])
            gain_sum[:, cols] += jnp.sum(grad * normed.astype(f32), axis=0, keepdims=True)
            if cont:
                local_ref[PB:, cols] = grad
            elif at_home:
                local_ref[:PB, cols] = grad
            else:
                shared_send[i % shared_slots, :, cols] = grad.astype(bf16)

        if shared_slots <= i < blocks - 2:
            shared_copies[i - shared_slots].wait_send()
        columns(block_column)
        if i < blocks - 2:
            shared_copies.append(
                push(shared_send.at[i % shared_slots], shared_recv.at[i], shared_sems, i, lines.peer(i + 1))
            )
        if not cont:
            advance(i)
    started.extend(shared_copies[-shared_slots:])

    def ready(j):
        if j > 0 or not early:
            pending[j, 0] = reduce_start(j, 0)

    done = 3 * rows_16
    for j in range(pieces):
        if (j + 1) * group <= done:
            ready(j)
    rows_ref[:tokens, :] = dq_ref[...].T.astype(bf16)

    def query_column(cols):
        put(3 * width, cols, dot_tn(normed_own_ref[...], rows_ref[:tokens, cols]))

    columns(query_column)
    for j in range(pieces):
        if (j + 1) * group > done:
            ready(j)

    def query_grad(cols):
        grad = dot_nt(rows_ref[:tokens, :], wq_ref[cols, :])
        gain_sum[:, cols] += jnp.sum(grad * normed_own_ref[:, cols].astype(f32), axis=0, keepdims=True)
        local_ref[:, cols] += grad

    columns(query_grad)
    small_ref[experts:, :] = jnp.zeros((small_ref.shape[0] - experts, width), f32)
    small_ref[experts : experts + 1, :] = gain_sum[...] / gain
    small_ref[experts + 1 : experts + 2, :] = moe_gain_ref[...]
    router_load.wait()
    per_row = width // TILE
    for head in range(hist_ref.shape[0]):
        row, lane = 2 + experts + head // per_row, head % per_row * TILE
        small_ref[row : row + 1, lane : lane + TILE] = jnp.sum(hist_ref[head], axis=0, keepdims=True)
    small_pending = small_start(0)

    slots = rows_ref.shape[0]

    def grads_of(n, c):
        if c == 0:
            if n == 0:
                for copy in weight_loads:
                    copy.wait()
            loads = [
                pltpu.make_async_copy(rows_hbm.at[n], rows_ref, load_sems.at[3 + 2 * n]),
                pltpu.make_async_copy(cot_hbm.at[n], cot_ref, load_sems.at[4 + 2 * n]),
            ]
            for copy in loads:
                copy.start()
            for copy in loads:
                copy.wait()
            lane = lax.broadcasted_iota(jnp.int32, (slots, TILE), 1)
            rows = rows_ref[...]
            probs = router_probs(dot_nn(rows, router_ref[...]), lane, experts)
            gate = jnp.sum(jnp.where(lane == me, probs, 0.0), axis=1, keepdims=True)
            cot_ref[...] = (gate * cot_ref[...].astype(f32)).astype(bf16)
            rows_t[...] = rows.T
        cols = slice(c * 256, c * 256 + 256)
        act, slope = gelu_parts(dot_nn(rows_ref[...], win_ref[:, cols]))
        pre_grad = (dot_nt(cot_ref[...], wout_ref[cols, :]) * slope).astype(bf16)
        out_part = dot_tn(act.astype(bf16), cot_ref[...])
        in_part = dot_nn(rows_t[...], pre_grad)
        if n == 0:
            out_out[cols, :] = out_part
            in_out[:, cols] = in_part
        else:
            out_out[cols, :] += out_part
            in_out[:, cols] += in_part

    def input_back():
        held = pltpu.make_async_copy(hidden_grad_hbm, input_out, load_sems.at[3 + 2 * dp_count])
        held.start()
        x_load = pltpu.make_async_copy(x_hbm, rows_ref.at[pl.ds(0, tokens)], load_sems.at[6 + 2 * dp_count])
        x_load.start()
        for copy in shared_copies:
            copy.wait_recv()
        held.wait()
        x_load.wait()
        for first, shared_rows in ((0, True), (PB, False)):
            rows = slice(first, PB if shared_rows else tokens)
            x = rows_ref[rows, :].astype(f32)
            inverse = inverse_rms(x)
            grad = local_ref[rows, :]
            if shared_rows:
                for n in range(ctx_count - 1):
                    grad = grad + shared_recv[n].astype(f32)
            through = grad * gain
            scaled = x * inverse
            shared = jnp.mean(through * scaled, axis=1, keepdims=True)
            input_out[rows, :] += inverse * (through - scaled * shared)

    def layer():
        held = pltpu.make_async_copy(hidden_hbm, local_ref, load_sems.at[4 + 2 * dp_count])
        held.start()
        own_result.wait()
        await_blocks(result_hbm, result_recv, result_sems, False, True)
        place = place_rows(slot_row[...], 0, slots, tokens)
        returned = dot_tn(place, result_recv[...].reshape(slots, width))
        held.wait()
        layer_out[...] = (local_ref[...] + returned).astype(bf16)

    work = [functools.partial(grads_of, n, c) for n in range(dp_count) for c in range(slice_width // 256)]
    work += [input_back, layer]
    for time in range(blocks - 1, max(begin) + 2 * stages):
        if time >= blocks:
            advance(time)
        elif early:
            advance(time)
        s = time - blocks
        if 0 <= s < len(whole_axes):
            small_finish(s, small_pending)
            if s + 1 < len(whole_axes):
                small_pending = small_start(s + 1)
        if work:
            work.pop(0)()
    for rest in work:
        rest()
    for copy in started:
        copy.wait_send()
    await_blocks(result_hbm, result_recv, result_sems, True, False)


def tail_plan(sizes, width):
    group = 1
    for size in sizes:
        group *= size
    units = 4 * width // 16
    pieces = -(-units // group)
    lengths, left = [], group
    for size in sizes:
        left //= size
        lengths.append(left)
    return group, pieces, lengths


def body(
    inputs, cotangent, route, arrival, branch, attn_gain, query_weight, key_weight, value_weight,
    output_weight, rel_table, moe_gain, router_weight, expert_in, expert_out,
):
    x = inputs[0]
    cot = cotangent[0]
    tokens, width = x.shape
    own = tokens - PB
    buckets, heads = rel_table.shape
    experts = router_weight.shape[1]
    capacity = 9 * tokens // (8 * experts)
    block_rows = capacity if capacity % 8 == 0 else -(-capacity // 16) * 16
    slots = experts * block_rows
    ctx_count = lax.axis_size("ctx")
    dp_count = lax.axis_size("dp")
    plen = PB * ctx_count
    keys_total = plen + own
    hidden_units = expert_in.shape[2]
    pairs = width // TILE
    attn_gain_row = attn_gain.reshape(1, width)
    moe_gain_row = moe_gain.reshape(1, width)
    onehot = bucket_onehot(buckets)
    by_distance = jnp.dot(onehot, rel_table.astype(f32), precision=lax.Precision.HIGHEST).T
    by_distance = by_distance - by_distance[:, TILE - 1 :]
    bias = jnp.pad(by_distance.reshape(pairs, 2, TILE), ((0, 0), (0, 6), (0, 0)))
    router_wide = jnp.pad(router_weight, ((0, 0), (0, TILE - experts)))
    route_col = route[0]
    route_row = route_col.reshape(1, tokens)
    arrive_row = arrival[0]
    arrive_col = arrive_row.reshape(tokens, 1)
    blocks = shape((experts, block_rows, width), bf16)
    block_space = pltpu.VMEM((experts, block_rows, width), bf16)
    block_sems = pltpu.SemaphoreType.DMA((2, experts - 1))
    any_space = pl.BlockSpec(memory_space=pl.ANY)

    slot_row, cot_sent, normed_own, normed_all, queries, keys, values, att, lse = pl.pallas_call(
        functools.partial(front_kernel, capacity),
        out_shape=[
            shape((1, tokens), jnp.int32),
            blocks,
            shape((tokens, width), bf16),
            shape((plen, width), bf16),
            shape((tokens, width), bf16),
            shape((keys_total, width), bf16),
            shape((keys_total, width), bf16),
            shape((width, tokens), bf16),
            shape((pairs, 8, tokens), f32),
        ],
        in_specs=[smem()] + [vmem()] * 11,
        out_specs=[vmem()] * 9,
        scratch_shapes=[
            pltpu.VMEM((ctx_count, PB, width), bf16),
            block_space,
            pltpu.VMEM((keys_total, tokens), f32),
            pltpu.VMEM((keys_total, tokens), bf16),
            pltpu.SemaphoreType.DMA((2, 2, ctx_count - 1)),
            block_sems,
        ],
        compiler_params=remote_params(1),
        cost_estimate=cost(40 * keys_total * tokens * width, 20 * width * width),
        name="front",
    )(
        branch, bias, x, cot, attn_gain_row, route_col, route_row, arrive_col, arrive_row,
        query_weight, key_weight, value_weight,
    )
    cot_all = lax.all_gather(cot_sent, "dp", axis=0, tiled=False)

    members = 2 * lax.axis_size("expert") if ctx_count % 2 == 0 else experts
    group_rows = members * block_rows
    (
        rows_sent, router_part, hidden_grad, wo_part, att_grad, delta, moe_gain_part,
        result, hidden,
    ) = pl.pallas_call(
        functools.partial(expert_kernel, experts),
        out_shape=[
            blocks, shape((TILE, width), f32), shape((tokens, width), f32), shape((width // 16, 16, width), bf16),
            shape((tokens, width), bf16), shape((pairs, 8, tokens), f32), shape((1, width), f32),
            blocks, shape((tokens, width), f32),
        ],
        in_specs=[vmem()] * 8 + [any_space] * 2,
        out_specs=[vmem()] * 9,
        scratch_shapes=[
            pltpu.VMEM((tokens, width), bf16),
            block_space,
            pltpu.VMEM((width, hidden_units), bf16),
            pltpu.VMEM((hidden_units, width), bf16),
            pltpu.VMEM((group_rows, width), bf16),
            pltpu.VMEM((group_rows, width), bf16),
            pltpu.VMEM((group_rows, width), f32),
            pltpu.VMEM((group_rows, width), f32),
            block_space, block_space,
            pltpu.VMEM((tokens, width), bf16),
            pltpu.VMEM((width, tokens), bf16),
            block_sems, block_sems,
            pltpu.SemaphoreType.DMA((2,)),
        ],
        compiler_params=remote_params(2),
        cost_estimate=cost(8 * slots * width * hidden_units, 12 * width * hidden_units),
        name="expert",
    )(
        att, x, output_weight, moe_gain_row, router_wide, slot_row, cot, cot_sent,
        expert_in[0], expert_out[0],
    )
    rows_all = lax.all_gather(rows_sent, "dp", axis=0, tiled=False)
    att_grad, cot_all = lax.optimization_barrier((att_grad, cot_all))

    expert_count = lax.axis_size("expert")
    dp_sizes = [2, 2] if dp_count == 4 else [dp_count]
    sizes = [expert_count, *dp_sizes, ctx_count]
    plan = tail_plan(sizes, width)
    group, pieces, lengths = plan
    units = group * pieces

    table_rows = heads * TILE // width
    small_rows = -(-(2 + experts + table_rows) // 8) * 8
    slice_width = hidden_units // dp_count
    weights, small, input_grad, in_grad, out_grad, layer_out = pl.pallas_call(
        functools.partial(back_kernel, experts, plan),
        out_shape=[
            shape((units, 16, width), bf16), shape((small_rows, width), f32), shape((tokens, width), f32),
            shape((width, slice_width), f32), shape((slice_width, width), f32), shape((tokens, width), bf16),
        ],
        in_specs=[
            smem(), vmem(), vmem(), any_space, any_space, vmem(), vmem(), vmem(), any_space, vmem(),
            vmem(), vmem(), vmem(), vmem(), any_space, vmem(), any_space, any_space, any_space,
            any_space, vmem(), any_space, any_space, any_space, any_space, any_space, vmem(),
        ],
        out_specs=[vmem()] * 6,
        scratch_shapes=[
            pltpu.VMEM((2, PB, width), bf16),
            pltpu.VMEM((2, PB, width), bf16),
            pltpu.VMEM((2, PB, width), bf16),
            pltpu.VMEM((PB, tokens), f32),
            pltpu.VMEM((PB, tokens), f32),
            pltpu.VMEM((PB, tokens), bf16),
            pltpu.VMEM((PB, tokens), bf16),
            pltpu.VMEM((width, tokens), f32),
            pltpu.VMEM((PB, width), bf16),
            pltpu.VMEM((PB, width), bf16),
            pltpu.VMEM((heads, 8, TILE), f32),
            pltpu.VMEM((1, width), f32),
            pltpu.VMEM((tokens, width), f32),
            pltpu.VMEM((min(ctx_count - 1, 3), PB, width), bf16),
            pltpu.VMEM((ctx_count - 1, PB, width), bf16),
            pltpu.VMEM((units, 16, width), bf16),
            [pltpu.VMEM((pieces, length, 16, width), bf16) for length in lengths[:-1]],
            [
                pltpu.VMEM((pieces, size - 1, length, 16, width), bf16)
                for size, length in zip(sizes, lengths)
            ],
            pltpu.VMEM((small_rows, width), f32),
            [pltpu.VMEM((size - 1, small_rows, width), f32) for size in (expert_count, dp_count, ctx_count)],
            block_space,
            pltpu.VMEM((width, slice_width), bf16),
            pltpu.VMEM((slice_width, width), bf16),
            pltpu.VMEM((slots, width), bf16),
            pltpu.VMEM((slots, width), bf16),
            pltpu.VMEM((width, slots), bf16),
            pltpu.SemaphoreType.DMA((ctx_count + 1, 3)),
            pltpu.SemaphoreType.DMA((8 + 2 * dp_count,)),
            pltpu.SemaphoreType.DMA((2, 2 * pieces * sum(size - 1 for size in sizes))),
            pltpu.SemaphoreType.DMA((2, expert_count + dp_count + ctx_count - 3)),
            pltpu.SemaphoreType.DMA((2, ctx_count - 1)),
            block_sems,
        ],
        compiler_params=remote_params(0),
        cost_estimate=cost(
            8 * dp_count * slots * width * slice_width + 80 * keys_total * tokens * width,
            60 * width * slice_width,
        ),
        name="back",
    )(
        branch, bias, queries, keys, values, att_grad, lse, delta, normed_all, normed_own,
        attn_gain_row, query_weight, key_weight, value_weight, wo_part, moe_gain_part, router_part, x,
        hidden_grad, hidden, slot_row, result,
        rows_all.reshape(dp_count, slots, width), cot_all.reshape(dp_count, slots, width),
        expert_in[0], expert_out[0], router_wide,
    )

    weights = weights.reshape(units * 16, width)[: 4 * width].astype(f32).reshape(4, width, width)
    router_grad = small[:experts].T
    hist_sum = small[2 + experts : 2 + experts + table_rows].reshape(heads, TILE)
    last = onehot[:, buckets - 1 :]
    spread = jnp.concatenate([onehot[:, : buckets - 1], last - 1.0], axis=1)
    table_grad = jnp.dot(spread.T, hist_sum.T, precision=lax.Precision.HIGHEST)
    return (
        layer_out[None],
        input_grad[None],
        small[experts],
        weights[3],
        weights[2],
        weights[1],
        weights[0],
        table_grad,
        small[experts + 1],
        router_grad,
        in_grad[None],
        out_grad[None],
    )


def solution(mesh):
    grouped = P(("dp", "expert"), "ctx", None)
    placed = (
        grouped, grouped, grouped, grouped, P(("dp", "expert"), "ctx"),
        P(), P(), P(), P(), P(), P(), P(), P(),
        P(("ctx", "expert"), None, None),
        P(("ctx", "expert"), None, None),
    )
    return jax.shard_map(
        body,
        mesh=mesh,
        in_specs=placed,
        out_specs=(
            grouped, grouped, P(), P(), P(), P(), P(), P(), P(), P(),
            P(("ctx", "expert"), None, "dp"),
            P(("ctx", "expert"), "dp", None),
        ),
        check_vma=False,
    )
```

```python
import functools

import jax
import jax.numpy as jnp
from jax import lax
from jax.experimental import pallas as pl
from jax.experimental.pallas import tpu as pltpu
from jax.sharding import PartitionSpec as P

PB = 256
TILE = 128
CHUNKS = 8
SHARED_CUTS = 4

bucket_edges = (19, 21, 24, 27, 31, 35, 40, 46, 52, 59, 67, 77, 87, 99, 113)
norm_eps = 1e-06
masked_score = -1e30
gelu_scale = 0.7978845608
gelu_cube = 0.044715

bf16 = jnp.bfloat16
f32 = jnp.float32
VMEM_LIMIT = 121 * 512 * 1024


def dot_nn(a, b):
    return jnp.dot(a, b, preferred_element_type=f32)


def dot_nt(a, b):
    return lax.dot_general(a, b, (((1,), (1,)), ((), ())), preferred_element_type=f32)


def dot_tn(a, b):
    return lax.dot_general(a, b, (((0,), (0,)), ((), ())), preferred_element_type=f32)


def two_parts(a):
    high = a.astype(bf16)
    return high, (a - high.astype(f32)).astype(bf16)


def vmem():
    return pl.BlockSpec(memory_space=pltpu.VMEM)


def smem():
    return pl.BlockSpec(memory_space=pltpu.SMEM)


def params():
    return pltpu.CompilerParams(vmem_limit_bytes=VMEM_LIMIT)


def remote_params(number):
    return pltpu.CompilerParams(
        vmem_limit_bytes=VMEM_LIMIT, collective_id=number, has_side_effects=True
    )


def cost(flops, nbytes):
    return pl.CostEstimate(flops=int(flops), bytes_accessed=int(nbytes), transcendentals=0)


def shape(dims, kind):
    return jax.ShapeDtypeStruct(dims, kind)


def inverse_rms(x):
    return lax.rsqrt(jnp.mean(x * x, axis=-1, keepdims=True) + norm_eps)


def bucket_onehot(buckets):
    distance = jnp.arange(TILE, dtype=jnp.int32)
    ids = jnp.minimum(distance, 16)
    for edge in bucket_edges:
        ids = ids + (distance >= edge).astype(jnp.int32)
    return (ids[:, None] == jnp.arange(buckets, dtype=jnp.int32)[None, :]).astype(f32)


def near_index(first):
    rows = lax.broadcasted_iota(jnp.int32, (TILE, TILE), 0)
    lanes = lax.broadcasted_iota(jnp.int32, (TILE, TILE), 1)
    return first + lanes - rows


def near_tiles(ctx_at, plen):
    start = ctx_at * PB
    return (
        (start, 0, 0, False),
        (start, TILE, TILE, False),
        (start + TILE, TILE, 0, False),
        (plen, PB, 0, False),
        (plen, PB + TILE, TILE, False),
        (plen + TILE, PB + TILE, 0, False),
        (start - TILE, 0, TILE, True),
    )


def add_near(s_ref, bias_row, ctx_at, branch, plen):
    source = jnp.broadcast_to(bias_row, (TILE, TILE))
    add_tiles(s_ref, source, ctx_at, near_tiles(ctx_at, plen))

    def window(i, _):
        rows = pl.ds(pl.multiple_of(i * TILE, TILE), TILE)
        lanes = slice(PB, PB + TILE)
        index = jnp.clip(near_index(branch - i * TILE), 0, TILE - 1)
        s_ref[rows, lanes] = s_ref[rows, lanes] + jnp.take_along_axis(source, index, axis=1)
        return 0

    lax.fori_loop(1, plen // TILE, window, 0)


def add_tiles(s_ref, source, ctx_at, tiles):
    for first_row, first_lane, gap, guarded in tiles:
        def work(first_row=first_row, first_lane=first_lane, gap=gap):
            rows = pl.ds(first_row if isinstance(first_row, int) else pl.multiple_of(first_row, 16), TILE)
            lanes = slice(first_lane, first_lane + TILE)
            index = jnp.clip(near_index(gap), 0, TILE - 1)
            s_ref[rows, lanes] = s_ref[rows, lanes] + jnp.take_along_axis(source, index, axis=1)

        if guarded:
            pl.when(ctx_at > 0)(work)
        else:
            work()


def scores_to(s_ref, keys, queries, plen):
    s_ref[:plen, :] = dot_nt(keys[:plen], queries)
    s_ref[plen:, PB:] = dot_nt(keys[plen:], queries[PB:])


def limits(ctx_at, branch, tokens):
    lane = lax.broadcasted_iota(jnp.int32, (1, tokens), 1)
    return jnp.where(lane < PB, ctx_at * PB + lane + 1, branch)


def row_steps(first, count, lanes):
    return first + lax.broadcasted_iota(jnp.int32, (count, lanes), 0)


def own_allowed(first, count, lanes):
    return row_steps(first, count, lanes) <= lax.broadcasted_iota(jnp.int32, (count, lanes), 1)


def head_lanes(half):
    return lax.broadcasted_iota(jnp.int32, (1, TILE), 1) // (TILE // 2) == half


def pick_rows(pieces, lanes):
    row = lax.broadcasted_iota(jnp.int32, (8, lanes), 0)
    return jnp.where(row == 0, pieces[0], jnp.where(row == 1, pieces[1], 0.0))


def fold8(x, op):
    return op(x.reshape(x.shape[0] // 8, 8, x.shape[1]), axis=0)


def owner_device(index):
    cores = lax.axis_size("expert")
    return {"ctx": index // cores, "expert": lax.rem(index, cores)}


def owners():
    cores = lax.axis_size("expert")
    count = cores * lax.axis_size("ctx")
    return count, lax.axis_index("ctx") * cores + lax.axis_index("expert")


def greet_owners():
    count, me = owners()
    barrier = pltpu.get_barrier_semaphore()

    def greet(ahead, _):
        pl.semaphore_signal(
            barrier, inc=1, device_id=owner_device(lax.rem(me + ahead, count)),
            device_id_type=pl.DeviceIdType.MESH,
        )
        return 0

    lax.fori_loop(1, count, greet, 0)
    pl.semaphore_wait(barrier, count - 1)


def block_copy(source, target, sems, ahead):
    count, me = owners()
    peer = lax.rem(me + ahead, count)
    return pltpu.make_async_remote_copy(
        src_ref=source.at[peer], dst_ref=target.at[me],
        send_sem=sems.at[0, ahead - 1], recv_sem=sems.at[1, ahead - 1],
        device_id=owner_device(peer), device_id_type=pl.DeviceIdType.MESH,
    )


def await_blocks(source, target, sems, sent, received):
    def one(ahead, _):
        copy = block_copy(source, target, sems, ahead)
        if received:
            copy.wait_recv()
        if sent:
            copy.wait_send()
        return 0

    lax.fori_loop(1, owners()[0], one, 0)


def place_rows(slot_row, index, block_rows, tokens):
    rows = lax.broadcasted_iota(jnp.int32, (block_rows, tokens), 0) + index * block_rows
    return (rows == slot_row).astype(bf16)


def front_kernel(
    capacity,
    branch_ref, bias_ref, x_ref, cot_ref, gain_ref, route_col, route_row, arrive_col, arrive_row,
    wq_ref, wk_ref, wv_ref,
    slot_out, cot_out, normed_own_out, normed_out, q_ref, k_out, v_out, att_out, lse_out,
    prompt_ref, send_ref, s_ref, p_ref, prompt_sems, cot_sems,
):
    branch = branch_ref[0, 0]
    ctx_at, ctx_count = lax.axis_index("ctx"), lax.axis_size("ctx")
    plen = PB * ctx_count
    tokens, width = x_ref.shape
    own = tokens - PB
    gain = gain_ref[...].astype(f32)
    count, me = owners()
    block_rows = send_ref.shape[1]
    greet_owners()

    chunk = PB // CHUNKS

    def pass_on(step, up, c):
        block = ctx_at - step if up else ctx_at + step
        ahead = ctx_at + 1 if up else ctx_at - 1
        fits = (block >= 0) & (ahead < ctx_count) if up else (block < ctx_count) & (ahead >= 0)
        piece = pl.ds(c * chunk, chunk)
        source = x_ref.at[piece] if step == 0 else prompt_ref.at[block, piece]
        copy = pltpu.make_async_remote_copy(
            src_ref=source, dst_ref=prompt_ref.at[block, piece],
            send_sem=prompt_sems.at[0, int(up), step, c], recv_sem=prompt_sems.at[1, int(up), step, c],
            device_id={"ctx": ahead}, device_id_type=pl.DeviceIdType.MESH,
        )
        return fits, copy

    def arrival(step, up, c):
        block = ctx_at - step - 1 if up else ctx_at + step + 1
        fits = block >= 0 if up else block < ctx_count
        place = prompt_ref.at[block, pl.ds(c * chunk, chunk)]
        copy = pltpu.make_async_remote_copy(
            src_ref=place, dst_ref=place,
            send_sem=prompt_sems.at[0, int(up), step, c], recv_sem=prompt_sems.at[1, int(up), step, c],
            device_id={"ctx": ctx_at}, device_id_type=pl.DeviceIdType.MESH,
        )
        return fits, block, copy

    for c in range(CHUNKS):
        for up in (True, False):
            fits, copy = pass_on(0, up, c)
            pl.when(fits)(copy.start)

    same = route_col[...] == route_row[...]
    earlier = arrive_col[...] < arrive_row[...]
    rank = jnp.sum(jnp.where(same & earlier, 1.0, 0.0), axis=0, keepdims=True).astype(jnp.int32)
    slot = jnp.where(rank < capacity, route_row[...] * block_rows + rank, count * block_rows)
    slot_out[...] = slot

    x = x_ref[...].astype(f32)
    normed_own_out[...] = (x * inverse_rms(x) * gain).astype(bf16)

    def column(i, _):
        cols = pl.ds(pl.multiple_of(i * 256, 256), 256)
        q_ref[:, cols] = dot_nn(normed_own_out[...], wq_ref[:, cols]).astype(bf16)
        k_out[plen:, cols] = dot_nn(normed_own_out[PB:, :], wk_ref[:, cols]).astype(bf16)
        v_out[plen:, cols] = dot_nn(normed_own_out[PB:, :], wv_ref[:, cols]).astype(bf16)
        return 0

    lax.fori_loop(0, width // 256, column, 0)

    def project(block):
        rows = pl.ds(pl.multiple_of(block * PB, PB), PB)

        def prompt_column(i, _):
            cols = pl.ds(pl.multiple_of(i * 256, 256), 256)
            k_out[rows, cols] = dot_nn(normed_out[rows, :], wk_ref[:, cols]).astype(bf16)
            v_out[rows, cols] = dot_nn(normed_out[rows, :], wv_ref[:, cols]).astype(bf16)
            return 0

        lax.fori_loop(0, width // 256, prompt_column, 0)

    normed_out[pl.ds(pl.multiple_of(ctx_at * PB, PB), PB), :] = normed_own_out[:PB, :]
    project(ctx_at)

    def take(block):
        x = prompt_ref[block].astype(f32)
        rows = pl.ds(pl.multiple_of(block * PB, PB), PB)
        normed_out[rows, :] = (x * inverse_rms(x) * gain).astype(bf16)
        project(block)

    for step in range(ctx_count - 1):
        for c in range(CHUNKS):
            for up in (True, False):
                fits, block, copy = arrival(step, up, c)
                pl.when(fits)(copy.wait_recv)
                if step < ctx_count - 2:
                    fits, copy = pass_on(step + 1, up, c)
                    pl.when(fits)(copy.start)
        if step == ctx_count - 2:
            def send_cot(ahead, _):
                peer = lax.rem(me + ahead, count)
                place = place_rows(slot_out[...], peer, block_rows, tokens)
                send_ref[peer] = dot_nn(place, cot_ref[...]).astype(bf16)
                block_copy(send_ref, cot_out, cot_sems, ahead).start()
                return 0

            lax.fori_loop(1, count, send_cot, 0)
            cot_out[me] = dot_nn(place_rows(slot, me, block_rows, tokens), cot_ref[...]).astype(bf16)
        for up in (True, False):
            fits, block, copy = arrival(step, up, 0)
            pl.when(fits)(functools.partial(take, block))

    p_ref[plen:, :PB] = jnp.zeros((own, PB), bf16)
    limit = limits(ctx_at, branch, tokens)

    def pair(g, _):
        lanes = pl.ds(pl.multiple_of(g * TILE, TILE), TILE)
        queries = q_ref[:, lanes]
        keys = k_out[:, lanes]
        values_t = v_out[:, lanes].T
        bias = bias_ref[g]
        lse_rows, att_rows = [], []
        for half in range(2):
            scores_to(s_ref, jnp.where(head_lanes(half), keys, jnp.zeros_like(keys)), queries, plen)
            add_near(s_ref, bias[half : half + 1, :], ctx_at, branch, plen)

            def top_of(i, top):
                rows = pl.ds(pl.multiple_of(i * TILE, TILE), TILE)
                s = jnp.where(row_steps(i * TILE, TILE, tokens) < limit, s_ref[rows, :], masked_score)
                s_ref[rows, :] = s
                return jnp.maximum(top, fold8(s, jnp.max))

            top = lax.fori_loop(0, plen // TILE, top_of, jnp.full((8, tokens), masked_score, f32))
            own_top = jnp.full((8, own), masked_score, f32)
            for i in range(own // TILE):
                rows = slice(plen + i * TILE, plen + (i + 1) * TILE)
                s = jnp.where(own_allowed(i * TILE, TILE, own), s_ref[rows, PB:], masked_score)
                s_ref[rows, PB:] = s
                own_top = jnp.maximum(own_top, fold8(s, jnp.max))
            top = jnp.concatenate([top[:, :PB], jnp.maximum(top[:, PB:], own_top)], axis=1)
            top = jnp.max(top, axis=0, keepdims=True)

            def weigh(i, total):
                rows = pl.ds(pl.multiple_of(i * TILE, TILE), TILE)
                p = jnp.exp(s_ref[rows, :] - top)
                p_ref[rows, :] = p.astype(bf16)
                return total + fold8(p, jnp.sum)

            total = lax.fori_loop(0, plen // TILE, weigh, jnp.zeros((8, tokens), f32))
            own_total = jnp.zeros((8, own), f32)
            for i in range(own // TILE):
                rows = slice(plen + i * TILE, plen + (i + 1) * TILE)
                p = jnp.exp(s_ref[rows, PB:] - top[:, PB:])
                p_ref[rows, PB:] = p.astype(bf16)
                own_total = own_total + fold8(p, jnp.sum)
            total = jnp.concatenate([total[:, :PB], total[:, PB:] + own_total], axis=1)
            total = jnp.sum(total, axis=0, keepdims=True)
            rows = slice(half * 64, half * 64 + 64)
            att_rows.append((dot_nn(values_t[rows, :], p_ref[...]) / total).astype(bf16))
            lse_rows.append(top + jnp.log(total))
        att_out[lanes, :] = jnp.concatenate(att_rows, axis=0)
        lse_out[g] = pick_rows(lse_rows, tokens)
        return 0

    lax.fori_loop(0, width // TILE, pair, 0)
    await_blocks(send_ref, cot_out, cot_sems, True, True)
    for step in range(ctx_count - 1):
        for c in range(CHUNKS):
            for up in (True, False):
                fits, copy = pass_on(step, up, c)
                pl.when(fits)(copy.wait_send)


def router_probs(logits, lane, experts):
    logits = jnp.where(lane < experts, logits, masked_score)
    logits = jnp.exp(logits - jnp.max(logits, axis=1, keepdims=True))
    return logits / jnp.sum(logits, axis=1, keepdims=True)


def gelu_parts(v):
    t = jnp.tanh(gelu_scale * (v + gelu_cube * (v * v * v)))
    half = 0.5 * (1.0 + t)
    slope = half + 0.5 * v * (1.0 - t * t) * (gelu_scale + (3.0 * gelu_scale * gelu_cube) * (v * v))
    return v * half, slope


def expert_kernel(
    experts,
    att_ref, x_ref, wo_ref, gain_ref, router_ref, slot_row, cot_ref, cot_rows, win_hbm, wout_hbm,
    rows_out, router_out, hidden_grad_out, wo_grad_out, att_grad_out, delta_out, gain_grad_out,
    result_out, hidden_ref,
    moe_ref, send_ref, win_ref, wout_ref, group_rows, sent_ref, result_acc, grad_acc,
    grad_send, grad_recv, low_ref, att_t_ref, rows_sems, grad_sems, load_sems,
):
    tokens, width = x_ref.shape
    count, me = owners()
    block_rows = send_ref.shape[1]
    hidden_units = win_ref.shape[1]
    loads = [
        pltpu.make_async_copy(win_hbm, win_ref, load_sems.at[0]),
        pltpu.make_async_copy(wout_hbm, wout_ref, load_sems.at[1]),
    ]
    for copy in loads:
        copy.start()
    greet_owners()

    def column(i, _):
        cols = pl.ds(pl.multiple_of(i * 256, 256), 256)
        hidden_ref[:, cols] = x_ref[:, cols].astype(f32) + dot_tn(att_ref[...], wo_ref[:, cols])
        return 0

    lax.fori_loop(0, width // 256, column, 0)
    hidden = hidden_ref[...]
    moe_ref[...] = (hidden * inverse_rms(hidden) * gain_ref[...].astype(f32)).astype(bf16)

    members = 2 * lax.axis_size("expert") if lax.axis_size("ctx") % 2 == 0 else count
    groups = count // members
    my_group = me // members

    def send_rows(ahead, _):
        peer = lax.rem(me + ahead, count)
        place = place_rows(slot_row[...], peer, block_rows, tokens)
        send_ref[peer] = dot_nn(place, moe_ref[...]).astype(bf16)
        block_copy(send_ref, rows_out, rows_sems, ahead).start()
        return 0

    def send_group(g, _):
        base = lax.rem(my_group + g, groups) * members

        def member(i, _):
            ahead = lax.rem(base + i - me + count, count)
            pl.when(ahead > 0)(lambda: (send_rows(ahead, 0), None)[1])
            return 0

        return lax.fori_loop(0, members, member, 0)

    lax.fori_loop(0, groups, send_group, 0)
    rows_out[me] = dot_nn(place_rows(slot_row[...], me, block_rows, tokens), moe_ref[...]).astype(bf16)

    router_out[...] = jnp.zeros_like(router_out)
    for copy in loads:
        copy.wait()

    def group(g, _):
        base = lax.rem(my_group + g, groups) * members

        def arrive(i, _):
            behind = lax.rem(me - base - i + count, count)
            pl.when(behind > 0)(lambda: block_copy(send_ref, rows_out, rows_sems, behind).wait_recv())
            return 0

        lax.fori_loop(0, members, arrive, 0)
        blocks = pl.ds(base, members)
        size = members * block_rows
        group_rows[...] = rows_out[blocks].reshape(size, width)
        slot_lane = lax.broadcasted_iota(jnp.int32, (size, TILE), 1)
        mine = slot_lane == me
        probs = router_probs(dot_nn(group_rows[...], router_ref[...]), slot_lane, experts)
        gate = jnp.sum(jnp.where(mine, probs, 0.0), axis=1, keepdims=True)
        cot_group = cot_rows[blocks].reshape(size, width).astype(f32)
        sent_ref[...] = (gate * cot_group).astype(bf16)
        result_acc[...] = jnp.zeros_like(result_acc)
        grad_acc[...] = jnp.zeros_like(grad_acc)

        def units(i, _):
            cols = pl.ds(pl.multiple_of(i * width, width), width)
            act, slope = gelu_parts(dot_nn(group_rows[...], win_ref[:, cols]))
            result_acc[...] += dot_nn(act.astype(bf16), wout_ref[cols, :])
            pre_grad = (dot_nt(sent_ref[...], wout_ref[cols, :]) * slope).astype(bf16)
            grad_acc[...] += dot_nt(pre_grad, win_ref[:, cols])
            return 0

        lax.fori_loop(0, hidden_units // width, units, 0)
        result = result_acc[...].astype(bf16)
        gate_grad = jnp.sum(cot_group * result.astype(f32), axis=1, keepdims=True)
        logit_grad = (gate_grad * gate) * (jnp.where(mine, 1.0, 0.0) - probs)
        high, low = two_parts(logit_grad)
        grad = grad_acc[...] + (dot_nt(high, router_ref[...]) + dot_nt(low, router_ref[...]))
        grad_send[blocks] = grad.astype(bf16).reshape(members, block_rows, width)
        gated = (gate * result.astype(f32)).astype(bf16)
        result_out[blocks] = gated.reshape(members, block_rows, width)

        def give(i, _):
            ahead = lax.rem(base + i - me + count, count)

            @pl.when(ahead > 0)
            def _():
                block_copy(grad_send, grad_recv, grad_sems, ahead).start()

            return 0

        lax.fori_loop(0, members, give, 0)
        router_out[...] += dot_tn(high, group_rows[...]) + dot_tn(low, group_rows[...])
        return 0

    lax.fori_loop(0, groups, group, 0)
    grad_recv[me] = grad_send[me]

    slots = count * block_rows
    place = place_rows(slot_row[...], 0, slots, tokens)
    await_blocks(grad_send, grad_recv, grad_sems, False, True)
    moe_grad = dot_tn(place, grad_recv[...].reshape(slots, width))
    hidden = hidden_ref[...]
    inverse = inverse_rms(hidden)
    scaled = hidden * inverse
    gain_grad_out[...] = jnp.sum(moe_grad * scaled, axis=0, keepdims=True)
    through = moe_grad * gain_ref[...].astype(f32)
    shared = jnp.mean(through * scaled, axis=1, keepdims=True)
    hidden_grad = cot_ref[...].astype(f32) + inverse * (through - scaled * shared)
    hidden_grad_out[...] = hidden_grad
    low_ref[...] = hidden_grad.astype(bf16)

    def back_column(i, _):
        cols = pl.ds(pl.multiple_of(i * 256, 256), 256)
        wo_grad = dot_nn(att_ref[...], low_ref[:, cols]).astype(bf16)
        wo_grad_out[:, :, cols] = wo_grad.reshape(width // 16, 16, 256)
        att_grad_out[:, cols] = dot_nt(low_ref[...], wo_ref[cols, :]).astype(bf16)
        att_t_ref[cols, :] = dot_nt(wo_ref[cols, :], low_ref[...]).astype(bf16)
        return 0

    lax.fori_loop(0, width // 256, back_column, 0)

    def pair(g, _):
        rows = pl.ds(pl.multiple_of(g * TILE, TILE), TILE)
        both = att_ref[rows, :].astype(f32) * att_t_ref[rows, :].astype(f32)
        delta_out[g] = pick_rows(
            [jnp.sum(both[:64], axis=0, keepdims=True), jnp.sum(both[64:], axis=0, keepdims=True)],
            tokens,
        )
        return 0

    lax.fori_loop(0, width // TILE, pair, 0)
    await_blocks(send_ref, rows_out, rows_sems, True, False)
    await_blocks(grad_send, grad_recv, grad_sems, True, False)


class Axis:
    def __init__(self, name, size, step=1):
        place = lax.axis_index(name)
        self.name, self.size, self.step, self.place = name, size, step, place
        self.index = lax.rem(place // step, size)

    def at(self, ahead):
        return lax.rem(self.index + ahead, self.size)

    def peer(self, ahead):
        return {self.name: self.place + (self.at(ahead) - self.index) * self.step}


def mesh_axes():
    dp, ctx, expert = lax.axis_size("dp"), lax.axis_size("ctx"), lax.axis_size("expert")
    cores, lines = Axis("expert", expert), Axis("ctx", ctx)
    if dp == 4:
        near, far = Axis("dp", 2, 1), Axis("dp", 2, 2)
        return [[cores, near, far, lines], [cores, far, near, lines]]
    return [[cores, Axis("dp", dp), lines]] * 2


def cuts_of(length):
    return 4 if length % 8 == 0 else 2 if length % 4 == 0 else 1


def push(source, target, sems, slot, device):
    copy = pltpu.make_async_remote_copy(
        src_ref=source, dst_ref=target, send_sem=sems.at[0, slot], recv_sem=sems.at[1, slot],
        device_id=device, device_id_type=pl.DeviceIdType.MESH,
    )
    copy.start()
    return copy


def back_kernel(
    experts, plan,
    branch_ref, bias_ref, q_ref, k_hbm, v_hbm, att_grad_ref, lse_ref, delta_ref, normed_hbm, normed_own_ref,
    gain_ref, wq_ref, wk_ref, wv_ref, wo_part_hbm, moe_gain_ref, router_part_hbm, x_hbm, hidden_grad_hbm,
    hidden_hbm, slot_row, result_hbm, rows_hbm, cot_hbm, win_hbm, wout_hbm, router_ref,
    full_ref, small_out, input_out, in_out, out_out, layer_out, rows_all,
    k_ref, v_ref, normed_ref, s_ref, dp_ref, p_ref, ds_ref, dq_ref, dk_ref, dv_ref, hist_ref, gain_sum,
    local_ref, shared_send, shared_recv, parts_ref, acc_refs, recv_refs, small_ref, small_recv,
    result_recv, win_ref, wout_ref, rows_ref, cot_ref, rows_t,
    block_sems, load_sems, sems, small_sems, shared_sems, result_sems, rows_sems,
):
    group, pieces, lengths = plan
    flows = mesh_axes()
    branch = branch_ref[0, 0]
    ctx_at = lax.axis_index("ctx")
    ctx_count, dp_count = lax.axis_size("ctx"), lax.axis_size("dp")
    tokens, width = q_ref.shape
    own = tokens - PB
    plen = PB * ctx_count
    count, me = owners()
    lines, columns_dp = Axis("ctx", ctx_count), Axis("dp", dp_count)
    whole_axes = [Axis("expert", lax.axis_size("expert")), columns_dp, lines]
    gain = gain_ref[...].astype(f32)
    limit = limits(ctx_at, branch, tokens)
    blocks = ctx_count + 1
    rows_16 = width // 16

    def block_loads(i):
        rows = plen if i == blocks - 1 else pl.multiple_of(lines.at(i + 1) * PB, PB)
        sources = [(k_hbm, k_ref, 0), (v_hbm, v_ref, 1)]
        if i < blocks - 2:
            sources.append((normed_hbm, normed_ref, 2))
        return [
            pltpu.make_async_copy(source.at[pl.ds(rows, PB)], target.at[i % 2], block_sems.at[i, n])
            for source, target, n in sources
        ]

    for copy in block_loads(0):
        copy.start()
    slice_width = win_ref.shape[1]
    part = pl.ds(pl.multiple_of(lax.axis_index("dp") * slice_width, slice_width), slice_width)
    weight_loads = [
        pltpu.make_async_copy(win_hbm.at[:, part], win_ref, load_sems.at[0]),
        pltpu.make_async_copy(wout_hbm.at[part], wout_ref, load_sems.at[1]),
    ]
    own_result = pltpu.make_async_copy(result_hbm.at[me], result_recv.at[me], load_sems.at[2])
    wo_load = pltpu.make_async_copy(wo_part_hbm, parts_ref.at[pl.ds(0, rows_16)], load_sems.at[5 + 2 * dp_count])
    router_load = pltpu.make_async_copy(
        router_part_hbm.at[pl.ds(0, experts)], small_ref.at[pl.ds(0, experts)], load_sems.at[7 + 2 * dp_count]
    )
    for copy in [wo_load, *weight_loads, own_result, router_load]:
        copy.start()

    barrier = pltpu.get_barrier_semaphore()

    def greet(ahead, _):
        pl.semaphore_signal(
            barrier, inc=1, device_id=owner_device(lax.rem(me + ahead, count)),
            device_id_type=pl.DeviceIdType.MESH,
        )
        return 0

    lax.fori_loop(1, count, greet, 0)
    for ahead in range(1, dp_count):
        pl.semaphore_signal(
            barrier, inc=1, device_id=columns_dp.peer(ahead), device_id_type=pl.DeviceIdType.MESH
        )
    pl.semaphore_wait(barrier, count - 1 + dp_count - 1)

    slots_of = {}

    def slot(*key):
        return slots_of.setdefault(key, len(slots_of))

    started = []

    def reduce_start(j, s):
        axis, length = flows[j % 2][s], lengths[s]
        copies = []
        for ahead in range(1, axis.size):
            target = axis.at(ahead)
            cuts = cuts_of(length)
            size = length // cuts
            for cut in range(cuts):
                first = target * length + cut * size
                if s == 0:
                    source = parts_ref.at[pl.ds(j * group + first, size)]
                else:
                    source = acc_refs[s - 1].at[j, pl.ds(first, size)]
                there = recv_refs[s].at[j, ahead - 1, pl.ds(cut * size, size)]
                copies.append(push(source, there, sems, slot("r", j, s, ahead, cut), axis.peer(ahead)))
        started.extend(copies)
        return copies

    def base_of(j, s):
        base = j * group
        for t in range(s + 1):
            base = base + flows[j % 2][t].index * lengths[t]
        return base

    def reduce_finish(j, s, copies):
        axis, length = flows[j % 2][s], lengths[s]
        for copy in copies:
            copy.wait_recv()
        last = s == len(lengths) - 1

        def unit(u, _):
            if s == 0:
                total = parts_ref[base_of(j, 0) + u].astype(f32)
            else:
                total = acc_refs[s - 1][j, axis.index * length + u].astype(f32)
            for ahead in range(1, axis.size):
                total = total + recv_refs[s][j, ahead - 1, u].astype(f32)
            if last:
                full_ref[base_of(j, s) + u] = total.astype(bf16)
            else:
                acc_refs[s][j, u] = total.astype(bf16)
            return 0

        lax.fori_loop(0, length, unit, 0)

    def spread_start(j, s):
        axis, length = flows[j % 2][s], lengths[s]
        cuts = cuts_of(length)
        size = length // cuts
        copies = []
        for ahead in range(1, axis.size):
            for cut in range(cuts):
                here = full_ref.at[pl.ds(base_of(j, s) + cut * size, size)]
                copies.append(push(here, here, sems, slot("s", j, s, ahead, cut), axis.peer(ahead)))
        started.extend(copies)
        return copies

    def small_slot(s, ahead):
        return sum(axis.size - 1 for axis in whole_axes[:s]) + ahead - 1

    def small_start(s):
        axis = whole_axes[s]
        copies = [
            push(small_ref, small_recv[s].at[ahead - 1], small_sems, small_slot(s, ahead), axis.peer(ahead))
            for ahead in range(1, axis.size)
        ]
        return copies

    def small_finish(s, copies):
        axis = whole_axes[s]
        for copy in copies:
            copy.wait()
        mine = small_ref[...]
        total = jnp.zeros_like(mine)
        for index in range(axis.size):
            piece = mine
            for ahead in range(1, axis.size):
                piece = jnp.where(axis.at(axis.size - ahead) == index, small_recv[s][ahead - 1], piece)
            total = total + piece
        if s == len(whole_axes) - 1:
            small_out[...] = total
        else:
            small_ref[...] = total

    stages = len(lengths)
    early = pieces > 1 and group <= rows_16
    begin = [blocks + j for j in range(pieces)]
    if early:
        begin = [0] + [blocks + j - 1 for j in range(1, pieces)]
    pending = {}

    def advance(time):
        for j in sorted(range(pieces), key=lambda j: begin[j]):
            s = time - begin[j]
            if not 0 <= s < 2 * stages:
                continue
            if s < stages:
                reduce_finish(j, s, pending[j, s])
                if s + 1 < stages:
                    pending[j, s + 1] = reduce_start(j, s + 1)
                else:
                    pending[j, s + 1] = spread_start(j, s)
            else:
                for copy in pending[j, s]:
                    copy.wait_recv()
                if s + 1 < 2 * stages:
                    pending[j, s + 1] = spread_start(j, 2 * stages - 1 - (s + 1))

    def put(first, cols, value):
        rows = value.shape[0]
        parts_ref[first // 16 : (first + rows) // 16, :, cols] = value.astype(bf16).reshape(
            rows // 16, 16, value.shape[1]
        )

    def columns(work):
        def column(i, _):
            work(pl.ds(pl.multiple_of(i * 256, 256), 256))
            return 0

        lax.fori_loop(0, width // 256, column, 0)

    if parts_ref.shape[0] > 4 * rows_16:
        extra = parts_ref.shape[0] - 4 * rows_16
        parts_ref[4 * rows_16 :] = jnp.zeros((extra, 16, width), bf16)
    wo_load.wait()
    if early:
        pending[0, 0] = reduce_start(0, 0)

    def give_result(ahead, _):
        block_copy(result_hbm, result_recv, result_sems, ahead).start()
        return 0

    lax.fori_loop(1, count, give_result, 0)

    def rows_copy(ahead, e):
        return pltpu.make_async_remote_copy(
            src_ref=rows_hbm.at[e], dst_ref=rows_all.at[ahead - 1, e],
            send_sem=rows_sems.at[0, ahead - 1, e], recv_sem=rows_sems.at[1, ahead - 1, e],
            device_id=columns_dp.peer(ahead), device_id_type=pl.DeviceIdType.MESH,
        )

    def each_row_block(act):
        def one(e, _):
            for ahead in range(1, dp_count):
                act(rows_copy(ahead, e))
            return 0

        lax.fori_loop(0, count, one, 0)

    each_row_block(lambda copy: copy.start())

    shared_copies = []
    shared_slots = shared_send.shape[0]
    hist_ref[...] = jnp.zeros_like(hist_ref)
    gain_sum[...] = jnp.zeros_like(gain_sum)
    for i in range(blocks):
        cont = i == blocks - 1
        at_home = i == blocks - 2
        for copy in block_loads(i):
            copy.wait()
        if i + 1 < blocks:
            for copy in block_loads(i + 1):
                copy.start()
        block = lines.at(i + 1)
        lanes_from = PB if cont else 0
        lanes_used = slice(lanes_from, tokens)
        near = []
        if cont or at_home:
            near = [
                (0, lanes_from, 0, None),
                (0, lanes_from + TILE, TILE, None),
                (TILE, lanes_from + TILE, 0, None),
            ]
        else:
            near = [(TILE, 0, TILE, block == ctx_at - 1)]
        if not cont:
            near += [(first, PB, branch - block * PB - first, None) for first in range(0, PB, TILE)]

        def pair(g, _, i=i, cont=cont, block=block, lanes_used=lanes_used, near=near):
            lanes = pl.ds(pl.multiple_of(g * TILE, TILE), TILE)
            queries = q_ref[lanes_used, lanes]
            grads = att_grad_ref[lanes_used, lanes]
            keys = k_ref[i % 2, :, lanes]
            values = v_ref[i % 2, :, lanes]
            keys_t = keys.T
            bias = bias_ref[g]
            dk_parts, dv_parts, dq_parts = [], [], []
            for half in range(2):
                mine = head_lanes(half)
                lse = lse_ref[g][half : half + 1, lanes_used]
                delta = delta_ref[g][half : half + 1, lanes_used]
                s_ref[:, lanes_used] = dot_nt(jnp.where(mine, keys, jnp.zeros_like(keys)), queries)
                dp_ref[:, lanes_used] = dot_nt(jnp.where(mine, values, jnp.zeros_like(values)), grads)
                source = jnp.broadcast_to(bias[half : half + 1, :], (TILE, TILE))
                for first, lane, gap, when in near:
                    def add(first=first, lane=lane, gap=gap):
                        there = (slice(first, first + TILE), slice(lane, lane + TILE))
                        index = jnp.clip(near_index(gap), 0, TILE - 1)
                        s_ref[there] = s_ref[there] + jnp.take_along_axis(source, index, axis=1)

                    add() if when is None else pl.when(when)(add)
                step = 32
                for first in range(0, PB, step):
                    rows = slice(first, first + step)
                    if cont:
                        allowed = own_allowed(first, step, own)
                    else:
                        allowed = row_steps(block * PB + first, step, tokens) < limit
                    p = jnp.where(allowed, jnp.exp(s_ref[rows, lanes_used] - lse), 0.0)
                    p_ref[rows, lanes_used] = p.astype(bf16)
                    ds_ref[rows, lanes_used] = (p * (dp_ref[rows, lanes_used] - delta)).astype(bf16)
                for first, lane, gap, when in near:
                    def collect(first=first, lane=lane, gap=gap):
                        tile = ds_ref[first : first + TILE, lane : lane + TILE].astype(f32)
                        if not isinstance(gap, int) or gap > 0:
                            tile = jnp.where(near_index(gap) < TILE, tile, 0.0)
                        turn = lax.broadcasted_iota(jnp.int32, (TILE, TILE), 1) + lax.broadcasted_iota(
                            jnp.int32, (TILE, TILE), 0
                        )
                        tile = jnp.take_along_axis(tile, (turn - gap) & (TILE - 1), axis=1)
                        hist_ref[g * 2 + half] += fold8(tile, jnp.sum)

                    collect() if when is None else pl.when(when)(collect)
                ds = ds_ref[:, lanes_used]
                dv_parts.append(dot_nn(p_ref[:, lanes_used], grads))
                dk_parts.append(dot_nn(ds, queries))
                dq_parts.append(dot_nn(keys_t[half * 64 : half * 64 + 64, :], ds))
            dq = jnp.concatenate(dq_parts, axis=0)
            if i == 0:
                dq_ref[lanes, :] = dq
            else:
                dq_ref[lanes, lanes_used] += dq
            mine = head_lanes(0)
            dv_ref[:, lanes] = jnp.where(mine, dv_parts[0], dv_parts[1]).astype(bf16)
            dk_ref[:, lanes] = jnp.where(mine, dk_parts[0], dk_parts[1]).astype(bf16)
            return 0

        lax.fori_loop(0, width // TILE, pair, 0)

        def block_column(cols, i=i, cont=cont, at_home=at_home):
            if cont:
                normed, whole = normed_own_ref[PB:, cols], normed_own_ref[PB:, :]
            elif at_home:
                normed, whole = normed_own_ref[:PB, cols], normed_own_ref[:PB, :]
            else:
                normed, whole = normed_ref[i % 2, :, cols], normed_ref[i % 2]
            wk_part, wv_part = dot_tn(whole, dk_ref[:, cols]), dot_tn(whole, dv_ref[:, cols])
            if i == 0:
                in_out[:, cols] = wk_part
                out_out[:, cols] = wv_part
            elif not cont:
                in_out[:, cols] += wk_part
                out_out[:, cols] += wv_part
            else:
                put(width, cols, out_out[:, cols] + wv_part)
                put(2 * width, cols, in_out[:, cols] + wk_part)
            grad = dot_nt(dk_ref[...], wk_ref[cols, :]) + dot_nt(dv_ref[...], wv_ref[cols, :])
            gain_sum[:, cols] += jnp.sum(grad * normed.astype(f32), axis=0, keepdims=True)
            if cont:
                local_ref[PB:, cols] = grad
            elif at_home:
                local_ref[:PB, cols] = grad
            else:
                shared_send[i % shared_slots, :, cols] = grad.astype(bf16)

        if shared_slots <= i < blocks - 2:
            for copy in shared_copies[i - shared_slots]:
                copy.wait_send()
        columns(block_column)
        if i < blocks - 2:
            size = PB // SHARED_CUTS
            shared_copies.append(
                [
                    push(
                        shared_send.at[i % shared_slots, pl.ds(cut * size, size)],
                        shared_recv.at[i, pl.ds(cut * size, size)],
                        shared_sems, i * SHARED_CUTS + cut, lines.peer(i + 1),
                    )
                    for cut in range(SHARED_CUTS)
                ]
            )
        if not cont:
            advance(i)
    for copies in shared_copies[-shared_slots:]:
        started.extend(copies)

    def ready(j):
        if j > 0 or not early:
            pending[j, 0] = reduce_start(j, 0)

    done = 3 * rows_16
    for j in range(pieces):
        if (j + 1) * group <= done:
            ready(j)
    rows_ref[:tokens, :] = dq_ref[...].T.astype(bf16)

    def query_column(cols):
        put(3 * width, cols, dot_tn(normed_own_ref[...], rows_ref[:tokens, cols]))

    columns(query_column)
    for j in range(pieces):
        if (j + 1) * group > done:
            ready(j)

    def query_grad(cols):
        grad = dot_nt(rows_ref[:tokens, :], wq_ref[cols, :])
        gain_sum[:, cols] += jnp.sum(grad * normed_own_ref[:, cols].astype(f32), axis=0, keepdims=True)
        local_ref[:, cols] += grad

    columns(query_grad)
    small_ref[experts:, :] = jnp.zeros((small_ref.shape[0] - experts, width), f32)
    small_ref[experts : experts + 1, :] = gain_sum[...] / gain
    small_ref[experts + 1 : experts + 2, :] = moe_gain_ref[...]
    router_load.wait()
    per_row = width // TILE
    for head in range(hist_ref.shape[0]):
        row, lane = 2 + experts + head // per_row, head % per_row * TILE
        small_ref[row : row + 1, lane : lane + TILE] = jnp.sum(hist_ref[head], axis=0, keepdims=True)
    small_pending = small_start(0)

    slots = rows_ref.shape[0]

    def grads_of(n, c):
        if c == 0:
            if n == 0:
                for copy in weight_loads:
                    copy.wait()
            if n == 1:
                each_row_block(lambda copy: copy.wait_recv())
            source = rows_hbm if n == 0 else rows_all.at[n - 1]
            load = pltpu.make_async_copy(source, result_recv, load_sems.at[3 + 2 * n])
            load.start()
            load.wait()
            rows_ref[...] = result_recv[...].reshape(slots, width)
            cot_from = columns_dp.at(dp_count - n)
            load = pltpu.make_async_copy(cot_hbm.at[cot_from], result_recv, load_sems.at[4 + 2 * n])
            load.start()
            lane = lax.broadcasted_iota(jnp.int32, (slots, TILE), 1)
            probs = router_probs(dot_nn(rows_ref[...], router_ref[...]), lane, experts)
            gate = jnp.sum(jnp.where(lane == me, probs, 0.0), axis=1, keepdims=True)
            load.wait()
            cot = result_recv[...].reshape(slots, width)
            cot_ref[...] = (gate * cot.astype(f32)).astype(bf16)
            rows_t[...] = rows_ref[...].T
        cols = slice(c * 256, c * 256 + 256)
        act, slope = gelu_parts(dot_nn(rows_ref[...], win_ref[:, cols]))
        pre_grad = (dot_nt(cot_ref[...], wout_ref[cols, :]) * slope).astype(bf16)
        out_part = dot_tn(act.astype(bf16), cot_ref[...])
        in_part = dot_nn(rows_t[...], pre_grad)
        if n == 0:
            out_out[cols, :] = out_part
            in_out[:, cols] = in_part
        else:
            out_out[cols, :] += out_part
            in_out[:, cols] += in_part

    def input_back():
        held = pltpu.make_async_copy(hidden_grad_hbm, input_out, load_sems.at[3 + 2 * dp_count])
        held.start()
        x_load = pltpu.make_async_copy(x_hbm, rows_ref.at[pl.ds(0, tokens)], load_sems.at[6 + 2 * dp_count])
        x_load.start()
        for copies in shared_copies:
            for copy in copies:
                copy.wait_recv()
        held.wait()
        x_load.wait()
        for first, shared_rows in ((0, True), (PB, False)):
            rows = slice(first, PB if shared_rows else tokens)
            x = rows_ref[rows, :].astype(f32)
            inverse = inverse_rms(x)
            grad = local_ref[rows, :]
            if shared_rows:
                for n in range(ctx_count - 1):
                    grad = grad + shared_recv[n].astype(f32)
            through = grad * gain
            scaled = x * inverse
            shared = jnp.mean(through * scaled, axis=1, keepdims=True)
            input_out[rows, :] += inverse * (through - scaled * shared)

    def layer():
        held = pltpu.make_async_copy(hidden_hbm, input_out, load_sems.at[4 + 2 * dp_count])
        held.start()
        own_result.wait()
        await_blocks(result_hbm, result_recv, result_sems, False, True)
        place = place_rows(slot_row[...], 0, slots, tokens)
        returned = dot_tn(place, result_recv[...].reshape(slots, width))
        held.wait()
        layer_out[...] = (input_out[...] + returned).astype(bf16)

    work = [layer]
    work += [functools.partial(grads_of, n, c) for n in range(dp_count) for c in range(slice_width // 256)]
    work += [input_back]
    for time in range(blocks - 1, max(begin) + 2 * stages):
        if time >= blocks:
            advance(time)
        elif early:
            advance(time)
        s = time - blocks
        if 0 <= s < len(whole_axes):
            small_finish(s, small_pending)
            if s + 1 < len(whole_axes):
                small_pending = small_start(s + 1)
        if work:
            work.pop(0)()
    for rest in work:
        rest()
    for copy in started:
        copy.wait_send()
    await_blocks(result_hbm, result_recv, result_sems, True, False)
    each_row_block(lambda copy: copy.wait_send())


def tail_plan(sizes, width):
    group = 1
    for size in sizes:
        group *= size
    units = 4 * width // 16
    pieces = -(-units // group)
    lengths, left = [], group
    for size in sizes:
        left //= size
        lengths.append(left)
    return group, pieces, lengths


def body(
    inputs, cotangent, route, arrival, branch, attn_gain, query_weight, key_weight, value_weight,
    output_weight, rel_table, moe_gain, router_weight, expert_in, expert_out,
):
    x = inputs[0]
    cot = cotangent[0]
    tokens, width = x.shape
    own = tokens - PB
    buckets, heads = rel_table.shape
    experts = router_weight.shape[1]
    capacity = 9 * tokens // (8 * experts)
    block_rows = capacity if capacity % 8 == 0 else -(-capacity // 16) * 16
    slots = experts * block_rows
    ctx_count = lax.axis_size("ctx")
    dp_count = lax.axis_size("dp")
    plen = PB * ctx_count
    keys_total = plen + own
    hidden_units = expert_in.shape[2]
    pairs = width // TILE
    attn_gain_row = attn_gain.reshape(1, width)
    moe_gain_row = moe_gain.reshape(1, width)
    onehot = bucket_onehot(buckets)
    by_distance = jnp.dot(onehot, rel_table.astype(f32), precision=lax.Precision.HIGHEST).T
    by_distance = by_distance - by_distance[:, TILE - 1 :]
    bias = jnp.pad(by_distance.reshape(pairs, 2, TILE), ((0, 0), (0, 6), (0, 0)))
    router_wide = jnp.pad(router_weight, ((0, 0), (0, TILE - experts)))
    route_col = route[0]
    route_row = route_col.reshape(1, tokens)
    arrive_row = arrival[0]
    arrive_col = arrive_row.reshape(tokens, 1)
    blocks = shape((experts, block_rows, width), bf16)
    block_space = pltpu.VMEM((experts, block_rows, width), bf16)
    block_sems = pltpu.SemaphoreType.DMA((2, experts - 1))
    any_space = pl.BlockSpec(memory_space=pl.ANY)

    slot_row, cot_sent, normed_own, normed_all, queries, keys, values, att, lse = pl.pallas_call(
        functools.partial(front_kernel, capacity),
        out_shape=[
            shape((1, tokens), jnp.int32),
            blocks,
            shape((tokens, width), bf16),
            shape((plen, width), bf16),
            shape((tokens, width), bf16),
            shape((keys_total, width), bf16),
            shape((keys_total, width), bf16),
            shape((width, tokens), bf16),
            shape((pairs, 8, tokens), f32),
        ],
        in_specs=[smem()] + [vmem()] * 11,
        out_specs=[vmem()] * 9,
        scratch_shapes=[
            pltpu.VMEM((ctx_count, PB, width), bf16),
            block_space,
            pltpu.VMEM((keys_total, tokens), f32),
            pltpu.VMEM((keys_total, tokens), bf16),
            pltpu.SemaphoreType.DMA((2, 2, ctx_count - 1, CHUNKS)),
            block_sems,
        ],
        compiler_params=remote_params(1),
        cost_estimate=cost(40 * keys_total * tokens * width, 20 * width * width),
        name="front",
    )(
        branch, bias, x, cot, attn_gain_row, route_col, route_row, arrive_col, arrive_row,
        query_weight, key_weight, value_weight,
    )
    cot_all = lax.all_gather(cot_sent, "dp", axis=0, tiled=False)

    members = 2 * lax.axis_size("expert") if ctx_count % 2 == 0 else experts
    group_rows = members * block_rows
    (
        rows_sent, router_part, hidden_grad, wo_part, att_grad, delta, moe_gain_part,
        result, hidden,
    ) = pl.pallas_call(
        functools.partial(expert_kernel, experts),
        out_shape=[
            blocks, shape((TILE, width), f32), shape((tokens, width), f32), shape((width // 16, 16, width), bf16),
            shape((tokens, width), bf16), shape((pairs, 8, tokens), f32), shape((1, width), f32),
            blocks, shape((tokens, width), f32),
        ],
        in_specs=[vmem()] * 8 + [any_space] * 2,
        out_specs=[vmem()] * 9,
        scratch_shapes=[
            pltpu.VMEM((tokens, width), bf16),
            block_space,
            pltpu.VMEM((width, hidden_units), bf16),
            pltpu.VMEM((hidden_units, width), bf16),
            pltpu.VMEM((group_rows, width), bf16),
            pltpu.VMEM((group_rows, width), bf16),
            pltpu.VMEM((group_rows, width), f32),
            pltpu.VMEM((group_rows, width), f32),
            block_space, block_space,
            pltpu.VMEM((tokens, width), bf16),
            pltpu.VMEM((width, tokens), bf16),
            block_sems, block_sems,
            pltpu.SemaphoreType.DMA((2,)),
        ],
        compiler_params=remote_params(2),
        cost_estimate=cost(8 * slots * width * hidden_units, 12 * width * hidden_units),
        name="expert",
    )(
        att, x, output_weight, moe_gain_row, router_wide, slot_row, cot, cot_sent,
        expert_in[0], expert_out[0],
    )
    att_grad, cot_all = lax.optimization_barrier((att_grad, cot_all))

    expert_count = lax.axis_size("expert")
    dp_sizes = [2, 2] if dp_count == 4 else [dp_count]
    sizes = [expert_count, *dp_sizes, ctx_count]
    plan = tail_plan(sizes, width)
    group, pieces, lengths = plan
    units = group * pieces

    table_rows = heads * TILE // width
    small_rows = -(-(2 + experts + table_rows) // 8) * 8
    slice_width = hidden_units // dp_count
    weights, small, input_grad, in_grad, out_grad, layer_out, _ = pl.pallas_call(
        functools.partial(back_kernel, experts, plan),
        out_shape=[
            shape((units, 16, width), bf16), shape((small_rows, width), f32), shape((tokens, width), f32),
            shape((width, slice_width), f32), shape((slice_width, width), f32), shape((tokens, width), bf16),
            shape((dp_count - 1, experts, block_rows, width), bf16),
        ],
        in_specs=[
            smem(), vmem(), vmem(), any_space, any_space, vmem(), vmem(), vmem(), any_space, vmem(),
            vmem(), vmem(), vmem(), vmem(), any_space, vmem(), any_space, any_space, any_space,
            any_space, vmem(), any_space, any_space, any_space, any_space, any_space, vmem(),
        ],
        out_specs=[vmem()] * 6 + [any_space],
        scratch_shapes=[
            pltpu.VMEM((2, PB, width), bf16),
            pltpu.VMEM((2, PB, width), bf16),
            pltpu.VMEM((2, PB, width), bf16),
            pltpu.VMEM((PB, tokens), f32),
            pltpu.VMEM((PB, tokens), f32),
            pltpu.VMEM((PB, tokens), bf16),
            pltpu.VMEM((PB, tokens), bf16),
            pltpu.VMEM((width, tokens), f32),
            pltpu.VMEM((PB, width), bf16),
            pltpu.VMEM((PB, width), bf16),
            pltpu.VMEM((heads, 8, TILE), f32),
            pltpu.VMEM((1, width), f32),
            pltpu.VMEM((tokens, width), f32),
            pltpu.VMEM((min(ctx_count - 1, 16 // ctx_count), PB, width), bf16),
            pltpu.VMEM((ctx_count - 1, PB, width), bf16),
            pltpu.VMEM((units, 16, width), bf16),
            [pltpu.VMEM((pieces, length, 16, width), bf16) for length in lengths[:-1]],
            [
                pltpu.VMEM((pieces, size - 1, length, 16, width), bf16)
                for size, length in zip(sizes, lengths)
            ],
            pltpu.VMEM((small_rows, width), f32),
            [pltpu.VMEM((size - 1, small_rows, width), f32) for size in (expert_count, dp_count, ctx_count)],
            block_space,
            pltpu.VMEM((width, slice_width), bf16),
            pltpu.VMEM((slice_width, width), bf16),
            pltpu.VMEM((slots, width), bf16),
            pltpu.VMEM((slots, width), bf16),
            pltpu.VMEM((width, slots), bf16),
            pltpu.SemaphoreType.DMA((ctx_count + 1, 3)),
            pltpu.SemaphoreType.DMA((8 + 2 * dp_count,)),
            pltpu.SemaphoreType.DMA(
                (2, 2 * pieces * sum((n - 1) * cuts_of(length) for n, length in zip(sizes, lengths)))
            ),
            pltpu.SemaphoreType.DMA((2, expert_count + dp_count + ctx_count - 3)),
            pltpu.SemaphoreType.DMA((2, (ctx_count - 1) * SHARED_CUTS)),
            block_sems,
            pltpu.SemaphoreType.DMA((2, dp_count - 1, experts)),
        ],
        compiler_params=remote_params(0),
        cost_estimate=cost(
            8 * dp_count * slots * width * slice_width + 80 * keys_total * tokens * width,
            60 * width * slice_width,
        ),
        name="back",
    )(
        branch, bias, queries, keys, values, att_grad, lse, delta, normed_all, normed_own,
        attn_gain_row, query_weight, key_weight, value_weight, wo_part, moe_gain_part, router_part, x,
        hidden_grad, hidden, slot_row, result,
        rows_sent, cot_all, expert_in[0], expert_out[0], router_wide,
    )

    weights = weights.reshape(units * 16, width)[: 4 * width].astype(f32).reshape(4, width, width)
    router_grad = small[:experts].T
    hist_sum = small[2 + experts : 2 + experts + table_rows].reshape(heads, TILE)
    last = onehot[:, buckets - 1 :]
    spread = jnp.concatenate([onehot[:, : buckets - 1], last - 1.0], axis=1)
    table_grad = jnp.dot(spread.T, hist_sum.T, precision=lax.Precision.HIGHEST)
    return (
        layer_out[None],
        input_grad[None],
        small[experts],
        weights[3],
        weights[2],
        weights[1],
        weights[0],
        table_grad,
        small[experts + 1],
        router_grad,
        in_grad[None],
        out_grad[None],
    )


def solution(mesh):
    grouped = P(("dp", "expert"), "ctx", None)
    placed = (
        grouped, grouped, grouped, grouped, P(("dp", "expert"), "ctx"),
        P(), P(), P(), P(), P(), P(), P(), P(),
        P(("ctx", "expert"), None, None),
        P(("ctx", "expert"), None, None),
    )
    return jax.shard_map(
        body,
        mesh=mesh,
        in_specs=placed,
        out_specs=(
            grouped, grouped, P(), P(), P(), P(), P(), P(), P(), P(),
            P(("ctx", "expert"), None, "dp"),
            P(("ctx", "expert"), "dp", None),
        ),
        check_vma=False,
    )
```

```python
import functools

import jax
import jax.numpy as jnp
from jax import lax
from jax.experimental import pallas as pl
from jax.experimental.pallas import tpu as pltpu
from jax.sharding import PartitionSpec as P

PB = 256
TILE = 128
CHUNKS = 8
SHARED_CUTS = 4

bucket_edges = (19, 21, 24, 27, 31, 35, 40, 46, 52, 59, 67, 77, 87, 99, 113)
norm_eps = 1e-06
masked_score = -1e30
gelu_scale = 0.7978845608
gelu_cube = 0.044715

bf16 = jnp.bfloat16
f32 = jnp.float32
VMEM_LIMIT = 121 * 512 * 1024


def dot_nn(a, b):
    return jnp.dot(a, b, preferred_element_type=f32)


def dot_nt(a, b):
    return lax.dot_general(a, b, (((1,), (1,)), ((), ())), preferred_element_type=f32)


def dot_tn(a, b):
    return lax.dot_general(a, b, (((0,), (0,)), ((), ())), preferred_element_type=f32)


def two_parts(a):
    high = a.astype(bf16)
    return high, (a - high.astype(f32)).astype(bf16)


def vmem():
    return pl.BlockSpec(memory_space=pltpu.VMEM)


def smem():
    return pl.BlockSpec(memory_space=pltpu.SMEM)


def params():
    return pltpu.CompilerParams(vmem_limit_bytes=VMEM_LIMIT)


def remote_params(number):
    return pltpu.CompilerParams(
        vmem_limit_bytes=VMEM_LIMIT, collective_id=number, has_side_effects=True
    )


def cost(flops, nbytes):
    return pl.CostEstimate(flops=int(flops), bytes_accessed=int(nbytes), transcendentals=0)


def shape(dims, kind):
    return jax.ShapeDtypeStruct(dims, kind)


def inverse_rms(x):
    return lax.rsqrt(jnp.mean(x * x, axis=-1, keepdims=True) + norm_eps)


def bucket_onehot(buckets):
    distance = jnp.arange(TILE, dtype=jnp.int32)
    ids = jnp.minimum(distance, 16)
    for edge in bucket_edges:
        ids = ids + (distance >= edge).astype(jnp.int32)
    return (ids[:, None] == jnp.arange(buckets, dtype=jnp.int32)[None, :]).astype(f32)


def near_index(first):
    rows = lax.broadcasted_iota(jnp.int32, (TILE, TILE), 0)
    lanes = lax.broadcasted_iota(jnp.int32, (TILE, TILE), 1)
    return first + lanes - rows


def near_tiles(ctx_at, plen):
    start = ctx_at * PB
    return (
        (start, 0, 0, False),
        (start, TILE, TILE, False),
        (start + TILE, TILE, 0, False),
        (plen, PB, 0, False),
        (plen, PB + TILE, TILE, False),
        (plen + TILE, PB + TILE, 0, False),
        (start - TILE, 0, TILE, True),
    )


def add_near(s_ref, bias_row, ctx_at, branch, plen):
    source = jnp.broadcast_to(bias_row, (TILE, TILE))
    add_tiles(s_ref, source, ctx_at, near_tiles(ctx_at, plen))

    def window(i, _):
        rows = pl.ds(pl.multiple_of(i * TILE, TILE), TILE)
        lanes = slice(PB, PB + TILE)
        index = jnp.clip(near_index(branch - i * TILE), 0, TILE - 1)
        s_ref[rows, lanes] = s_ref[rows, lanes] + jnp.take_along_axis(source, index, axis=1)
        return 0

    lax.fori_loop(1, plen // TILE, window, 0)


def add_tiles(s_ref, source, ctx_at, tiles):
    for first_row, first_lane, gap, guarded in tiles:
        def work(first_row=first_row, first_lane=first_lane, gap=gap):
            rows = pl.ds(first_row if isinstance(first_row, int) else pl.multiple_of(first_row, 16), TILE)
            lanes = slice(first_lane, first_lane + TILE)
            index = jnp.clip(near_index(gap), 0, TILE - 1)
            s_ref[rows, lanes] = s_ref[rows, lanes] + jnp.take_along_axis(source, index, axis=1)

        if guarded:
            pl.when(ctx_at > 0)(work)
        else:
            work()


def scores_to(s_ref, keys, queries, plen):
    s_ref[:plen, :] = dot_nt(keys[:plen], queries)
    s_ref[plen:, PB:] = dot_nt(keys[plen:], queries[PB:])


def limits(ctx_at, branch, tokens):
    lane = lax.broadcasted_iota(jnp.int32, (1, tokens), 1)
    return jnp.where(lane < PB, ctx_at * PB + lane + 1, branch)


def row_steps(first, count, lanes):
    return first + lax.broadcasted_iota(jnp.int32, (count, lanes), 0)


def own_allowed(first, count, lanes):
    return row_steps(first, count, lanes) <= lax.broadcasted_iota(jnp.int32, (count, lanes), 1)


def head_lanes(half):
    return lax.broadcasted_iota(jnp.int32, (1, TILE), 1) // (TILE // 2) == half


def pick_rows(pieces, lanes):
    row = lax.broadcasted_iota(jnp.int32, (8, lanes), 0)
    return jnp.where(row == 0, pieces[0], jnp.where(row == 1, pieces[1], 0.0))


def fold8(x, op):
    return op(x.reshape(x.shape[0] // 8, 8, x.shape[1]), axis=0)


def owner_device(index):
    cores = lax.axis_size("expert")
    return {"ctx": index // cores, "expert": lax.rem(index, cores)}


def owners():
    cores = lax.axis_size("expert")
    count = cores * lax.axis_size("ctx")
    return count, lax.axis_index("ctx") * cores + lax.axis_index("expert")


def greet_owners():
    count, me = owners()
    barrier = pltpu.get_barrier_semaphore()

    def greet(ahead, _):
        pl.semaphore_signal(
            barrier, inc=1, device_id=owner_device(lax.rem(me + ahead, count)),
            device_id_type=pl.DeviceIdType.MESH,
        )
        return 0

    lax.fori_loop(1, count, greet, 0)
    pl.semaphore_wait(barrier, count - 1)


def block_copy(source, target, sems, ahead):
    count, me = owners()
    peer = lax.rem(me + ahead, count)
    return pltpu.make_async_remote_copy(
        src_ref=source.at[peer], dst_ref=target.at[me],
        send_sem=sems.at[0, ahead - 1], recv_sem=sems.at[1, ahead - 1],
        device_id=owner_device(peer), device_id_type=pl.DeviceIdType.MESH,
    )


def await_blocks(source, target, sems, sent, received):
    def one(ahead, _):
        copy = block_copy(source, target, sems, ahead)
        if received:
            copy.wait_recv()
        if sent:
            copy.wait_send()
        return 0

    lax.fori_loop(1, owners()[0], one, 0)


def place_rows(slot_row, index, block_rows, tokens):
    rows = lax.broadcasted_iota(jnp.int32, (block_rows, tokens), 0) + index * block_rows
    return (rows == slot_row).astype(bf16)


def front_kernel(
    capacity,
    branch_ref, bias_ref, x_ref, cot_ref, gain_ref, route_row, arrive_row,
    wq_ref, wk_ref, wv_ref,
    slot_out, cot_out, normed_own_out, normed_out, q_ref, k_out, v_out, att_out, lse_out,
    prompt_ref, send_ref, s_ref, p_ref, prompt_sems, cot_sems,
):
    branch = branch_ref[0, 0]
    ctx_at, ctx_count = lax.axis_index("ctx"), lax.axis_size("ctx")
    plen = PB * ctx_count
    tokens, width = x_ref.shape
    own = tokens - PB
    gain = gain_ref[...].astype(f32)
    count, me = owners()
    block_rows = send_ref.shape[1]
    greet_owners()

    chunk = PB // CHUNKS

    def pass_on(step, up, c):
        block = ctx_at - step if up else ctx_at + step
        ahead = ctx_at + 1 if up else ctx_at - 1
        fits = (block >= 0) & (ahead < ctx_count) if up else (block < ctx_count) & (ahead >= 0)
        piece = pl.ds(c * chunk, chunk)
        source = x_ref.at[piece] if step == 0 else prompt_ref.at[block, piece]
        copy = pltpu.make_async_remote_copy(
            src_ref=source, dst_ref=prompt_ref.at[block, piece],
            send_sem=prompt_sems.at[0, int(up), step, c], recv_sem=prompt_sems.at[1, int(up), step, c],
            device_id={"ctx": ahead}, device_id_type=pl.DeviceIdType.MESH,
        )
        return fits, copy

    def arrival(step, up, c):
        block = ctx_at - step - 1 if up else ctx_at + step + 1
        fits = block >= 0 if up else block < ctx_count
        place = prompt_ref.at[block, pl.ds(c * chunk, chunk)]
        copy = pltpu.make_async_remote_copy(
            src_ref=place, dst_ref=place,
            send_sem=prompt_sems.at[0, int(up), step, c], recv_sem=prompt_sems.at[1, int(up), step, c],
            device_id={"ctx": ctx_at}, device_id_type=pl.DeviceIdType.MESH,
        )
        return fits, block, copy

    for c in range(CHUNKS):
        for up in (True, False):
            fits, copy = pass_on(0, up, c)
            pl.when(fits)(copy.start)

    x = x_ref[...].astype(f32)
    normed_own_out[...] = (x * inverse_rms(x) * gain).astype(bf16)

    def column(i, _):
        cols = pl.ds(pl.multiple_of(i * 256, 256), 256)
        q_ref[:, cols] = dot_nn(normed_own_out[...], wq_ref[:, cols]).astype(bf16)
        k_out[plen:, cols] = dot_nn(normed_own_out[PB:, :], wk_ref[:, cols]).astype(bf16)
        v_out[plen:, cols] = dot_nn(normed_own_out[PB:, :], wv_ref[:, cols]).astype(bf16)
        return 0

    lax.fori_loop(0, width // 256, column, 0)

    def project(block):
        rows = pl.ds(pl.multiple_of(block * PB, PB), PB)

        def prompt_column(i, _):
            cols = pl.ds(pl.multiple_of(i * 256, 256), 256)
            k_out[rows, cols] = dot_nn(normed_out[rows, :], wk_ref[:, cols]).astype(bf16)
            v_out[rows, cols] = dot_nn(normed_out[rows, :], wv_ref[:, cols]).astype(bf16)
            return 0

        lax.fori_loop(0, width // 256, prompt_column, 0)

    def take(block):
        x = prompt_ref[block].astype(f32)
        rows = pl.ds(pl.multiple_of(block * PB, PB), PB)
        normed_out[rows, :] = (x * inverse_rms(x) * gain).astype(bf16)
        project(block)

    for step in range(ctx_count - 1):
        for c in range(CHUNKS):
            for up in (True, False):
                fits, block, copy = arrival(step, up, c)
                pl.when(fits)(copy.wait_recv)
                if step < ctx_count - 2:
                    fits, copy = pass_on(step + 1, up, c)
                    pl.when(fits)(copy.start)
        if step == 0:
            normed_out[pl.ds(pl.multiple_of(ctx_at * PB, PB), PB), :] = normed_own_out[:PB, :]
            project(ctx_at)
        for up in (True, False):
            fits, block, copy = arrival(step, up, 0)
            pl.when(fits)(functools.partial(take, block))

    def down(row):
        column = jnp.broadcast_to(row[...].astype(f32), (TILE, tokens)).T
        return jnp.concatenate([column] * (tokens // TILE), axis=1)

    same = down(route_row) == route_row[...].astype(f32)
    earlier = down(arrive_row) < arrive_row[...].astype(f32)
    rank = jnp.sum(jnp.where(same & earlier, 1.0, 0.0), axis=0, keepdims=True).astype(jnp.int32)
    slot = jnp.where(rank < capacity, route_row[...] * block_rows + rank, count * block_rows)
    slot_out[...] = slot

    def send_cot(ahead, _):
        peer = lax.rem(me + ahead, count)
        place = place_rows(slot_out[...], peer, block_rows, tokens)
        send_ref[peer] = dot_nn(place, cot_ref[...]).astype(bf16)
        block_copy(send_ref, cot_out, cot_sems, ahead).start()
        return 0

    def send_cots():
        lax.fori_loop(1, count, send_cot, 0)
        cot_out[me] = dot_nn(place_rows(slot_out[...], me, block_rows, tokens), cot_ref[...]).astype(bf16)

    p_ref[plen:, :PB] = jnp.zeros((own, PB), bf16)
    limit = limits(ctx_at, branch, tokens)

    def pair(g, _):
        pl.when(g == 1)(send_cots)
        lanes = pl.ds(pl.multiple_of(g * TILE, TILE), TILE)
        queries = q_ref[:, lanes]
        keys = k_out[:, lanes]
        values_t = v_out[:, lanes].T
        bias = bias_ref[g]
        lse_rows, att_rows = [], []
        for half in range(2):
            scores_to(s_ref, jnp.where(head_lanes(half), keys, jnp.zeros_like(keys)), queries, plen)
            add_near(s_ref, bias[half : half + 1, :], ctx_at, branch, plen)

            def top_of(i, top):
                for part in range(0, TILE, 32):
                    first = pl.multiple_of(i * TILE + part, 32)
                    rows = pl.ds(first, 32)
                    s = jnp.where(row_steps(first, 32, tokens) < limit, s_ref[rows, :], masked_score)
                    s_ref[rows, :] = s
                    top = jnp.maximum(top, fold8(s, jnp.max))
                return top

            top = lax.fori_loop(0, plen // TILE, top_of, jnp.full((8, tokens), masked_score, f32))
            own_top = jnp.full((8, own), masked_score, f32)
            for i in range(own // TILE):
                rows = slice(plen + i * TILE, plen + (i + 1) * TILE)
                s = jnp.where(own_allowed(i * TILE, TILE, own), s_ref[rows, PB:], masked_score)
                s_ref[rows, PB:] = s
                own_top = jnp.maximum(own_top, fold8(s, jnp.max))
            top = jnp.concatenate([top[:, :PB], jnp.maximum(top[:, PB:], own_top)], axis=1)
            top = jnp.max(top, axis=0, keepdims=True)

            def weigh(i, total):
                for part in range(0, TILE, 32):
                    rows = pl.ds(pl.multiple_of(i * TILE + part, 32), 32)
                    p = jnp.exp(s_ref[rows, :] - top)
                    p_ref[rows, :] = p.astype(bf16)
                    total = total + fold8(p, jnp.sum)
                return total

            total = lax.fori_loop(0, plen // TILE, weigh, jnp.zeros((8, tokens), f32))
            own_total = jnp.zeros((8, own), f32)
            for i in range(own // TILE):
                rows = slice(plen + i * TILE, plen + (i + 1) * TILE)
                p = jnp.exp(s_ref[rows, PB:] - top[:, PB:])
                p_ref[rows, PB:] = p.astype(bf16)
                own_total = own_total + fold8(p, jnp.sum)
            total = jnp.concatenate([total[:, :PB], total[:, PB:] + own_total], axis=1)
            total = jnp.sum(total, axis=0, keepdims=True)
            rows = slice(half * 64, half * 64 + 64)
            att_rows.append((dot_nn(values_t[rows, :], p_ref[...]) / total).astype(bf16))
            lse_rows.append(top + jnp.log(total))
        att_out[lanes, :] = jnp.concatenate(att_rows, axis=0)
        lse_out[g] = pick_rows(lse_rows, tokens)
        return 0

    lax.fori_loop(0, width // TILE, pair, 0)
    await_blocks(send_ref, cot_out, cot_sems, True, True)
    for step in range(ctx_count - 1):
        for c in range(CHUNKS):
            for up in (True, False):
                fits, copy = pass_on(step, up, c)
                pl.when(fits)(copy.wait_send)


def router_probs(logits, lane, experts):
    logits = jnp.where(lane < experts, logits, masked_score)
    logits = jnp.exp(logits - jnp.max(logits, axis=1, keepdims=True))
    return logits / jnp.sum(logits, axis=1, keepdims=True)


def gelu_parts(v):
    t = jnp.tanh(gelu_scale * (v + gelu_cube * (v * v * v)))
    half = 0.5 * (1.0 + t)
    slope = half + 0.5 * v * (1.0 - t * t) * (gelu_scale + (3.0 * gelu_scale * gelu_cube) * (v * v))
    return v * half, slope


def expert_kernel(
    experts,
    att_ref, x_ref, wo_ref, gain_ref, router_ref, slot_row, cot_ref, cot_rows, win_hbm, wout_hbm,
    rows_out, router_out, hidden_grad_out, wo_grad_out, att_grad_out, delta_out, gain_grad_out,
    result_out, hidden_ref,
    moe_ref, send_ref, win_ref, wout_ref, group_rows, sent_ref, result_acc, grad_acc,
    grad_send, grad_recv, low_ref, att_t_ref, rows_sems, grad_sems, load_sems,
):
    tokens, width = x_ref.shape
    count, me = owners()
    block_rows = send_ref.shape[1]
    hidden_units = win_ref.shape[1]
    loads = [
        pltpu.make_async_copy(win_hbm, win_ref, load_sems.at[0]),
        pltpu.make_async_copy(wout_hbm, wout_ref, load_sems.at[1]),
    ]
    for copy in loads:
        copy.start()
    greet_owners()

    def column(i, _):
        cols = pl.ds(pl.multiple_of(i * 256, 256), 256)
        hidden_ref[:, cols] = x_ref[:, cols].astype(f32) + dot_tn(att_ref[...], wo_ref[:, cols])
        return 0

    lax.fori_loop(0, width // 256, column, 0)
    hidden = hidden_ref[...]
    moe_ref[...] = (hidden * inverse_rms(hidden) * gain_ref[...].astype(f32)).astype(bf16)

    members = 2 * lax.axis_size("expert") if lax.axis_size("ctx") % 2 == 0 else count
    groups = count // members
    my_group = me // members

    def send_rows(ahead, _):
        peer = lax.rem(me + ahead, count)
        place = place_rows(slot_row[...], peer, block_rows, tokens)
        send_ref[peer] = dot_nn(place, moe_ref[...]).astype(bf16)
        block_copy(send_ref, rows_out, rows_sems, ahead).start()
        return 0

    def send_group(g, _):
        base = lax.rem(my_group + g, groups) * members

        def member(i, _):
            ahead = lax.rem(base + i - me + count, count)
            pl.when(ahead > 0)(lambda: (send_rows(ahead, 0), None)[1])
            return 0

        return lax.fori_loop(0, members, member, 0)

    lax.fori_loop(0, groups, send_group, 0)
    rows_out[me] = dot_nn(place_rows(slot_row[...], me, block_rows, tokens), moe_ref[...]).astype(bf16)

    router_out[...] = jnp.zeros_like(router_out)
    for copy in loads:
        copy.wait()

    def group(g, _):
        base = lax.rem(my_group + g, groups) * members

        def arrive(i, _):
            behind = lax.rem(me - base - i + count, count)
            pl.when(behind > 0)(lambda: block_copy(send_ref, rows_out, rows_sems, behind).wait_recv())
            return 0

        lax.fori_loop(0, members, arrive, 0)
        blocks = pl.ds(base, members)
        size = members * block_rows
        group_rows[...] = rows_out[blocks].reshape(size, width)
        slot_lane = lax.broadcasted_iota(jnp.int32, (size, TILE), 1)
        mine = slot_lane == me
        probs = router_probs(dot_nn(group_rows[...], router_ref[...]), slot_lane, experts)
        gate = jnp.sum(jnp.where(mine, probs, 0.0), axis=1, keepdims=True)
        cot_group = cot_rows[blocks].reshape(size, width).astype(f32)
        sent_ref[...] = (gate * cot_group).astype(bf16)
        result_acc[...] = jnp.zeros_like(result_acc)
        grad_acc[...] = jnp.zeros_like(grad_acc)

        def units(i, _):
            cols = pl.ds(pl.multiple_of(i * width, width), width)
            act, slope = gelu_parts(dot_nn(group_rows[...], win_ref[:, cols]))
            result_acc[...] += dot_nn(act.astype(bf16), wout_ref[cols, :])
            pre_grad = (dot_nt(sent_ref[...], wout_ref[cols, :]) * slope).astype(bf16)
            grad_acc[...] += dot_nt(pre_grad, win_ref[:, cols])
            return 0

        lax.fori_loop(0, hidden_units // width, units, 0)
        result = result_acc[...].astype(bf16)
        gate_grad = jnp.sum(cot_group * result.astype(f32), axis=1, keepdims=True)
        logit_grad = (gate_grad * gate) * (jnp.where(mine, 1.0, 0.0) - probs)
        high, low = two_parts(logit_grad)
        grad = grad_acc[...] + (dot_nt(high, router_ref[...]) + dot_nt(low, router_ref[...]))
        grad_send[blocks] = grad.astype(bf16).reshape(members, block_rows, width)
        gated = (gate * result.astype(f32)).astype(bf16)
        result_out[blocks] = gated.reshape(members, block_rows, width)

        def give(i, _):
            ahead = lax.rem(base + i - me + count, count)

            @pl.when(ahead > 0)
            def _():
                block_copy(grad_send, grad_recv, grad_sems, ahead).start()

            return 0

        lax.fori_loop(0, members, give, 0)
        router_out[...] += dot_tn(high, group_rows[...]) + dot_tn(low, group_rows[...])
        return 0

    lax.fori_loop(0, groups, group, 0)
    grad_recv[me] = grad_send[me]

    slots = count * block_rows
    place = place_rows(slot_row[...], 0, slots, tokens)
    await_blocks(grad_send, grad_recv, grad_sems, False, True)
    moe_grad = dot_tn(place, grad_recv[...].reshape(slots, width))
    hidden = hidden_ref[...]
    inverse = inverse_rms(hidden)
    scaled = hidden * inverse
    gain_grad_out[...] = jnp.sum(moe_grad * scaled, axis=0, keepdims=True)
    through = moe_grad * gain_ref[...].astype(f32)
    shared = jnp.mean(through * scaled, axis=1, keepdims=True)
    hidden_grad = cot_ref[...].astype(f32) + inverse * (through - scaled * shared)
    hidden_grad_out[...] = hidden_grad
    low_ref[...] = hidden_grad.astype(bf16)

    def back_column(i, _):
        cols = pl.ds(pl.multiple_of(i * 256, 256), 256)
        wo_grad = dot_nn(att_ref[...], low_ref[:, cols]).astype(bf16)
        wo_grad_out[:, :, cols] = wo_grad.reshape(width // 16, 16, 256)
        att_grad_out[:, cols] = dot_nt(low_ref[...], wo_ref[cols, :]).astype(bf16)
        att_t_ref[cols, :] = dot_nt(wo_ref[cols, :], low_ref[...]).astype(bf16)
        return 0

    lax.fori_loop(0, width // 256, back_column, 0)

    def pair(g, _):
        rows = pl.ds(pl.multiple_of(g * TILE, TILE), TILE)
        both = att_ref[rows, :].astype(f32) * att_t_ref[rows, :].astype(f32)
        delta_out[g] = pick_rows(
            [jnp.sum(both[:64], axis=0, keepdims=True), jnp.sum(both[64:], axis=0, keepdims=True)],
            tokens,
        )
        return 0

    lax.fori_loop(0, width // TILE, pair, 0)
    await_blocks(send_ref, rows_out, rows_sems, True, False)
    await_blocks(grad_send, grad_recv, grad_sems, True, False)


class Axis:
    def __init__(self, name, size, step=1):
        place = lax.axis_index(name)
        self.name, self.size, self.step, self.place = name, size, step, place
        self.index = lax.rem(place // step, size)

    def at(self, ahead):
        return lax.rem(self.index + ahead, self.size)

    def peer(self, ahead):
        return {self.name: self.place + (self.at(ahead) - self.index) * self.step}


def mesh_axes():
    dp, ctx, expert = lax.axis_size("dp"), lax.axis_size("ctx"), lax.axis_size("expert")
    cores, lines = Axis("expert", expert), Axis("ctx", ctx)
    if dp == 4:
        near, far = Axis("dp", 2, 1), Axis("dp", 2, 2)
        return [[cores, near, far, lines], [cores, far, near, lines]]
    return [[cores, Axis("dp", dp), lines]] * 2


def cuts_of(length):
    return 4 if length % 8 == 0 else 2 if length % 4 == 0 else 1


def push(source, target, sems, slot, device):
    copy = pltpu.make_async_remote_copy(
        src_ref=source, dst_ref=target, send_sem=sems.at[0, slot], recv_sem=sems.at[1, slot],
        device_id=device, device_id_type=pl.DeviceIdType.MESH,
    )
    copy.start()
    return copy


def back_kernel(
    experts, plan,
    branch_ref, bias_ref, q_ref, k_hbm, v_hbm, att_grad_ref, lse_ref, delta_ref, normed_hbm, normed_own_ref,
    gain_ref, wq_ref, wk_ref, wv_ref, wo_part_hbm, moe_gain_ref, router_part_hbm, x_hbm, hidden_grad_hbm,
    hidden_hbm, slot_row, result_hbm, rows_hbm, cot_hbm, win_hbm, wout_hbm, router_ref,
    full_ref, small_out, input_out, in_out, out_out, layer_out, rows_all,
    k_ref, v_ref, normed_ref, s_ref, dp_ref, p_ref, ds_ref, dq_ref, dk_ref, dv_ref, hist_ref, gain_sum,
    local_ref, shared_send, shared_recv, parts_ref, acc_refs, recv_refs, small_ref, small_recv,
    result_recv, win_ref, wout_ref, rows_ref, cot_ref, rows_t,
    block_sems, load_sems, sems, small_sems, shared_sems, result_sems, rows_sems,
):
    group, pieces, lengths = plan
    flows = mesh_axes()
    branch = branch_ref[0, 0]
    ctx_at = lax.axis_index("ctx")
    ctx_count, dp_count = lax.axis_size("ctx"), lax.axis_size("dp")
    tokens, width = q_ref.shape
    own = tokens - PB
    plen = PB * ctx_count
    count, me = owners()
    lines, columns_dp = Axis("ctx", ctx_count), Axis("dp", dp_count)
    whole_axes = [Axis("expert", lax.axis_size("expert")), columns_dp, lines]
    gain = gain_ref[...].astype(f32)
    limit = limits(ctx_at, branch, tokens)
    blocks = ctx_count + 1
    rows_16 = width // 16

    def block_loads(i):
        rows = plen if i == blocks - 1 else pl.multiple_of(lines.at(i + 1) * PB, PB)
        sources = [(k_hbm, k_ref, 0), (v_hbm, v_ref, 1)]
        if i < blocks - 2:
            sources.append((normed_hbm, normed_ref, 2))
        return [
            pltpu.make_async_copy(source.at[pl.ds(rows, PB)], target.at[i % 2], block_sems.at[i, n])
            for source, target, n in sources
        ]

    for copy in block_loads(0):
        copy.start()
    slice_width = win_ref.shape[1]
    part = pl.ds(pl.multiple_of(lax.axis_index("dp") * slice_width, slice_width), slice_width)
    weight_loads = [
        pltpu.make_async_copy(win_hbm.at[:, part], win_ref, load_sems.at[0]),
        pltpu.make_async_copy(wout_hbm.at[part], wout_ref, load_sems.at[1]),
    ]
    own_result = pltpu.make_async_copy(result_hbm.at[me], result_recv.at[me], load_sems.at[2])
    wo_load = pltpu.make_async_copy(wo_part_hbm, parts_ref.at[pl.ds(0, rows_16)], load_sems.at[5 + 2 * dp_count])
    router_load = pltpu.make_async_copy(
        router_part_hbm.at[pl.ds(0, experts)], small_ref.at[pl.ds(0, experts)], load_sems.at[7 + 2 * dp_count]
    )
    for copy in [wo_load, *weight_loads, own_result, router_load]:
        copy.start()

    barrier = pltpu.get_barrier_semaphore()

    def greet(ahead, _):
        pl.semaphore_signal(
            barrier, inc=1, device_id=owner_device(lax.rem(me + ahead, count)),
            device_id_type=pl.DeviceIdType.MESH,
        )
        return 0

    lax.fori_loop(1, count, greet, 0)
    for ahead in range(1, dp_count):
        pl.semaphore_signal(
            barrier, inc=1, device_id=columns_dp.peer(ahead), device_id_type=pl.DeviceIdType.MESH
        )
    pl.semaphore_wait(barrier, count - 1 + dp_count - 1)

    slots_of = {}

    def slot(*key):
        return slots_of.setdefault(key, len(slots_of))

    started = []

    def reduce_start(j, s):
        axis, length = flows[j % 2][s], lengths[s]
        copies = []
        for ahead in range(1, axis.size):
            target = axis.at(ahead)
            cuts = cuts_of(length)
            size = length // cuts
            for cut in range(cuts):
                first = target * length + cut * size
                if s == 0:
                    source = parts_ref.at[pl.ds(j * group + first, size)]
                else:
                    source = acc_refs[s - 1].at[j, pl.ds(first, size)]
                there = recv_refs[s].at[j, ahead - 1, pl.ds(cut * size, size)]
                copies.append(push(source, there, sems, slot("r", j, s, ahead, cut), axis.peer(ahead)))
        started.extend(copies)
        return copies

    def base_of(j, s):
        base = j * group
        for t in range(s + 1):
            base = base + flows[j % 2][t].index * lengths[t]
        return base

    def reduce_finish(j, s, copies):
        axis, length = flows[j % 2][s], lengths[s]
        for copy in copies:
            copy.wait_recv()
        last = s == len(lengths) - 1

        size = 4 if length % 4 == 0 else 1

        def some(u, _):
            if s == 0:
                total = parts_ref[pl.ds(base_of(j, 0) + u * size, size)].astype(f32)
            else:
                total = acc_refs[s - 1][j, pl.ds(axis.index * length + u * size, size)].astype(f32)
            for ahead in range(1, axis.size):
                total = total + recv_refs[s][j, ahead - 1, pl.ds(u * size, size)].astype(f32)
            if last:
                full_ref[pl.ds(base_of(j, s) + u * size, size)] = total.astype(bf16)
            else:
                acc_refs[s][j, pl.ds(u * size, size)] = total.astype(bf16)
            return 0

        lax.fori_loop(0, length // size, some, 0)

    def spread_start(j, s):
        axis, length = flows[j % 2][s], lengths[s]
        cuts = cuts_of(length)
        size = length // cuts
        copies = []
        for ahead in range(1, axis.size):
            for cut in range(cuts):
                here = full_ref.at[pl.ds(base_of(j, s) + cut * size, size)]
                copies.append(push(here, here, sems, slot("s", j, s, ahead, cut), axis.peer(ahead)))
        started.extend(copies)
        return copies

    def small_slot(s, ahead):
        return sum(axis.size - 1 for axis in whole_axes[:s]) + ahead - 1

    def small_start(s):
        axis = whole_axes[s]
        copies = [
            push(small_ref, small_recv[s].at[ahead - 1], small_sems, small_slot(s, ahead), axis.peer(ahead))
            for ahead in range(1, axis.size)
        ]
        return copies

    def small_finish(s, copies):
        axis = whole_axes[s]
        for copy in copies:
            copy.wait()
        mine = small_ref[...]
        total = jnp.zeros_like(mine)
        for index in range(axis.size):
            piece = mine
            for ahead in range(1, axis.size):
                piece = jnp.where(axis.at(axis.size - ahead) == index, small_recv[s][ahead - 1], piece)
            total = total + piece
        if s == len(whole_axes) - 1:
            small_out[...] = total
        else:
            small_ref[...] = total

    stages = len(lengths)
    early = pieces > 1 and group <= rows_16
    begin = [blocks + j // 2 for j in range(pieces)]
    if early:
        begin = [blocks - 1] + [blocks + (j - 1) // 2 for j in range(1, pieces)]
    pending = {}

    def advance(time):
        for j in sorted(range(pieces), key=lambda j: begin[j]):
            s = time - begin[j]
            if not 0 <= s < 2 * stages:
                continue
            if s < stages:
                reduce_finish(j, s, pending[j, s])
                if s + 1 < stages:
                    pending[j, s + 1] = reduce_start(j, s + 1)
                else:
                    pending[j, s + 1] = spread_start(j, s)
            else:
                for copy in pending[j, s]:
                    copy.wait_recv()
                if s + 1 < 2 * stages:
                    pending[j, s + 1] = spread_start(j, 2 * stages - 1 - (s + 1))

    def put(first, cols, value):
        rows = value.shape[0]
        parts_ref[first // 16 : (first + rows) // 16, :, cols] = value.astype(bf16).reshape(
            rows // 16, 16, value.shape[1]
        )

    def columns(work):
        def column(i, _):
            work(pl.ds(pl.multiple_of(i * 256, 256), 256))
            return 0

        lax.fori_loop(0, width // 256, column, 0)

    if parts_ref.shape[0] > 4 * rows_16:
        extra = parts_ref.shape[0] - 4 * rows_16
        parts_ref[4 * rows_16 :] = jnp.zeros((extra, 16, width), bf16)
    wo_load.wait()
    if early:
        pending[0, 0] = reduce_start(0, 0)

    def give_result(ahead, _):
        block_copy(result_hbm, result_recv, result_sems, ahead).start()
        return 0

    lax.fori_loop(1, count, give_result, 0)

    def rows_copy(ahead, e):
        return pltpu.make_async_remote_copy(
            src_ref=rows_hbm.at[e], dst_ref=rows_all.at[ahead - 1, e],
            send_sem=rows_sems.at[0, ahead - 1, e], recv_sem=rows_sems.at[1, ahead - 1, e],
            device_id=columns_dp.peer(ahead), device_id_type=pl.DeviceIdType.MESH,
        )

    def each_row_block(act):
        def one(e, _):
            for ahead in range(1, dp_count):
                act(rows_copy(ahead, e))
            return 0

        lax.fori_loop(0, count, one, 0)

    each_row_block(lambda copy: copy.start())

    shared_copies = []
    shared_slots = shared_send.shape[0]
    hist_ref[...] = jnp.zeros_like(hist_ref)
    gain_sum[...] = jnp.zeros_like(gain_sum)
    for i in range(blocks):
        cont = i == blocks - 1
        at_home = i == blocks - 2
        for copy in block_loads(i):
            copy.wait()
        if i + 1 < blocks:
            for copy in block_loads(i + 1):
                copy.start()
        block = lines.at(i + 1)
        lanes_from = PB if cont else 0
        lanes_used = slice(lanes_from, tokens)
        near = []
        if cont or at_home:
            near = [
                (0, lanes_from, 0, None),
                (0, lanes_from + TILE, TILE, None),
                (TILE, lanes_from + TILE, 0, None),
            ]
        else:
            near = [(TILE, 0, TILE, block == ctx_at - 1)]
        if not cont:
            near += [(first, PB, branch - block * PB - first, None) for first in range(0, PB, TILE)]

        def pair(g, _, i=i, cont=cont, block=block, lanes_used=lanes_used, near=near):
            lanes = pl.ds(pl.multiple_of(g * TILE, TILE), TILE)
            queries = q_ref[lanes_used, lanes]
            grads = att_grad_ref[lanes_used, lanes]
            keys = k_ref[i % 2, :, lanes]
            values = v_ref[i % 2, :, lanes]
            keys_t = keys.T
            bias = bias_ref[g]
            dk_parts, dv_parts, dq_parts = [], [], []
            for half in range(2):
                mine = head_lanes(half)
                lse = lse_ref[g][half : half + 1, lanes_used]
                delta = delta_ref[g][half : half + 1, lanes_used]
                s_ref[:, lanes_used] = dot_nt(jnp.where(mine, keys, jnp.zeros_like(keys)), queries)
                dp_ref[:, lanes_used] = dot_nt(jnp.where(mine, values, jnp.zeros_like(values)), grads)
                source = jnp.broadcast_to(bias[half : half + 1, :], (TILE, TILE))
                for first, lane, gap, when in near:
                    def add(first=first, lane=lane, gap=gap):
                        there = (slice(first, first + TILE), slice(lane, lane + TILE))
                        index = jnp.clip(near_index(gap), 0, TILE - 1)
                        s_ref[there] = s_ref[there] + jnp.take_along_axis(source, index, axis=1)

                    add() if when is None else pl.when(when)(add)
                step = 32
                for first in range(0, PB, step):
                    rows = slice(first, first + step)
                    if cont:
                        allowed = own_allowed(first, step, own)
                    else:
                        allowed = row_steps(block * PB + first, step, tokens) < limit
                    p = jnp.where(allowed, jnp.exp(s_ref[rows, lanes_used] - lse), 0.0)
                    p_ref[rows, lanes_used] = p.astype(bf16)
                    ds_ref[rows, lanes_used] = (p * (dp_ref[rows, lanes_used] - delta)).astype(bf16)
                for first, lane, gap, when in near:
                    def collect(first=first, lane=lane, gap=gap):
                        tile = ds_ref[first : first + TILE, lane : lane + TILE].astype(f32)
                        if not isinstance(gap, int) or gap > 0:
                            tile = jnp.where(near_index(gap) < TILE, tile, 0.0)
                        turn = lax.broadcasted_iota(jnp.int32, (TILE, TILE), 1) + lax.broadcasted_iota(
                            jnp.int32, (TILE, TILE), 0
                        )
                        tile = jnp.take_along_axis(tile, (turn - gap) & (TILE - 1), axis=1)
                        hist_ref[g * 2 + half] += fold8(tile, jnp.sum)

                    collect() if when is None else pl.when(when)(collect)
                ds = ds_ref[:, lanes_used]
                dv_parts.append(dot_nn(p_ref[:, lanes_used], grads))
                dk_parts.append(dot_nn(ds, queries))
                dq_parts.append(dot_nn(keys_t[half * 64 : half * 64 + 64, :], ds))
            dq = jnp.concatenate(dq_parts, axis=0)
            if i == 0:
                dq_ref[lanes, :] = dq
            else:
                dq_ref[lanes, lanes_used] += dq
            mine = head_lanes(0)
            dv_ref[:, lanes] = jnp.where(mine, dv_parts[0], dv_parts[1]).astype(bf16)
            dk_ref[:, lanes] = jnp.where(mine, dk_parts[0], dk_parts[1]).astype(bf16)
            return 0

        lax.fori_loop(0, width // TILE, pair, 0)

        def block_column(cols, i=i, cont=cont, at_home=at_home):
            if cont:
                normed = normed_own_ref[PB:, cols]
            elif at_home:
                normed = normed_own_ref[:PB, cols]
            else:
                normed = normed_ref[i % 2, :, cols]
            wk_part = dot_nn(rows_t[:, :PB], dk_ref[:, cols])
            wv_part = dot_nn(rows_t[:, :PB], dv_ref[:, cols])
            if i == 0:
                in_out[:, cols] = wk_part
                out_out[:, cols] = wv_part
            elif not cont:
                in_out[:, cols] += wk_part
                out_out[:, cols] += wv_part
            else:
                put(width, cols, out_out[:, cols] + wv_part)
                put(2 * width, cols, in_out[:, cols] + wk_part)
            grad = dot_nt(dk_ref[...], wk_ref[cols, :]) + dot_nt(dv_ref[...], wv_ref[cols, :])
            gain_sum[:, cols] += jnp.sum(grad * normed.astype(f32), axis=0, keepdims=True)
            if cont:
                local_ref[PB:, cols] = grad
            elif at_home:
                local_ref[:PB, cols] = grad
            else:
                shared_send[i % shared_slots, :, cols] = grad.astype(bf16)

        if shared_slots <= i < blocks - 2:
            for copy in shared_copies[i - shared_slots]:
                copy.wait_send()
        if cont:
            rows_t[:, :PB] = normed_own_ref[PB:, :].T
        elif at_home:
            rows_t[:, :PB] = normed_own_ref[:PB, :].T
        else:
            rows_t[:, :PB] = normed_ref[i % 2].T
        columns(block_column)
        if i < blocks - 2:
            size = PB // SHARED_CUTS
            shared_copies.append(
                [
                    push(
                        shared_send.at[i % shared_slots, pl.ds(cut * size, size)],
                        shared_recv.at[i, pl.ds(cut * size, size)],
                        shared_sems, i * SHARED_CUTS + cut, lines.peer(i + 1),
                    )
                    for cut in range(SHARED_CUTS)
                ]
            )
    for copies in shared_copies[-shared_slots:]:
        started.extend(copies)

    def ready(j):
        if j > 0 or not early:
            pending[j, 0] = reduce_start(j, 0)

    done = 3 * rows_16
    for j in range(pieces):
        if (j + 1) * group <= done:
            ready(j)
    rows_ref[:tokens, :] = dq_ref[...].T.astype(bf16)
    rows_t[:, :tokens] = normed_own_ref[...].T

    def query_column(cols):
        put(3 * width, cols, dot_nn(rows_t[:, :tokens], rows_ref[:tokens, cols]))

    columns(query_column)
    for j in range(pieces):
        if (j + 1) * group > done:
            ready(j)

    def query_grad(cols):
        grad = dot_nt(rows_ref[:tokens, :], wq_ref[cols, :])
        gain_sum[:, cols] += jnp.sum(grad * normed_own_ref[:, cols].astype(f32), axis=0, keepdims=True)
        local_ref[:, cols] += grad

    columns(query_grad)
    small_ref[experts:, :] = jnp.zeros((small_ref.shape[0] - experts, width), f32)
    small_ref[experts : experts + 1, :] = gain_sum[...] / gain
    small_ref[experts + 1 : experts + 2, :] = moe_gain_ref[...]
    router_load.wait()
    per_row = width // TILE
    for head in range(hist_ref.shape[0]):
        row, lane = 2 + experts + head // per_row, head % per_row * TILE
        small_ref[row : row + 1, lane : lane + TILE] = jnp.sum(hist_ref[head], axis=0, keepdims=True)
    small_pending = small_start(0)

    slots = rows_ref.shape[0]

    def grads_of(n, c):
        if c == 0:
            if n == 0:
                for copy in weight_loads:
                    copy.wait()
            if n == 1:
                each_row_block(lambda copy: copy.wait_recv())
            source = rows_hbm if n == 0 else rows_all.at[n - 1]
            load = pltpu.make_async_copy(source, result_recv, load_sems.at[3 + 2 * n])
            load.start()
            load.wait()
            rows_ref[...] = result_recv[...].reshape(slots, width)
            cot_from = columns_dp.at(dp_count - n)
            load = pltpu.make_async_copy(cot_hbm.at[cot_from], result_recv, load_sems.at[4 + 2 * n])
            load.start()
            lane = lax.broadcasted_iota(jnp.int32, (slots, TILE), 1)
            probs = router_probs(dot_nn(rows_ref[...], router_ref[...]), lane, experts)
            gate = jnp.sum(jnp.where(lane == me, probs, 0.0), axis=1, keepdims=True)
            load.wait()
            cot = result_recv[...].reshape(slots, width)
            cot_ref[...] = (gate * cot.astype(f32)).astype(bf16)
            rows_t[...] = rows_ref[...].T
        cols = slice(c * 256, c * 256 + 256)
        act, slope = gelu_parts(dot_nn(rows_ref[...], win_ref[:, cols]))
        pre_grad = (dot_nt(cot_ref[...], wout_ref[cols, :]) * slope).astype(bf16)
        out_part = dot_tn(act.astype(bf16), cot_ref[...])
        in_part = dot_nn(rows_t[...], pre_grad)
        if n == 0:
            out_out[cols, :] = out_part
            in_out[:, cols] = in_part
        else:
            out_out[cols, :] += out_part
            in_out[:, cols] += in_part

    def input_back():
        held = pltpu.make_async_copy(hidden_grad_hbm, input_out, load_sems.at[3 + 2 * dp_count])
        held.start()
        x_load = pltpu.make_async_copy(x_hbm, rows_ref.at[pl.ds(0, tokens)], load_sems.at[6 + 2 * dp_count])
        x_load.start()
        for copies in shared_copies:
            for copy in copies:
                copy.wait_recv()
        held.wait()
        x_load.wait()
        for first, shared_rows in ((0, True), (PB, False)):
            rows = slice(first, PB if shared_rows else tokens)
            x = rows_ref[rows, :].astype(f32)
            inverse = inverse_rms(x)
            grad = local_ref[rows, :]
            if shared_rows:
                for n in range(ctx_count - 1):
                    grad = grad + shared_recv[n].astype(f32)
            through = grad * gain
            scaled = x * inverse
            shared = jnp.mean(through * scaled, axis=1, keepdims=True)
            input_out[rows, :] += inverse * (through - scaled * shared)

    def layer():
        held = pltpu.make_async_copy(hidden_hbm, input_out, load_sems.at[4 + 2 * dp_count])
        held.start()
        own_result.wait()
        await_blocks(result_hbm, result_recv, result_sems, False, True)
        place = place_rows(slot_row[...], 0, slots, tokens)
        returned = dot_tn(place, result_recv[...].reshape(slots, width))
        held.wait()
        layer_out[...] = (input_out[...] + returned).astype(bf16)

    work = [layer]
    work += [functools.partial(grads_of, n, c) for n in range(dp_count) for c in range(slice_width // 256)]
    work += [input_back]
    for time in range(blocks - 1, max(begin) + 2 * stages):
        if time >= blocks:
            advance(time)
        elif early:
            advance(time)
        s = time - blocks
        if 0 <= s < len(whole_axes):
            small_finish(s, small_pending)
            if s + 1 < len(whole_axes):
                small_pending = small_start(s + 1)
        if work:
            work.pop(0)()
    for rest in work:
        rest()
    for copy in started:
        copy.wait_send()
    await_blocks(result_hbm, result_recv, result_sems, True, False)
    each_row_block(lambda copy: copy.wait_send())


def finish_kernel(full_ref, in_ref, out_ref, input_ref, layer_ref, *results):
    weights, rest = results[:4], results[4:]
    for n, weight in enumerate(weights):
        weight[...] = full_ref[n].astype(f32).reshape(weight.shape)
    for source, target in zip((in_ref, out_ref, input_ref, layer_ref), rest):
        target[...] = source[...]


def tail_plan(sizes, width):
    group = 1
    for size in sizes:
        group *= size
    units = 4 * width // 16
    pieces = -(-units // group)
    lengths, left = [], group
    for size in sizes:
        left //= size
        lengths.append(left)
    return group, pieces, lengths


def body(
    inputs, cotangent, route, arrival, branch, attn_gain, query_weight, key_weight, value_weight,
    output_weight, rel_table, moe_gain, router_weight, expert_in, expert_out,
):
    x = inputs[0]
    cot = cotangent[0]
    tokens, width = x.shape
    own = tokens - PB
    buckets, heads = rel_table.shape
    experts = router_weight.shape[1]
    capacity = 9 * tokens // (8 * experts)
    block_rows = capacity if capacity % 8 == 0 else -(-capacity // 16) * 16
    slots = experts * block_rows
    ctx_count = lax.axis_size("ctx")
    dp_count = lax.axis_size("dp")
    plen = PB * ctx_count
    keys_total = plen + own
    hidden_units = expert_in.shape[2]
    pairs = width // TILE
    attn_gain_row = attn_gain.reshape(1, width)
    moe_gain_row = moe_gain.reshape(1, width)
    onehot = bucket_onehot(buckets)
    by_distance = jnp.dot(onehot, rel_table.astype(f32), precision=lax.Precision.HIGHEST).T
    by_distance = by_distance - by_distance[:, TILE - 1 :]
    bias = jnp.pad(by_distance.reshape(pairs, 2, TILE), ((0, 0), (0, 6), (0, 0)))
    router_wide = jnp.pad(router_weight, ((0, 0), (0, TILE - experts)))
    route_row = route.reshape(1, tokens)
    arrive_row = arrival[0]
    blocks = shape((experts, block_rows, width), bf16)
    block_space = pltpu.VMEM((experts, block_rows, width), bf16)
    block_sems = pltpu.SemaphoreType.DMA((2, experts - 1))
    any_space = pl.BlockSpec(memory_space=pl.ANY)

    slot_row, cot_sent, normed_own, normed_all, queries, keys, values, att, lse = pl.pallas_call(
        functools.partial(front_kernel, capacity),
        out_shape=[
            shape((1, tokens), jnp.int32),
            blocks,
            shape((tokens, width), bf16),
            shape((plen, width), bf16),
            shape((tokens, width), bf16),
            shape((keys_total, width), bf16),
            shape((keys_total, width), bf16),
            shape((width, tokens), bf16),
            shape((pairs, 8, tokens), f32),
        ],
        in_specs=[smem()] + [vmem()] * 9,
        out_specs=[vmem()] * 9,
        scratch_shapes=[
            pltpu.VMEM((ctx_count, PB, width), bf16),
            block_space,
            pltpu.VMEM((keys_total, tokens), f32),
            pltpu.VMEM((keys_total, tokens), bf16),
            pltpu.SemaphoreType.DMA((2, 2, ctx_count - 1, CHUNKS)),
            block_sems,
        ],
        compiler_params=remote_params(1),
        cost_estimate=cost(40 * keys_total * tokens * width, 20 * width * width),
        name="front",
    )(
        branch, bias, x, cot, attn_gain_row, route_row, arrive_row,
        query_weight, key_weight, value_weight,
    )
    cot_all = lax.all_gather(cot_sent, "dp", axis=0, tiled=False)

    members = 2 * lax.axis_size("expert") if ctx_count % 2 == 0 else experts
    group_rows = members * block_rows
    (
        rows_sent, router_part, hidden_grad, wo_part, att_grad, delta, moe_gain_part,
        result, hidden,
    ) = pl.pallas_call(
        functools.partial(expert_kernel, experts),
        out_shape=[
            blocks, shape((TILE, width), f32), shape((tokens, width), f32), shape((width // 16, 16, width), bf16),
            shape((tokens, width), bf16), shape((pairs, 8, tokens), f32), shape((1, width), f32),
            blocks, shape((tokens, width), f32),
        ],
        in_specs=[vmem()] * 8 + [any_space] * 2,
        out_specs=[vmem()] * 9,
        scratch_shapes=[
            pltpu.VMEM((tokens, width), bf16),
            block_space,
            pltpu.VMEM((width, hidden_units), bf16),
            pltpu.VMEM((hidden_units, width), bf16),
            pltpu.VMEM((group_rows, width), bf16),
            pltpu.VMEM((group_rows, width), bf16),
            pltpu.VMEM((group_rows, width), f32),
            pltpu.VMEM((group_rows, width), f32),
            block_space, block_space,
            pltpu.VMEM((tokens, width), bf16),
            pltpu.VMEM((width, tokens), bf16),
            block_sems, block_sems,
            pltpu.SemaphoreType.DMA((2,)),
        ],
        compiler_params=remote_params(2),
        cost_estimate=cost(8 * slots * width * hidden_units, 12 * width * hidden_units),
        name="expert",
    )(
        att, x, output_weight, moe_gain_row, router_wide, slot_row, cot, cot_sent,
        expert_in[0], expert_out[0],
    )
    att_grad, cot_all = lax.optimization_barrier((att_grad, cot_all))

    expert_count = lax.axis_size("expert")
    dp_sizes = [2, 2] if dp_count == 4 else [dp_count]
    sizes = [expert_count, *dp_sizes, ctx_count]
    plan = tail_plan(sizes, width)
    group, pieces, lengths = plan
    units = group * pieces

    table_rows = heads * TILE // width
    small_rows = -(-(2 + experts + table_rows) // 8) * 8
    slice_width = hidden_units // dp_count
    weights, small, input_grad, in_grad, out_grad, layer_out, _ = pl.pallas_call(
        functools.partial(back_kernel, experts, plan),
        out_shape=[
            shape((units, 16, width), bf16), shape((small_rows, width), f32), shape((tokens, width), f32),
            shape((width, slice_width), f32), shape((slice_width, width), f32), shape((tokens, width), bf16),
            shape((dp_count - 1, experts, block_rows, width), bf16),
        ],
        in_specs=[
            smem(), vmem(), vmem(), any_space, any_space, vmem(), vmem(), vmem(), any_space, vmem(),
            vmem(), vmem(), vmem(), vmem(), any_space, vmem(), any_space, any_space, any_space,
            any_space, vmem(), any_space, any_space, any_space, any_space, any_space, vmem(),
        ],
        out_specs=[vmem()] * 6 + [any_space],
        scratch_shapes=[
            pltpu.VMEM((2, PB, width), bf16),
            pltpu.VMEM((2, PB, width), bf16),
            pltpu.VMEM((2, PB, width), bf16),
            pltpu.VMEM((PB, tokens), f32),
            pltpu.VMEM((PB, tokens), f32),
            pltpu.VMEM((PB, tokens), bf16),
            pltpu.VMEM((PB, tokens), bf16),
            pltpu.VMEM((width, tokens), f32),
            pltpu.VMEM((PB, width), bf16),
            pltpu.VMEM((PB, width), bf16),
            pltpu.VMEM((heads, 8, TILE), f32),
            pltpu.VMEM((1, width), f32),
            pltpu.VMEM((tokens, width), f32),
            pltpu.VMEM((min(ctx_count - 1, 16 // ctx_count), PB, width), bf16),
            pltpu.VMEM((ctx_count - 1, PB, width), bf16),
            pltpu.VMEM((units, 16, width), bf16),
            [pltpu.VMEM((pieces, length, 16, width), bf16) for length in lengths[:-1]],
            [
                pltpu.VMEM((pieces, size - 1, length, 16, width), bf16)
                for size, length in zip(sizes, lengths)
            ],
            pltpu.VMEM((small_rows, width), f32),
            [pltpu.VMEM((size - 1, small_rows, width), f32) for size in (expert_count, dp_count, ctx_count)],
            block_space,
            pltpu.VMEM((width, slice_width), bf16),
            pltpu.VMEM((slice_width, width), bf16),
            pltpu.VMEM((slots, width), bf16),
            pltpu.VMEM((slots, width), bf16),
            pltpu.VMEM((width, slots), bf16),
            pltpu.SemaphoreType.DMA((ctx_count + 1, 3)),
            pltpu.SemaphoreType.DMA((8 + 2 * dp_count,)),
            pltpu.SemaphoreType.DMA(
                (2, 2 * pieces * sum((n - 1) * cuts_of(length) for n, length in zip(sizes, lengths)))
            ),
            pltpu.SemaphoreType.DMA((2, expert_count + dp_count + ctx_count - 3)),
            pltpu.SemaphoreType.DMA((2, (ctx_count - 1) * SHARED_CUTS)),
            block_sems,
            pltpu.SemaphoreType.DMA((2, dp_count - 1, experts)),
        ],
        compiler_params=remote_params(0),
        cost_estimate=cost(
            8 * dp_count * slots * width * slice_width + 80 * keys_total * tokens * width,
            60 * width * slice_width,
        ),
        name="back",
    )(
        branch, bias, queries, keys, values, att_grad, lse, delta, normed_all, normed_own,
        attn_gain_row, query_weight, key_weight, value_weight, wo_part, moe_gain_part, router_part, x,
        hidden_grad, hidden, slot_row, result,
        rows_sent, cot_all, expert_in[0], expert_out[0], router_wide,
    )

    matrix_units = width // 16
    steps = 4

    def part_rows(rows, columns=width):
        return pl.BlockSpec((rows // steps, columns), lambda i: (i, 0))

    weights = weights[: 4 * matrix_units].reshape(4, matrix_units, 16, width)
    *weights, in_grad, out_grad, input_grad, layer_out = pl.pallas_call(
        finish_kernel,
        grid=(steps,),
        out_shape=[shape((width, width), f32)] * 4
        + [
            shape((width, slice_width), f32), shape((slice_width, width), f32),
            shape((tokens, width), f32), shape((tokens, width), bf16),
        ],
        in_specs=[
            pl.BlockSpec((4, matrix_units // steps, 16, width), lambda i: (0, i, 0, 0)),
            part_rows(width, slice_width), part_rows(slice_width), part_rows(tokens), part_rows(tokens),
        ],
        out_specs=[part_rows(width)] * 4
        + [part_rows(width, slice_width), part_rows(slice_width), part_rows(tokens), part_rows(tokens)],
        compiler_params=params(),
        cost_estimate=cost(8 * width * width, 48 * width * width),
        name="finish",
    )(weights, in_grad, out_grad, input_grad, layer_out)
    router_grad = small[:experts].T
    hist_sum = small[2 + experts : 2 + experts + table_rows].reshape(heads, TILE)
    last = onehot[:, buckets - 1 :]
    spread = jnp.concatenate([onehot[:, : buckets - 1], last - 1.0], axis=1)
    table_grad = jnp.dot(spread.T, hist_sum.T, precision=lax.Precision.HIGHEST)
    return (
        layer_out[None],
        input_grad[None],
        small[experts],
        weights[3],
        weights[2],
        weights[1],
        weights[0],
        table_grad,
        small[experts + 1],
        router_grad,
        in_grad[None],
        out_grad[None],
    )


def solution(mesh):
    grouped = P(("dp", "expert"), "ctx", None)
    placed = (
        grouped, grouped, grouped, grouped, P(("dp", "expert"), "ctx"),
        P(), P(), P(), P(), P(), P(), P(), P(),
        P(("ctx", "expert"), None, None),
        P(("ctx", "expert"), None, None),
    )
    return jax.shard_map(
        body,
        mesh=mesh,
        in_specs=placed,
        out_specs=(
            grouped, grouped, P(), P(), P(), P(), P(), P(), P(), P(),
            P(("ctx", "expert"), None, "dp"),
            P(("ctx", "expert"), "dp", None),
        ),
        check_vma=False,
    )
```

```python
import functools

import jax
import jax.numpy as jnp
from jax import lax
from jax.experimental import pallas as pl
from jax.experimental.pallas import tpu as pltpu
from jax.sharding import PartitionSpec as P

PB = 256
TILE = 128
CHUNKS = 8
SHARED_CUTS = 4

bucket_edges = (19, 21, 24, 27, 31, 35, 40, 46, 52, 59, 67, 77, 87, 99, 113)
norm_eps = 1e-06
masked_score = -1e30
gelu_scale = 0.7978845608
gelu_cube = 0.044715

bf16 = jnp.bfloat16
f32 = jnp.float32
VMEM_LIMIT = 121 * 512 * 1024


def dot_nn(a, b):
    return jnp.dot(a, b, preferred_element_type=f32)


def dot_nt(a, b):
    return lax.dot_general(a, b, (((1,), (1,)), ((), ())), preferred_element_type=f32)


def dot_tn(a, b):
    return lax.dot_general(a, b, (((0,), (0,)), ((), ())), preferred_element_type=f32)


def two_parts(a):
    high = a.astype(bf16)
    return high, (a - high.astype(f32)).astype(bf16)


def vmem():
    return pl.BlockSpec(memory_space=pltpu.VMEM)


def smem():
    return pl.BlockSpec(memory_space=pltpu.SMEM)


def params():
    return pltpu.CompilerParams(vmem_limit_bytes=VMEM_LIMIT)


def remote_params(number):
    return pltpu.CompilerParams(
        vmem_limit_bytes=VMEM_LIMIT, collective_id=number, has_side_effects=True
    )


def cost(flops, nbytes):
    return pl.CostEstimate(flops=int(flops), bytes_accessed=int(nbytes), transcendentals=0)


def shape(dims, kind):
    return jax.ShapeDtypeStruct(dims, kind)


def inverse_rms(x):
    return lax.rsqrt(jnp.mean(x * x, axis=-1, keepdims=True) + norm_eps)


def bucket_onehot(buckets):
    distance = jnp.arange(TILE, dtype=jnp.int32)
    ids = jnp.minimum(distance, 16)
    for edge in bucket_edges:
        ids = ids + (distance >= edge).astype(jnp.int32)
    return (ids[:, None] == jnp.arange(buckets, dtype=jnp.int32)[None, :]).astype(f32)


def near_index(first):
    rows = lax.broadcasted_iota(jnp.int32, (TILE, TILE), 0)
    lanes = lax.broadcasted_iota(jnp.int32, (TILE, TILE), 1)
    return first + lanes - rows


def near_tiles(ctx_at, plen):
    start = ctx_at * PB
    return (
        (start, 0, 0, False),
        (start, TILE, TILE, False),
        (start + TILE, TILE, 0, False),
        (plen, PB, 0, False),
        (plen, PB + TILE, TILE, False),
        (plen + TILE, PB + TILE, 0, False),
        (start - TILE, 0, TILE, True),
    )


def add_near(s_ref, bias_row, ctx_at, branch, plen):
    source = jnp.broadcast_to(bias_row, (TILE, TILE))
    add_tiles(s_ref, source, ctx_at, near_tiles(ctx_at, plen))

    def window(i, _):
        rows = pl.ds(pl.multiple_of(i * TILE, TILE), TILE)
        lanes = slice(PB, PB + TILE)
        index = jnp.clip(near_index(branch - i * TILE), 0, TILE - 1)
        s_ref[rows, lanes] = s_ref[rows, lanes] + jnp.take_along_axis(source, index, axis=1)
        return 0

    lax.fori_loop(1, plen // TILE, window, 0)


def add_tiles(s_ref, source, ctx_at, tiles):
    for first_row, first_lane, gap, guarded in tiles:
        def work(first_row=first_row, first_lane=first_lane, gap=gap):
            rows = pl.ds(first_row if isinstance(first_row, int) else pl.multiple_of(first_row, 16), TILE)
            lanes = slice(first_lane, first_lane + TILE)
            index = jnp.clip(near_index(gap), 0, TILE - 1)
            s_ref[rows, lanes] = s_ref[rows, lanes] + jnp.take_along_axis(source, index, axis=1)

        if guarded:
            pl.when(ctx_at > 0)(work)
        else:
            work()


def scores_to(s_ref, keys, queries, plen):
    s_ref[:plen, :] = dot_nt(keys[:plen], queries)
    s_ref[plen:, PB:] = dot_nt(keys[plen:], queries[PB:])


def limits(ctx_at, branch, tokens):
    lane = lax.broadcasted_iota(jnp.int32, (1, tokens), 1)
    return jnp.where(lane < PB, ctx_at * PB + lane + 1, branch)


def row_steps(first, count, lanes):
    return first + lax.broadcasted_iota(jnp.int32, (count, lanes), 0)


def own_allowed(first, count, lanes):
    return row_steps(first, count, lanes) <= lax.broadcasted_iota(jnp.int32, (count, lanes), 1)


def head_lanes(half):
    return lax.broadcasted_iota(jnp.int32, (1, TILE), 1) // (TILE // 2) == half


def pick_rows(pieces, lanes):
    row = lax.broadcasted_iota(jnp.int32, (8, lanes), 0)
    return jnp.where(row == 0, pieces[0], jnp.where(row == 1, pieces[1], 0.0))


def fold8(x, op):
    return op(x.reshape(x.shape[0] // 8, 8, x.shape[1]), axis=0)


def owner_device(index):
    cores = lax.axis_size("expert")
    return {"ctx": index // cores, "expert": lax.rem(index, cores)}


def owners():
    cores = lax.axis_size("expert")
    count = cores * lax.axis_size("ctx")
    return count, lax.axis_index("ctx") * cores + lax.axis_index("expert")


def greet_owners():
    count, me = owners()
    barrier = pltpu.get_barrier_semaphore()

    def greet(ahead, _):
        pl.semaphore_signal(
            barrier, inc=1, device_id=owner_device(lax.rem(me + ahead, count)),
            device_id_type=pl.DeviceIdType.MESH,
        )
        return 0

    lax.fori_loop(1, count, greet, 0)
    pl.semaphore_wait(barrier, count - 1)


def block_copy(source, target, sems, ahead):
    count, me = owners()
    peer = lax.rem(me + ahead, count)
    return pltpu.make_async_remote_copy(
        src_ref=source.at[peer], dst_ref=target.at[me],
        send_sem=sems.at[0, ahead - 1], recv_sem=sems.at[1, ahead - 1],
        device_id=owner_device(peer), device_id_type=pl.DeviceIdType.MESH,
    )


def await_blocks(source, target, sems, sent, received):
    def one(ahead, _):
        copy = block_copy(source, target, sems, ahead)
        if received:
            copy.wait_recv()
        if sent:
            copy.wait_send()
        return 0

    lax.fori_loop(1, owners()[0], one, 0)


def place_rows(slot_row, index, block_rows, tokens):
    rows = lax.broadcasted_iota(jnp.int32, (block_rows, tokens), 0) + index * block_rows
    return (rows == slot_row).astype(bf16)


def front_kernel(
    capacity,
    branch_ref, bias_ref, x_ref, cot_ref, gain_ref, route_row, arrive_row,
    wq_ref, wk_ref, wv_ref,
    slot_out, cot_out, normed_own_out, normed_out, q_ref, k_out, v_out, att_out, lse_out,
    prompt_ref, send_ref, s_ref, p_ref, prompt_sems, cot_sems,
):
    branch = branch_ref[0, 0]
    ctx_at, ctx_count = lax.axis_index("ctx"), lax.axis_size("ctx")
    plen = PB * ctx_count
    tokens, width = x_ref.shape
    own = tokens - PB
    gain = gain_ref[...].astype(f32)
    count, me = owners()
    block_rows = send_ref.shape[1]
    greet_owners()

    chunk = PB // CHUNKS

    def pass_on(step, up, c):
        block = ctx_at - step if up else ctx_at + step
        ahead = ctx_at + 1 if up else ctx_at - 1
        fits = (block >= 0) & (ahead < ctx_count) if up else (block < ctx_count) & (ahead >= 0)
        piece = pl.ds(c * chunk, chunk)
        source = x_ref.at[piece] if step == 0 else prompt_ref.at[block, piece]
        copy = pltpu.make_async_remote_copy(
            src_ref=source, dst_ref=prompt_ref.at[block, piece],
            send_sem=prompt_sems.at[0, int(up), step, c], recv_sem=prompt_sems.at[1, int(up), step, c],
            device_id={"ctx": ahead}, device_id_type=pl.DeviceIdType.MESH,
        )
        return fits, copy

    def arrival(step, up, c):
        block = ctx_at - step - 1 if up else ctx_at + step + 1
        fits = block >= 0 if up else block < ctx_count
        place = prompt_ref.at[block, pl.ds(c * chunk, chunk)]
        copy = pltpu.make_async_remote_copy(
            src_ref=place, dst_ref=place,
            send_sem=prompt_sems.at[0, int(up), step, c], recv_sem=prompt_sems.at[1, int(up), step, c],
            device_id={"ctx": ctx_at}, device_id_type=pl.DeviceIdType.MESH,
        )
        return fits, block, copy

    for c in range(CHUNKS):
        for up in (True, False):
            fits, copy = pass_on(0, up, c)
            pl.when(fits)(copy.start)

    x = x_ref[...].astype(f32)
    normed_own_out[...] = (x * inverse_rms(x) * gain).astype(bf16)

    def column(i, _):
        cols = pl.ds(pl.multiple_of(i * 256, 256), 256)
        q_ref[:, cols] = dot_nn(normed_own_out[...], wq_ref[:, cols]).astype(bf16)
        k_out[plen:, cols] = dot_nn(normed_own_out[PB:, :], wk_ref[:, cols]).astype(bf16)
        v_out[plen:, cols] = dot_nn(normed_own_out[PB:, :], wv_ref[:, cols]).astype(bf16)
        return 0

    lax.fori_loop(0, width // 256, column, 0)

    def project(block):
        rows = pl.ds(pl.multiple_of(block * PB, PB), PB)

        def prompt_column(i, _):
            cols = pl.ds(pl.multiple_of(i * 256, 256), 256)
            k_out[rows, cols] = dot_nn(normed_out[rows, :], wk_ref[:, cols]).astype(bf16)
            v_out[rows, cols] = dot_nn(normed_out[rows, :], wv_ref[:, cols]).astype(bf16)
            return 0

        lax.fori_loop(0, width // 256, prompt_column, 0)

    def take(block):
        x = prompt_ref[block].astype(f32)
        rows = pl.ds(pl.multiple_of(block * PB, PB), PB)
        normed_out[rows, :] = (x * inverse_rms(x) * gain).astype(bf16)
        project(block)

    for step in range(ctx_count - 1):
        for c in range(CHUNKS):
            for up in (True, False):
                fits, block, copy = arrival(step, up, c)
                pl.when(fits)(copy.wait_recv)
                if step < ctx_count - 2:
                    fits, copy = pass_on(step + 1, up, c)
                    pl.when(fits)(copy.start)
        if step == 0:
            normed_out[pl.ds(pl.multiple_of(ctx_at * PB, PB), PB), :] = normed_own_out[:PB, :]
            project(ctx_at)
        for up in (True, False):
            fits, block, copy = arrival(step, up, 0)
            pl.when(fits)(functools.partial(take, block))

    def down(row):
        column = jnp.broadcast_to(row[...].astype(f32), (TILE, tokens)).T
        return jnp.concatenate([column] * (tokens // TILE), axis=1)

    same = down(route_row) == route_row[...].astype(f32)
    earlier = down(arrive_row) < arrive_row[...].astype(f32)
    rank = jnp.sum(jnp.where(same & earlier, 1.0, 0.0), axis=0, keepdims=True).astype(jnp.int32)
    slot = jnp.where(rank < capacity, route_row[...] * block_rows + rank, count * block_rows)
    slot_out[...] = slot

    def send_cot(ahead, _):
        peer = lax.rem(me + ahead, count)
        place = place_rows(slot_out[...], peer, block_rows, tokens)
        send_ref[peer] = dot_nn(place, cot_ref[...]).astype(bf16)
        block_copy(send_ref, cot_out, cot_sems, ahead).start()
        return 0

    def send_cots():
        lax.fori_loop(1, count, send_cot, 0)
        cot_out[me] = dot_nn(place_rows(slot_out[...], me, block_rows, tokens), cot_ref[...]).astype(bf16)

    p_ref[plen:, :PB] = jnp.zeros((own, PB), bf16)
    limit = limits(ctx_at, branch, tokens)

    def pair(g, _):
        pl.when(g == 1)(send_cots)
        lanes = pl.ds(pl.multiple_of(g * TILE, TILE), TILE)
        queries = q_ref[:, lanes]
        keys = k_out[:, lanes]
        values_t = v_out[:, lanes].T
        bias = bias_ref[g]
        lse_rows, att_rows = [], []
        for half in range(2):
            scores_to(s_ref, jnp.where(head_lanes(half), keys, jnp.zeros_like(keys)), queries, plen)
            add_near(s_ref, bias[half : half + 1, :], ctx_at, branch, plen)

            def top_of(i, top):
                for part in range(0, TILE, 32):
                    first = pl.multiple_of(i * TILE + part, 32)
                    rows = pl.ds(first, 32)
                    s = jnp.where(row_steps(first, 32, tokens) < limit, s_ref[rows, :], masked_score)
                    s_ref[rows, :] = s
                    top = jnp.maximum(top, fold8(s, jnp.max))
                return top

            top = lax.fori_loop(0, plen // TILE, top_of, jnp.full((8, tokens), masked_score, f32))
            own_top = jnp.full((8, own), masked_score, f32)
            for i in range(own // TILE):
                rows = slice(plen + i * TILE, plen + (i + 1) * TILE)
                s = jnp.where(own_allowed(i * TILE, TILE, own), s_ref[rows, PB:], masked_score)
                s_ref[rows, PB:] = s
                own_top = jnp.maximum(own_top, fold8(s, jnp.max))
            top = jnp.concatenate([top[:, :PB], jnp.maximum(top[:, PB:], own_top)], axis=1)
            top = jnp.max(top, axis=0, keepdims=True)

            def weigh(i, total):
                for part in range(0, TILE, 32):
                    rows = pl.ds(pl.multiple_of(i * TILE + part, 32), 32)
                    p = jnp.exp(s_ref[rows, :] - top)
                    p_ref[rows, :] = p.astype(bf16)
                    total = total + fold8(p, jnp.sum)
                return total

            total = lax.fori_loop(0, plen // TILE, weigh, jnp.zeros((8, tokens), f32))
            own_total = jnp.zeros((8, own), f32)
            for i in range(own // TILE):
                rows = slice(plen + i * TILE, plen + (i + 1) * TILE)
                p = jnp.exp(s_ref[rows, PB:] - top[:, PB:])
                p_ref[rows, PB:] = p.astype(bf16)
                own_total = own_total + fold8(p, jnp.sum)
            total = jnp.concatenate([total[:, :PB], total[:, PB:] + own_total], axis=1)
            total = jnp.sum(total, axis=0, keepdims=True)
            rows = slice(half * 64, half * 64 + 64)
            att_rows.append((dot_nn(values_t[rows, :], p_ref[...]) / total).astype(bf16))
            lse_rows.append(top + jnp.log(total))
        att_out[lanes, :] = jnp.concatenate(att_rows, axis=0)
        lse_out[g] = pick_rows(lse_rows, tokens)
        return 0

    lax.fori_loop(0, width // TILE, pair, 0)
    await_blocks(send_ref, cot_out, cot_sems, True, True)
    for step in range(ctx_count - 1):
        for c in range(CHUNKS):
            for up in (True, False):
                fits, copy = pass_on(step, up, c)
                pl.when(fits)(copy.wait_send)


def router_probs(logits, lane, experts):
    logits = jnp.where(lane < experts, logits, masked_score)
    logits = jnp.exp(logits - jnp.max(logits, axis=1, keepdims=True))
    return logits / jnp.sum(logits, axis=1, keepdims=True)


def gelu_parts(v):
    t = jnp.tanh(gelu_scale * (v + gelu_cube * (v * v * v)))
    half = 0.5 * (1.0 + t)
    slope = half + 0.5 * v * (1.0 - t * t) * (gelu_scale + (3.0 * gelu_scale * gelu_cube) * (v * v))
    return v * half, slope


def expert_kernel(
    experts,
    att_ref, x_ref, wo_ref, gain_ref, router_ref, slot_row, cot_ref, cot_rows, win_hbm, wout_hbm,
    rows_out, router_out, hidden_grad_out, wo_grad_out, att_grad_out, delta_out, gain_grad_out,
    result_out, hidden_ref,
    moe_ref, send_ref, win_ref, wout_ref, group_rows, sent_ref, result_acc, grad_acc,
    grad_send, grad_recv, low_ref, att_t_ref, rows_sems, grad_sems, load_sems,
):
    tokens, width = x_ref.shape
    count, me = owners()
    block_rows = send_ref.shape[1]
    hidden_units = win_ref.shape[1]
    loads = [
        pltpu.make_async_copy(win_hbm, win_ref, load_sems.at[0]),
        pltpu.make_async_copy(wout_hbm, wout_ref, load_sems.at[1]),
    ]
    for copy in loads:
        copy.start()
    greet_owners()

    def column(i, _):
        cols = pl.ds(pl.multiple_of(i * 256, 256), 256)
        hidden_ref[:, cols] = x_ref[:, cols].astype(f32) + dot_tn(att_ref[...], wo_ref[:, cols])
        return 0

    lax.fori_loop(0, width // 256, column, 0)
    hidden = hidden_ref[...]
    moe_ref[...] = (hidden * inverse_rms(hidden) * gain_ref[...].astype(f32)).astype(bf16)

    members = 2 * lax.axis_size("expert") if lax.axis_size("ctx") % 2 == 0 else count
    groups = count // members
    my_group = me // members

    def send_rows(ahead, _):
        peer = lax.rem(me + ahead, count)
        place = place_rows(slot_row[...], peer, block_rows, tokens)
        send_ref[peer] = dot_nn(place, moe_ref[...]).astype(bf16)
        block_copy(send_ref, rows_out, rows_sems, ahead).start()
        return 0

    def send_group(g, _):
        base = lax.rem(my_group + g, groups) * members

        def member(i, _):
            ahead = lax.rem(base + i - me + count, count)
            pl.when(ahead > 0)(lambda: (send_rows(ahead, 0), None)[1])
            return 0

        return lax.fori_loop(0, members, member, 0)

    lax.fori_loop(0, groups, send_group, 0)
    rows_out[me] = dot_nn(place_rows(slot_row[...], me, block_rows, tokens), moe_ref[...]).astype(bf16)

    router_out[...] = jnp.zeros_like(router_out)
    for copy in loads:
        copy.wait()

    def group(g, _):
        base = lax.rem(my_group + g, groups) * members

        def arrive(i, _):
            behind = lax.rem(me - base - i + count, count)
            pl.when(behind > 0)(lambda: block_copy(send_ref, rows_out, rows_sems, behind).wait_recv())
            return 0

        lax.fori_loop(0, members, arrive, 0)
        blocks = pl.ds(base, members)
        size = members * block_rows
        group_rows[...] = rows_out[blocks].reshape(size, width)
        slot_lane = lax.broadcasted_iota(jnp.int32, (size, TILE), 1)
        mine = slot_lane == me
        probs = router_probs(dot_nn(group_rows[...], router_ref[...]), slot_lane, experts)
        gate = jnp.sum(jnp.where(mine, probs, 0.0), axis=1, keepdims=True)
        cot_group = cot_rows[blocks].reshape(size, width).astype(f32)
        sent_ref[...] = (gate * cot_group).astype(bf16)
        result_acc[...] = jnp.zeros_like(result_acc)
        grad_acc[...] = jnp.zeros_like(grad_acc)

        def units(i, _):
            cols = pl.ds(pl.multiple_of(i * width, width), width)
            act, slope = gelu_parts(dot_nn(group_rows[...], win_ref[:, cols]))
            result_acc[...] += dot_nn(act.astype(bf16), wout_ref[cols, :])
            pre_grad = (dot_nt(sent_ref[...], wout_ref[cols, :]) * slope).astype(bf16)
            grad_acc[...] += dot_nt(pre_grad, win_ref[:, cols])
            return 0

        lax.fori_loop(0, hidden_units // width, units, 0)
        result = result_acc[...].astype(bf16)
        gate_grad = jnp.sum(cot_group * result.astype(f32), axis=1, keepdims=True)
        logit_grad = (gate_grad * gate) * (jnp.where(mine, 1.0, 0.0) - probs)
        high, low = two_parts(logit_grad)
        grad = grad_acc[...] + (dot_nt(high, router_ref[...]) + dot_nt(low, router_ref[...]))
        grad_send[blocks] = grad.astype(bf16).reshape(members, block_rows, width)
        gated = (gate * result.astype(f32)).astype(bf16)
        result_out[blocks] = gated.reshape(members, block_rows, width)

        def give(i, _):
            ahead = lax.rem(base + i - me + count, count)

            @pl.when(ahead > 0)
            def _():
                block_copy(grad_send, grad_recv, grad_sems, ahead).start()

            return 0

        lax.fori_loop(0, members, give, 0)
        router_out[...] += dot_tn(high, group_rows[...]) + dot_tn(low, group_rows[...])
        return 0

    lax.fori_loop(0, groups, group, 0)
    grad_recv[me] = grad_send[me]

    slots = count * block_rows
    place = place_rows(slot_row[...], 0, slots, tokens)
    await_blocks(grad_send, grad_recv, grad_sems, False, True)
    moe_grad = dot_tn(place, grad_recv[...].reshape(slots, width))
    hidden = hidden_ref[...]
    inverse = inverse_rms(hidden)
    scaled = hidden * inverse
    gain_grad_out[...] = jnp.sum(moe_grad * scaled, axis=0, keepdims=True)
    through = moe_grad * gain_ref[...].astype(f32)
    shared = jnp.mean(through * scaled, axis=1, keepdims=True)
    hidden_grad = cot_ref[...].astype(f32) + inverse * (through - scaled * shared)
    hidden_grad_out[...] = hidden_grad
    low_ref[...] = hidden_grad.astype(bf16)

    def back_column(i, _):
        cols = pl.ds(pl.multiple_of(i * 256, 256), 256)
        wo_grad = dot_nn(att_ref[...], low_ref[:, cols]).astype(bf16).reshape(width // 16, 16, 256)
        if wo_grad_out.shape[0] == 1:
            wo_grad_out[0, :, :, cols] = wo_grad
        else:
            wo_grad_out[i] = wo_grad
        att_grad_out[:, cols] = dot_nt(low_ref[...], wo_ref[cols, :]).astype(bf16)
        att_t_ref[cols, :] = dot_nt(wo_ref[cols, :], low_ref[...]).astype(bf16)
        return 0

    lax.fori_loop(0, width // 256, back_column, 0)

    def pair(g, _):
        rows = pl.ds(pl.multiple_of(g * TILE, TILE), TILE)
        both = att_ref[rows, :].astype(f32) * att_t_ref[rows, :].astype(f32)
        delta_out[g] = pick_rows(
            [jnp.sum(both[:64], axis=0, keepdims=True), jnp.sum(both[64:], axis=0, keepdims=True)],
            tokens,
        )
        return 0

    lax.fori_loop(0, width // TILE, pair, 0)
    await_blocks(send_ref, rows_out, rows_sems, True, False)
    await_blocks(grad_send, grad_recv, grad_sems, True, False)


class Axis:
    def __init__(self, name, size, step=1):
        place = lax.axis_index(name)
        self.name, self.size, self.step, self.place = name, size, step, place
        self.index = lax.rem(place // step, size)

    def at(self, ahead):
        return lax.rem(self.index + ahead, self.size)

    def peer(self, ahead):
        return {self.name: self.place + (self.at(ahead) - self.index) * self.step}


def mesh_axes():
    dp, ctx, expert = lax.axis_size("dp"), lax.axis_size("ctx"), lax.axis_size("expert")
    cores, lines = Axis("expert", expert), Axis("ctx", ctx)
    if dp == 4:
        near, far = Axis("dp", 2, 1), Axis("dp", 2, 2)
        return [[cores, near, far, lines], [cores, far, near, lines]]
    return [[cores, Axis("dp", dp), lines]] * 2


def cuts_of(length):
    return 4 if length % 8 == 0 else 2 if length % 4 == 0 else 1


def push(source, target, sems, slot, device):
    copy = pltpu.make_async_remote_copy(
        src_ref=source, dst_ref=target, send_sem=sems.at[0, slot], recv_sem=sems.at[1, slot],
        device_id=device, device_id_type=pl.DeviceIdType.MESH,
    )
    copy.start()
    return copy


def back_kernel(
    experts, plan,
    branch_ref, bias_ref, q_ref, k_hbm, v_hbm, att_grad_ref, lse_ref, delta_ref, normed_hbm, normed_own_ref,
    gain_ref, wq_ref, wk_ref, wv_ref, wo_part_hbm, moe_gain_ref, router_part_hbm, x_hbm, hidden_grad_hbm,
    hidden_hbm, slot_row, result_hbm, rows_hbm, cot_hbm, win_hbm, wout_hbm, router_ref,
    full_ref, small_out, input_out, in_out, out_out, layer_out, rows_all,
    k_ref, v_ref, normed_ref, s_ref, dp_ref, p_ref, ds_ref, dq_ref, dk_ref, dv_ref, hist_ref, gain_sum,
    local_ref, shared_send, shared_recv, parts_ref, acc_refs, recv_refs, small_ref, small_recv,
    result_recv, win_ref, wout_ref, rows_ref, cot_ref, rows_t,
    block_sems, load_sems, sems, small_sems, shared_sems, result_sems, rows_sems,
):
    group, pieces, lengths = plan
    flows = mesh_axes()
    branch = branch_ref[0, 0]
    ctx_at = lax.axis_index("ctx")
    ctx_count, dp_count = lax.axis_size("ctx"), lax.axis_size("dp")
    tokens, width = q_ref.shape
    own = tokens - PB
    plen = PB * ctx_count
    count, me = owners()
    lines, columns_dp = Axis("ctx", ctx_count), Axis("dp", dp_count)
    whole_axes = [Axis("expert", lax.axis_size("expert")), columns_dp, lines]
    gain = gain_ref[...].astype(f32)
    limit = limits(ctx_at, branch, tokens)
    blocks = ctx_count + 1
    rows_16 = width // 16

    def block_loads(i):
        rows = plen if i == blocks - 1 else pl.multiple_of(lines.at(i + 1) * PB, PB)
        sources = [(k_hbm, k_ref, 0), (v_hbm, v_ref, 1)]
        if i < blocks - 2:
            sources.append((normed_hbm, normed_ref, 2))
        return [
            pltpu.make_async_copy(source.at[pl.ds(rows, PB)], target.at[i % 2], block_sems.at[i, n])
            for source, target, n in sources
        ]

    for copy in block_loads(0):
        copy.start()
    slice_width = win_ref.shape[1]
    part = pl.ds(pl.multiple_of(lax.axis_index("dp") * slice_width, slice_width), slice_width)
    weight_loads = [
        pltpu.make_async_copy(win_hbm.at[:, part], win_ref, load_sems.at[0]),
        pltpu.make_async_copy(wout_hbm.at[part], wout_ref, load_sems.at[1]),
    ]
    own_result = pltpu.make_async_copy(result_hbm.at[me], result_recv.at[me], load_sems.at[2])
    wo_load = pltpu.make_async_copy(wo_part_hbm.at[0], parts_ref.at[pl.ds(0, rows_16)], load_sems.at[5 + 2 * dp_count])
    router_load = pltpu.make_async_copy(
        router_part_hbm.at[pl.ds(0, experts)], small_ref.at[pl.ds(0, experts)], load_sems.at[7 + 2 * dp_count]
    )
    for copy in [wo_load, *weight_loads, own_result, router_load]:
        copy.start()

    barrier = pltpu.get_barrier_semaphore()

    def greet(ahead, _):
        pl.semaphore_signal(
            barrier, inc=1, device_id=owner_device(lax.rem(me + ahead, count)),
            device_id_type=pl.DeviceIdType.MESH,
        )
        return 0

    lax.fori_loop(1, count, greet, 0)
    for ahead in range(1, dp_count):
        pl.semaphore_signal(
            barrier, inc=1, device_id=columns_dp.peer(ahead), device_id_type=pl.DeviceIdType.MESH
        )
    pl.semaphore_wait(barrier, count - 1 + dp_count - 1)

    slots_of = {}

    def slot(*key):
        return slots_of.setdefault(key, len(slots_of))

    started = []

    def reduce_start(j, s):
        axis, length = flows[j % 2][s], lengths[s]
        copies = []
        for ahead in range(1, axis.size):
            target = axis.at(ahead)
            cuts = cuts_of(length)
            size = length // cuts
            for cut in range(cuts):
                first = target * length + cut * size
                if s == 0:
                    source = parts_ref.at[pl.ds(j * group + first, size)]
                else:
                    source = acc_refs[s - 1].at[j, pl.ds(first, size)]
                there = recv_refs[s].at[j, ahead - 1, pl.ds(cut * size, size)]
                copies.append(push(source, there, sems, slot("r", j, s, ahead, cut), axis.peer(ahead)))
        started.extend(copies)
        return copies

    def base_of(j, s):
        base = j * group
        for t in range(s + 1):
            base = base + flows[j % 2][t].index * lengths[t]
        return base

    def reduce_finish(j, s, copies):
        axis, length = flows[j % 2][s], lengths[s]
        for copy in copies:
            copy.wait_recv()
        last = s == len(lengths) - 1

        size = 4 if length % 4 == 0 else 1

        def some(u, _):
            if s == 0:
                total = parts_ref[pl.ds(base_of(j, 0) + u * size, size)].astype(f32)
            else:
                total = acc_refs[s - 1][j, pl.ds(axis.index * length + u * size, size)].astype(f32)
            for ahead in range(1, axis.size):
                total = total + recv_refs[s][j, ahead - 1, pl.ds(u * size, size)].astype(f32)
            if last:
                full_ref[pl.ds(base_of(j, s) + u * size, size)] = total.astype(bf16)
            else:
                acc_refs[s][j, pl.ds(u * size, size)] = total.astype(bf16)
            return 0

        lax.fori_loop(0, length // size, some, 0)

    def spread_start(j, s):
        axis, length = flows[j % 2][s], lengths[s]
        cuts = cuts_of(length)
        size = length // cuts
        copies = []
        for ahead in range(1, axis.size):
            for cut in range(cuts):
                here = full_ref.at[pl.ds(base_of(j, s) + cut * size, size)]
                copies.append(push(here, here, sems, slot("s", j, s, ahead, cut), axis.peer(ahead)))
        started.extend(copies)
        return copies

    def small_slot(s, ahead):
        return sum(axis.size - 1 for axis in whole_axes[:s]) + ahead - 1

    def small_start(s):
        axis = whole_axes[s]
        copies = [
            push(small_ref, small_recv[s].at[ahead - 1], small_sems, small_slot(s, ahead), axis.peer(ahead))
            for ahead in range(1, axis.size)
        ]
        return copies

    def small_finish(s, copies):
        axis = whole_axes[s]
        for copy in copies:
            copy.wait()
        mine = small_ref[...]
        total = jnp.zeros_like(mine)
        for index in range(axis.size):
            piece = mine
            for ahead in range(1, axis.size):
                piece = jnp.where(axis.at(axis.size - ahead) == index, small_recv[s][ahead - 1], piece)
            total = total + piece
        if s == len(whole_axes) - 1:
            small_out[...] = total
        else:
            small_ref[...] = total

    stages = len(lengths)
    early = pieces > 1 and group <= rows_16
    begin = [blocks + j // 2 for j in range(pieces)]
    if early:
        begin = [blocks - 1] + [blocks + (j - 1) // 2 for j in range(1, pieces)]
    pending = {}

    def advance(time):
        for j in sorted(range(pieces), key=lambda j: begin[j]):
            s = time - begin[j]
            if not 0 <= s < 2 * stages:
                continue
            if s < stages:
                reduce_finish(j, s, pending[j, s])
                if s + 1 < stages:
                    pending[j, s + 1] = reduce_start(j, s + 1)
                else:
                    pending[j, s + 1] = spread_start(j, s)
            else:
                for copy in pending[j, s]:
                    copy.wait_recv()
                if s + 1 < 2 * stages:
                    pending[j, s + 1] = spread_start(j, 2 * stages - 1 - (s + 1))

    def put(first, cols, value):
        rows = value.shape[0]
        parts_ref[first // 16 : (first + rows) // 16, :, cols] = value.astype(bf16).reshape(
            rows // 16, 16, value.shape[1]
        )

    def columns(work):
        def column(i, _):
            work(pl.ds(pl.multiple_of(i * 256, 256), 256))
            return 0

        lax.fori_loop(0, width // 256, column, 0)

    if parts_ref.shape[0] > 4 * rows_16:
        extra = parts_ref.shape[0] - 4 * rows_16
        parts_ref[4 * rows_16 :] = jnp.zeros((extra, 16, width), bf16)
    wo_load.wait()
    if early:
        pending[0, 0] = reduce_start(0, 0)

    def give_result(ahead, _):
        block_copy(result_hbm, result_recv, result_sems, ahead).start()
        return 0

    lax.fori_loop(1, count, give_result, 0)

    def rows_copy(ahead, e):
        return pltpu.make_async_remote_copy(
            src_ref=rows_hbm.at[e], dst_ref=rows_all.at[ahead - 1, e],
            send_sem=rows_sems.at[0, ahead - 1, e], recv_sem=rows_sems.at[1, ahead - 1, e],
            device_id=columns_dp.peer(ahead), device_id_type=pl.DeviceIdType.MESH,
        )

    def each_row_block(act):
        def one(e, _):
            for ahead in range(1, dp_count):
                act(rows_copy(ahead, e))
            return 0

        lax.fori_loop(0, count, one, 0)

    each_row_block(lambda copy: copy.start())

    shared_copies = []
    shared_slots = shared_send.shape[0]
    hist_ref[...] = jnp.zeros_like(hist_ref)
    gain_sum[...] = jnp.zeros_like(gain_sum)
    for i in range(blocks):
        cont = i == blocks - 1
        at_home = i == blocks - 2
        for copy in block_loads(i):
            copy.wait()
        if i + 1 < blocks:
            for copy in block_loads(i + 1):
                copy.start()
        block = lines.at(i + 1)
        lanes_from = PB if cont else 0
        lanes_used = slice(lanes_from, tokens)
        near = []
        if cont or at_home:
            near = [
                (0, lanes_from, 0, None),
                (0, lanes_from + TILE, TILE, None),
                (TILE, lanes_from + TILE, 0, None),
            ]
        else:
            near = [(TILE, 0, TILE, block == ctx_at - 1)]
        if not cont:
            near += [(first, PB, branch - block * PB - first, None) for first in range(0, PB, TILE)]

        def pair(g, _, i=i, cont=cont, block=block, lanes_used=lanes_used, near=near):
            lanes = pl.ds(pl.multiple_of(g * TILE, TILE), TILE)
            queries = q_ref[lanes_used, lanes]
            grads = att_grad_ref[lanes_used, lanes]
            keys = k_ref[i % 2, :, lanes]
            values = v_ref[i % 2, :, lanes]
            keys_t = keys.T
            bias = bias_ref[g]
            dk_parts, dv_parts, dq_parts = [], [], []
            for half in range(2):
                mine = head_lanes(half)
                lse = lse_ref[g][half : half + 1, lanes_used]
                delta = delta_ref[g][half : half + 1, lanes_used]
                s_ref[:, lanes_used] = dot_nt(jnp.where(mine, keys, jnp.zeros_like(keys)), queries)
                dp_ref[:, lanes_used] = dot_nt(jnp.where(mine, values, jnp.zeros_like(values)), grads)
                source = jnp.broadcast_to(bias[half : half + 1, :], (TILE, TILE))
                for first, lane, gap, when in near:
                    def add(first=first, lane=lane, gap=gap):
                        there = (slice(first, first + TILE), slice(lane, lane + TILE))
                        index = jnp.clip(near_index(gap), 0, TILE - 1)
                        s_ref[there] = s_ref[there] + jnp.take_along_axis(source, index, axis=1)

                    add() if when is None else pl.when(when)(add)
                step = 32
                for first in range(0, PB, step):
                    rows = slice(first, first + step)
                    if cont:
                        allowed = own_allowed(first, step, own)
                    else:
                        allowed = row_steps(block * PB + first, step, tokens) < limit
                    p = jnp.where(allowed, jnp.exp(s_ref[rows, lanes_used] - lse), 0.0)
                    p_ref[rows, lanes_used] = p.astype(bf16)
                    ds_ref[rows, lanes_used] = (p * (dp_ref[rows, lanes_used] - delta)).astype(bf16)
                for first, lane, gap, when in near:
                    def collect(first=first, lane=lane, gap=gap):
                        tile = ds_ref[first : first + TILE, lane : lane + TILE].astype(f32)
                        if not isinstance(gap, int) or gap > 0:
                            tile = jnp.where(near_index(gap) < TILE, tile, 0.0)
                        turn = lax.broadcasted_iota(jnp.int32, (TILE, TILE), 1) + lax.broadcasted_iota(
                            jnp.int32, (TILE, TILE), 0
                        )
                        tile = jnp.take_along_axis(tile, (turn - gap) & (TILE - 1), axis=1)
                        hist_ref[g * 2 + half] += fold8(tile, jnp.sum)

                    collect() if when is None else pl.when(when)(collect)
                ds = ds_ref[:, lanes_used]
                dv_parts.append(dot_nn(p_ref[:, lanes_used], grads))
                dk_parts.append(dot_nn(ds, queries))
                dq_parts.append(dot_nn(keys_t[half * 64 : half * 64 + 64, :], ds))
            dq = jnp.concatenate(dq_parts, axis=0)
            if i == 0:
                dq_ref[lanes, :] = dq
            else:
                dq_ref[lanes, lanes_used] += dq
            mine = head_lanes(0)
            dv_ref[:, lanes] = jnp.where(mine, dv_parts[0], dv_parts[1]).astype(bf16)
            dk_ref[:, lanes] = jnp.where(mine, dk_parts[0], dk_parts[1]).astype(bf16)
            return 0

        lax.fori_loop(0, width // TILE, pair, 0)

        def block_column(cols, i=i, cont=cont, at_home=at_home):
            if cont:
                normed = normed_own_ref[PB:, cols]
            elif at_home:
                normed = normed_own_ref[:PB, cols]
            else:
                normed = normed_ref[i % 2, :, cols]
            wk_part = dot_nn(rows_t[:, :PB], dk_ref[:, cols])
            wv_part = dot_nn(rows_t[:, :PB], dv_ref[:, cols])
            if i == 0:
                in_out[:, cols] = wk_part
                out_out[:, cols] = wv_part
            elif not cont:
                in_out[:, cols] += wk_part
                out_out[:, cols] += wv_part
            else:
                put(width, cols, out_out[:, cols] + wv_part)
                put(2 * width, cols, in_out[:, cols] + wk_part)
            grad = dot_nt(dk_ref[...], wk_ref[cols, :]) + dot_nt(dv_ref[...], wv_ref[cols, :])
            gain_sum[:, cols] += jnp.sum(grad * normed.astype(f32), axis=0, keepdims=True)
            if cont:
                local_ref[PB:, cols] = grad
            elif at_home:
                local_ref[:PB, cols] = grad
            else:
                shared_send[i % shared_slots, :, cols] = grad.astype(bf16)

        if shared_slots <= i < blocks - 2:
            for copy in shared_copies[i - shared_slots]:
                copy.wait_send()
        if cont:
            rows_t[:, :PB] = normed_own_ref[PB:, :].T
        elif at_home:
            rows_t[:, :PB] = normed_own_ref[:PB, :].T
        else:
            rows_t[:, :PB] = normed_ref[i % 2].T
        columns(block_column)
        if i < blocks - 2:
            size = PB // SHARED_CUTS
            shared_copies.append(
                [
                    push(
                        shared_send.at[i % shared_slots, pl.ds(cut * size, size)],
                        shared_recv.at[i, pl.ds(cut * size, size)],
                        shared_sems, i * SHARED_CUTS + cut, lines.peer(i + 1),
                    )
                    for cut in range(SHARED_CUTS)
                ]
            )
    for copies in shared_copies[-shared_slots:]:
        started.extend(copies)

    def ready(j):
        if j > 0 or not early:
            pending[j, 0] = reduce_start(j, 0)

    done = 3 * rows_16
    for j in range(pieces):
        if (j + 1) * group <= done:
            ready(j)
    rows_ref[:tokens, :] = dq_ref[...].T.astype(bf16)
    rows_t[:, :tokens] = normed_own_ref[...].T

    def query_column(cols):
        put(3 * width, cols, dot_nn(rows_t[:, :tokens], rows_ref[:tokens, cols]))

    columns(query_column)
    for j in range(pieces):
        if (j + 1) * group > done:
            ready(j)

    def query_grad(cols):
        grad = dot_nt(rows_ref[:tokens, :], wq_ref[cols, :])
        gain_sum[:, cols] += jnp.sum(grad * normed_own_ref[:, cols].astype(f32), axis=0, keepdims=True)
        local_ref[:, cols] += grad

    columns(query_grad)
    small_ref[experts:, :] = jnp.zeros((small_ref.shape[0] - experts, width), f32)
    small_ref[experts : experts + 1, :] = gain_sum[...] / gain
    small_ref[experts + 1 : experts + 2, :] = moe_gain_ref[...]
    router_load.wait()
    per_row = width // TILE
    for head in range(hist_ref.shape[0]):
        row, lane = 2 + experts + head // per_row, head % per_row * TILE
        small_ref[row : row + 1, lane : lane + TILE] = jnp.sum(hist_ref[head], axis=0, keepdims=True)
    small_pending = small_start(0)

    slots = rows_ref.shape[0]

    def grads_of(n, c):
        if c == 0:
            if n == 0:
                for copy in weight_loads:
                    copy.wait()
            if n == 1:
                each_row_block(lambda copy: copy.wait_recv())
            source = rows_hbm if n == 0 else rows_all.at[n - 1]
            load = pltpu.make_async_copy(source, result_recv, load_sems.at[3 + 2 * n])
            load.start()
            load.wait()
            rows_ref[...] = result_recv[...].reshape(slots, width)
            cot_from = columns_dp.at(dp_count - n)
            load = pltpu.make_async_copy(cot_hbm.at[cot_from], result_recv, load_sems.at[4 + 2 * n])
            load.start()
            lane = lax.broadcasted_iota(jnp.int32, (slots, TILE), 1)
            probs = router_probs(dot_nn(rows_ref[...], router_ref[...]), lane, experts)
            gate = jnp.sum(jnp.where(lane == me, probs, 0.0), axis=1, keepdims=True)
            load.wait()
            cot = result_recv[...].reshape(slots, width)
            cot_ref[...] = (gate * cot.astype(f32)).astype(bf16)
            rows_t[...] = rows_ref[...].T
        cols = slice(c * 256, c * 256 + 256)
        act, slope = gelu_parts(dot_nn(rows_ref[...], win_ref[:, cols]))
        pre_grad = (dot_nt(cot_ref[...], wout_ref[cols, :]) * slope).astype(bf16)
        out_part = dot_tn(act.astype(bf16), cot_ref[...])
        in_part = dot_nn(rows_t[...], pre_grad)
        if n == 0:
            out_out[cols, :] = out_part
            in_out[:, cols] = in_part
        else:
            out_out[cols, :] += out_part
            in_out[:, cols] += in_part

    def input_back():
        held = pltpu.make_async_copy(hidden_grad_hbm, input_out, load_sems.at[3 + 2 * dp_count])
        held.start()
        x_load = pltpu.make_async_copy(x_hbm, rows_ref.at[pl.ds(0, tokens)], load_sems.at[6 + 2 * dp_count])
        x_load.start()
        for copies in shared_copies:
            for copy in copies:
                copy.wait_recv()
        held.wait()
        x_load.wait()
        for first, shared_rows in ((0, True), (PB, False)):
            rows = slice(first, PB if shared_rows else tokens)
            x = rows_ref[rows, :].astype(f32)
            inverse = inverse_rms(x)
            grad = local_ref[rows, :]
            if shared_rows:
                for n in range(ctx_count - 1):
                    grad = grad + shared_recv[n].astype(f32)
            through = grad * gain
            scaled = x * inverse
            shared = jnp.mean(through * scaled, axis=1, keepdims=True)
            input_out[rows, :] += inverse * (through - scaled * shared)

    def layer():
        held = pltpu.make_async_copy(hidden_hbm, input_out, load_sems.at[4 + 2 * dp_count])
        held.start()
        own_result.wait()
        await_blocks(result_hbm, result_recv, result_sems, False, True)
        place = place_rows(slot_row[...], 0, slots, tokens)
        returned = dot_tn(place, result_recv[...].reshape(slots, width))
        held.wait()
        layer_out[...] = (input_out[...] + returned).astype(bf16)

    work = [layer]
    work += [functools.partial(grads_of, n, c) for n in range(dp_count) for c in range(slice_width // 256)]
    work += [input_back]
    for time in range(blocks - 1, max(begin) + 2 * stages):
        if time >= blocks:
            advance(time)
        elif early:
            advance(time)
        s = time - blocks
        if 0 <= s < len(whole_axes):
            small_finish(s, small_pending)
            if s + 1 < len(whole_axes):
                small_pending = small_start(s + 1)
        if work:
            work.pop(0)()
    for rest in work:
        rest()
    for copy in started:
        copy.wait_send()
    await_blocks(result_hbm, result_recv, result_sems, True, False)
    each_row_block(lambda copy: copy.wait_send())


def head_kernel(
    experts, plan,
    branch_ref, bias_ref, q_ref, k_hbm, v_hbm, att_grad_ref, lse_ref, delta_ref, normed_hbm, normed_own_hbm,
    gain_ref, wq_ref, wk_ref, wv_ref, wo_part_hbm, moe_gain_ref, router_part_hbm, x_hbm, hidden_grad_hbm,
    hidden_hbm, slot_row, result_hbm, rows_hbm, cot_hbm, win_hbm, wout_hbm, router_ref,
    full_ref, small_out, input_out, in_out, out_out, layer_out, rows_all,
    k_ref, v_ref, normed_ref, nt_ref, s_ref, dp_ref, p_ref, ds_ref, dq_ref, dk_ref, dv_ref, hist_ref, gain_sum,
    near_ref, turn_ref, grad_ref, shared_send, shared_recv, parts_ref, acc_refs, recv_refs, small_ref, small_recv,
    result_recv, win_ref, wout_ref, rows_ref, cot_ref,
    slab_sems, load_sems, sems, small_sems, shared_sems, result_sems, rows_sems,
):
    group, pieces, lengths = plan
    flows = mesh_axes()
    branch = branch_ref[0, 0]
    ctx_at = lax.axis_index("ctx")
    ctx_count, dp_count = lax.axis_size("ctx"), lax.axis_size("dp")
    tokens, width = q_ref.shape
    own = tokens - PB
    plen = PB * ctx_count
    count, me = owners()
    lines, columns_dp = Axis("ctx", ctx_count), Axis("dp", dp_count)
    whole_axes = [Axis("expert", lax.axis_size("expert")), columns_dp, lines]
    gain = gain_ref[...].astype(f32)
    limit = limits(ctx_at, branch, tokens)
    rows_16 = width // 16
    quads = width // 256
    rows_t = nt_ref.at[:, pl.ds(0, rows_ref.shape[0])]

    def slab_loads(q):
        cols = pl.ds(q * 256, 256)
        return [
            pltpu.make_async_copy(k_hbm.at[:, cols], k_ref.at[q % 2], slab_sems.at[q, 0]),
            pltpu.make_async_copy(v_hbm.at[:, cols], v_ref.at[q % 2], slab_sems.at[q, 1]),
        ]

    for copy in slab_loads(0):
        copy.start()
    slice_width = win_ref.shape[1]
    part = pl.ds(pl.multiple_of(lax.axis_index("dp") * slice_width, slice_width), slice_width)
    weight_loads = [
        pltpu.make_async_copy(win_hbm.at[:, part], win_ref, load_sems.at[0]),
        pltpu.make_async_copy(wout_hbm.at[part], wout_ref, load_sems.at[1]),
    ]
    own_result = pltpu.make_async_copy(result_hbm.at[me], result_recv.at[me], load_sems.at[2])
    router_load = pltpu.make_async_copy(
        router_part_hbm.at[pl.ds(0, experts)], small_ref.at[pl.ds(0, experts)], load_sems.at[7 + 2 * dp_count]
    )
    normed_loads = [
        pltpu.make_async_copy(normed_hbm, normed_ref.at[pl.ds(0, plen)], load_sems.at[8 + 2 * dp_count]),
        pltpu.make_async_copy(
            normed_own_hbm.at[pl.ds(PB, own)], normed_ref.at[pl.ds(plen, own)], load_sems.at[9 + 2 * dp_count]
        ),
    ]
    per_quad = pieces * group // quads
    wo_loads = [
        pltpu.make_async_copy(
            wo_part_hbm.at[q], parts_ref.at[pl.ds(q * per_quad, rows_16)], load_sems.at[10 + 2 * dp_count + q]
        )
        for q in range(quads)
    ]
    for copy in [*normed_loads, *wo_loads, *weight_loads, own_result, router_load]:
        copy.start()

    barrier = pltpu.get_barrier_semaphore()

    def greet(ahead, _):
        pl.semaphore_signal(
            barrier, inc=1, device_id=owner_device(lax.rem(me + ahead, count)),
            device_id_type=pl.DeviceIdType.MESH,
        )
        return 0

    lax.fori_loop(1, count, greet, 0)
    for ahead in range(1, dp_count):
        pl.semaphore_signal(
            barrier, inc=1, device_id=columns_dp.peer(ahead), device_id_type=pl.DeviceIdType.MESH
        )
    pl.semaphore_wait(barrier, count - 1 + dp_count - 1)

    slots_of = {}

    def slot(*key):
        return slots_of.setdefault(key, len(slots_of))

    started = []

    def reduce_start(j, s):
        axis, length = flows[j % 2][s], lengths[s]
        copies = []
        for ahead in range(1, axis.size):
            target = axis.at(ahead)
            cuts = cuts_of(length)
            size = length // cuts
            for cut in range(cuts):
                first = target * length + cut * size
                if s == 0:
                    source = parts_ref.at[pl.ds(j * group + first, size)]
                else:
                    source = acc_refs[s - 1].at[j, pl.ds(first, size)]
                there = recv_refs[s].at[j, ahead - 1, pl.ds(cut * size, size)]
                copies.append(push(source, there, sems, slot("r", j, s, ahead, cut), axis.peer(ahead)))
        started.extend(copies)
        return copies

    def base_of(j, s):
        base = j * group
        for t in range(s + 1):
            base = base + flows[j % 2][t].index * lengths[t]
        return base

    def reduce_finish(j, s, copies):
        axis, length = flows[j % 2][s], lengths[s]
        for copy in copies:
            copy.wait_recv()
        last = s == len(lengths) - 1

        size = 4 if length % 4 == 0 else 1

        def some(u, _):
            if s == 0:
                total = parts_ref[pl.ds(base_of(j, 0) + u * size, size)].astype(f32)
            else:
                total = acc_refs[s - 1][j, pl.ds(axis.index * length + u * size, size)].astype(f32)
            for ahead in range(1, axis.size):
                total = total + recv_refs[s][j, ahead - 1, pl.ds(u * size, size)].astype(f32)
            if last:
                full_ref[pl.ds(base_of(j, s) + u * size, size)] = total.astype(bf16)
            else:
                acc_refs[s][j, pl.ds(u * size, size)] = total.astype(bf16)
            return 0

        lax.fori_loop(0, length // size, some, 0)

    def spread_start(j, s):
        axis, length = flows[j % 2][s], lengths[s]
        cuts = cuts_of(length)
        size = length // cuts
        copies = []
        for ahead in range(1, axis.size):
            for cut in range(cuts):
                here = full_ref.at[pl.ds(base_of(j, s) + cut * size, size)]
                copies.append(push(here, here, sems, slot("s", j, s, ahead, cut), axis.peer(ahead)))
        started.extend(copies)
        return copies

    def small_slot(s, ahead):
        return sum(axis.size - 1 for axis in whole_axes[:s]) + ahead - 1

    def small_start(s):
        axis = whole_axes[s]
        copies = [
            push(small_ref, small_recv[s].at[ahead - 1], small_sems, small_slot(s, ahead), axis.peer(ahead))
            for ahead in range(1, axis.size)
        ]
        return copies

    def small_finish(s, copies):
        axis = whole_axes[s]
        for copy in copies:
            copy.wait()
        mine = small_ref[...]
        total = jnp.zeros_like(mine)
        for index in range(axis.size):
            piece = mine
            for ahead in range(1, axis.size):
                piece = jnp.where(axis.at(axis.size - ahead) == index, small_recv[s][ahead - 1], piece)
            total = total + piece
        if s == len(whole_axes) - 1:
            small_out[...] = total
        else:
            small_ref[...] = total

    stages = len(lengths)
    heads_per_quad = 4
    begin = [heads_per_quad * (j * quads // pieces + 1) for j in range(pieces)]
    pending = {}

    def advance(time):
        for j in sorted(range(pieces), key=lambda j: begin[j]):
            s = time - begin[j]
            if not 0 <= s < 2 * stages:
                continue
            if s < stages:
                reduce_finish(j, s, pending[j, s])
                if s + 1 < stages:
                    pending[j, s + 1] = reduce_start(j, s + 1)
                else:
                    pending[j, s + 1] = spread_start(j, s)
            else:
                for copy in pending[j, s]:
                    copy.wait_recv()
                if s + 1 < 2 * stages:
                    pending[j, s + 1] = spread_start(j, 2 * stages - 1 - (s + 1))

    def put(q, matrix, value):
        first = q * per_quad + matrix * rows_16
        parts_ref[first : first + rows_16] = value.astype(bf16).reshape(rows_16, 16, 256)

    def columns(work):
        def column(i, _):
            work(pl.ds(pl.multiple_of(i * 256, 256), 256))
            return 0

        lax.fori_loop(0, width // 256, column, 0)

    def give_result(ahead, _):
        block_copy(result_hbm, result_recv, result_sems, ahead).start()
        return 0

    lax.fori_loop(1, count, give_result, 0)

    def rows_copy(ahead, e):
        return pltpu.make_async_remote_copy(
            src_ref=rows_hbm.at[e], dst_ref=rows_all.at[ahead - 1, e],
            send_sem=rows_sems.at[0, ahead - 1, e], recv_sem=rows_sems.at[1, ahead - 1, e],
            device_id=columns_dp.peer(ahead), device_id_type=pl.DeviceIdType.MESH,
        )

    row_blocks = [(ahead, e) for ahead in range(1, dp_count) for e in range(count)]
    at_once = -(-len(row_blocks) // (quads * heads_per_quad))

    def each_row_block(act):
        def one(e, _):
            for ahead in range(1, dp_count):
                act(rows_copy(ahead, e))
            return 0

        lax.fori_loop(0, count, one, 0)

    start = ctx_at * PB
    near_ref[0] = jnp.clip(near_index(0), 0, TILE - 1)
    near_ref[1] = jnp.clip(near_index(TILE), 0, TILE - 1)
    for i in range(1, plen // TILE):
        near_ref[1 + i] = jnp.clip(near_index(branch - i * TILE), 0, TILE - 1)
    turn = lax.broadcasted_iota(jnp.int32, (TILE, TILE), 1) + lax.broadcasted_iota(jnp.int32, (TILE, TILE), 0)
    turn_ref[0] = turn & (TILE - 1)
    turn_ref[1] = (turn - branch) & (TILE - 1)
    hist_ref[...] = jnp.zeros_like(hist_ref)
    for copy in normed_loads:
        copy.wait()
    nt_ref[...] = normed_ref[...].T

    def each_near(act):
        act(start, 0, 0, 0)
        act(start, TILE, 1, 0)
        act(start + TILE, TILE, 0, 0)
        pl.when(ctx_at > 0)(lambda: act(start - TILE, 0, 1, 0))

        def window(i, _):
            act(i * TILE, PB, 1 + i, 1)
            return 0

        lax.fori_loop(1, plen // TILE, window, 0)

    def each_near_own(act):
        act(0, PB, 0, 0)
        act(0, PB + TILE, 1, 0)
        act(TILE, PB + TILE, 0, 0)

    def one_head(q, number):
        half = number % 2
        pair = number // 2
        g, head = q * 2 + pair, q * 4 + number
        lanes = slice(pair * TILE, pair * TILE + TILE)
        here = slice(g * TILE, g * TILE + TILE)
        features = slice(number * 64, number * 64 + 64)
        mine = head_lanes(half)
        lse = lse_ref[g][half : half + 1, :]
        delta = delta_ref[g][half : half + 1, :]
        source = jnp.broadcast_to(bias_ref[g][half : half + 1, :], (TILE, TILE))

        def add(row, lane, slot, turned):
            rows = pl.ds(row if isinstance(row, int) else pl.multiple_of(row, TILE), TILE)
            cols = slice(lane, lane + TILE)
            s_ref[rows, cols] = s_ref[rows, cols] + jnp.take_along_axis(source, near_ref[slot], axis=1)

        def collect(row, lane, slot, turned):
            rows = pl.ds(row if isinstance(row, int) else pl.multiple_of(row, TILE), TILE)
            tile = ds_ref[rows, lane : lane + TILE].astype(f32)
            tile = jnp.where(near_ref[slot] < TILE - 1, tile, 0.0)
            tile = jnp.take_along_axis(tile, turn_ref[turned], axis=1)
            hist_ref[head] += fold8(tile, jnp.sum)

        def keep(target, rows, value):
            if half == 0:
                target[rows, lanes] = value.astype(bf16)
            else:
                target[rows, lanes] = jnp.where(mine, value, target[rows, lanes].astype(f32)).astype(bf16)

        prompt = slice(0, plen)
        keys = k_ref[q % 2, prompt, lanes]
        values = v_ref[q % 2, prompt, lanes]
        queries = q_ref[:, here]
        grads = att_grad_ref[:, here]
        s_ref[...] = dot_nt(jnp.where(mine, keys, jnp.zeros_like(keys)), queries)
        dp_ref[...] = dot_nt(jnp.where(mine, values, jnp.zeros_like(values)), grads)
        each_near(add)

        def some_rows(i, _):
            for sub in range(0, TILE, 32):
                first = pl.multiple_of(i * TILE + sub, 32)
                rows = pl.ds(first, 32)
                allowed = row_steps(first, 32, tokens) < limit
                p = jnp.where(allowed, jnp.exp(s_ref[rows, :] - lse), 0.0)
                p_ref[rows, :] = p.astype(bf16)
                ds_ref[rows, :] = (p * (dp_ref[rows, :] - delta)).astype(bf16)
            return 0

        lax.fori_loop(0, plen // TILE, some_rows, 0)
        each_near(collect)
        keep(dv_ref, prompt, dot_nn(p_ref[...], grads))
        keep(dk_ref, prompt, dot_nn(ds_ref[...], queries))
        dq_ref[features, :] = dot_nn(keys.T[half * 64 : half * 64 + 64, :], ds_ref[...])

        cont = slice(plen, plen + own)
        keys = k_ref[q % 2, cont, lanes]
        values = v_ref[q % 2, cont, lanes]
        queries = q_ref[PB:, here]
        grads = att_grad_ref[PB:, here]
        s_ref[:own, PB:] = dot_nt(jnp.where(mine, keys, jnp.zeros_like(keys)), queries)
        dp_ref[:own, PB:] = dot_nt(jnp.where(mine, values, jnp.zeros_like(values)), grads)
        each_near_own(add)
        for first in range(0, own, 32):
            rows = slice(first, first + 32)
            p = jnp.where(own_allowed(first, 32, own), jnp.exp(s_ref[rows, PB:] - lse[:, PB:]), 0.0)
            p_ref[rows, PB:] = p.astype(bf16)
            ds_ref[rows, PB:] = (p * (dp_ref[rows, PB:] - delta[:, PB:])).astype(bf16)
        each_near_own(collect)
        ds = ds_ref[:own, PB:]
        keep(dv_ref, cont, dot_nn(p_ref[:own, PB:], grads))
        keep(dk_ref, cont, dot_nn(ds, queries))
        dq_ref[features, PB:] += dot_nn(keys.T[half * 64 : half * 64 + 64, :], ds)

    dq_low = rows_ref
    home = pl.ds(pl.multiple_of(start, PB), PB)
    for q in range(quads):
        for copy in slab_loads(q):
            copy.wait()
        if q + 1 < quads:
            for copy in slab_loads(q + 1):
                copy.start()
        for number in range(heads_per_quad):
            time = q * heads_per_quad + number
            for ahead, e in row_blocks[time * at_once : (time + 1) * at_once]:
                rows_copy(ahead, e).start()
            one_head(q, number)
            advance(time)
        those = slice(q * 256, q * 256 + 256)
        wo_loads[q].wait()
        put(q, 1, dot_nn(nt_ref[...], dv_ref[...]))
        put(q, 2, dot_nn(nt_ref[...], dk_ref[...]))
        dq_low[:tokens, :256] = dq_ref[...].T.astype(bf16)
        put(
            q, 3,
            dot_nn(nt_ref[:, home], dq_low[:PB, :256]) + dot_nn(nt_ref[:, plen:], dq_low[PB:tokens, :256]),
        )
        for j in range(pieces):
            if begin[j] == heads_per_quad * (q + 1):
                pending[j, 0] = reduce_start(j, 0)

        def normed_grad(cols, q=q, those=those):
            grad = dot_nt(dk_ref[...], wk_ref[cols, those]) + dot_nt(dv_ref[...], wv_ref[cols, those])
            if q == 0:
                grad_ref[:, cols] = grad
            else:
                grad_ref[:, cols] += grad
            grad = dot_nt(dq_low[:tokens, :256], wq_ref[cols, those])
            grad_ref[home, cols] += grad[:PB]
            grad_ref[plen:, cols] += grad[PB:]

        columns(normed_grad)

    shared_copies = []
    for i in range(ctx_count - 1):
        block = pl.ds(pl.multiple_of(lines.at(i + 1) * PB, PB), PB)
        shared_send[i] = grad_ref[block, :].astype(bf16)
        size = PB // SHARED_CUTS
        shared_copies.append(
            [
                push(
                    shared_send.at[i, pl.ds(cut * size, size)], shared_recv.at[i, pl.ds(cut * size, size)],
                    shared_sems, i * SHARED_CUTS + cut, lines.peer(i + 1),
                )
                for cut in range(SHARED_CUTS)
            ]
        )
        started.extend(shared_copies[-1])

    def gain_part(cols):
        gain_sum[:, cols] = jnp.sum(grad_ref[:, cols] * normed_ref[:, cols].astype(f32), axis=0, keepdims=True)

    columns(gain_part)
    small_ref[experts:, :] = jnp.zeros((small_ref.shape[0] - experts, width), f32)
    small_ref[experts : experts + 1, :] = gain_sum[...] / gain
    small_ref[experts + 1 : experts + 2, :] = moe_gain_ref[...]
    router_load.wait()
    per_row = width // TILE
    for head in range(hist_ref.shape[0]):
        row, lane = 2 + experts + head // per_row, head % per_row * TILE
        small_ref[row : row + 1, lane : lane + TILE] = jnp.sum(hist_ref[head], axis=0, keepdims=True)
    small_pending = small_start(0)

    slots = rows_ref.shape[0]

    def grads_of(n, c):
        if c == 0:
            if n == 0:
                for copy in weight_loads:
                    copy.wait()
            if n == 1:
                each_row_block(lambda copy: copy.wait_recv())
            source = rows_hbm if n == 0 else rows_all.at[n - 1]
            load = pltpu.make_async_copy(source, result_recv, load_sems.at[3 + 2 * n])
            load.start()
            load.wait()
            rows_ref[...] = result_recv[...].reshape(slots, width)
            cot_from = columns_dp.at(dp_count - n)
            load = pltpu.make_async_copy(cot_hbm.at[cot_from], result_recv, load_sems.at[4 + 2 * n])
            load.start()
            lane = lax.broadcasted_iota(jnp.int32, (slots, TILE), 1)
            probs = router_probs(dot_nn(rows_ref[...], router_ref[...]), lane, experts)
            gate = jnp.sum(jnp.where(lane == me, probs, 0.0), axis=1, keepdims=True)
            load.wait()
            cot = result_recv[...].reshape(slots, width)
            cot_ref[...] = (gate * cot.astype(f32)).astype(bf16)
            rows_t[...] = rows_ref[...].T
        cols = slice(c * 256, c * 256 + 256)
        act, slope = gelu_parts(dot_nn(rows_ref[...], win_ref[:, cols]))
        pre_grad = (dot_nt(cot_ref[...], wout_ref[cols, :]) * slope).astype(bf16)
        out_part = dot_tn(act.astype(bf16), cot_ref[...])
        in_part = dot_nn(rows_t[...], pre_grad)
        if n == 0:
            out_out[cols, :] = out_part
            in_out[:, cols] = in_part
        else:
            out_out[cols, :] += out_part
            in_out[:, cols] += in_part

    def input_back():
        held = pltpu.make_async_copy(hidden_grad_hbm, input_out, load_sems.at[3 + 2 * dp_count])
        held.start()
        x_load = pltpu.make_async_copy(x_hbm, rows_ref.at[pl.ds(0, tokens)], load_sems.at[6 + 2 * dp_count])
        x_load.start()
        for copies in shared_copies:
            for copy in copies:
                copy.wait_recv()
        held.wait()
        x_load.wait()
        for first, shared_rows in ((0, True), (PB, False)):
            rows = slice(first, PB if shared_rows else tokens)
            x = rows_ref[rows, :].astype(f32)
            inverse = inverse_rms(x)
            grad = grad_ref[home if shared_rows else pl.ds(plen, own), :]
            if shared_rows:
                for n in range(ctx_count - 1):
                    grad = grad + shared_recv[n].astype(f32)
            through = grad * gain
            scaled = x * inverse
            shared = jnp.mean(through * scaled, axis=1, keepdims=True)
            input_out[rows, :] += inverse * (through - scaled * shared)

    def layer():
        held = pltpu.make_async_copy(hidden_hbm, input_out, load_sems.at[4 + 2 * dp_count])
        held.start()
        own_result.wait()
        await_blocks(result_hbm, result_recv, result_sems, False, True)
        place = place_rows(slot_row[...], 0, slots, tokens)
        returned = dot_tn(place, result_recv[...].reshape(slots, width))
        held.wait()
        layer_out[...] = (input_out[...] + returned).astype(bf16)

    work = [layer]
    work += [functools.partial(grads_of, n, c) for n in range(dp_count) for c in range(slice_width // 256)]
    work += [input_back]
    first_step, last_step = quads * heads_per_quad, max(begin) + 2 * stages
    for time in range(first_step, last_step):
        advance(time)
        s = time - first_step
        if s < len(whole_axes):
            small_finish(s, small_pending)
            if s + 1 < len(whole_axes):
                small_pending = small_start(s + 1)
        for _ in range(-(-len(work) // (last_step - time))):
            work.pop(0)()
    for copy in started:
        copy.wait_send()
    await_blocks(result_hbm, result_recv, result_sems, True, False)
    each_row_block(lambda copy: copy.wait_send())


def finish_kernel(full_ref, in_ref, out_ref, input_ref, layer_ref, *results):
    weights, rest = results[:4], results[4:]
    columns = full_ref.shape[-1]
    for n, weight in enumerate(weights):
        for q in range(full_ref.shape[0]):
            there = slice(q * columns, (q + 1) * columns)
            weight[:, there] = full_ref[q, n].astype(f32).reshape(weight.shape[0], columns)
    for source, target in zip((in_ref, out_ref, input_ref, layer_ref), rest):
        target[...] = source[...]


def tail_plan(sizes, width, quads):
    devices = 1
    for size in sizes:
        devices *= size
    units = 4 * width // 16
    if quads == 1:
        group, pieces = devices, -(-units // devices)
    else:
        cuts = 2 if units % (2 * devices) == 0 else 1
        group, pieces = -(-units // (cuts * devices)) * devices, cuts * quads
    lengths, left = [], group
    for size in sizes:
        left //= size
        lengths.append(left)
    return group, pieces, lengths


def body(
    inputs, cotangent, route, arrival, branch, attn_gain, query_weight, key_weight, value_weight,
    output_weight, rel_table, moe_gain, router_weight, expert_in, expert_out,
):
    x = inputs[0]
    cot = cotangent[0]
    tokens, width = x.shape
    own = tokens - PB
    buckets, heads = rel_table.shape
    experts = router_weight.shape[1]
    capacity = 9 * tokens // (8 * experts)
    block_rows = capacity if capacity % 8 == 0 else -(-capacity // 16) * 16
    slots = experts * block_rows
    ctx_count = lax.axis_size("ctx")
    dp_count = lax.axis_size("dp")
    plen = PB * ctx_count
    keys_total = plen + own
    hidden_units = expert_in.shape[2]
    pairs = width // TILE
    attn_gain_row = attn_gain.reshape(1, width)
    moe_gain_row = moe_gain.reshape(1, width)
    onehot = bucket_onehot(buckets)
    by_distance = jnp.dot(onehot, rel_table.astype(f32), precision=lax.Precision.HIGHEST).T
    by_distance = by_distance - by_distance[:, TILE - 1 :]
    bias = jnp.pad(by_distance.reshape(pairs, 2, TILE), ((0, 0), (0, 6), (0, 0)))
    router_wide = jnp.pad(router_weight, ((0, 0), (0, TILE - experts)))
    route_row = route.reshape(1, tokens)
    arrive_row = arrival[0]
    blocks = shape((experts, block_rows, width), bf16)
    block_space = pltpu.VMEM((experts, block_rows, width), bf16)
    block_sems = pltpu.SemaphoreType.DMA((2, experts - 1))
    any_space = pl.BlockSpec(memory_space=pl.ANY)

    slot_row, cot_sent, normed_own, normed_all, queries, keys, values, att, lse = pl.pallas_call(
        functools.partial(front_kernel, capacity),
        out_shape=[
            shape((1, tokens), jnp.int32),
            blocks,
            shape((tokens, width), bf16),
            shape((plen, width), bf16),
            shape((tokens, width), bf16),
            shape((keys_total, width), bf16),
            shape((keys_total, width), bf16),
            shape((width, tokens), bf16),
            shape((pairs, 8, tokens), f32),
        ],
        in_specs=[smem()] + [vmem()] * 9,
        out_specs=[vmem()] * 9,
        scratch_shapes=[
            pltpu.VMEM((ctx_count, PB, width), bf16),
            block_space,
            pltpu.VMEM((keys_total, tokens), f32),
            pltpu.VMEM((keys_total, tokens), bf16),
            pltpu.SemaphoreType.DMA((2, 2, ctx_count - 1, CHUNKS)),
            block_sems,
        ],
        compiler_params=remote_params(1),
        cost_estimate=cost(40 * keys_total * tokens * width, 20 * width * width),
        name="front",
    )(
        branch, bias, x, cot, attn_gain_row, route_row, arrive_row,
        query_weight, key_weight, value_weight,
    )
    cot_all = lax.all_gather(cot_sent, "dp", axis=0, tiled=False)

    by_heads = ctx_count <= 4
    quads = width // 256 if by_heads else 1
    members = 2 * lax.axis_size("expert") if ctx_count % 2 == 0 else experts
    group_rows = members * block_rows
    (
        rows_sent, router_part, hidden_grad, wo_part, att_grad, delta, moe_gain_part,
        result, hidden,
    ) = pl.pallas_call(
        functools.partial(expert_kernel, experts),
        out_shape=[
            blocks, shape((TILE, width), f32), shape((tokens, width), f32), shape((quads, width // 16, 16, width // quads), bf16),
            shape((tokens, width), bf16), shape((pairs, 8, tokens), f32), shape((1, width), f32),
            blocks, shape((tokens, width), f32),
        ],
        in_specs=[vmem()] * 8 + [any_space] * 2,
        out_specs=[vmem()] * 9,
        scratch_shapes=[
            pltpu.VMEM((tokens, width), bf16),
            block_space,
            pltpu.VMEM((width, hidden_units), bf16),
            pltpu.VMEM((hidden_units, width), bf16),
            pltpu.VMEM((group_rows, width), bf16),
            pltpu.VMEM((group_rows, width), bf16),
            pltpu.VMEM((group_rows, width), f32),
            pltpu.VMEM((group_rows, width), f32),
            block_space, block_space,
            pltpu.VMEM((tokens, width), bf16),
            pltpu.VMEM((width, tokens), bf16),
            block_sems, block_sems,
            pltpu.SemaphoreType.DMA((2,)),
        ],
        compiler_params=remote_params(2),
        cost_estimate=cost(8 * slots * width * hidden_units, 12 * width * hidden_units),
        name="expert",
    )(
        att, x, output_weight, moe_gain_row, router_wide, slot_row, cot, cot_sent,
        expert_in[0], expert_out[0],
    )
    att_grad, cot_all = lax.optimization_barrier((att_grad, cot_all))

    expert_count = lax.axis_size("expert")
    dp_sizes = [2, 2] if dp_count == 4 else [dp_count]
    sizes = [expert_count, *dp_sizes, ctx_count]
    plan = tail_plan(sizes, width, quads)
    group, pieces, lengths = plan
    units = group * pieces

    table_rows = heads * TILE // width
    small_rows = -(-(2 + experts + table_rows) // 8) * 8
    slice_width = hidden_units // dp_count
    block_scratch = [
        pltpu.VMEM((2, PB, width), bf16),
        pltpu.VMEM((2, PB, width), bf16),
        pltpu.VMEM((2, PB, width), bf16),
        pltpu.VMEM((PB, tokens), f32),
        pltpu.VMEM((PB, tokens), f32),
        pltpu.VMEM((PB, tokens), bf16),
        pltpu.VMEM((PB, tokens), bf16),
        pltpu.VMEM((width, tokens), f32),
        pltpu.VMEM((PB, width), bf16),
        pltpu.VMEM((PB, width), bf16),
        pltpu.VMEM((heads, 8, TILE), f32),
        pltpu.VMEM((1, width), f32),
        pltpu.VMEM((tokens, width), f32),
        pltpu.VMEM((min(ctx_count - 1, 16 // ctx_count), PB, width), bf16),
        pltpu.VMEM((ctx_count - 1, PB, width), bf16),
        pltpu.VMEM((units, 16, width), bf16),
        [pltpu.VMEM((pieces, length, 16, width), bf16) for length in lengths[:-1]],
        [
            pltpu.VMEM((pieces, size - 1, length, 16, width), bf16)
            for size, length in zip(sizes, lengths)
        ],
        pltpu.VMEM((small_rows, width), f32),
        [pltpu.VMEM((size - 1, small_rows, width), f32) for size in (expert_count, dp_count, ctx_count)],
        block_space,
        pltpu.VMEM((width, slice_width), bf16),
        pltpu.VMEM((slice_width, width), bf16),
        pltpu.VMEM((slots, width), bf16),
        pltpu.VMEM((slots, width), bf16),
        pltpu.VMEM((width, slots), bf16),
        pltpu.SemaphoreType.DMA((ctx_count + 1, 3)),
        pltpu.SemaphoreType.DMA((8 + 2 * dp_count,)),
        pltpu.SemaphoreType.DMA(
            (2, 2 * pieces * sum((n - 1) * cuts_of(length) for n, length in zip(sizes, lengths)))
        ),
        pltpu.SemaphoreType.DMA((2, expert_count + dp_count + ctx_count - 3)),
        pltpu.SemaphoreType.DMA((2, (ctx_count - 1) * SHARED_CUTS)),
        block_sems,
        pltpu.SemaphoreType.DMA((2, dp_count - 1, experts)),
    ]
    head_scratch = [
        pltpu.VMEM((2, keys_total, 256), bf16),
        pltpu.VMEM((2, keys_total, 256), bf16),
        pltpu.VMEM((keys_total, width), bf16),
        pltpu.VMEM((width, keys_total), bf16),
        pltpu.VMEM((plen, tokens), f32),
        pltpu.VMEM((plen, tokens), f32),
        pltpu.VMEM((plen, tokens), bf16),
        pltpu.VMEM((plen, tokens), bf16),
        pltpu.VMEM((256, tokens), f32),
        pltpu.VMEM((keys_total, 256), bf16),
        pltpu.VMEM((keys_total, 256), bf16),
        pltpu.VMEM((heads, 8, TILE), f32),
        pltpu.VMEM((1, width), f32),
        pltpu.VMEM((1 + plen // TILE, TILE, TILE), jnp.int32),
        pltpu.VMEM((2, TILE, TILE), jnp.int32),
        pltpu.VMEM((keys_total, width), f32),
        pltpu.VMEM((ctx_count - 1, PB, width), bf16),
        pltpu.VMEM((ctx_count - 1, PB, width), bf16),
        pltpu.VMEM((units, 16, width // quads), bf16),
        [pltpu.VMEM((pieces, length, 16, width // quads), bf16) for length in lengths[:-1]],
        [
            pltpu.VMEM((pieces, size - 1, length, 16, width // quads), bf16)
            for size, length in zip(sizes, lengths)
        ],
        pltpu.VMEM((small_rows, width), f32),
        [pltpu.VMEM((size - 1, small_rows, width), f32) for size in (expert_count, dp_count, ctx_count)],
        block_space,
        pltpu.VMEM((width, slice_width), bf16),
        pltpu.VMEM((slice_width, width), bf16),
        pltpu.VMEM((slots, width), bf16),
        pltpu.VMEM((slots, width), bf16),
        pltpu.SemaphoreType.DMA((quads, 2)),
        pltpu.SemaphoreType.DMA((10 + 2 * dp_count + quads,)),
        pltpu.SemaphoreType.DMA(
            (2, 2 * pieces * sum((n - 1) * cuts_of(length) for n, length in zip(sizes, lengths)))
        ),
        pltpu.SemaphoreType.DMA((2, expert_count + dp_count + ctx_count - 3)),
        pltpu.SemaphoreType.DMA((2, (ctx_count - 1) * SHARED_CUTS)),
        block_sems,
        pltpu.SemaphoreType.DMA((2, dp_count - 1, experts)),
    ]
    weights, small, input_grad, in_grad, out_grad, layer_out, _ = pl.pallas_call(
        functools.partial(head_kernel if by_heads else back_kernel, experts, plan),
        out_shape=[
            shape((units, 16, width // quads), bf16), shape((small_rows, width), f32), shape((tokens, width), f32),
            shape((width, slice_width), f32), shape((slice_width, width), f32), shape((tokens, width), bf16),
            shape((dp_count - 1, experts, block_rows, width), bf16),
        ],
        in_specs=[
            smem(), vmem(), vmem(), any_space, any_space, vmem(), vmem(), vmem(), any_space, any_space if by_heads else vmem(),
            vmem(), vmem(), vmem(), vmem(), any_space, vmem(), any_space, any_space, any_space,
            any_space, vmem(), any_space, any_space, any_space, any_space, any_space, vmem(),
        ],
        out_specs=[vmem()] * 6 + [any_space],
        scratch_shapes=head_scratch if by_heads else block_scratch,
        compiler_params=remote_params(0),
        cost_estimate=cost(
            8 * dp_count * slots * width * slice_width + 80 * keys_total * tokens * width,
            60 * width * slice_width,
        ),
        name="back",
    )(
        branch, bias, queries, keys, values, att_grad, lse, delta, normed_all, normed_own,
        attn_gain_row, query_weight, key_weight, value_weight, wo_part, moe_gain_part, router_part, x,
        hidden_grad, hidden, slot_row, result,
        rows_sent, cot_all, expert_in[0], expert_out[0], router_wide,
    )

    matrix_units = width // 16
    steps = 4

    def part_rows(rows, columns=width):
        return pl.BlockSpec((rows // steps, columns), lambda i: (i, 0))

    weights = weights.reshape(quads, units // quads, 16, width // quads)
    weights = weights[:, : 4 * matrix_units].reshape(quads, 4, matrix_units, 16, width // quads)
    *weights, in_grad, out_grad, input_grad, layer_out = pl.pallas_call(
        finish_kernel,
        grid=(steps,),
        out_shape=[shape((width, width), f32)] * 4
        + [
            shape((width, slice_width), f32), shape((slice_width, width), f32),
            shape((tokens, width), f32), shape((tokens, width), bf16),
        ],
        in_specs=[
            pl.BlockSpec(
                (quads, 4, matrix_units // steps, 16, width // quads), lambda i: (0, 0, i, 0, 0)
            ),
            part_rows(width, slice_width), part_rows(slice_width), part_rows(tokens), part_rows(tokens),
        ],
        out_specs=[part_rows(width)] * 4
        + [part_rows(width, slice_width), part_rows(slice_width), part_rows(tokens), part_rows(tokens)],
        compiler_params=params(),
        cost_estimate=cost(8 * width * width, 48 * width * width),
        name="finish",
    )(weights, in_grad, out_grad, input_grad, layer_out)
    router_grad = small[:experts].T
    hist_sum = small[2 + experts : 2 + experts + table_rows].reshape(heads, TILE)
    last = onehot[:, buckets - 1 :]
    spread = jnp.concatenate([onehot[:, : buckets - 1], last - 1.0], axis=1)
    table_grad = jnp.dot(spread.T, hist_sum.T, precision=lax.Precision.HIGHEST)
    return (
        layer_out[None],
        input_grad[None],
        small[experts],
        weights[3],
        weights[2],
        weights[1],
        weights[0],
        table_grad,
        small[experts + 1],
        router_grad,
        in_grad[None],
        out_grad[None],
    )


def solution(mesh):
    grouped = P(("dp", "expert"), "ctx", None)
    placed = (
        grouped, grouped, grouped, grouped, P(("dp", "expert"), "ctx"),
        P(), P(), P(), P(), P(), P(), P(), P(),
        P(("ctx", "expert"), None, None),
        P(("ctx", "expert"), None, None),
    )
    return jax.shard_map(
        body,
        mesh=mesh,
        in_specs=placed,
        out_specs=(
            grouped, grouped, P(), P(), P(), P(), P(), P(), P(), P(),
            P(("ctx", "expert"), None, "dp"),
            P(("ctx", "expert"), "dp", None),
        ),
        check_vma=False,
    )
```

```python
import functools

import jax
import jax.numpy as jnp
from jax import lax
from jax.experimental import pallas as pl
from jax.experimental.pallas import tpu as pltpu
from jax.sharding import PartitionSpec as P

PB = 256
TILE = 128
CHUNKS = 8
SHARED_CUTS = 4

bucket_edges = (19, 21, 24, 27, 31, 35, 40, 46, 52, 59, 67, 77, 87, 99, 113)
norm_eps = 1e-06
masked_score = -1e30
gelu_scale = 0.7978845608
gelu_cube = 0.044715

bf16 = jnp.bfloat16
f32 = jnp.float32
VMEM_LIMIT = 121 * 512 * 1024


def dot_nn(a, b):
    return jnp.dot(a, b, preferred_element_type=f32)


def dot_nt(a, b):
    return lax.dot_general(a, b, (((1,), (1,)), ((), ())), preferred_element_type=f32)


def dot_tn(a, b):
    return lax.dot_general(a, b, (((0,), (0,)), ((), ())), preferred_element_type=f32)


def two_parts(a):
    high = a.astype(bf16)
    return high, (a - high.astype(f32)).astype(bf16)


def vmem():
    return pl.BlockSpec(memory_space=pltpu.VMEM)


def smem():
    return pl.BlockSpec(memory_space=pltpu.SMEM)


def params():
    return pltpu.CompilerParams(vmem_limit_bytes=VMEM_LIMIT)


def remote_params(number):
    return pltpu.CompilerParams(
        vmem_limit_bytes=VMEM_LIMIT, collective_id=number, has_side_effects=True
    )


def cost(flops, nbytes):
    return pl.CostEstimate(flops=int(flops), bytes_accessed=int(nbytes), transcendentals=0)


def shape(dims, kind):
    return jax.ShapeDtypeStruct(dims, kind)


def inverse_rms(x):
    return lax.rsqrt(jnp.mean(x * x, axis=-1, keepdims=True) + norm_eps)


def bucket_onehot(buckets):
    distance = jnp.arange(TILE, dtype=jnp.int32)
    ids = jnp.minimum(distance, 16)
    for edge in bucket_edges:
        ids = ids + (distance >= edge).astype(jnp.int32)
    return (ids[:, None] == jnp.arange(buckets, dtype=jnp.int32)[None, :]).astype(f32)


def near_index(first):
    rows = lax.broadcasted_iota(jnp.int32, (TILE, TILE), 0)
    lanes = lax.broadcasted_iota(jnp.int32, (TILE, TILE), 1)
    return first + lanes - rows


def near_tiles(ctx_at, plen):
    start = ctx_at * PB
    return (
        (start, 0, 0, False),
        (start, TILE, TILE, False),
        (start + TILE, TILE, 0, False),
        (plen, PB, 0, False),
        (plen, PB + TILE, TILE, False),
        (plen + TILE, PB + TILE, 0, False),
        (start - TILE, 0, TILE, True),
    )


def add_near(s_ref, bias_row, ctx_at, branch, plen):
    source = jnp.broadcast_to(bias_row, (TILE, TILE))
    add_tiles(s_ref, source, ctx_at, near_tiles(ctx_at, plen))

    def window(i, _):
        rows = pl.ds(pl.multiple_of(i * TILE, TILE), TILE)
        lanes = slice(PB, PB + TILE)
        index = jnp.clip(near_index(branch - i * TILE), 0, TILE - 1)
        s_ref[rows, lanes] = s_ref[rows, lanes] + jnp.take_along_axis(source, index, axis=1)
        return 0

    lax.fori_loop(1, plen // TILE, window, 0)


def add_tiles(s_ref, source, ctx_at, tiles):
    for first_row, first_lane, gap, guarded in tiles:
        def work(first_row=first_row, first_lane=first_lane, gap=gap):
            rows = pl.ds(first_row if isinstance(first_row, int) else pl.multiple_of(first_row, 16), TILE)
            lanes = slice(first_lane, first_lane + TILE)
            index = jnp.clip(near_index(gap), 0, TILE - 1)
            s_ref[rows, lanes] = s_ref[rows, lanes] + jnp.take_along_axis(source, index, axis=1)

        if guarded:
            pl.when(ctx_at > 0)(work)
        else:
            work()


def scores_to(s_ref, keys, queries, plen):
    s_ref[:plen, :] = dot_nt(keys[:plen], queries)
    s_ref[plen:, PB:] = dot_nt(keys[plen:], queries[PB:])


def limits(ctx_at, branch, tokens):
    lane = lax.broadcasted_iota(jnp.int32, (1, tokens), 1)
    return jnp.where(lane < PB, ctx_at * PB + lane + 1, branch)


def row_steps(first, count, lanes):
    return first + lax.broadcasted_iota(jnp.int32, (count, lanes), 0)


def own_allowed(first, count, lanes):
    return row_steps(first, count, lanes) <= lax.broadcasted_iota(jnp.int32, (count, lanes), 1)


def head_lanes(half):
    return lax.broadcasted_iota(jnp.int32, (1, TILE), 1) // (TILE // 2) == half


def pick_rows(pieces, lanes):
    row = lax.broadcasted_iota(jnp.int32, (8, lanes), 0)
    return jnp.where(row == 0, pieces[0], jnp.where(row == 1, pieces[1], 0.0))


def fold8(x, op):
    return op(x.reshape(x.shape[0] // 8, 8, x.shape[1]), axis=0)


def owner_device(index):
    cores = lax.axis_size("expert")
    return {"ctx": index // cores, "expert": lax.rem(index, cores)}


def owners():
    cores = lax.axis_size("expert")
    count = cores * lax.axis_size("ctx")
    return count, lax.axis_index("ctx") * cores + lax.axis_index("expert")


def greet_owners():
    count, me = owners()
    barrier = pltpu.get_barrier_semaphore()

    def greet(ahead, _):
        pl.semaphore_signal(
            barrier, inc=1, device_id=owner_device(lax.rem(me + ahead, count)),
            device_id_type=pl.DeviceIdType.MESH,
        )
        return 0

    lax.fori_loop(1, count, greet, 0)
    pl.semaphore_wait(barrier, count - 1)


def block_copy(source, target, sems, ahead):
    count, me = owners()
    peer = lax.rem(me + ahead, count)
    return pltpu.make_async_remote_copy(
        src_ref=source.at[peer], dst_ref=target.at[me],
        send_sem=sems.at[0, ahead - 1], recv_sem=sems.at[1, ahead - 1],
        device_id=owner_device(peer), device_id_type=pl.DeviceIdType.MESH,
    )


def await_blocks(source, target, sems, sent, received):
    def one(ahead, _):
        copy = block_copy(source, target, sems, ahead)
        if received:
            copy.wait_recv()
        if sent:
            copy.wait_send()
        return 0

    lax.fori_loop(1, owners()[0], one, 0)


def place_rows(slot_row, index, block_rows, tokens):
    rows = lax.broadcasted_iota(jnp.int32, (block_rows, tokens), 0) + index * block_rows
    return (rows == slot_row).astype(bf16)


def front_kernel(
    capacity,
    branch_ref, bias_ref, x_ref, cot_ref, gain_ref, route_row, arrive_row,
    wq_ref, wk_ref, wv_ref,
    slot_out, cot_out, normed_own_out, normed_out, q_ref, k_out, v_out, att_out, lse_out,
    prompt_ref, send_ref, s_ref, p_ref, prompt_sems, cot_sems,
):
    branch = branch_ref[0, 0]
    ctx_at, ctx_count = lax.axis_index("ctx"), lax.axis_size("ctx")
    plen = PB * ctx_count
    tokens, width = x_ref.shape
    own = tokens - PB
    gain = gain_ref[...].astype(f32)
    count, me = owners()
    block_rows = send_ref.shape[1]
    greet_owners()

    chunk = PB // CHUNKS

    def pass_on(step, up, c):
        block = ctx_at - step if up else ctx_at + step
        ahead = ctx_at + 1 if up else ctx_at - 1
        fits = (block >= 0) & (ahead < ctx_count) if up else (block < ctx_count) & (ahead >= 0)
        piece = pl.ds(c * chunk, chunk)
        source = x_ref.at[piece] if step == 0 else prompt_ref.at[block, piece]
        copy = pltpu.make_async_remote_copy(
            src_ref=source, dst_ref=prompt_ref.at[block, piece],
            send_sem=prompt_sems.at[0, int(up), step, c], recv_sem=prompt_sems.at[1, int(up), step, c],
            device_id={"ctx": ahead}, device_id_type=pl.DeviceIdType.MESH,
        )
        return fits, copy

    def arrival(step, up, c):
        block = ctx_at - step - 1 if up else ctx_at + step + 1
        fits = block >= 0 if up else block < ctx_count
        place = prompt_ref.at[block, pl.ds(c * chunk, chunk)]
        copy = pltpu.make_async_remote_copy(
            src_ref=place, dst_ref=place,
            send_sem=prompt_sems.at[0, int(up), step, c], recv_sem=prompt_sems.at[1, int(up), step, c],
            device_id={"ctx": ctx_at}, device_id_type=pl.DeviceIdType.MESH,
        )
        return fits, block, copy

    for c in range(CHUNKS):
        for up in (True, False):
            fits, copy = pass_on(0, up, c)
            pl.when(fits)(copy.start)

    x = x_ref[...].astype(f32)
    normed_own_out[...] = (x * inverse_rms(x) * gain).astype(bf16)

    def column(i, _):
        cols = pl.ds(pl.multiple_of(i * 256, 256), 256)
        q_ref[:, cols] = dot_nn(normed_own_out[...], wq_ref[:, cols]).astype(bf16)
        k_out[plen:, cols] = dot_nn(normed_own_out[PB:, :], wk_ref[:, cols]).astype(bf16)
        v_out[plen:, cols] = dot_nn(normed_own_out[PB:, :], wv_ref[:, cols]).astype(bf16)
        return 0

    lax.fori_loop(0, width // 256, column, 0)

    def project(block):
        rows = pl.ds(pl.multiple_of(block * PB, PB), PB)

        def prompt_column(i, _):
            cols = pl.ds(pl.multiple_of(i * 256, 256), 256)
            k_out[rows, cols] = dot_nn(normed_out[rows, :], wk_ref[:, cols]).astype(bf16)
            v_out[rows, cols] = dot_nn(normed_out[rows, :], wv_ref[:, cols]).astype(bf16)
            return 0

        lax.fori_loop(0, width // 256, prompt_column, 0)

    def take(block):
        x = prompt_ref[block].astype(f32)
        rows = pl.ds(pl.multiple_of(block * PB, PB), PB)
        normed_out[rows, :] = (x * inverse_rms(x) * gain).astype(bf16)
        project(block)

    for step in range(ctx_count - 1):
        for c in range(CHUNKS):
            for up in (True, False):
                fits, block, copy = arrival(step, up, c)
                pl.when(fits)(copy.wait_recv)
                if step < ctx_count - 2:
                    fits, copy = pass_on(step + 1, up, c)
                    pl.when(fits)(copy.start)
        if step == 0:
            normed_out[pl.ds(pl.multiple_of(ctx_at * PB, PB), PB), :] = normed_own_out[:PB, :]
            project(ctx_at)
        for up in (True, False):
            fits, block, copy = arrival(step, up, 0)
            pl.when(fits)(functools.partial(take, block))

    def down(row):
        column = jnp.broadcast_to(row[...].astype(f32), (TILE, tokens)).T
        return jnp.concatenate([column] * (tokens // TILE), axis=1)

    same = down(route_row) == route_row[...].astype(f32)
    earlier = down(arrive_row) < arrive_row[...].astype(f32)
    rank = jnp.sum(jnp.where(same & earlier, 1.0, 0.0), axis=0, keepdims=True).astype(jnp.int32)
    slot = jnp.where(rank < capacity, route_row[...] * block_rows + rank, count * block_rows)
    slot_out[...] = slot

    def send_cot(ahead, _):
        peer = lax.rem(me + ahead, count)
        place = place_rows(slot_out[...], peer, block_rows, tokens)
        send_ref[peer] = dot_nn(place, cot_ref[...]).astype(bf16)
        block_copy(send_ref, cot_out, cot_sems, ahead).start()
        return 0

    def send_cots():
        lax.fori_loop(1, count, send_cot, 0)
        cot_out[me] = dot_nn(place_rows(slot_out[...], me, block_rows, tokens), cot_ref[...]).astype(bf16)

    p_ref[plen:, :PB] = jnp.zeros((own, PB), bf16)
    limit = limits(ctx_at, branch, tokens)

    def pair(g, _):
        pl.when(g == 1)(send_cots)
        lanes = pl.ds(pl.multiple_of(g * TILE, TILE), TILE)
        queries = q_ref[:, lanes]
        keys = k_out[:, lanes]
        values_t = v_out[:, lanes].T
        bias = bias_ref[g]
        lse_rows, att_rows = [], []
        for half in range(2):
            scores_to(s_ref, jnp.where(head_lanes(half), keys, jnp.zeros_like(keys)), queries, plen)
            add_near(s_ref, bias[half : half + 1, :], ctx_at, branch, plen)

            def top_of(i, top):
                rows = pl.ds(pl.multiple_of(i * TILE, TILE), TILE)
                s = jnp.where(row_steps(i * TILE, TILE, tokens) < limit, s_ref[rows, :], masked_score)
                s_ref[rows, :] = s
                return jnp.maximum(top, fold8(s, jnp.max))

            top = lax.fori_loop(0, plen // TILE, top_of, jnp.full((8, tokens), masked_score, f32))
            own_top = jnp.full((8, own), masked_score, f32)
            for i in range(own // TILE):
                rows = slice(plen + i * TILE, plen + (i + 1) * TILE)
                s = jnp.where(own_allowed(i * TILE, TILE, own), s_ref[rows, PB:], masked_score)
                s_ref[rows, PB:] = s
                own_top = jnp.maximum(own_top, fold8(s, jnp.max))
            top = jnp.concatenate([top[:, :PB], jnp.maximum(top[:, PB:], own_top)], axis=1)
            top = jnp.max(top, axis=0, keepdims=True)

            def weigh(i, total):
                rows = pl.ds(pl.multiple_of(i * TILE, TILE), TILE)
                p = jnp.exp(s_ref[rows, :] - top)
                p_ref[rows, :] = p.astype(bf16)
                return total + fold8(p, jnp.sum)

            total = lax.fori_loop(0, plen // TILE, weigh, jnp.zeros((8, tokens), f32))
            own_total = jnp.zeros((8, own), f32)
            for i in range(own // TILE):
                rows = slice(plen + i * TILE, plen + (i + 1) * TILE)
                p = jnp.exp(s_ref[rows, PB:] - top[:, PB:])
                p_ref[rows, PB:] = p.astype(bf16)
                own_total = own_total + fold8(p, jnp.sum)
            total = jnp.concatenate([total[:, :PB], total[:, PB:] + own_total], axis=1)
            total = jnp.sum(total, axis=0, keepdims=True)
            rows = slice(half * 64, half * 64 + 64)
            att_rows.append((dot_nn(values_t[rows, :], p_ref[...]) / total).astype(bf16))
            lse_rows.append(top + jnp.log(total))
        att_out[lanes, :] = jnp.concatenate(att_rows, axis=0)
        lse_out[g] = pick_rows(lse_rows, tokens)
        return 0

    lax.fori_loop(0, width // TILE, pair, 0)
    await_blocks(send_ref, cot_out, cot_sems, True, True)
    for step in range(ctx_count - 1):
        for c in range(CHUNKS):
            for up in (True, False):
                fits, copy = pass_on(step, up, c)
                pl.when(fits)(copy.wait_send)


def router_probs(logits, lane, experts):
    logits = jnp.where(lane < experts, logits, masked_score)
    logits = jnp.exp(logits - jnp.max(logits, axis=1, keepdims=True))
    return logits / jnp.sum(logits, axis=1, keepdims=True)


def gelu_parts(v):
    t = jnp.tanh(gelu_scale * (v + gelu_cube * (v * v * v)))
    half = 0.5 * (1.0 + t)
    slope = half + 0.5 * v * (1.0 - t * t) * (gelu_scale + (3.0 * gelu_scale * gelu_cube) * (v * v))
    return v * half, slope


def expert_kernel(
    experts,
    att_ref, x_ref, wo_ref, gain_ref, router_ref, slot_row, cot_ref, cot_rows, win_hbm, wout_hbm,
    rows_out, router_out, hidden_grad_out, wo_grad_out, att_grad_out, delta_out, gain_grad_out,
    result_out, hidden_ref,
    moe_ref, send_ref, win_ref, wout_ref, group_rows, sent_ref, result_acc, grad_acc,
    grad_send, grad_recv, low_ref, att_t_ref, rows_sems, grad_sems, load_sems,
):
    tokens, width = x_ref.shape
    count, me = owners()
    block_rows = send_ref.shape[1]
    hidden_units = win_ref.shape[1]
    loads = [
        pltpu.make_async_copy(win_hbm, win_ref, load_sems.at[0]),
        pltpu.make_async_copy(wout_hbm, wout_ref, load_sems.at[1]),
    ]
    for copy in loads:
        copy.start()
    greet_owners()

    def column(i, _):
        cols = pl.ds(pl.multiple_of(i * 256, 256), 256)
        hidden_ref[:, cols] = x_ref[:, cols].astype(f32) + dot_tn(att_ref[...], wo_ref[:, cols])
        return 0

    lax.fori_loop(0, width // 256, column, 0)
    hidden = hidden_ref[...]
    moe_ref[...] = (hidden * inverse_rms(hidden) * gain_ref[...].astype(f32)).astype(bf16)

    members = 2 * lax.axis_size("expert") if lax.axis_size("ctx") % 2 == 0 else count
    groups = count // members
    my_group = me // members

    def send_rows(ahead, _):
        peer = lax.rem(me + ahead, count)
        place = place_rows(slot_row[...], peer, block_rows, tokens)
        send_ref[peer] = dot_nn(place, moe_ref[...]).astype(bf16)
        block_copy(send_ref, rows_out, rows_sems, ahead).start()
        return 0

    def send_group(g, _):
        base = lax.rem(my_group + g, groups) * members

        def member(i, _):
            ahead = lax.rem(base + i - me + count, count)
            pl.when(ahead > 0)(lambda: (send_rows(ahead, 0), None)[1])
            return 0

        return lax.fori_loop(0, members, member, 0)

    lax.fori_loop(0, groups, send_group, 0)
    rows_out[me] = dot_nn(place_rows(slot_row[...], me, block_rows, tokens), moe_ref[...]).astype(bf16)

    router_out[...] = jnp.zeros_like(router_out)
    for copy in loads:
        copy.wait()

    def group(g, _):
        base = lax.rem(my_group + g, groups) * members

        def arrive(i, _):
            behind = lax.rem(me - base - i + count, count)
            pl.when(behind > 0)(lambda: block_copy(send_ref, rows_out, rows_sems, behind).wait_recv())
            return 0

        lax.fori_loop(0, members, arrive, 0)
        blocks = pl.ds(base, members)
        size = members * block_rows
        group_rows[...] = rows_out[blocks].reshape(size, width)
        slot_lane = lax.broadcasted_iota(jnp.int32, (size, TILE), 1)
        mine = slot_lane == me
        probs = router_probs(dot_nn(group_rows[...], router_ref[...]), slot_lane, experts)
        gate = jnp.sum(jnp.where(mine, probs, 0.0), axis=1, keepdims=True)
        cot_group = cot_rows[blocks].reshape(size, width).astype(f32)
        sent_ref[...] = (gate * cot_group).astype(bf16)
        result_acc[...] = jnp.zeros_like(result_acc)
        grad_acc[...] = jnp.zeros_like(grad_acc)

        def units(i, _):
            cols = pl.ds(pl.multiple_of(i * width, width), width)
            act, slope = gelu_parts(dot_nn(group_rows[...], win_ref[:, cols]))
            result_acc[...] += dot_nn(act.astype(bf16), wout_ref[cols, :])
            pre_grad = (dot_nt(sent_ref[...], wout_ref[cols, :]) * slope).astype(bf16)
            grad_acc[...] += dot_nt(pre_grad, win_ref[:, cols])
            return 0

        lax.fori_loop(0, hidden_units // width, units, 0)
        result = result_acc[...].astype(bf16)
        gate_grad = jnp.sum(cot_group * result.astype(f32), axis=1, keepdims=True)
        logit_grad = (gate_grad * gate) * (jnp.where(mine, 1.0, 0.0) - probs)
        high, low = two_parts(logit_grad)
        grad = grad_acc[...] + (dot_nt(high, router_ref[...]) + dot_nt(low, router_ref[...]))
        grad_send[blocks] = grad.astype(bf16).reshape(members, block_rows, width)
        gated = (gate * result.astype(f32)).astype(bf16)
        result_out[blocks] = gated.reshape(members, block_rows, width)

        def give(i, _):
            ahead = lax.rem(base + i - me + count, count)

            @pl.when(ahead > 0)
            def _():
                block_copy(grad_send, grad_recv, grad_sems, ahead).start()

            return 0

        lax.fori_loop(0, members, give, 0)
        router_out[...] += dot_tn(high, group_rows[...]) + dot_tn(low, group_rows[...])
        return 0

    lax.fori_loop(0, groups, group, 0)
    grad_recv[me] = grad_send[me]

    slots = count * block_rows
    place = place_rows(slot_row[...], 0, slots, tokens)
    await_blocks(grad_send, grad_recv, grad_sems, False, True)
    moe_grad = dot_tn(place, grad_recv[...].reshape(slots, width))
    hidden = hidden_ref[...]
    inverse = inverse_rms(hidden)
    scaled = hidden * inverse
    gain_grad_out[...] = jnp.sum(moe_grad * scaled, axis=0, keepdims=True)
    through = moe_grad * gain_ref[...].astype(f32)
    shared = jnp.mean(through * scaled, axis=1, keepdims=True)
    hidden_grad = cot_ref[...].astype(f32) + inverse * (through - scaled * shared)
    hidden_grad_out[...] = hidden_grad
    low_ref[...] = hidden_grad.astype(bf16)

    def back_column(i, _):
        cols = pl.ds(pl.multiple_of(i * 256, 256), 256)
        wo_grad = dot_nn(att_ref[...], low_ref[:, cols]).astype(bf16).reshape(width // 16, 16, 256)
        if wo_grad_out.shape[0] == 1:
            wo_grad_out[0, :, :, cols] = wo_grad
        else:
            wo_grad_out[i] = wo_grad
        att_grad_out[:, cols] = dot_nt(low_ref[...], wo_ref[cols, :]).astype(bf16)
        att_t_ref[cols, :] = dot_nt(wo_ref[cols, :], low_ref[...]).astype(bf16)
        return 0

    lax.fori_loop(0, width // 256, back_column, 0)

    def pair(g, _):
        rows = pl.ds(pl.multiple_of(g * TILE, TILE), TILE)
        both = att_ref[rows, :].astype(f32) * att_t_ref[rows, :].astype(f32)
        delta_out[g] = pick_rows(
            [jnp.sum(both[:64], axis=0, keepdims=True), jnp.sum(both[64:], axis=0, keepdims=True)],
            tokens,
        )
        return 0

    lax.fori_loop(0, width // TILE, pair, 0)
    await_blocks(send_ref, rows_out, rows_sems, True, False)
    await_blocks(grad_send, grad_recv, grad_sems, True, False)


class Axis:
    def __init__(self, name, size, step=1):
        place = lax.axis_index(name)
        self.name, self.size, self.step, self.place = name, size, step, place
        self.index = lax.rem(place // step, size)

    def at(self, ahead):
        return lax.rem(self.index + ahead, self.size)

    def peer(self, ahead):
        return {self.name: self.place + (self.at(ahead) - self.index) * self.step}


def mesh_axes():
    dp, ctx, expert = lax.axis_size("dp"), lax.axis_size("ctx"), lax.axis_size("expert")
    cores, lines = Axis("expert", expert), Axis("ctx", ctx)
    if dp == 4:
        near, far = Axis("dp", 2, 1), Axis("dp", 2, 2)
        return [[cores, near, far, lines], [cores, far, near, lines]]
    return [[cores, Axis("dp", dp), lines]] * 2


def cuts_of(length):
    return 4 if length % 8 == 0 else 2 if length % 4 == 0 else 1


def push(source, target, sems, slot, device):
    copy = pltpu.make_async_remote_copy(
        src_ref=source, dst_ref=target, send_sem=sems.at[0, slot], recv_sem=sems.at[1, slot],
        device_id=device, device_id_type=pl.DeviceIdType.MESH,
    )
    copy.start()
    return copy


def back_kernel(
    experts, plan,
    branch_ref, bias_ref, q_ref, k_hbm, v_hbm, att_grad_ref, lse_ref, delta_ref, normed_hbm, normed_own_ref,
    gain_ref, wq_ref, wk_ref, wv_ref, wo_part_hbm, moe_gain_ref, router_part_hbm, x_hbm, hidden_grad_hbm,
    hidden_hbm, slot_row, result_hbm, rows_hbm, cot_hbm, win_hbm, wout_hbm, router_ref,
    full_ref, small_out, input_out, in_out, out_out, layer_out, rows_all,
    k_ref, v_ref, normed_ref, s_ref, dp_ref, p_ref, ds_ref, dq_ref, dk_ref, dv_ref, hist_ref, gain_sum,
    local_ref, shared_send, shared_recv, parts_ref, acc_refs, recv_refs, small_ref, small_recv,
    result_recv, win_ref, wout_ref, rows_ref, cot_ref, rows_t,
    block_sems, load_sems, sems, small_sems, shared_sems, result_sems, rows_sems,
):
    group, pieces, lengths = plan
    flows = mesh_axes()
    branch = branch_ref[0, 0]
    ctx_at = lax.axis_index("ctx")
    ctx_count, dp_count = lax.axis_size("ctx"), lax.axis_size("dp")
    tokens, width = q_ref.shape
    own = tokens - PB
    plen = PB * ctx_count
    count, me = owners()
    lines, columns_dp = Axis("ctx", ctx_count), Axis("dp", dp_count)
    whole_axes = [Axis("expert", lax.axis_size("expert")), columns_dp, lines]
    gain = gain_ref[...].astype(f32)
    limit = limits(ctx_at, branch, tokens)
    blocks = ctx_count + 1
    rows_16 = width // 16

    def block_loads(i):
        rows = plen if i == blocks - 1 else pl.multiple_of(lines.at(i + 1) * PB, PB)
        sources = [(k_hbm, k_ref, 0), (v_hbm, v_ref, 1)]
        if i < blocks - 2:
            sources.append((normed_hbm, normed_ref, 2))
        return [
            pltpu.make_async_copy(source.at[pl.ds(rows, PB)], target.at[i % 2], block_sems.at[i, n])
            for source, target, n in sources
        ]

    for copy in block_loads(0):
        copy.start()
    slice_width = win_ref.shape[1]
    part = pl.ds(pl.multiple_of(lax.axis_index("dp") * slice_width, slice_width), slice_width)
    weight_loads = [
        pltpu.make_async_copy(win_hbm.at[:, part], win_ref, load_sems.at[0]),
        pltpu.make_async_copy(wout_hbm.at[part], wout_ref, load_sems.at[1]),
    ]
    own_result = pltpu.make_async_copy(result_hbm.at[me], result_recv.at[me], load_sems.at[2])
    wo_load = pltpu.make_async_copy(wo_part_hbm.at[0], parts_ref.at[pl.ds(0, rows_16)], load_sems.at[5 + 2 * dp_count])
    router_load = pltpu.make_async_copy(
        router_part_hbm.at[pl.ds(0, experts)], small_ref.at[pl.ds(0, experts)], load_sems.at[7 + 2 * dp_count]
    )
    for copy in [wo_load, *weight_loads, own_result, router_load]:
        copy.start()

    barrier = pltpu.get_barrier_semaphore()

    def greet(ahead, _):
        pl.semaphore_signal(
            barrier, inc=1, device_id=owner_device(lax.rem(me + ahead, count)),
            device_id_type=pl.DeviceIdType.MESH,
        )
        return 0

    lax.fori_loop(1, count, greet, 0)
    for ahead in range(1, dp_count):
        pl.semaphore_signal(
            barrier, inc=1, device_id=columns_dp.peer(ahead), device_id_type=pl.DeviceIdType.MESH
        )
    pl.semaphore_wait(barrier, count - 1 + dp_count - 1)

    slots_of = {}

    def slot(*key):
        return slots_of.setdefault(key, len(slots_of))

    started = []

    def reduce_start(j, s):
        axis, length = flows[j % 2][s], lengths[s]
        copies = []
        for ahead in range(1, axis.size):
            target = axis.at(ahead)
            cuts = cuts_of(length)
            size = length // cuts
            for cut in range(cuts):
                first = target * length + cut * size
                if s == 0:
                    source = parts_ref.at[pl.ds(j * group + first, size)]
                else:
                    source = acc_refs[s - 1].at[j, pl.ds(first, size)]
                there = recv_refs[s].at[j, ahead - 1, pl.ds(cut * size, size)]
                copies.append(push(source, there, sems, slot("r", j, s, ahead, cut), axis.peer(ahead)))
        started.extend(copies)
        return copies

    def base_of(j, s):
        base = j * group
        for t in range(s + 1):
            base = base + flows[j % 2][t].index * lengths[t]
        return base

    def reduce_finish(j, s, copies):
        axis, length = flows[j % 2][s], lengths[s]
        for copy in copies:
            copy.wait_recv()
        last = s == len(lengths) - 1

        size = 4 if length % 4 == 0 else 1

        def some(u, _):
            if s == 0:
                total = parts_ref[pl.ds(base_of(j, 0) + u * size, size)].astype(f32)
            else:
                total = acc_refs[s - 1][j, pl.ds(axis.index * length + u * size, size)].astype(f32)
            for ahead in range(1, axis.size):
                total = total + recv_refs[s][j, ahead - 1, pl.ds(u * size, size)].astype(f32)
            if last:
                full_ref[pl.ds(base_of(j, s) + u * size, size)] = total.astype(bf16)
            else:
                acc_refs[s][j, pl.ds(u * size, size)] = total.astype(bf16)
            return 0

        lax.fori_loop(0, length // size, some, 0)

    def spread_start(j, s):
        axis, length = flows[j % 2][s], lengths[s]
        cuts = cuts_of(length)
        size = length // cuts
        copies = []
        for ahead in range(1, axis.size):
            for cut in range(cuts):
                here = full_ref.at[pl.ds(base_of(j, s) + cut * size, size)]
                copies.append(push(here, here, sems, slot("s", j, s, ahead, cut), axis.peer(ahead)))
        started.extend(copies)
        return copies

    def small_slot(s, ahead):
        return sum(axis.size - 1 for axis in whole_axes[:s]) + ahead - 1

    def small_start(s):
        axis = whole_axes[s]
        copies = [
            push(small_ref, small_recv[s].at[ahead - 1], small_sems, small_slot(s, ahead), axis.peer(ahead))
            for ahead in range(1, axis.size)
        ]
        return copies

    def small_finish(s, copies):
        axis = whole_axes[s]
        for copy in copies:
            copy.wait()
        mine = small_ref[...]
        total = jnp.zeros_like(mine)
        for index in range(axis.size):
            piece = mine
            for ahead in range(1, axis.size):
                piece = jnp.where(axis.at(axis.size - ahead) == index, small_recv[s][ahead - 1], piece)
            total = total + piece
        if s == len(whole_axes) - 1:
            small_out[...] = total
        else:
            small_ref[...] = total

    stages = len(lengths)
    early = pieces > 1 and group <= rows_16
    begin = [blocks + j // 2 for j in range(pieces)]
    if early:
        begin = [blocks - 1] + [blocks + (j - 1) // 2 for j in range(1, pieces)]
    pending = {}

    def advance(time):
        for j in sorted(range(pieces), key=lambda j: begin[j]):
            s = time - begin[j]
            if not 0 <= s < 2 * stages:
                continue
            if s < stages:
                reduce_finish(j, s, pending[j, s])
                if s + 1 < stages:
                    pending[j, s + 1] = reduce_start(j, s + 1)
                else:
                    pending[j, s + 1] = spread_start(j, s)
            else:
                for copy in pending[j, s]:
                    copy.wait_recv()
                if s + 1 < 2 * stages:
                    pending[j, s + 1] = spread_start(j, 2 * stages - 1 - (s + 1))

    def put(first, cols, value):
        rows = value.shape[0]
        parts_ref[first // 16 : (first + rows) // 16, :, cols] = value.astype(bf16).reshape(
            rows // 16, 16, value.shape[1]
        )

    def columns(work):
        def column(i, _):
            work(pl.ds(pl.multiple_of(i * 256, 256), 256))
            return 0

        lax.fori_loop(0, width // 256, column, 0)

    if parts_ref.shape[0] > 4 * rows_16:
        extra = parts_ref.shape[0] - 4 * rows_16
        parts_ref[4 * rows_16 :] = jnp.zeros((extra, 16, width), bf16)
    wo_load.wait()
    if early:
        pending[0, 0] = reduce_start(0, 0)

    def give_result(ahead, _):
        block_copy(result_hbm, result_recv, result_sems, ahead).start()
        return 0

    lax.fori_loop(1, count, give_result, 0)

    def rows_copy(ahead, e):
        return pltpu.make_async_remote_copy(
            src_ref=rows_hbm.at[e], dst_ref=rows_all.at[ahead - 1, e],
            send_sem=rows_sems.at[0, ahead - 1, e], recv_sem=rows_sems.at[1, ahead - 1, e],
            device_id=columns_dp.peer(ahead), device_id_type=pl.DeviceIdType.MESH,
        )

    def each_row_block(act):
        def one(e, _):
            for ahead in range(1, dp_count):
                act(rows_copy(ahead, e))
            return 0

        lax.fori_loop(0, count, one, 0)

    each_row_block(lambda copy: copy.start())

    shared_copies = []
    shared_slots = shared_send.shape[0]
    hist_ref[...] = jnp.zeros_like(hist_ref)
    gain_sum[...] = jnp.zeros_like(gain_sum)
    for i in range(blocks):
        cont = i == blocks - 1
        at_home = i == blocks - 2
        for copy in block_loads(i):
            copy.wait()
        if i + 1 < blocks:
            for copy in block_loads(i + 1):
                copy.start()
        block = lines.at(i + 1)
        lanes_from = PB if cont else 0
        lanes_used = slice(lanes_from, tokens)
        near = []
        if cont or at_home:
            near = [
                (0, lanes_from, 0, None),
                (0, lanes_from + TILE, TILE, None),
                (TILE, lanes_from + TILE, 0, None),
            ]
        else:
            near = [(TILE, 0, TILE, block == ctx_at - 1)]
        if not cont:
            near += [(first, PB, branch - block * PB - first, None) for first in range(0, PB, TILE)]

        def pair(g, _, i=i, cont=cont, block=block, lanes_used=lanes_used, near=near):
            lanes = pl.ds(pl.multiple_of(g * TILE, TILE), TILE)
            queries = q_ref[lanes_used, lanes]
            grads = att_grad_ref[lanes_used, lanes]
            keys = k_ref[i % 2, :, lanes]
            values = v_ref[i % 2, :, lanes]
            keys_t = keys.T
            bias = bias_ref[g]
            dk_parts, dv_parts, dq_parts = [], [], []
            for half in range(2):
                mine = head_lanes(half)
                lse = lse_ref[g][half : half + 1, lanes_used]
                delta = delta_ref[g][half : half + 1, lanes_used]
                s_ref[:, lanes_used] = dot_nt(jnp.where(mine, keys, jnp.zeros_like(keys)), queries)
                dp_ref[:, lanes_used] = dot_nt(jnp.where(mine, values, jnp.zeros_like(values)), grads)
                source = jnp.broadcast_to(bias[half : half + 1, :], (TILE, TILE))
                for first, lane, gap, when in near:
                    def add(first=first, lane=lane, gap=gap):
                        there = (slice(first, first + TILE), slice(lane, lane + TILE))
                        index = jnp.clip(near_index(gap), 0, TILE - 1)
                        s_ref[there] = s_ref[there] + jnp.take_along_axis(source, index, axis=1)

                    add() if when is None else pl.when(when)(add)
                step = 32
                for first in range(0, PB, step):
                    rows = slice(first, first + step)
                    if cont:
                        allowed = own_allowed(first, step, own)
                    else:
                        allowed = row_steps(block * PB + first, step, tokens) < limit
                    p = jnp.where(allowed, jnp.exp(s_ref[rows, lanes_used] - lse), 0.0)
                    p_ref[rows, lanes_used] = p.astype(bf16)
                    ds_ref[rows, lanes_used] = (p * (dp_ref[rows, lanes_used] - delta)).astype(bf16)
                for first, lane, gap, when in near:
                    def collect(first=first, lane=lane, gap=gap):
                        tile = ds_ref[first : first + TILE, lane : lane + TILE].astype(f32)
                        if not isinstance(gap, int) or gap > 0:
                            tile = jnp.where(near_index(gap) < TILE, tile, 0.0)
                        turn = lax.broadcasted_iota(jnp.int32, (TILE, TILE), 1) + lax.broadcasted_iota(
                            jnp.int32, (TILE, TILE), 0
                        )
                        tile = jnp.take_along_axis(tile, (turn - gap) & (TILE - 1), axis=1)
                        hist_ref[g * 2 + half] += fold8(tile, jnp.sum)

                    collect() if when is None else pl.when(when)(collect)
                ds = ds_ref[:, lanes_used]
                dv_parts.append(dot_nn(p_ref[:, lanes_used], grads))
                dk_parts.append(dot_nn(ds, queries))
                dq_parts.append(dot_nn(keys_t[half * 64 : half * 64 + 64, :], ds))
            dq = jnp.concatenate(dq_parts, axis=0)
            if i == 0:
                dq_ref[lanes, :] = dq
            else:
                dq_ref[lanes, lanes_used] += dq
            mine = head_lanes(0)
            dv_ref[:, lanes] = jnp.where(mine, dv_parts[0], dv_parts[1]).astype(bf16)
            dk_ref[:, lanes] = jnp.where(mine, dk_parts[0], dk_parts[1]).astype(bf16)
            return 0

        lax.fori_loop(0, width // TILE, pair, 0)

        def block_column(cols, i=i, cont=cont, at_home=at_home):
            if cont:
                normed = normed_own_ref[PB:, cols]
            elif at_home:
                normed = normed_own_ref[:PB, cols]
            else:
                normed = normed_ref[i % 2, :, cols]
            wk_part = dot_nn(rows_t[:, :PB], dk_ref[:, cols])
            wv_part = dot_nn(rows_t[:, :PB], dv_ref[:, cols])
            if i == 0:
                in_out[:, cols] = wk_part
                out_out[:, cols] = wv_part
            elif not cont:
                in_out[:, cols] += wk_part
                out_out[:, cols] += wv_part
            else:
                put(width, cols, out_out[:, cols] + wv_part)
                put(2 * width, cols, in_out[:, cols] + wk_part)
            grad = dot_nt(dk_ref[...], wk_ref[cols, :]) + dot_nt(dv_ref[...], wv_ref[cols, :])
            gain_sum[:, cols] += jnp.sum(grad * normed.astype(f32), axis=0, keepdims=True)
            if cont:
                local_ref[PB:, cols] = grad
            elif at_home:
                local_ref[:PB, cols] = grad
            else:
                shared_send[i % shared_slots, :, cols] = grad.astype(bf16)

        if shared_slots <= i < blocks - 2:
            for copy in shared_copies[i - shared_slots]:
                copy.wait_send()
        if cont:
            rows_t[:, :PB] = normed_own_ref[PB:, :].T
        elif at_home:
            rows_t[:, :PB] = normed_own_ref[:PB, :].T
        else:
            rows_t[:, :PB] = normed_ref[i % 2].T
        columns(block_column)
        if i < blocks - 2:
            size = PB // SHARED_CUTS
            shared_copies.append(
                [
                    push(
                        shared_send.at[i % shared_slots, pl.ds(cut * size, size)],
                        shared_recv.at[i, pl.ds(cut * size, size)],
                        shared_sems, i * SHARED_CUTS + cut, lines.peer(i + 1),
                    )
                    for cut in range(SHARED_CUTS)
                ]
            )
    for copies in shared_copies[-shared_slots:]:
        started.extend(copies)

    def ready(j):
        if j > 0 or not early:
            pending[j, 0] = reduce_start(j, 0)

    done = 3 * rows_16
    for j in range(pieces):
        if (j + 1) * group <= done:
            ready(j)
    rows_ref[:tokens, :] = dq_ref[...].T.astype(bf16)
    rows_t[:, :tokens] = normed_own_ref[...].T

    def query_column(cols):
        put(3 * width, cols, dot_nn(rows_t[:, :tokens], rows_ref[:tokens, cols]))

    columns(query_column)
    for j in range(pieces):
        if (j + 1) * group > done:
            ready(j)

    def query_grad(cols):
        grad = dot_nt(rows_ref[:tokens, :], wq_ref[cols, :])
        gain_sum[:, cols] += jnp.sum(grad * normed_own_ref[:, cols].astype(f32), axis=0, keepdims=True)
        local_ref[:, cols] += grad

    columns(query_grad)
    small_ref[experts:, :] = jnp.zeros((small_ref.shape[0] - experts, width), f32)
    small_ref[experts : experts + 1, :] = gain_sum[...] / gain
    small_ref[experts + 1 : experts + 2, :] = moe_gain_ref[...]
    router_load.wait()
    per_row = width // TILE
    for head in range(hist_ref.shape[0]):
        row, lane = 2 + experts + head // per_row, head % per_row * TILE
        small_ref[row : row + 1, lane : lane + TILE] = jnp.sum(hist_ref[head], axis=0, keepdims=True)
    small_pending = small_start(0)

    slots = rows_ref.shape[0]

    def grads_of(n, c):
        if c == 0:
            if n == 0:
                for copy in weight_loads:
                    copy.wait()
            if n == 1:
                each_row_block(lambda copy: copy.wait_recv())
            source = rows_hbm if n == 0 else rows_all.at[n - 1]
            load = pltpu.make_async_copy(source, result_recv, load_sems.at[3 + 2 * n])
            load.start()
            load.wait()
            rows_ref[...] = result_recv[...].reshape(slots, width)
            cot_from = columns_dp.at(dp_count - n)
            load = pltpu.make_async_copy(cot_hbm.at[cot_from], result_recv, load_sems.at[4 + 2 * n])
            load.start()
            lane = lax.broadcasted_iota(jnp.int32, (slots, TILE), 1)
            probs = router_probs(dot_nn(rows_ref[...], router_ref[...]), lane, experts)
            gate = jnp.sum(jnp.where(lane == me, probs, 0.0), axis=1, keepdims=True)
            load.wait()
            cot = result_recv[...].reshape(slots, width)
            cot_ref[...] = (gate * cot.astype(f32)).astype(bf16)
            rows_t[...] = rows_ref[...].T
        cols = slice(c * 256, c * 256 + 256)
        act, slope = gelu_parts(dot_nn(rows_ref[...], win_ref[:, cols]))
        pre_grad = (dot_nt(cot_ref[...], wout_ref[cols, :]) * slope).astype(bf16)
        out_part = dot_tn(act.astype(bf16), cot_ref[...])
        in_part = dot_nn(rows_t[...], pre_grad)
        if n == 0:
            out_out[cols, :] = out_part
            in_out[:, cols] = in_part
        else:
            out_out[cols, :] += out_part
            in_out[:, cols] += in_part

    def input_back():
        held = pltpu.make_async_copy(hidden_grad_hbm, input_out, load_sems.at[3 + 2 * dp_count])
        held.start()
        x_load = pltpu.make_async_copy(x_hbm, rows_ref.at[pl.ds(0, tokens)], load_sems.at[6 + 2 * dp_count])
        x_load.start()
        for copies in shared_copies:
            for copy in copies:
                copy.wait_recv()
        held.wait()
        x_load.wait()
        for first, shared_rows in ((0, True), (PB, False)):
            rows = slice(first, PB if shared_rows else tokens)
            x = rows_ref[rows, :].astype(f32)
            inverse = inverse_rms(x)
            grad = local_ref[rows, :]
            if shared_rows:
                for n in range(ctx_count - 1):
                    grad = grad + shared_recv[n].astype(f32)
            through = grad * gain
            scaled = x * inverse
            shared = jnp.mean(through * scaled, axis=1, keepdims=True)
            input_out[rows, :] += inverse * (through - scaled * shared)

    def layer():
        held = pltpu.make_async_copy(hidden_hbm, input_out, load_sems.at[4 + 2 * dp_count])
        held.start()
        own_result.wait()
        await_blocks(result_hbm, result_recv, result_sems, False, True)
        place = place_rows(slot_row[...], 0, slots, tokens)
        returned = dot_tn(place, result_recv[...].reshape(slots, width))
        held.wait()
        layer_out[...] = (input_out[...] + returned).astype(bf16)

    work = [layer]
    work += [functools.partial(grads_of, n, c) for n in range(dp_count) for c in range(slice_width // 256)]
    work += [input_back]
    for time in range(blocks - 1, max(begin) + 2 * stages):
        if time >= blocks:
            advance(time)
        elif early:
            advance(time)
        s = time - blocks
        if 0 <= s < len(whole_axes):
            small_finish(s, small_pending)
            if s + 1 < len(whole_axes):
                small_pending = small_start(s + 1)
        if work:
            work.pop(0)()
    for rest in work:
        rest()
    for copy in started:
        copy.wait_send()
    await_blocks(result_hbm, result_recv, result_sems, True, False)
    each_row_block(lambda copy: copy.wait_send())


def head_kernel(
    branch_ref, bias_ref, q_ref, k_hbm, v_hbm, att_grad_ref, lse_ref, delta_ref, normed_hbm, normed_own_hbm,
    wq_ref, wk_ref, wv_ref, wo_part_hbm, result_hbm, rows_hbm,
    parts_ref, shared_out, local_out, gain_sum, hist_ref, result_recv, rows_all,
    k_ref, v_ref, normed_ref, nt_ref, s_ref, dp_ref, p_ref, ds_ref, dq_ref, dk_ref, dv_ref,
    near_ref, turn_ref, grad_ref, dq_low,
    slab_sems, load_sems, result_sems, rows_sems,
):
    branch = branch_ref[0, 0]
    ctx_at = lax.axis_index("ctx")
    ctx_count, dp_count = lax.axis_size("ctx"), lax.axis_size("dp")
    tokens, width = q_ref.shape
    own = tokens - PB
    plen = PB * ctx_count
    count, me = owners()
    columns_dp = Axis("dp", dp_count)
    limit = limits(ctx_at, branch, tokens)
    rows_16 = width // 16
    quads = width // 256
    heads_per_quad = 4

    def slab_loads(q):
        cols = pl.ds(q * 256, 256)
        return [
            pltpu.make_async_copy(k_hbm.at[:, cols], k_ref.at[q % 2], slab_sems.at[q, 0]),
            pltpu.make_async_copy(v_hbm.at[:, cols], v_ref.at[q % 2], slab_sems.at[q, 1]),
        ]

    for copy in slab_loads(0):
        copy.start()
    own_result = pltpu.make_async_copy(result_hbm.at[me], result_recv.at[me], load_sems.at[0])
    normed_loads = [
        pltpu.make_async_copy(normed_hbm, normed_ref.at[pl.ds(0, plen)], load_sems.at[1]),
        pltpu.make_async_copy(normed_own_hbm.at[pl.ds(PB, own)], normed_ref.at[pl.ds(plen, own)], load_sems.at[2]),
    ]
    per_quad = parts_ref.shape[0] // quads
    wo_loads = [
        pltpu.make_async_copy(wo_part_hbm.at[q], parts_ref.at[pl.ds(q * per_quad, rows_16)], load_sems.at[3 + q])
        for q in range(quads)
    ]
    for copy in [*normed_loads, *wo_loads, own_result]:
        copy.start()

    barrier = pltpu.get_barrier_semaphore()

    def greet(ahead, _):
        pl.semaphore_signal(
            barrier, inc=1, device_id=owner_device(lax.rem(me + ahead, count)),
            device_id_type=pl.DeviceIdType.MESH,
        )
        return 0

    lax.fori_loop(1, count, greet, 0)
    for ahead in range(1, dp_count):
        pl.semaphore_signal(
            barrier, inc=1, device_id=columns_dp.peer(ahead), device_id_type=pl.DeviceIdType.MESH
        )
    pl.semaphore_wait(barrier, count - 1 + dp_count - 1)

    def put(q, matrix, value):
        first = q * per_quad + matrix * rows_16
        parts_ref[first : first + rows_16] = value.astype(bf16).reshape(rows_16, 16, 256)

    def columns(work):
        def column(i, _):
            work(pl.ds(pl.multiple_of(i * 256, 256), 256))
            return 0

        lax.fori_loop(0, width // 256, column, 0)

    def give_result(ahead, _):
        block_copy(result_hbm, result_recv, result_sems, ahead).start()
        return 0

    lax.fori_loop(1, count, give_result, 0)

    def rows_copy(ahead, e):
        return pltpu.make_async_remote_copy(
            src_ref=rows_hbm.at[e], dst_ref=rows_all.at[ahead - 1, e],
            send_sem=rows_sems.at[0, ahead - 1, e], recv_sem=rows_sems.at[1, ahead - 1, e],
            device_id=columns_dp.peer(ahead), device_id_type=pl.DeviceIdType.MESH,
        )

    row_blocks = [(ahead, e) for ahead in range(1, dp_count) for e in range(count)]
    at_once = -(-len(row_blocks) // (quads * heads_per_quad))

    def each_row_block(act):
        def one(e, _):
            for ahead in range(1, dp_count):
                act(rows_copy(ahead, e))
            return 0

        lax.fori_loop(0, count, one, 0)

    start = ctx_at * PB
    near_ref[0] = jnp.clip(near_index(0), 0, TILE - 1)
    near_ref[1] = jnp.clip(near_index(TILE), 0, TILE - 1)
    for i in range(1, plen // TILE):
        near_ref[1 + i] = jnp.clip(near_index(branch - i * TILE), 0, TILE - 1)
    turn = lax.broadcasted_iota(jnp.int32, (TILE, TILE), 1) + lax.broadcasted_iota(jnp.int32, (TILE, TILE), 0)
    turn_ref[0] = turn & (TILE - 1)
    turn_ref[1] = (turn - branch) & (TILE - 1)
    hist_ref[...] = jnp.zeros_like(hist_ref)
    for copy in normed_loads:
        copy.wait()
    nt_ref[...] = normed_ref[...].T

    def each_near(act):
        act(start, 0, 0, 0)
        act(start, TILE, 1, 0)
        act(start + TILE, TILE, 0, 0)
        pl.when(ctx_at > 0)(lambda: act(start - TILE, 0, 1, 0))

        def window(i, _):
            act(i * TILE, PB, 1 + i, 1)
            return 0

        lax.fori_loop(1, plen // TILE, window, 0)

    def each_near_own(act):
        act(0, PB, 0, 0)
        act(0, PB + TILE, 1, 0)
        act(TILE, PB + TILE, 0, 0)

    def one_head(q, number):
        half = number % 2
        pair = number // 2
        g, head = q * 2 + pair, q * 4 + number
        lanes = slice(pair * TILE, pair * TILE + TILE)
        here = slice(g * TILE, g * TILE + TILE)
        features = slice(number * 64, number * 64 + 64)
        mine = head_lanes(half)
        lse = lse_ref[g][half : half + 1, :]
        delta = delta_ref[g][half : half + 1, :]
        source = jnp.broadcast_to(bias_ref[g][half : half + 1, :], (TILE, TILE))

        def add(row, lane, slot, turned):
            rows = pl.ds(row if isinstance(row, int) else pl.multiple_of(row, TILE), TILE)
            cols = slice(lane, lane + TILE)
            s_ref[rows, cols] = s_ref[rows, cols] + jnp.take_along_axis(source, near_ref[slot], axis=1)

        def collect(row, lane, slot, turned):
            rows = pl.ds(row if isinstance(row, int) else pl.multiple_of(row, TILE), TILE)
            tile = ds_ref[rows, lane : lane + TILE].astype(f32)
            tile = jnp.where(near_ref[slot] < TILE - 1, tile, 0.0)
            tile = jnp.take_along_axis(tile, turn_ref[turned], axis=1)
            hist_ref[head] += fold8(tile, jnp.sum)

        def keep(target, rows, value):
            if half == 0:
                target[rows, lanes] = value.astype(bf16)
            else:
                target[rows, lanes] = jnp.where(mine, value, target[rows, lanes].astype(f32)).astype(bf16)

        prompt = slice(0, plen)
        keys = k_ref[q % 2, prompt, lanes]
        values = v_ref[q % 2, prompt, lanes]
        queries = q_ref[:, here]
        grads = att_grad_ref[:, here]
        s_ref[...] = dot_nt(jnp.where(mine, keys, jnp.zeros_like(keys)), queries)
        dp_ref[...] = dot_nt(jnp.where(mine, values, jnp.zeros_like(values)), grads)
        each_near(add)

        def some_rows(i, _):
            for sub in range(0, TILE, 32):
                first = pl.multiple_of(i * TILE + sub, 32)
                rows = pl.ds(first, 32)
                allowed = row_steps(first, 32, tokens) < limit
                p = jnp.where(allowed, jnp.exp(s_ref[rows, :] - lse), 0.0)
                p_ref[rows, :] = p.astype(bf16)
                ds_ref[rows, :] = (p * (dp_ref[rows, :] - delta)).astype(bf16)
            return 0

        lax.fori_loop(0, plen // TILE, some_rows, 0)
        each_near(collect)
        keep(dv_ref, prompt, dot_nn(p_ref[...], grads))
        keep(dk_ref, prompt, dot_nn(ds_ref[...], queries))
        dq_ref[features, :] = dot_nn(keys.T[half * 64 : half * 64 + 64, :], ds_ref[...])

        cont = slice(plen, plen + own)
        keys = k_ref[q % 2, cont, lanes]
        values = v_ref[q % 2, cont, lanes]
        queries = q_ref[PB:, here]
        grads = att_grad_ref[PB:, here]
        s_ref[:own, PB:] = dot_nt(jnp.where(mine, keys, jnp.zeros_like(keys)), queries)
        dp_ref[:own, PB:] = dot_nt(jnp.where(mine, values, jnp.zeros_like(values)), grads)
        each_near_own(add)
        for first in range(0, own, 32):
            rows = slice(first, first + 32)
            p = jnp.where(own_allowed(first, 32, own), jnp.exp(s_ref[rows, PB:] - lse[:, PB:]), 0.0)
            p_ref[rows, PB:] = p.astype(bf16)
            ds_ref[rows, PB:] = (p * (dp_ref[rows, PB:] - delta[:, PB:])).astype(bf16)
        each_near_own(collect)
        ds = ds_ref[:own, PB:]
        keep(dv_ref, cont, dot_nn(p_ref[:own, PB:], grads))
        keep(dk_ref, cont, dot_nn(ds, queries))
        dq_ref[features, PB:] += dot_nn(keys.T[half * 64 : half * 64 + 64, :], ds)

    home = pl.ds(pl.multiple_of(start, PB), PB)
    for q in range(quads):
        for copy in slab_loads(q):
            copy.wait()
        if q + 1 < quads:
            for copy in slab_loads(q + 1):
                copy.start()
        for number in range(heads_per_quad):
            time = q * heads_per_quad + number
            for ahead, e in row_blocks[time * at_once : (time + 1) * at_once]:
                rows_copy(ahead, e).start()
            one_head(q, number)
        those = slice(q * 256, q * 256 + 256)
        wo_loads[q].wait()
        put(q, 1, dot_nn(nt_ref[...], dv_ref[...]))
        put(q, 2, dot_nn(nt_ref[...], dk_ref[...]))
        dq_low[...] = dq_ref[...].T.astype(bf16)
        put(
            q, 3,
            dot_nn(nt_ref[:, home], dq_low[:PB]) + dot_nn(nt_ref[:, plen:], dq_low[PB:]),
        )

        def normed_grad(cols, q=q, those=those):
            grad = dot_nt(dk_ref[...], wk_ref[cols, those]) + dot_nt(dv_ref[...], wv_ref[cols, those])
            if q == 0:
                grad_ref[:, cols] = grad
            else:
                grad_ref[:, cols] += grad
            grad = dot_nt(dq_low[...], wq_ref[cols, those])
            grad_ref[home, cols] += grad[:PB]
            grad_ref[plen:, cols] += grad[PB:]

        columns(normed_grad)

    shared_out[...] = grad_ref[:plen, :].astype(bf16).reshape(ctx_count, PB, width)
    local_out[:PB, :] = grad_ref[home, :]
    local_out[PB:, :] = grad_ref[plen:, :]

    def gain_part(cols):
        gain_sum[:, cols] = jnp.sum(grad_ref[:, cols] * normed_ref[:, cols].astype(f32), axis=0, keepdims=True)

    columns(gain_part)
    own_result.wait()
    await_blocks(result_hbm, result_recv, result_sems, True, True)
    each_row_block(lambda copy: copy.wait())


def tail_kernel(
    experts, plan,
    parts_ref, shared_hbm, local_hbm, gain_sum_ref, hist_ref, gain_ref, moe_gain_ref, router_part_hbm, x_hbm,
    hidden_grad_hbm, hidden_hbm, slot_row, result_hbm, rows_hbm, rows_all, cot_hbm, win_hbm, wout_hbm, router_ref,
    full_ref, small_out, input_out, in_out, out_out, layer_out,
    local_ref, shared_recv, acc_refs, recv_refs, small_ref, small_recv,
    block_ref, win_ref, wout_ref, rows_ref, cot_ref, rows_t,
    load_sems, sems, small_sems, shared_sems,
):
    group, pieces, lengths = plan
    flows = mesh_axes()
    ctx_count, dp_count = lax.axis_size("ctx"), lax.axis_size("dp")
    tokens, width = x_hbm.shape
    count, me = owners()
    lines, columns_dp = Axis("ctx", ctx_count), Axis("dp", dp_count)
    whole_axes = [Axis("expert", lax.axis_size("expert")), columns_dp, lines]
    gain = gain_ref[...].astype(f32)

    slice_width = win_ref.shape[1]
    part = pl.ds(pl.multiple_of(lax.axis_index("dp") * slice_width, slice_width), slice_width)
    weight_loads = [
        pltpu.make_async_copy(win_hbm.at[:, part], win_ref, load_sems.at[0]),
        pltpu.make_async_copy(wout_hbm.at[part], wout_ref, load_sems.at[1]),
    ]
    router_load = pltpu.make_async_copy(
        router_part_hbm.at[pl.ds(0, experts)], small_ref.at[pl.ds(0, experts)], load_sems.at[7 + 2 * dp_count]
    )
    local_loads = [pltpu.make_async_copy(local_hbm, local_ref, load_sems.at[8 + 2 * dp_count])]
    for copy in [router_load, *weight_loads, *local_loads]:
        copy.start()

    barrier = pltpu.get_barrier_semaphore()

    def greet(ahead, _):
        pl.semaphore_signal(
            barrier, inc=1, device_id=owner_device(lax.rem(me + ahead, count)),
            device_id_type=pl.DeviceIdType.MESH,
        )
        return 0

    lax.fori_loop(1, count, greet, 0)
    for ahead in range(1, dp_count):
        pl.semaphore_signal(
            barrier, inc=1, device_id=columns_dp.peer(ahead), device_id_type=pl.DeviceIdType.MESH
        )
    pl.semaphore_wait(barrier, count - 1 + dp_count - 1)

    slots_of = {}

    def slot(*key):
        return slots_of.setdefault(key, len(slots_of))

    started = []

    def reduce_start(j, s):
        axis, length = flows[j % 2][s], lengths[s]
        copies = []
        for ahead in range(1, axis.size):
            target = axis.at(ahead)
            cuts = cuts_of(length)
            size = length // cuts
            for cut in range(cuts):
                first = target * length + cut * size
                if s == 0:
                    source = parts_ref.at[pl.ds(j * group + first, size)]
                else:
                    source = acc_refs[s - 1].at[j, pl.ds(first, size)]
                there = recv_refs[s].at[j, ahead - 1, pl.ds(cut * size, size)]
                copies.append(push(source, there, sems, slot("r", j, s, ahead, cut), axis.peer(ahead)))
        started.extend(copies)
        return copies

    def base_of(j, s):
        base = j * group
        for t in range(s + 1):
            base = base + flows[j % 2][t].index * lengths[t]
        return base

    def reduce_finish(j, s, copies):
        axis, length = flows[j % 2][s], lengths[s]
        for copy in copies:
            copy.wait_recv()
        last = s == len(lengths) - 1

        size = 4 if length % 4 == 0 else 1

        def some(u, _):
            if s == 0:
                total = parts_ref[pl.ds(base_of(j, 0) + u * size, size)].astype(f32)
            else:
                total = acc_refs[s - 1][j, pl.ds(axis.index * length + u * size, size)].astype(f32)
            for ahead in range(1, axis.size):
                total = total + recv_refs[s][j, ahead - 1, pl.ds(u * size, size)].astype(f32)
            if last:
                full_ref[pl.ds(base_of(j, s) + u * size, size)] = total.astype(bf16)
            else:
                acc_refs[s][j, pl.ds(u * size, size)] = total.astype(bf16)
            return 0

        lax.fori_loop(0, length // size, some, 0)

    def spread_start(j, s):
        axis, length = flows[j % 2][s], lengths[s]
        cuts = cuts_of(length)
        size = length // cuts
        copies = []
        for ahead in range(1, axis.size):
            for cut in range(cuts):
                here = full_ref.at[pl.ds(base_of(j, s) + cut * size, size)]
                copies.append(push(here, here, sems, slot("s", j, s, ahead, cut), axis.peer(ahead)))
        started.extend(copies)
        return copies

    def small_slot(s, ahead):
        return sum(axis.size - 1 for axis in whole_axes[:s]) + ahead - 1

    def small_start(s):
        axis = whole_axes[s]
        copies = [
            push(small_ref, small_recv[s].at[ahead - 1], small_sems, small_slot(s, ahead), axis.peer(ahead))
            for ahead in range(1, axis.size)
        ]
        return copies

    def small_finish(s, copies):
        axis = whole_axes[s]
        for copy in copies:
            copy.wait()
        mine = small_ref[...]
        total = jnp.zeros_like(mine)
        for index in range(axis.size):
            piece = mine
            for ahead in range(1, axis.size):
                piece = jnp.where(axis.at(axis.size - ahead) == index, small_recv[s][ahead - 1], piece)
            total = total + piece
        if s == len(whole_axes) - 1:
            small_out[...] = total
        else:
            small_ref[...] = total

    stages = len(lengths)
    begin = [j // 2 for j in range(pieces)]
    pending = {}

    def advance(time):
        for j in sorted(range(pieces), key=lambda j: begin[j]):
            s = time - begin[j]
            if not 0 <= s < 2 * stages:
                continue
            if s < stages:
                reduce_finish(j, s, pending[j, s])
                if s + 1 < stages:
                    pending[j, s + 1] = reduce_start(j, s + 1)
                else:
                    pending[j, s + 1] = spread_start(j, s)
            else:
                for copy in pending[j, s]:
                    copy.wait_recv()
                if s + 1 < 2 * stages:
                    pending[j, s + 1] = spread_start(j, 2 * stages - 1 - (s + 1))

    for j in range(pieces):
        pending[j, 0] = reduce_start(j, 0)

    shared_copies = []
    for i in range(ctx_count - 1):
        block = pl.ds(pl.multiple_of(lines.at(i + 1) * PB, PB), PB)
        size = PB // SHARED_CUTS
        shared_copies.append(
            [
                push(
                    shared_hbm.at[lines.at(i + 1), pl.ds(cut * size, size)], shared_recv.at[i, pl.ds(cut * size, size)],
                    shared_sems, i * SHARED_CUTS + cut, lines.peer(i + 1),
                )
                for cut in range(SHARED_CUTS)
            ]
        )
        started.extend(shared_copies[-1])

    small_ref[experts:, :] = jnp.zeros((small_ref.shape[0] - experts, width), f32)
    small_ref[experts : experts + 1, :] = gain_sum_ref[...] / gain
    small_ref[experts + 1 : experts + 2, :] = moe_gain_ref[...]
    router_load.wait()
    per_row = width // TILE
    for head in range(hist_ref.shape[0]):
        row, lane = 2 + experts + head // per_row, head % per_row * TILE
        small_ref[row : row + 1, lane : lane + TILE] = jnp.sum(hist_ref[head], axis=0, keepdims=True)
    small_pending = small_start(0)

    slots = rows_ref.shape[0]

    def grads_of(n, c):
        if c == 0:
            if n == 0:
                for copy in weight_loads:
                    copy.wait()
            source = rows_hbm if n == 0 else rows_all.at[n - 1]
            load = pltpu.make_async_copy(source, block_ref, load_sems.at[3 + 2 * n])
            load.start()
            load.wait()
            rows_ref[...] = block_ref[...].reshape(slots, width)
            cot_from = columns_dp.at(dp_count - n)
            load = pltpu.make_async_copy(cot_hbm.at[cot_from], block_ref, load_sems.at[4 + 2 * n])
            load.start()
            lane = lax.broadcasted_iota(jnp.int32, (slots, TILE), 1)
            probs = router_probs(dot_nn(rows_ref[...], router_ref[...]), lane, experts)
            gate = jnp.sum(jnp.where(lane == me, probs, 0.0), axis=1, keepdims=True)
            load.wait()
            cot = block_ref[...].reshape(slots, width)
            cot_ref[...] = (gate * cot.astype(f32)).astype(bf16)
            rows_t[...] = rows_ref[...].T
        cols = slice(c * 256, c * 256 + 256)
        act, slope = gelu_parts(dot_nn(rows_ref[...], win_ref[:, cols]))
        pre_grad = (dot_nt(cot_ref[...], wout_ref[cols, :]) * slope).astype(bf16)
        out_part = dot_tn(act.astype(bf16), cot_ref[...])
        in_part = dot_nn(rows_t[...], pre_grad)
        if n == 0:
            out_out[cols, :] = out_part
            in_out[:, cols] = in_part
        else:
            out_out[cols, :] += out_part
            in_out[:, cols] += in_part

    def input_back():
        held = pltpu.make_async_copy(hidden_grad_hbm, input_out, load_sems.at[3 + 2 * dp_count])
        held.start()
        x_load = pltpu.make_async_copy(x_hbm, rows_ref.at[pl.ds(0, tokens)], load_sems.at[6 + 2 * dp_count])
        x_load.start()
        for copies in shared_copies:
            for copy in copies:
                copy.wait_recv()
        held.wait()
        x_load.wait()
        for copy in local_loads:
            copy.wait()
        for first, shared_rows in ((0, True), (PB, False)):
            rows = slice(first, PB if shared_rows else tokens)
            x = rows_ref[rows, :].astype(f32)
            inverse = inverse_rms(x)
            grad = local_ref[rows, :]
            if shared_rows:
                for n in range(ctx_count - 1):
                    grad = grad + shared_recv[n].astype(f32)
            through = grad * gain
            scaled = x * inverse
            shared = jnp.mean(through * scaled, axis=1, keepdims=True)
            input_out[rows, :] += inverse * (through - scaled * shared)

    def layer():
        held = pltpu.make_async_copy(hidden_hbm, input_out, load_sems.at[4 + 2 * dp_count])
        held.start()
        load = pltpu.make_async_copy(result_hbm, block_ref, load_sems.at[2])
        load.start()
        load.wait()
        place = place_rows(slot_row[...], 0, slots, tokens)
        returned = dot_tn(place, block_ref[...].reshape(slots, width))
        held.wait()
        layer_out[...] = (input_out[...] + returned).astype(bf16)

    work = [layer]
    work += [functools.partial(grads_of, n, c) for n in range(dp_count) for c in range(slice_width // 256)]
    work += [input_back]
    first_step, last_step = 0, max(begin) + 2 * stages
    for time in range(first_step, last_step):
        advance(time)
        s = time - first_step
        if s < len(whole_axes):
            small_finish(s, small_pending)
            if s + 1 < len(whole_axes):
                small_pending = small_start(s + 1)
        for _ in range(-(-len(work) // (last_step - time))):
            work.pop(0)()
    for copy in started:
        copy.wait_send()


def finish_kernel(full_ref, in_ref, out_ref, input_ref, layer_ref, *results):
    weights, rest = results[:4], results[4:]
    columns = full_ref.shape[-1]
    for n, weight in enumerate(weights):
        for q in range(full_ref.shape[0]):
            there = slice(q * columns, (q + 1) * columns)
            weight[:, there] = full_ref[q, n].astype(f32).reshape(weight.shape[0], columns)
    for source, target in zip((in_ref, out_ref, input_ref, layer_ref), rest):
        target[...] = source[...]


def tail_plan(sizes, width, quads):
    devices = 1
    for size in sizes:
        devices *= size
    units = 4 * width // 16
    if quads == 1:
        group, pieces = devices, -(-units // devices)
    else:
        cuts = 2 if units % (2 * devices) == 0 else 1
        group, pieces = -(-units // (cuts * devices)) * devices, cuts * quads
    lengths, left = [], group
    for size in sizes:
        left //= size
        lengths.append(left)
    return group, pieces, lengths


def body(
    inputs, cotangent, route, arrival, branch, attn_gain, query_weight, key_weight, value_weight,
    output_weight, rel_table, moe_gain, router_weight, expert_in, expert_out,
):
    x = inputs[0]
    cot = cotangent[0]
    tokens, width = x.shape
    own = tokens - PB
    buckets, heads = rel_table.shape
    experts = router_weight.shape[1]
    capacity = 9 * tokens // (8 * experts)
    block_rows = capacity if capacity % 8 == 0 else -(-capacity // 16) * 16
    slots = experts * block_rows
    ctx_count = lax.axis_size("ctx")
    dp_count = lax.axis_size("dp")
    plen = PB * ctx_count
    keys_total = plen + own
    hidden_units = expert_in.shape[2]
    pairs = width // TILE
    attn_gain_row = attn_gain.reshape(1, width)
    moe_gain_row = moe_gain.reshape(1, width)
    onehot = bucket_onehot(buckets)
    by_distance = jnp.dot(onehot, rel_table.astype(f32), precision=lax.Precision.HIGHEST).T
    by_distance = by_distance - by_distance[:, TILE - 1 :]
    bias = jnp.pad(by_distance.reshape(pairs, 2, TILE), ((0, 0), (0, 6), (0, 0)))
    router_wide = jnp.pad(router_weight, ((0, 0), (0, TILE - experts)))
    route_row = route.reshape(1, tokens)
    arrive_row = arrival[0]
    blocks = shape((experts, block_rows, width), bf16)
    block_space = pltpu.VMEM((experts, block_rows, width), bf16)
    block_sems = pltpu.SemaphoreType.DMA((2, experts - 1))
    any_space = pl.BlockSpec(memory_space=pl.ANY)

    slot_row, cot_sent, normed_own, normed_all, queries, keys, values, att, lse = pl.pallas_call(
        functools.partial(front_kernel, capacity),
        out_shape=[
            shape((1, tokens), jnp.int32),
            blocks,
            shape((tokens, width), bf16),
            shape((plen, width), bf16),
            shape((tokens, width), bf16),
            shape((keys_total, width), bf16),
            shape((keys_total, width), bf16),
            shape((width, tokens), bf16),
            shape((pairs, 8, tokens), f32),
        ],
        in_specs=[smem()] + [vmem()] * 9,
        out_specs=[vmem()] * 9,
        scratch_shapes=[
            pltpu.VMEM((ctx_count, PB, width), bf16),
            block_space,
            pltpu.VMEM((keys_total, tokens), f32),
            pltpu.VMEM((keys_total, tokens), bf16),
            pltpu.SemaphoreType.DMA((2, 2, ctx_count - 1, CHUNKS)),
            block_sems,
        ],
        compiler_params=remote_params(1),
        cost_estimate=cost(40 * keys_total * tokens * width, 20 * width * width),
        name="front",
    )(
        branch, bias, x, cot, attn_gain_row, route_row, arrive_row,
        query_weight, key_weight, value_weight,
    )
    cot_all = lax.all_gather(cot_sent, "dp", axis=0, tiled=False)

    by_heads = ctx_count <= 4
    quads = width // 256 if by_heads else 1
    members = 2 * lax.axis_size("expert") if ctx_count % 2 == 0 else experts
    group_rows = members * block_rows
    (
        rows_sent, router_part, hidden_grad, wo_part, att_grad, delta, moe_gain_part,
        result, hidden,
    ) = pl.pallas_call(
        functools.partial(expert_kernel, experts),
        out_shape=[
            blocks, shape((TILE, width), f32), shape((tokens, width), f32), shape((quads, width // 16, 16, width // quads), bf16),
            shape((tokens, width), bf16), shape((pairs, 8, tokens), f32), shape((1, width), f32),
            blocks, shape((tokens, width), f32),
        ],
        in_specs=[vmem()] * 8 + [any_space] * 2,
        out_specs=[vmem()] * 9,
        scratch_shapes=[
            pltpu.VMEM((tokens, width), bf16),
            block_space,
            pltpu.VMEM((width, hidden_units), bf16),
            pltpu.VMEM((hidden_units, width), bf16),
            pltpu.VMEM((group_rows, width), bf16),
            pltpu.VMEM((group_rows, width), bf16),
            pltpu.VMEM((group_rows, width), f32),
            pltpu.VMEM((group_rows, width), f32),
            block_space, block_space,
            pltpu.VMEM((tokens, width), bf16),
            pltpu.VMEM((width, tokens), bf16),
            block_sems, block_sems,
            pltpu.SemaphoreType.DMA((2,)),
        ],
        compiler_params=remote_params(2),
        cost_estimate=cost(8 * slots * width * hidden_units, 12 * width * hidden_units),
        name="expert",
    )(
        att, x, output_weight, moe_gain_row, router_wide, slot_row, cot, cot_sent,
        expert_in[0], expert_out[0],
    )
    att_grad, cot_all = lax.optimization_barrier((att_grad, cot_all))

    expert_count = lax.axis_size("expert")
    dp_sizes = [2, 2] if dp_count == 4 else [dp_count]
    sizes = [expert_count, *dp_sizes, ctx_count]
    plan = tail_plan(sizes, width, quads)
    group, pieces, lengths = plan
    units = group * pieces

    table_rows = heads * TILE // width
    small_rows = -(-(2 + experts + table_rows) // 8) * 8
    slice_width = hidden_units // dp_count
    if by_heads:
        (
            weight_parts, shared_part, local_grad, gain_part, hist, result_back, rows_all,
        ) = pl.pallas_call(
            head_kernel,
            out_shape=[
                shape((units, 16, width // quads), bf16), shape((ctx_count, PB, width), bf16),
                shape((tokens, width), f32), shape((1, width), f32), shape((heads, 8, TILE), f32),
                blocks, shape((dp_count - 1, experts, block_rows, width), bf16),
            ],
            in_specs=[
                smem(), vmem(), vmem(), any_space, any_space, vmem(), vmem(), vmem(), any_space, any_space,
                vmem(), vmem(), vmem(), any_space, any_space, any_space,
            ],
            out_specs=[vmem()] * 6 + [any_space],
            scratch_shapes=[
                pltpu.VMEM((2, keys_total, 256), bf16),
                pltpu.VMEM((2, keys_total, 256), bf16),
                pltpu.VMEM((keys_total, width), bf16),
                pltpu.VMEM((width, keys_total), bf16),
                pltpu.VMEM((plen, tokens), f32),
                pltpu.VMEM((plen, tokens), f32),
                pltpu.VMEM((plen, tokens), bf16),
                pltpu.VMEM((plen, tokens), bf16),
                pltpu.VMEM((256, tokens), f32),
                pltpu.VMEM((keys_total, 256), bf16),
                pltpu.VMEM((keys_total, 256), bf16),
                pltpu.VMEM((1 + plen // TILE, TILE, TILE), jnp.int32),
                pltpu.VMEM((2, TILE, TILE), jnp.int32),
                pltpu.VMEM((keys_total, width), f32),
                pltpu.VMEM((tokens, 256), bf16),
                pltpu.SemaphoreType.DMA((quads, 2)),
                pltpu.SemaphoreType.DMA((3 + quads,)),
                block_sems,
                pltpu.SemaphoreType.DMA((2, dp_count - 1, experts)),
            ],
            compiler_params=remote_params(3),
            cost_estimate=cost(80 * keys_total * tokens * width, 40 * width * width),
            name="attend_back",
        )(
            branch, bias, queries, keys, values, att_grad, lse, delta, normed_all, normed_own,
            query_weight, key_weight, value_weight, wo_part, result, rows_sent,
        )
        weights, small, input_grad, in_grad, out_grad, layer_out = pl.pallas_call(
            functools.partial(tail_kernel, experts, plan),
            out_shape=[
                shape((units, 16, width // quads), bf16), shape((small_rows, width), f32),
                shape((tokens, width), f32), shape((width, slice_width), f32),
                shape((slice_width, width), f32), shape((tokens, width), bf16),
            ],
            in_specs=[
                vmem(), any_space, any_space, vmem(), vmem(), vmem(), vmem(), any_space, any_space,
                any_space, any_space, vmem(), any_space, any_space, any_space, any_space, any_space, any_space, vmem(),
            ],
            out_specs=[vmem()] * 6,
            scratch_shapes=[
                pltpu.VMEM((tokens, width), f32),
                pltpu.VMEM((ctx_count - 1, PB, width), bf16),
                [pltpu.VMEM((pieces, length, 16, width // quads), bf16) for length in lengths[:-1]],
                [
                    pltpu.VMEM((pieces, size - 1, length, 16, width // quads), bf16)
                    for size, length in zip(sizes, lengths)
                ],
                pltpu.VMEM((small_rows, width), f32),
                [
                    pltpu.VMEM((size - 1, small_rows, width), f32)
                    for size in (expert_count, dp_count, ctx_count)
                ],
                block_space,
                pltpu.VMEM((width, slice_width), bf16),
                pltpu.VMEM((slice_width, width), bf16),
                pltpu.VMEM((slots, width), bf16),
                pltpu.VMEM((slots, width), bf16),
                pltpu.VMEM((width, slots), bf16),
                pltpu.SemaphoreType.DMA((9 + 2 * dp_count,)),
                pltpu.SemaphoreType.DMA(
                    (2, 2 * pieces * sum((n - 1) * cuts_of(length) for n, length in zip(sizes, lengths)))
                ),
                pltpu.SemaphoreType.DMA((2, expert_count + dp_count + ctx_count - 3)),
                pltpu.SemaphoreType.DMA((2, (ctx_count - 1) * SHARED_CUTS)),
            ],
            compiler_params=remote_params(0),
            cost_estimate=cost(8 * dp_count * slots * width * slice_width, 60 * width * slice_width),
            name="tail",
        )(
            weight_parts, shared_part, local_grad, gain_part, hist, attn_gain_row, moe_gain_part, router_part, x,
            hidden_grad, hidden, slot_row, result_back, rows_sent, rows_all, cot_all,
            expert_in[0], expert_out[0], router_wide,
        )
    else:
        block_scratch = [
            pltpu.VMEM((2, PB, width), bf16),
            pltpu.VMEM((2, PB, width), bf16),
            pltpu.VMEM((2, PB, width), bf16),
            pltpu.VMEM((PB, tokens), f32),
            pltpu.VMEM((PB, tokens), f32),
            pltpu.VMEM((PB, tokens), bf16),
            pltpu.VMEM((PB, tokens), bf16),
            pltpu.VMEM((width, tokens), f32),
            pltpu.VMEM((PB, width), bf16),
            pltpu.VMEM((PB, width), bf16),
            pltpu.VMEM((heads, 8, TILE), f32),
            pltpu.VMEM((1, width), f32),
            pltpu.VMEM((tokens, width), f32),
            pltpu.VMEM((min(ctx_count - 1, 16 // ctx_count), PB, width), bf16),
            pltpu.VMEM((ctx_count - 1, PB, width), bf16),
            pltpu.VMEM((units, 16, width), bf16),
            [pltpu.VMEM((pieces, length, 16, width), bf16) for length in lengths[:-1]],
            [
                pltpu.VMEM((pieces, size - 1, length, 16, width), bf16)
                for size, length in zip(sizes, lengths)
            ],
            pltpu.VMEM((small_rows, width), f32),
            [pltpu.VMEM((size - 1, small_rows, width), f32) for size in (expert_count, dp_count, ctx_count)],
            block_space,
            pltpu.VMEM((width, slice_width), bf16),
            pltpu.VMEM((slice_width, width), bf16),
            pltpu.VMEM((slots, width), bf16),
            pltpu.VMEM((slots, width), bf16),
            pltpu.VMEM((width, slots), bf16),
            pltpu.SemaphoreType.DMA((ctx_count + 1, 3)),
            pltpu.SemaphoreType.DMA((8 + 2 * dp_count,)),
            pltpu.SemaphoreType.DMA(
                (2, 2 * pieces * sum((n - 1) * cuts_of(length) for n, length in zip(sizes, lengths)))
            ),
            pltpu.SemaphoreType.DMA((2, expert_count + dp_count + ctx_count - 3)),
            pltpu.SemaphoreType.DMA((2, (ctx_count - 1) * SHARED_CUTS)),
            block_sems,
            pltpu.SemaphoreType.DMA((2, dp_count - 1, experts)),
        ]
        weights, small, input_grad, in_grad, out_grad, layer_out, _ = pl.pallas_call(
            functools.partial(back_kernel, experts, plan),
            out_shape=[
                shape((units, 16, width // quads), bf16), shape((small_rows, width), f32), shape((tokens, width), f32),
                shape((width, slice_width), f32), shape((slice_width, width), f32), shape((tokens, width), bf16),
                shape((dp_count - 1, experts, block_rows, width), bf16),
            ],
            in_specs=[
                smem(), vmem(), vmem(), any_space, any_space, vmem(), vmem(), vmem(), any_space, vmem(),
                vmem(), vmem(), vmem(), vmem(), any_space, vmem(), any_space, any_space, any_space,
                any_space, vmem(), any_space, any_space, any_space, any_space, any_space, vmem(),
            ],
            out_specs=[vmem()] * 6 + [any_space],
            scratch_shapes=block_scratch,
            compiler_params=remote_params(0),
            cost_estimate=cost(
                8 * dp_count * slots * width * slice_width + 80 * keys_total * tokens * width,
                60 * width * slice_width,
            ),
            name="back",
        )(
            branch, bias, queries, keys, values, att_grad, lse, delta, normed_all, normed_own,
            attn_gain_row, query_weight, key_weight, value_weight, wo_part, moe_gain_part, router_part, x,
            hidden_grad, hidden, slot_row, result,
            rows_sent, cot_all, expert_in[0], expert_out[0], router_wide,
        )

    matrix_units = width // 16
    steps = 4

    def part_rows(rows, columns=width):
        return pl.BlockSpec((rows // steps, columns), lambda i: (i, 0))

    weights = weights.reshape(quads, units // quads, 16, width // quads)
    weights = weights[:, : 4 * matrix_units].reshape(quads, 4, matrix_units, 16, width // quads)
    *weights, in_grad, out_grad, input_grad, layer_out = pl.pallas_call(
        finish_kernel,
        grid=(steps,),
        out_shape=[shape((width, width), f32)] * 4
        + [
            shape((width, slice_width), f32), shape((slice_width, width), f32),
            shape((tokens, width), f32), shape((tokens, width), bf16),
        ],
        in_specs=[
            pl.BlockSpec(
                (quads, 4, matrix_units // steps, 16, width // quads), lambda i: (0, 0, i, 0, 0)
            ),
            part_rows(width, slice_width), part_rows(slice_width), part_rows(tokens), part_rows(tokens),
        ],
        out_specs=[part_rows(width)] * 4
        + [part_rows(width, slice_width), part_rows(slice_width), part_rows(tokens), part_rows(tokens)],
        compiler_params=params(),
        cost_estimate=cost(8 * width * width, 48 * width * width),
        name="finish",
    )(weights, in_grad, out_grad, input_grad, layer_out)
    router_grad = small[:experts].T
    hist_sum = small[2 + experts : 2 + experts + table_rows].reshape(heads, TILE)
    last = onehot[:, buckets - 1 :]
    spread = jnp.concatenate([onehot[:, : buckets - 1], last - 1.0], axis=1)
    table_grad = jnp.dot(spread.T, hist_sum.T, precision=lax.Precision.HIGHEST)
    return (
        layer_out[None],
        input_grad[None],
        small[experts],
        weights[3],
        weights[2],
        weights[1],
        weights[0],
        table_grad,
        small[experts + 1],
        router_grad,
        in_grad[None],
        out_grad[None],
    )


def solution(mesh):
    grouped = P(("dp", "expert"), "ctx", None)
    placed = (
        grouped, grouped, grouped, grouped, P(("dp", "expert"), "ctx"),
        P(), P(), P(), P(), P(), P(), P(), P(),
        P(("ctx", "expert"), None, None),
        P(("ctx", "expert"), None, None),
    )
    return jax.shard_map(
        body,
        mesh=mesh,
        in_specs=placed,
        out_specs=(
            grouped, grouped, P(), P(), P(), P(), P(), P(), P(), P(),
            P(("ctx", "expert"), None, "dp"),
            P(("ctx", "expert"), "dp", None),
        ),
        check_vma=False,
    )
```

```python
import functools

import jax
import jax.numpy as jnp
from jax import lax
from jax.experimental import pallas as pl
from jax.experimental.pallas import tpu as pltpu
from jax.sharding import PartitionSpec as P

PB = 256
TILE = 128
CHUNKS = 2

bucket_edges = (19, 21, 24, 27, 31, 35, 40, 46, 52, 59, 67, 77, 87, 99, 113)
norm_eps = 1e-06
masked_score = -1e30
gelu_scale = 0.7978845608
gelu_cube = 0.044715

bf16 = jnp.bfloat16
f32 = jnp.float32
VMEM_LIMIT = 121 * 512 * 1024


def dot_nn(a, b):
    return jnp.dot(a, b, preferred_element_type=f32)


def dot_nt(a, b):
    return lax.dot_general(a, b, (((1,), (1,)), ((), ())), preferred_element_type=f32)


def dot_tn(a, b):
    return lax.dot_general(a, b, (((0,), (0,)), ((), ())), preferred_element_type=f32)


def two_parts(a):
    high = a.astype(bf16)
    return high, (a - high.astype(f32)).astype(bf16)


def vmem():
    return pl.BlockSpec(memory_space=pltpu.VMEM)


def smem():
    return pl.BlockSpec(memory_space=pltpu.SMEM)


def params():
    return pltpu.CompilerParams(vmem_limit_bytes=VMEM_LIMIT)


def remote_params(number):
    return pltpu.CompilerParams(
        vmem_limit_bytes=VMEM_LIMIT, collective_id=number, has_side_effects=True
    )


def cost(flops, nbytes):
    return pl.CostEstimate(flops=int(flops), bytes_accessed=int(nbytes), transcendentals=0)


def shape(dims, kind):
    return jax.ShapeDtypeStruct(dims, kind)


def inverse_rms(x):
    return lax.rsqrt(jnp.mean(x * x, axis=-1, keepdims=True) + norm_eps)


def bucket_onehot(buckets):
    distance = jnp.arange(TILE, dtype=jnp.int32)
    ids = jnp.minimum(distance, 16)
    for edge in bucket_edges:
        ids = ids + (distance >= edge).astype(jnp.int32)
    return (ids[:, None] == jnp.arange(buckets, dtype=jnp.int32)[None, :]).astype(f32)


def near_index(first):
    rows = lax.broadcasted_iota(jnp.int32, (TILE, TILE), 0)
    lanes = lax.broadcasted_iota(jnp.int32, (TILE, TILE), 1)
    return first + lanes - rows


def near_tiles(ctx_at, plen):
    start = ctx_at * PB
    return (
        (start, 0, 0, False),
        (start, TILE, TILE, False),
        (start + TILE, TILE, 0, False),
        (plen, PB, 0, False),
        (plen, PB + TILE, TILE, False),
        (plen + TILE, PB + TILE, 0, False),
        (plen + PB, PB, TILE, False),
        (start - TILE, 0, TILE, True),
    )


def add_near(s_ref, bias_row, ctx_at, plen):
    source = jnp.broadcast_to(bias_row, (TILE, TILE))
    add_tiles(s_ref, source, ctx_at, near_tiles(ctx_at, plen))


def add_tiles(s_ref, source, ctx_at, tiles):
    for first_row, first_lane, gap, guarded in tiles:
        def work(first_row=first_row, first_lane=first_lane, gap=gap):
            rows = pl.ds(first_row if isinstance(first_row, int) else pl.multiple_of(first_row, 16), TILE)
            lanes = slice(first_lane, first_lane + TILE)
            index = jnp.clip(near_index(gap), 0, TILE - 1)
            s_ref[rows, lanes] = s_ref[rows, lanes] + jnp.take_along_axis(source, index, axis=1)

        if guarded:
            pl.when(ctx_at > 0)(work)
        else:
            work()


def scores_to(s_ref, keys, queries, plen):
    s_ref[:plen, :] = dot_nt(keys[:plen], queries)
    s_ref[plen:, PB:] = dot_nt(keys[plen:], queries[PB:])


def limits(ctx_at, branch, tokens):
    lane = lax.broadcasted_iota(jnp.int32, (1, tokens), 1)
    return jnp.where(lane < PB, ctx_at * PB + lane + 1, branch - TILE)


def window_rows(first, count, branch):
    rows = lax.broadcasted_iota(jnp.int32, (TILE, count), 0)
    places = lax.broadcasted_iota(jnp.int32, (TILE, count), 1) + first
    return (places == rows + (branch - TILE)).astype(bf16)


def row_steps(first, count, lanes):
    return first + lax.broadcasted_iota(jnp.int32, (count, lanes), 0)


def own_allowed(first, count, lanes):
    return row_steps(first, count, lanes) <= lax.broadcasted_iota(jnp.int32, (count, lanes), 1)


def head_lanes(half):
    return lax.broadcasted_iota(jnp.int32, (1, TILE), 1) // (TILE // 2) == half


def pick_rows(pieces, lanes):
    row = lax.broadcasted_iota(jnp.int32, (8, lanes), 0)
    return jnp.where(row == 0, pieces[0], jnp.where(row == 1, pieces[1], 0.0))


def fold8(x, op):
    return op(x.reshape(x.shape[0] // 8, 8, x.shape[1]), axis=0)


def owner_device(index):
    cores = lax.axis_size("expert")
    return {"ctx": index // cores, "expert": lax.rem(index, cores)}


def owners():
    cores = lax.axis_size("expert")
    count = cores * lax.axis_size("ctx")
    return count, lax.axis_index("ctx") * cores + lax.axis_index("expert")


def greet_owners():
    count, me = owners()
    barrier = pltpu.get_barrier_semaphore()

    def greet(ahead, _):
        pl.semaphore_signal(
            barrier, inc=1, device_id=owner_device(lax.rem(me + ahead, count)),
            device_id_type=pl.DeviceIdType.MESH,
        )
        return 0

    lax.fori_loop(1, count, greet, 0)
    pl.semaphore_wait(barrier, count - 1)


def block_copy(source, target, sems, ahead):
    count, me = owners()
    peer = lax.rem(me + ahead, count)
    return pltpu.make_async_remote_copy(
        src_ref=source.at[peer], dst_ref=target.at[me],
        send_sem=sems.at[0, ahead - 1], recv_sem=sems.at[1, ahead - 1],
        device_id=owner_device(peer), device_id_type=pl.DeviceIdType.MESH,
    )


def await_blocks(source, target, sems, sent, received):
    def one(ahead, _):
        copy = block_copy(source, target, sems, ahead)
        if received:
            copy.wait_recv()
        if sent:
            copy.wait_send()
        return 0

    lax.fori_loop(1, owners()[0], one, 0)


def place_rows(slot_row, index, block_rows, tokens):
    rows = lax.broadcasted_iota(jnp.int32, (block_rows, tokens), 0) + index * block_rows
    return (rows == slot_row).astype(bf16)


def front_kernel(
    capacity,
    branch_ref, bias_ref, x_ref, cot_ref, gain_ref, route_row, arrive_row,
    wq_ref, wk_ref, wv_ref,
    slot_out, cot_out, normed_own_out, normed_out, q_ref, k_out, v_out, att_out, lse_out,
    prompt_ref, send_ref, s_ref, p_ref, prompt_sems, cot_sems,
):
    branch = branch_ref[0, 0]
    ctx_at, ctx_count = lax.axis_index("ctx"), lax.axis_size("ctx")
    plen = PB * ctx_count
    tokens, width = x_ref.shape
    own = tokens - PB
    gain = gain_ref[...].astype(f32)
    count, me = owners()
    block_rows = send_ref.shape[1]
    greet_owners()

    chunk = PB // CHUNKS

    def pass_on(step, up, c):
        block = ctx_at - step if up else ctx_at + step
        ahead = ctx_at + 1 if up else ctx_at - 1
        fits = (block >= 0) & (ahead < ctx_count) if up else (block < ctx_count) & (ahead >= 0)
        piece = pl.ds(c * chunk, chunk)
        source = x_ref.at[piece] if step == 0 else prompt_ref.at[block, piece]
        copy = pltpu.make_async_remote_copy(
            src_ref=source, dst_ref=prompt_ref.at[block, piece],
            send_sem=prompt_sems.at[0, int(up), step, c], recv_sem=prompt_sems.at[1, int(up), step, c],
            device_id={"ctx": ahead}, device_id_type=pl.DeviceIdType.MESH,
        )
        return fits, copy

    def arrival(step, up, c):
        block = ctx_at - step - 1 if up else ctx_at + step + 1
        fits = block >= 0 if up else block < ctx_count
        place = prompt_ref.at[block, pl.ds(c * chunk, chunk)]
        copy = pltpu.make_async_remote_copy(
            src_ref=place, dst_ref=place,
            send_sem=prompt_sems.at[0, int(up), step, c], recv_sem=prompt_sems.at[1, int(up), step, c],
            device_id={"ctx": ctx_at}, device_id_type=pl.DeviceIdType.MESH,
        )
        return fits, block, copy

    for c in range(CHUNKS):
        for up in (True, False):
            fits, copy = pass_on(0, up, c)
            pl.when(fits)(copy.start)

    x = x_ref[...].astype(f32)
    normed_own_out[...] = (x * inverse_rms(x) * gain).astype(bf16)

    def column(i, _):
        cols = pl.ds(pl.multiple_of(i * 256, 256), 256)
        q_ref[:, cols] = dot_nn(normed_own_out[...], wq_ref[:, cols]).astype(bf16)
        k_out[plen : plen + own, cols] = dot_nn(normed_own_out[PB:, :], wk_ref[:, cols]).astype(bf16)
        v_out[plen : plen + own, cols] = dot_nn(normed_own_out[PB:, :], wv_ref[:, cols]).astype(bf16)
        return 0

    lax.fori_loop(0, width // 256, column, 0)

    def project(block):
        rows = pl.ds(pl.multiple_of(block * PB, PB), PB)

        def prompt_column(i, _):
            cols = pl.ds(pl.multiple_of(i * 256, 256), 256)
            k_out[rows, cols] = dot_nn(normed_out[rows, :], wk_ref[:, cols]).astype(bf16)
            v_out[rows, cols] = dot_nn(normed_out[rows, :], wv_ref[:, cols]).astype(bf16)
            return 0

        lax.fori_loop(0, width // 256, prompt_column, 0)

    def take(block):
        x = prompt_ref[block].astype(f32)
        rows = pl.ds(pl.multiple_of(block * PB, PB), PB)
        normed_out[rows, :] = (x * inverse_rms(x) * gain).astype(bf16)
        project(block)

    for step in range(ctx_count - 1):
        for c in range(CHUNKS):
            for up in (True, False):
                fits, block, copy = arrival(step, up, c)
                pl.when(fits)(copy.wait_recv)
                if step < ctx_count - 2:
                    fits, copy = pass_on(step + 1, up, c)
                    pl.when(fits)(copy.start)
        if step == 0:
            normed_out[pl.ds(pl.multiple_of(ctx_at * PB, PB), PB), :] = normed_own_out[:PB, :]
            project(ctx_at)
        for up in (True, False):
            fits, block, copy = arrival(step, up, 0)
            pl.when(fits)(functools.partial(take, block))

    def down(row):
        column = jnp.broadcast_to(row[...].astype(f32), (TILE, tokens)).T
        return jnp.concatenate([column] * (tokens // TILE), axis=1)

    same = down(route_row) == route_row[...].astype(f32)
    earlier = down(arrive_row) < arrive_row[...].astype(f32)
    rank = jnp.sum(jnp.where(same & earlier, 1.0, 0.0), axis=0, keepdims=True).astype(jnp.int32)
    slot = jnp.where(rank < capacity, route_row[...] * block_rows + rank, count * block_rows)
    slot_out[...] = slot

    def send_cot(ahead, _):
        peer = lax.rem(me + ahead, count)
        place = place_rows(slot_out[...], peer, block_rows, tokens)
        send_ref[peer] = dot_nn(place, cot_ref[...]).astype(bf16)
        block_copy(send_ref, cot_out, cot_sems, ahead).start()
        return 0

    def send_cots():
        lax.fori_loop(1, count, send_cot, 0)
        cot_out[me] = dot_nn(place_rows(slot_out[...], me, block_rows, tokens), cot_ref[...]).astype(bf16)

    def window_column(i, _):
        cols = pl.ds(pl.multiple_of(i * 256, 256), 256)
        window = window_rows(0, plen, branch)
        k_out[plen + own :, cols] = dot_nn(window, k_out[:plen, cols]).astype(bf16)
        v_out[plen + own :, cols] = dot_nn(window, v_out[:plen, cols]).astype(bf16)
        return 0

    lax.fori_loop(0, width // 256, window_column, 0)
    p_ref[plen:, :PB] = jnp.zeros((own + TILE, PB), bf16)
    limit = limits(ctx_at, branch, tokens)

    def pair(g, _):
        pl.when(g == 1)(send_cots)
        lanes = pl.ds(pl.multiple_of(g * TILE, TILE), TILE)
        queries = q_ref[:, lanes]
        keys = k_out[:, lanes]
        values_t = v_out[:, lanes].T
        bias = bias_ref[g]
        lse_rows, att_rows = [], []
        for half in range(2):
            scores_to(s_ref, jnp.where(head_lanes(half), keys, jnp.zeros_like(keys)), queries, plen)
            add_near(s_ref, bias[half : half + 1, :], ctx_at, plen)

            def top_of(i, top):
                for part in range(0, TILE, 32):
                    first = pl.multiple_of(i * TILE + part, 32)
                    rows = pl.ds(first, 32)
                    s = jnp.where(row_steps(first, 32, tokens) < limit, s_ref[rows, :], masked_score)
                    s_ref[rows, :] = s
                    top = jnp.maximum(top, fold8(s, jnp.max))
                return top

            top = lax.fori_loop(0, plen // TILE, top_of, jnp.full((8, tokens), masked_score, f32))
            own_top = jnp.full((8, own), masked_score, f32)
            for i in range(own // TILE + 1):
                rows = slice(plen + i * TILE, plen + (i + 1) * TILE)
                s = s_ref[rows, PB:]
                if i < own // TILE:
                    s = jnp.where(own_allowed(i * TILE, TILE, own), s, masked_score)
                    s_ref[rows, PB:] = s
                own_top = jnp.maximum(own_top, fold8(s, jnp.max))
            top = jnp.concatenate([top[:, :PB], jnp.maximum(top[:, PB:], own_top)], axis=1)
            top = jnp.max(top, axis=0, keepdims=True)

            def weigh(i, total):
                for part in range(0, TILE, 32):
                    rows = pl.ds(pl.multiple_of(i * TILE + part, 32), 32)
                    p = jnp.exp(s_ref[rows, :] - top)
                    p_ref[rows, :] = p.astype(bf16)
                    total = total + fold8(p, jnp.sum)
                return total

            total = lax.fori_loop(0, plen // TILE, weigh, jnp.zeros((8, tokens), f32))
            own_total = jnp.zeros((8, own), f32)
            for i in range(own // TILE + 1):
                rows = slice(plen + i * TILE, plen + (i + 1) * TILE)
                p = jnp.exp(s_ref[rows, PB:] - top[:, PB:])
                p_ref[rows, PB:] = p.astype(bf16)
                own_total = own_total + fold8(p, jnp.sum)
            total = jnp.concatenate([total[:, :PB], total[:, PB:] + own_total], axis=1)
            total = jnp.sum(total, axis=0, keepdims=True)
            rows = slice(half * 64, half * 64 + 64)
            att_rows.append((dot_nn(values_t[rows, :], p_ref[...]) / total).astype(bf16))
            lse_rows.append(top + jnp.log(total))
        att_out[lanes, :] = jnp.concatenate(att_rows, axis=0)
        lse_out[g] = pick_rows(lse_rows, tokens)
        return 0

    lax.fori_loop(0, width // TILE, pair, 0)
    await_blocks(send_ref, cot_out, cot_sems, True, True)
    for step in range(ctx_count - 1):
        for c in range(CHUNKS):
            for up in (True, False):
                fits, copy = pass_on(step, up, c)
                pl.when(fits)(copy.wait_send)


def router_probs(logits, lane, experts):
    logits = jnp.where(lane < experts, logits, masked_score)
    logits = jnp.exp(logits - jnp.max(logits, axis=1, keepdims=True))
    return logits / jnp.sum(logits, axis=1, keepdims=True)


def gelu_parts(v):
    t = jnp.tanh(gelu_scale * (v + gelu_cube * (v * v * v)))
    half = 0.5 * (1.0 + t)
    slope = half + 0.5 * v * (1.0 - t * t) * (gelu_scale + (3.0 * gelu_scale * gelu_cube) * (v * v))
    return v * half, slope


def expert_kernel(
    experts,
    att_ref, x_ref, wo_ref, gain_ref, router_ref, slot_row, cot_ref, cot_rows, win_hbm, wout_hbm,
    rows_out, router_out, hidden_grad_out, wo_grad_out, att_grad_out, delta_out, gain_grad_out,
    result_out, hidden_ref,
    moe_ref, send_ref, win_ref, wout_ref, group_rows, sent_ref, result_acc, grad_acc,
    grad_send, grad_recv, low_ref, att_t_ref, rows_sems, grad_sems, load_sems,
):
    tokens, width = x_ref.shape
    count, me = owners()
    block_rows = send_ref.shape[1]
    hidden_units = win_ref.shape[1]
    loads = [
        pltpu.make_async_copy(win_hbm, win_ref, load_sems.at[0]),
        pltpu.make_async_copy(wout_hbm, wout_ref, load_sems.at[1]),
    ]
    for copy in loads:
        copy.start()
    greet_owners()

    def column(i, _):
        cols = pl.ds(pl.multiple_of(i * 256, 256), 256)
        hidden_ref[:, cols] = x_ref[:, cols].astype(f32) + dot_tn(att_ref[...], wo_ref[:, cols])
        return 0

    lax.fori_loop(0, width // 256, column, 0)
    hidden = hidden_ref[...]
    moe_ref[...] = (hidden * inverse_rms(hidden) * gain_ref[...].astype(f32)).astype(bf16)

    members = 2 * lax.axis_size("expert") if lax.axis_size("ctx") % 2 == 0 else count
    groups = count // members
    my_group = me // members

    def send_rows(ahead, _):
        peer = lax.rem(me + ahead, count)
        place = place_rows(slot_row[...], peer, block_rows, tokens)
        send_ref[peer] = dot_nn(place, moe_ref[...]).astype(bf16)
        block_copy(send_ref, rows_out, rows_sems, ahead).start()
        return 0

    def send_group(g, _):
        base = lax.rem(my_group + g, groups) * members

        def member(i, _):
            ahead = lax.rem(base + i - me + count, count)
            pl.when(ahead > 0)(lambda: (send_rows(ahead, 0), None)[1])
            return 0

        return lax.fori_loop(0, members, member, 0)

    lax.fori_loop(0, groups, send_group, 0)
    rows_out[me] = dot_nn(place_rows(slot_row[...], me, block_rows, tokens), moe_ref[...]).astype(bf16)

    router_out[...] = jnp.zeros_like(router_out)
    for copy in loads:
        copy.wait()

    def group(g, _):
        base = lax.rem(my_group + g, groups) * members

        def arrive(i, _):
            behind = lax.rem(me - base - i + count, count)
            pl.when(behind > 0)(lambda: block_copy(send_ref, rows_out, rows_sems, behind).wait_recv())
            return 0

        lax.fori_loop(0, members, arrive, 0)
        blocks = pl.ds(base, members)
        size = members * block_rows
        group_rows[...] = rows_out[blocks].reshape(size, width)
        slot_lane = lax.broadcasted_iota(jnp.int32, (size, TILE), 1)
        mine = slot_lane == me
        probs = router_probs(dot_nn(group_rows[...], router_ref[...]), slot_lane, experts)
        gate = jnp.sum(jnp.where(mine, probs, 0.0), axis=1, keepdims=True)
        cot_group = cot_rows[blocks].reshape(size, width).astype(f32)
        sent_ref[...] = (gate * cot_group).astype(bf16)
        result_acc[...] = jnp.zeros_like(result_acc)
        grad_acc[...] = jnp.zeros_like(grad_acc)

        def units(i, _):
            cols = pl.ds(pl.multiple_of(i * width, width), width)
            act, slope = gelu_parts(dot_nn(group_rows[...], win_ref[:, cols]))
            result_acc[...] += dot_nn(act.astype(bf16), wout_ref[cols, :])
            pre_grad = (dot_nt(sent_ref[...], wout_ref[cols, :]) * slope).astype(bf16)
            grad_acc[...] += dot_nt(pre_grad, win_ref[:, cols])
            return 0

        lax.fori_loop(0, hidden_units // width, units, 0)
        result = result_acc[...].astype(bf16)
        gate_grad = jnp.sum(cot_group * result.astype(f32), axis=1, keepdims=True)
        logit_grad = (gate_grad * gate) * (jnp.where(mine, 1.0, 0.0) - probs)
        high, low = two_parts(logit_grad)
        grad = grad_acc[...] + (dot_nt(high, router_ref[...]) + dot_nt(low, router_ref[...]))
        grad_send[blocks] = grad.astype(bf16).reshape(members, block_rows, width)
        gated = (gate * result.astype(f32)).astype(bf16)
        result_out[blocks] = gated.reshape(members, block_rows, width)

        def give(i, _):
            ahead = lax.rem(base + i - me + count, count)

            @pl.when(ahead > 0)
            def _():
                block_copy(grad_send, grad_recv, grad_sems, ahead).start()

            return 0

        lax.fori_loop(0, members, give, 0)
        router_out[...] += dot_tn(high, group_rows[...]) + dot_tn(low, group_rows[...])
        return 0

    lax.fori_loop(0, groups, group, 0)
    grad_recv[me] = grad_send[me]

    slots = count * block_rows
    place = place_rows(slot_row[...], 0, slots, tokens)
    await_blocks(grad_send, grad_recv, grad_sems, False, True)
    moe_grad = dot_tn(place, grad_recv[...].reshape(slots, width))
    hidden = hidden_ref[...]
    inverse = inverse_rms(hidden)
    scaled = hidden * inverse
    gain_grad_out[...] = jnp.sum(moe_grad * scaled, axis=0, keepdims=True)
    through = moe_grad * gain_ref[...].astype(f32)
    shared = jnp.mean(through * scaled, axis=1, keepdims=True)
    hidden_grad = cot_ref[...].astype(f32) + inverse * (through - scaled * shared)
    hidden_grad_out[...] = hidden_grad
    low_ref[...] = hidden_grad.astype(bf16)

    def back_column(i, _):
        cols = pl.ds(pl.multiple_of(i * 256, 256), 256)
        wo_grad = dot_nn(att_ref[...], low_ref[:, cols]).astype(bf16)
        wo_grad_out[:, :, cols] = wo_grad.reshape(width // 16, 16, 256)
        att_grad_out[:, cols] = dot_nt(low_ref[...], wo_ref[cols, :]).astype(bf16)
        att_t_ref[cols, :] = dot_nt(wo_ref[cols, :], low_ref[...]).astype(bf16)
        return 0

    lax.fori_loop(0, width // 256, back_column, 0)

    def pair(g, _):
        rows = pl.ds(pl.multiple_of(g * TILE, TILE), TILE)
        both = att_ref[rows, :].astype(f32) * att_t_ref[rows, :].astype(f32)
        delta_out[g] = pick_rows(
            [jnp.sum(both[:64], axis=0, keepdims=True), jnp.sum(both[64:], axis=0, keepdims=True)],
            tokens,
        )
        return 0

    lax.fori_loop(0, width // TILE, pair, 0)
    await_blocks(send_ref, rows_out, rows_sems, True, False)
    await_blocks(grad_send, grad_recv, grad_sems, True, False)


class Axis:
    def __init__(self, name, size, step=1):
        place = lax.axis_index(name)
        self.name, self.size, self.step, self.place = name, size, step, place
        self.index = lax.rem(place // step, size)

    def at(self, ahead):
        return lax.rem(self.index + ahead, self.size)

    def peer(self, ahead):
        return {self.name: self.place + (self.at(ahead) - self.index) * self.step}


def mesh_axes():
    dp, ctx, expert = lax.axis_size("dp"), lax.axis_size("ctx"), lax.axis_size("expert")
    cores, lines = Axis("expert", expert), Axis("ctx", ctx)
    if dp == 4:
        near, far = Axis("dp", 2, 1), Axis("dp", 2, 2)
        return [[cores, near, far, lines], [cores, far, near, lines]]
    return [[cores, Axis("dp", dp), lines]] * 2


def push(source, target, sems, slot, device):
    copy = pltpu.make_async_remote_copy(
        src_ref=source, dst_ref=target, send_sem=sems.at[0, slot], recv_sem=sems.at[1, slot],
        device_id=device, device_id_type=pl.DeviceIdType.MESH,
    )
    copy.start()
    return copy


def back_kernel(
    experts, plan,
    branch_ref, bias_ref, q_ref, k_hbm, v_hbm, att_grad_ref, lse_ref, delta_ref, normed_hbm, normed_own_ref,
    gain_ref, wq_ref, wk_ref, wv_ref, wo_part_hbm, moe_gain_ref, router_part_hbm, x_hbm, hidden_grad_hbm,
    hidden_hbm, slot_row, result_hbm, rows_hbm, cot_hbm, win_hbm, wout_hbm, router_ref,
    full_ref, small_out, input_out, in_out, out_out, layer_out, rows_all,
    k_ref, v_ref, normed_ref, s_ref, dp_ref, p_ref, ds_ref, dq_ref, dk_ref, dv_ref, window_k, window_v,
    hist_ref, gain_sum,
    local_ref, shared_send, shared_recv, parts_ref, acc_refs, recv_refs, small_ref, small_recv,
    result_recv, win_ref, wout_ref, rows_ref, cot_ref, rows_t,
    block_sems, load_sems, sems, small_sems, shared_sems, result_sems, rows_sems,
):
    group, pieces, lengths = plan
    flows = mesh_axes()
    branch = branch_ref[0, 0]
    ctx_at = lax.axis_index("ctx")
    ctx_count, dp_count = lax.axis_size("ctx"), lax.axis_size("dp")
    tokens, width = q_ref.shape
    own = tokens - PB
    plen = PB * ctx_count
    count, me = owners()
    lines, columns_dp = Axis("ctx", ctx_count), Axis("dp", dp_count)
    whole_axes = [Axis("expert", lax.axis_size("expert")), columns_dp, lines]
    gain = gain_ref[...].astype(f32)
    limit = limits(ctx_at, branch, tokens)
    blocks = ctx_count + 2
    rows_16 = width // 16

    def block_loads(i):
        size = TILE if i == 1 else PB
        rows = (plen, plen + own)[i] if i < 2 else pl.multiple_of(lines.at(i - 1) * PB, PB)
        sources = [(k_hbm, k_ref, 0), (v_hbm, v_ref, 1)]
        if 2 <= i < blocks - 1:
            sources.append((normed_hbm, normed_ref, 2))
        return [
            pltpu.make_async_copy(
                source.at[pl.ds(rows, size)], target.at[i % 2, pl.ds(0, size)], block_sems.at[i, n]
            )
            for source, target, n in sources
        ]

    for copy in block_loads(0):
        copy.start()
    slice_width = win_ref.shape[1]
    part = pl.ds(pl.multiple_of(lax.axis_index("dp") * slice_width, slice_width), slice_width)
    weight_loads = [
        pltpu.make_async_copy(win_hbm.at[:, part], win_ref, load_sems.at[0]),
        pltpu.make_async_copy(wout_hbm.at[part], wout_ref, load_sems.at[1]),
    ]
    own_result = pltpu.make_async_copy(result_hbm.at[me], result_recv.at[me], load_sems.at[2])
    wo_load = pltpu.make_async_copy(wo_part_hbm, parts_ref.at[pl.ds(0, rows_16)], load_sems.at[5 + 2 * dp_count])
    router_load = pltpu.make_async_copy(
        router_part_hbm.at[pl.ds(0, experts)], small_ref.at[pl.ds(0, experts)], load_sems.at[7 + 2 * dp_count]
    )
    for copy in [wo_load, *weight_loads, own_result, router_load]:
        copy.start()

    barrier = pltpu.get_barrier_semaphore()

    def greet(ahead, _):
        pl.semaphore_signal(
            barrier, inc=1, device_id=owner_device(lax.rem(me + ahead, count)),
            device_id_type=pl.DeviceIdType.MESH,
        )
        return 0

    lax.fori_loop(1, count, greet, 0)
    for ahead in range(1, dp_count):
        pl.semaphore_signal(
            barrier, inc=1, device_id=columns_dp.peer(ahead), device_id_type=pl.DeviceIdType.MESH
        )
    pl.semaphore_wait(barrier, count - 1 + dp_count - 1)

    slots_of = {}

    def slot(*key):
        return slots_of.setdefault(key, len(slots_of))

    started = []

    def reduce_start(j, s):
        axis, length = flows[j % 2][s], lengths[s]
        copies = []
        for ahead in range(1, axis.size):
            target = axis.at(ahead)
            if s == 0:
                source = parts_ref.at[pl.ds(j * group + target * length, length)]
            else:
                source = acc_refs[s - 1].at[j, pl.ds(target * length, length)]
            there = recv_refs[s].at[j, ahead - 1]
            copies.append(push(source, there, sems, slot("r", j, s, ahead), axis.peer(ahead)))
        started.extend(copies)
        return copies

    def base_of(j, s):
        base = j * group
        for t in range(s + 1):
            base = base + flows[j % 2][t].index * lengths[t]
        return base

    def reduce_finish(j, s, copies):
        axis, length = flows[j % 2][s], lengths[s]
        for copy in copies:
            copy.wait_recv()
        last = s == len(lengths) - 1

        size = 4 if length % 4 == 0 else 1

        def some(u, _):
            if s == 0:
                total = parts_ref[pl.ds(base_of(j, 0) + u * size, size)].astype(f32)
            else:
                total = acc_refs[s - 1][j, pl.ds(axis.index * length + u * size, size)].astype(f32)
            for ahead in range(1, axis.size):
                total = total + recv_refs[s][j, ahead - 1, pl.ds(u * size, size)].astype(f32)
            if last:
                full_ref[pl.ds(base_of(j, s) + u * size, size)] = total.astype(bf16)
            else:
                acc_refs[s][j, pl.ds(u * size, size)] = total.astype(bf16)
            return 0

        lax.fori_loop(0, length // size, some, 0)

    def spread_start(j, s):
        axis, length = flows[j % 2][s], lengths[s]
        here = full_ref.at[pl.ds(base_of(j, s), length)]
        copies = [
            push(here, here, sems, slot("s", j, s, ahead), axis.peer(ahead))
            for ahead in range(1, axis.size)
        ]
        started.extend(copies)
        return copies

    def small_slot(s, ahead):
        return sum(axis.size - 1 for axis in whole_axes[:s]) + ahead - 1

    def small_start(s):
        axis = whole_axes[s]
        copies = [
            push(small_ref, small_recv[s].at[ahead - 1], small_sems, small_slot(s, ahead), axis.peer(ahead))
            for ahead in range(1, axis.size)
        ]
        return copies

    def small_finish(s, copies):
        axis = whole_axes[s]
        for copy in copies:
            copy.wait()
        mine = small_ref[...]
        total = jnp.zeros_like(mine)
        for index in range(axis.size):
            piece = mine
            for ahead in range(1, axis.size):
                piece = jnp.where(axis.at(axis.size - ahead) == index, small_recv[s][ahead - 1], piece)
            total = total + piece
        if s == len(whole_axes) - 1:
            small_out[...] = total
        else:
            small_ref[...] = total

    stages = len(lengths)
    early = pieces > 1 and group <= rows_16
    begin = [blocks + j // 2 for j in range(pieces)]
    if early:
        begin = [blocks - 1] + [blocks + (j - 1) // 2 for j in range(1, pieces)]
    pending = {}

    def advance(time):
        for j in sorted(range(pieces), key=lambda j: begin[j]):
            s = time - begin[j]
            if not 0 <= s < 2 * stages:
                continue
            if s < stages:
                reduce_finish(j, s, pending[j, s])
                if s + 1 < stages:
                    pending[j, s + 1] = reduce_start(j, s + 1)
                else:
                    pending[j, s + 1] = spread_start(j, s)
            else:
                for copy in pending[j, s]:
                    copy.wait_recv()
                if s + 1 < 2 * stages:
                    pending[j, s + 1] = spread_start(j, 2 * stages - 1 - (s + 1))

    def put(first, cols, value):
        rows = value.shape[0]
        parts_ref[first // 16 : (first + rows) // 16, :, cols] = value.astype(bf16).reshape(
            rows // 16, 16, value.shape[1]
        )

    def columns(work):
        def column(i, _):
            work(pl.ds(pl.multiple_of(i * 256, 256), 256))
            return 0

        lax.fori_loop(0, width // 256, column, 0)

    if parts_ref.shape[0] > 4 * rows_16:
        extra = parts_ref.shape[0] - 4 * rows_16
        parts_ref[4 * rows_16 :] = jnp.zeros((extra, 16, width), bf16)
    wo_load.wait()
    if early:
        pending[0, 0] = reduce_start(0, 0)

    def give_result(ahead, _):
        block_copy(result_hbm, result_recv, result_sems, ahead).start()
        return 0

    lax.fori_loop(1, count, give_result, 0)

    def rows_copy(ahead, e):
        return pltpu.make_async_remote_copy(
            src_ref=rows_hbm.at[e], dst_ref=rows_all.at[ahead - 1, e],
            send_sem=rows_sems.at[0, ahead - 1, e], recv_sem=rows_sems.at[1, ahead - 1, e],
            device_id=columns_dp.peer(ahead), device_id_type=pl.DeviceIdType.MESH,
        )

    def each_row_block(act):
        def one(e, _):
            for ahead in range(1, dp_count):
                act(rows_copy(ahead, e))
            return 0

        lax.fori_loop(0, count, one, 0)

    each_row_block(lambda copy: copy.start())

    shared_copies = []
    shared_slots = shared_send.shape[0]
    hist_ref[...] = jnp.zeros_like(hist_ref)
    gain_sum[...] = jnp.zeros_like(gain_sum)
    for i in range(blocks):
        cont, window, at_home = i == 0, i == 1, i == blocks - 1
        remote = i - 1
        size = TILE if window else PB
        for copy in block_loads(i):
            copy.wait()
        if i + 1 < blocks:
            for copy in block_loads(i + 1):
                copy.start()
        block = lines.at(max(remote, 0))
        lanes_from = PB if cont or window else 0
        lanes_used = slice(lanes_from, tokens)
        if cont or at_home:
            near = [
                (0, lanes_from, 0, None),
                (0, lanes_from + TILE, TILE, None),
                (TILE, lanes_from + TILE, 0, None),
            ]
        elif window:
            near = [(0, PB, TILE, None)]
        else:
            near = [(TILE, 0, TILE, block == ctx_at - 1)]

        def pair(g, _, i=i, cont=cont, window=window, size=size, block=block, lanes_used=lanes_used, near=near):
            lanes = pl.ds(pl.multiple_of(g * TILE, TILE), TILE)
            queries = q_ref[lanes_used, lanes]
            grads = att_grad_ref[lanes_used, lanes]
            keys = k_ref[i % 2, :size, lanes]
            values = v_ref[i % 2, :size, lanes]
            keys_t = keys.T
            bias = bias_ref[g]
            dk_parts, dv_parts, dq_parts = [], [], []
            for half in range(2):
                mine = head_lanes(half)
                lse = lse_ref[g][half : half + 1, lanes_used]
                delta = delta_ref[g][half : half + 1, lanes_used]
                s_ref[:size, lanes_used] = dot_nt(jnp.where(mine, keys, jnp.zeros_like(keys)), queries)
                dp_ref[:size, lanes_used] = dot_nt(jnp.where(mine, values, jnp.zeros_like(values)), grads)
                source = jnp.broadcast_to(bias[half : half + 1, :], (TILE, TILE))
                for first, lane, gap, when in near:
                    def add(first=first, lane=lane, gap=gap):
                        there = (slice(first, first + TILE), slice(lane, lane + TILE))
                        index = jnp.clip(near_index(gap), 0, TILE - 1)
                        s_ref[there] = s_ref[there] + jnp.take_along_axis(source, index, axis=1)

                    add() if when is None else pl.when(when)(add)
                step = 32
                for first in range(0, size, step):
                    rows = slice(first, first + step)
                    p = jnp.exp(s_ref[rows, lanes_used] - lse)
                    if cont:
                        p = jnp.where(own_allowed(first, step, own), p, 0.0)
                    elif not window:
                        p = jnp.where(row_steps(block * PB + first, step, tokens) < limit, p, 0.0)
                    p_ref[rows, lanes_used] = p.astype(bf16)
                    ds_ref[rows, lanes_used] = (p * (dp_ref[rows, lanes_used] - delta)).astype(bf16)
                for first, lane, gap, when in near:
                    def collect(first=first, lane=lane, gap=gap):
                        tile = ds_ref[first : first + TILE, lane : lane + TILE].astype(f32)
                        if not isinstance(gap, int) or gap > 0:
                            tile = jnp.where(near_index(gap) < TILE, tile, 0.0)
                        turn = lax.broadcasted_iota(jnp.int32, (TILE, TILE), 1) + lax.broadcasted_iota(
                            jnp.int32, (TILE, TILE), 0
                        )
                        tile = jnp.take_along_axis(tile, (turn - gap) & (TILE - 1), axis=1)
                        hist_ref[g * 2 + half] += fold8(tile, jnp.sum)

                    collect() if when is None else pl.when(when)(collect)
                ds = ds_ref[:size, lanes_used]
                dv_parts.append(dot_nn(p_ref[:size, lanes_used], grads))
                dk_parts.append(dot_nn(ds, queries))
                dq_parts.append(dot_nn(keys_t[half * 64 : half * 64 + 64, :], ds))
            dq = jnp.concatenate(dq_parts, axis=0)
            if cont:
                dq_ref[lanes, :PB] = jnp.zeros((TILE, PB), f32)
                dq_ref[lanes, PB:] = dq
            else:
                dq_ref[lanes, lanes_used] += dq
            mine = head_lanes(0)
            dv, dk = jnp.where(mine, dv_parts[0], dv_parts[1]), jnp.where(mine, dk_parts[0], dk_parts[1])
            if window:
                window_v[:, lanes], window_k[:, lanes] = dv.astype(bf16), dk.astype(bf16)
            else:
                if not cont:
                    picked = window_rows(block * PB, PB, branch)
                    dv = dv + dot_tn(picked, window_v[:, lanes])
                    dk = dk + dot_tn(picked, window_k[:, lanes])
                dv_ref[:, lanes], dk_ref[:, lanes] = dv.astype(bf16), dk.astype(bf16)
            return 0

        lax.fori_loop(0, width // TILE, pair, 0)

        def block_column(cols, i=i, cont=cont, at_home=at_home, remote=remote):
            if cont:
                normed = normed_own_ref[PB:, cols]
            elif at_home:
                normed = normed_own_ref[:PB, cols]
            else:
                normed = normed_ref[i % 2, :, cols]
            wk_part = dot_nn(rows_t[:, :PB], dk_ref[:, cols])
            wv_part = dot_nn(rows_t[:, :PB], dv_ref[:, cols])
            if cont:
                in_out[:, cols] = wk_part
                out_out[:, cols] = wv_part
            elif not at_home:
                in_out[:, cols] += wk_part
                out_out[:, cols] += wv_part
            else:
                put(width, cols, out_out[:, cols] + wv_part)
                put(2 * width, cols, in_out[:, cols] + wk_part)
            grad = dot_nt(dk_ref[...], wk_ref[cols, :]) + dot_nt(dv_ref[...], wv_ref[cols, :])
            gain_sum[:, cols] += jnp.sum(grad * normed.astype(f32), axis=0, keepdims=True)
            if cont:
                local_ref[PB:, cols] = grad
            elif at_home:
                local_ref[:PB, cols] = grad
            else:
                shared_send[(remote - 1) % shared_slots, :, cols] = grad.astype(bf16)

        if window:
            continue
        if shared_slots < remote < ctx_count:
            shared_copies[remote - 1 - shared_slots].wait_send()
        if cont:
            rows_t[:, :PB] = normed_own_ref[PB:, :].T
        elif at_home:
            rows_t[:, :PB] = normed_own_ref[:PB, :].T
        else:
            rows_t[:, :PB] = normed_ref[i % 2].T
        columns(block_column)
        if 1 <= remote < ctx_count:
            n = remote - 1
            shared_copies.append(
                push(shared_send.at[n % shared_slots], shared_recv.at[n], shared_sems, n, lines.peer(remote))
            )
    started.extend(shared_copies[-shared_slots:])

    def ready(j):
        if j > 0 or not early:
            pending[j, 0] = reduce_start(j, 0)

    done = 3 * rows_16
    for j in range(pieces):
        if (j + 1) * group <= done:
            ready(j)
    rows_ref[:tokens, :] = dq_ref[...].T.astype(bf16)
    rows_t[:, :tokens] = normed_own_ref[...].T

    def query_column(cols):
        put(3 * width, cols, dot_nn(rows_t[:, :tokens], rows_ref[:tokens, cols]))

    columns(query_column)
    for j in range(pieces):
        if (j + 1) * group > done:
            ready(j)

    def query_grad(cols):
        grad = dot_nt(rows_ref[:tokens, :], wq_ref[cols, :])
        gain_sum[:, cols] += jnp.sum(grad * normed_own_ref[:, cols].astype(f32), axis=0, keepdims=True)
        local_ref[:, cols] += grad

    columns(query_grad)
    small_ref[experts:, :] = jnp.zeros((small_ref.shape[0] - experts, width), f32)
    small_ref[experts : experts + 1, :] = gain_sum[...] / gain
    small_ref[experts + 1 : experts + 2, :] = moe_gain_ref[...]
    router_load.wait()
    per_row = width // TILE
    for head in range(hist_ref.shape[0]):
        row, lane = 2 + experts + head // per_row, head % per_row * TILE
        small_ref[row : row + 1, lane : lane + TILE] = jnp.sum(hist_ref[head], axis=0, keepdims=True)
    small_pending = small_start(0)

    slots = rows_ref.shape[0]

    def rows_load(n):
        source = rows_hbm if n == 0 else rows_all.at[n - 1]
        return pltpu.make_async_copy(source, result_recv, load_sems.at[3 + 2 * n])

    hidden_load = pltpu.make_async_copy(hidden_hbm, input_out, load_sems.at[4 + 2 * dp_count])
    hidden_load.start()
    grad_load = pltpu.make_async_copy(hidden_grad_hbm, input_out, load_sems.at[3 + 2 * dp_count])
    x_loads = [
        pltpu.make_async_copy(x_hbm.at[pl.ds(n * PB, PB)], normed_ref.at[n], load_sems.at[6 + 2 * dp_count + 2 * n])
        for n in range(2)
    ]
    for copy in x_loads:
        copy.start()

    def grads_of(n, c):
        if c == 0:
            if n == 0:
                for copy in weight_loads:
                    copy.wait()
            rows_load(n).wait()
            rows_ref[...] = result_recv[...].reshape(slots, width)
            cot_from = columns_dp.at(dp_count - n)
            load = pltpu.make_async_copy(cot_hbm.at[cot_from], result_recv, load_sems.at[4 + 2 * n])
            load.start()
            lane = lax.broadcasted_iota(jnp.int32, (slots, TILE), 1)
            probs = router_probs(dot_nn(rows_ref[...], router_ref[...]), lane, experts)
            gate = jnp.sum(jnp.where(lane == me, probs, 0.0), axis=1, keepdims=True)
            load.wait()
            cot = result_recv[...].reshape(slots, width)
            cot_ref[...] = (gate * cot.astype(f32)).astype(bf16)
            if n == 0:
                each_row_block(lambda copy: copy.wait_recv())
            if n + 1 < dp_count:
                rows_load(n + 1).start()
            rows_t[...] = rows_ref[...].T
        cols = slice(c * 256, c * 256 + 256)
        act, slope = gelu_parts(dot_nn(rows_ref[...], win_ref[:, cols]))
        pre_grad = (dot_nt(cot_ref[...], wout_ref[cols, :]) * slope).astype(bf16)
        out_part = dot_tn(act.astype(bf16), cot_ref[...])
        in_part = dot_nn(rows_t[...], pre_grad)
        if n == 0:
            out_out[cols, :] = out_part
            in_out[:, cols] = in_part
        else:
            out_out[cols, :] += out_part
            in_out[:, cols] += in_part

    def input_back():
        for copy in shared_copies:
            copy.wait_recv()
        for copy in x_loads:
            copy.wait()
        grad_load.wait()
        for first, shared_rows in ((0, True), (PB, False)):
            rows = slice(first, PB if shared_rows else tokens)
            x = normed_ref[0 if shared_rows else 1].astype(f32)
            inverse = inverse_rms(x)
            grad = local_ref[rows, :]
            if shared_rows:
                for n in range(ctx_count - 1):
                    grad = grad + shared_recv[n].astype(f32)
            through = grad * gain
            scaled = x * inverse
            shared = jnp.mean(through * scaled, axis=1, keepdims=True)
            input_out[rows, :] += inverse * (through - scaled * shared)

    def layer():
        own_result.wait()
        await_blocks(result_hbm, result_recv, result_sems, False, True)
        place = place_rows(slot_row[...], 0, slots, tokens)
        returned = dot_tn(place, result_recv[...].reshape(slots, width))
        hidden_load.wait()
        layer_out[...] = (input_out[...] + returned).astype(bf16)
        rows_load(0).start()
        grad_load.start()

    work = [layer]
    work += [functools.partial(grads_of, n, c) for n in range(dp_count) for c in range(slice_width // 256)]
    work += [input_back]
    for time in range(blocks - 1, max(begin) + 2 * stages):
        if time >= blocks:
            advance(time)
        elif early:
            advance(time)
        s = time - blocks
        if 0 <= s < len(whole_axes):
            small_finish(s, small_pending)
            if s + 1 < len(whole_axes):
                small_pending = small_start(s + 1)
        if work:
            work.pop(0)()
    for rest in work:
        rest()
    for copy in started:
        copy.wait_send()
    await_blocks(result_hbm, result_recv, result_sems, True, False)
    each_row_block(lambda copy: copy.wait_send())


def finish_kernel(full_ref, in_ref, out_ref, input_ref, layer_ref, *results):
    weights, rest = results[:4], results[4:]
    for n, weight in enumerate(weights):
        weight[...] = full_ref[n].astype(f32).reshape(weight.shape)
    for source, target in zip((in_ref, out_ref, input_ref, layer_ref), rest):
        target[...] = source[...]


def tail_plan(sizes, width):
    group = 1
    for size in sizes:
        group *= size
    units = 4 * width // 16
    pieces = -(-units // group)
    lengths, left = [], group
    for size in sizes:
        left //= size
        lengths.append(left)
    return group, pieces, lengths


def body(
    inputs, cotangent, route, arrival, branch, attn_gain, query_weight, key_weight, value_weight,
    output_weight, rel_table, moe_gain, router_weight, expert_in, expert_out,
):
    x = inputs[0]
    cot = cotangent[0]
    tokens, width = x.shape
    own = tokens - PB
    buckets, heads = rel_table.shape
    experts = router_weight.shape[1]
    capacity = 9 * tokens // (8 * experts)
    block_rows = capacity if capacity % 8 == 0 else -(-capacity // 16) * 16
    slots = experts * block_rows
    ctx_count = lax.axis_size("ctx")
    dp_count = lax.axis_size("dp")
    plen = PB * ctx_count
    keys_total = plen + own + TILE
    hidden_units = expert_in.shape[2]
    pairs = width // TILE
    attn_gain_row = attn_gain.reshape(1, width)
    moe_gain_row = moe_gain.reshape(1, width)
    onehot = bucket_onehot(buckets)
    by_distance = jnp.dot(onehot, rel_table.astype(f32), precision=lax.Precision.HIGHEST).T
    by_distance = by_distance - by_distance[:, TILE - 1 :]
    bias = jnp.pad(by_distance.reshape(pairs, 2, TILE), ((0, 0), (0, 6), (0, 0)))
    router_wide = jnp.pad(router_weight, ((0, 0), (0, TILE - experts)))
    route_row = route.reshape(1, tokens)
    arrive_row = arrival[0]
    blocks = shape((experts, block_rows, width), bf16)
    block_space = pltpu.VMEM((experts, block_rows, width), bf16)
    block_sems = pltpu.SemaphoreType.DMA((2, experts - 1))
    any_space = pl.BlockSpec(memory_space=pl.ANY)

    slot_row, cot_sent, normed_own, normed_all, queries, keys, values, att, lse = pl.pallas_call(
        functools.partial(front_kernel, capacity),
        out_shape=[
            shape((1, tokens), jnp.int32),
            blocks,
            shape((tokens, width), bf16),
            shape((plen, width), bf16),
            shape((tokens, width), bf16),
            shape((keys_total, width), bf16),
            shape((keys_total, width), bf16),
            shape((width, tokens), bf16),
            shape((pairs, 8, tokens), f32),
        ],
        in_specs=[smem()] + [vmem()] * 9,
        out_specs=[vmem()] * 9,
        scratch_shapes=[
            pltpu.VMEM((ctx_count, PB, width), bf16),
            block_space,
            pltpu.VMEM((keys_total, tokens), f32),
            pltpu.VMEM((keys_total, tokens), bf16),
            pltpu.SemaphoreType.DMA((2, 2, ctx_count - 1, CHUNKS)),
            block_sems,
        ],
        compiler_params=remote_params(1),
        cost_estimate=cost(40 * keys_total * tokens * width, 20 * width * width),
        name="front",
    )(
        branch, bias, x, cot, attn_gain_row, route_row, arrive_row,
        query_weight, key_weight, value_weight,
    )
    cot_all = lax.all_gather(cot_sent, "dp", axis=0, tiled=False)

    members = 2 * lax.axis_size("expert") if ctx_count % 2 == 0 else experts
    group_rows = members * block_rows
    (
        rows_sent, router_part, hidden_grad, wo_part, att_grad, delta, moe_gain_part,
        result, hidden,
    ) = pl.pallas_call(
        functools.partial(expert_kernel, experts),
        out_shape=[
            blocks, shape((TILE, width), f32), shape((tokens, width), f32), shape((width // 16, 16, width), bf16),
            shape((tokens, width), bf16), shape((pairs, 8, tokens), f32), shape((1, width), f32),
            blocks, shape((tokens, width), f32),
        ],
        in_specs=[vmem()] * 8 + [any_space] * 2,
        out_specs=[vmem()] * 9,
        scratch_shapes=[
            pltpu.VMEM((tokens, width), bf16),
            block_space,
            pltpu.VMEM((width, hidden_units), bf16),
            pltpu.VMEM((hidden_units, width), bf16),
            pltpu.VMEM((group_rows, width), bf16),
            pltpu.VMEM((group_rows, width), bf16),
            pltpu.VMEM((group_rows, width), f32),
            pltpu.VMEM((group_rows, width), f32),
            block_space, block_space,
            pltpu.VMEM((tokens, width), bf16),
            pltpu.VMEM((width, tokens), bf16),
            block_sems, block_sems,
            pltpu.SemaphoreType.DMA((2,)),
        ],
        compiler_params=remote_params(2),
        cost_estimate=cost(8 * slots * width * hidden_units, 12 * width * hidden_units),
        name="expert",
    )(
        att, x, output_weight, moe_gain_row, router_wide, slot_row, cot, cot_sent,
        expert_in[0], expert_out[0],
    )
    att_grad, cot_all = lax.optimization_barrier((att_grad, cot_all))

    expert_count = lax.axis_size("expert")
    dp_sizes = [2, 2] if dp_count == 4 else [dp_count]
    sizes = [expert_count, *dp_sizes, ctx_count]
    plan = tail_plan(sizes, width)
    group, pieces, lengths = plan
    units = group * pieces

    table_rows = heads * TILE // width
    small_rows = -(-(2 + experts + table_rows) // 8) * 8
    slice_width = hidden_units // dp_count
    weights, small, input_grad, in_grad, out_grad, layer_out, _ = pl.pallas_call(
        functools.partial(back_kernel, experts, plan),
        out_shape=[
            shape((units, 16, width), bf16), shape((small_rows, width), f32), shape((tokens, width), f32),
            shape((width, slice_width), f32), shape((slice_width, width), f32), shape((tokens, width), bf16),
            shape((dp_count - 1, experts, block_rows, width), bf16),
        ],
        in_specs=[
            smem(), vmem(), vmem(), any_space, any_space, vmem(), vmem(), vmem(), any_space, vmem(),
            vmem(), vmem(), vmem(), vmem(), any_space, vmem(), any_space, any_space, any_space,
            any_space, vmem(), any_space, any_space, any_space, any_space, any_space, vmem(),
        ],
        out_specs=[vmem()] * 6 + [any_space],
        scratch_shapes=[
            pltpu.VMEM((2, PB, width), bf16),
            pltpu.VMEM((2, PB, width), bf16),
            pltpu.VMEM((2, PB, width), bf16),
            pltpu.VMEM((PB, tokens), f32),
            pltpu.VMEM((PB, tokens), f32),
            pltpu.VMEM((PB, tokens), bf16),
            pltpu.VMEM((PB, tokens), bf16),
            pltpu.VMEM((width, tokens), f32),
            pltpu.VMEM((PB, width), bf16),
            pltpu.VMEM((PB, width), bf16),
            pltpu.VMEM((TILE, width), bf16),
            pltpu.VMEM((TILE, width), bf16),
            pltpu.VMEM((heads, 8, TILE), f32),
            pltpu.VMEM((1, width), f32),
            pltpu.VMEM((tokens, width), f32),
            pltpu.VMEM((ctx_count - 1 if ctx_count <= 4 else 1, PB, width), bf16),
            pltpu.VMEM((ctx_count - 1, PB, width), bf16),
            pltpu.VMEM((units, 16, width), bf16),
            [pltpu.VMEM((pieces, length, 16, width), bf16) for length in lengths[:-1]],
            [
                pltpu.VMEM((pieces, size - 1, length, 16, width), bf16)
                for size, length in zip(sizes, lengths)
            ],
            pltpu.VMEM((small_rows, width), f32),
            [pltpu.VMEM((size - 1, small_rows, width), f32) for size in (expert_count, dp_count, ctx_count)],
            block_space,
            pltpu.VMEM((width, slice_width), bf16),
            pltpu.VMEM((slice_width, width), bf16),
            pltpu.VMEM((slots, width), bf16),
            pltpu.VMEM((slots, width), bf16),
            pltpu.VMEM((width, slots), bf16),
            pltpu.SemaphoreType.DMA((ctx_count + 2, 3)),
            pltpu.SemaphoreType.DMA((9 + 2 * dp_count,)),
            pltpu.SemaphoreType.DMA((2, 2 * pieces * sum(size - 1 for size in sizes))),
            pltpu.SemaphoreType.DMA((2, expert_count + dp_count + ctx_count - 3)),
            pltpu.SemaphoreType.DMA((2, ctx_count - 1)),
            block_sems,
            pltpu.SemaphoreType.DMA((2, dp_count - 1, experts)),
        ],
        compiler_params=remote_params(0),
        cost_estimate=cost(
            8 * dp_count * slots * width * slice_width + 80 * keys_total * tokens * width,
            60 * width * slice_width,
        ),
        name="back",
    )(
        branch, bias, queries, keys, values, att_grad, lse, delta, normed_all, normed_own,
        attn_gain_row, query_weight, key_weight, value_weight, wo_part, moe_gain_part, router_part, x,
        hidden_grad, hidden, slot_row, result,
        rows_sent, cot_all, expert_in[0], expert_out[0], router_wide,
    )

    matrix_units = width // 16
    steps = 4

    def part_rows(rows, columns=width):
        return pl.BlockSpec((rows // steps, columns), lambda i: (i, 0))

    weights = weights[: 4 * matrix_units].reshape(4, matrix_units, 16, width)
    *weights, in_grad, out_grad, input_grad, layer_out = pl.pallas_call(
        finish_kernel,
        grid=(steps,),
        out_shape=[shape((width, width), f32)] * 4
        + [
            shape((width, slice_width), f32), shape((slice_width, width), f32),
            shape((tokens, width), f32), shape((tokens, width), bf16),
        ],
        in_specs=[
            pl.BlockSpec((4, matrix_units // steps, 16, width), lambda i: (0, i, 0, 0)),
            part_rows(width, slice_width), part_rows(slice_width), part_rows(tokens), part_rows(tokens),
        ],
        out_specs=[part_rows(width)] * 4
        + [part_rows(width, slice_width), part_rows(slice_width), part_rows(tokens), part_rows(tokens)],
        compiler_params=params(),
        cost_estimate=cost(8 * width * width, 48 * width * width),
        name="finish",
    )(weights, in_grad, out_grad, input_grad, layer_out)
    router_grad = small[:experts].T
    hist_sum = small[2 + experts : 2 + experts + table_rows].reshape(heads, TILE)
    last = onehot[:, buckets - 1 :]
    spread = jnp.concatenate([onehot[:, : buckets - 1], last - 1.0], axis=1)
    table_grad = jnp.dot(spread.T, hist_sum.T, precision=lax.Precision.HIGHEST)
    return (
        layer_out[None],
        input_grad[None],
        small[experts],
        weights[3],
        weights[2],
        weights[1],
        weights[0],
        table_grad,
        small[experts + 1],
        router_grad,
        in_grad[None],
        out_grad[None],
    )


def solution(mesh):
    grouped = P(("dp", "expert"), "ctx", None)
    placed = (
        grouped, grouped, grouped, grouped, P(("dp", "expert"), "ctx"),
        P(), P(), P(), P(), P(), P(), P(), P(),
        P(("ctx", "expert"), None, None),
        P(("ctx", "expert"), None, None),
    )
    return jax.shard_map(
        body,
        mesh=mesh,
        in_specs=placed,
        out_specs=(
            grouped, grouped, P(), P(), P(), P(), P(), P(), P(), P(),
            P(("ctx", "expert"), None, "dp"),
            P(("ctx", "expert"), "dp", None),
        ),
        check_vma=False,
    )
```

```python
import functools

import jax
import jax.numpy as jnp
from jax import lax
from jax.experimental import pallas as pl
from jax.experimental.pallas import tpu as pltpu
from jax.sharding import PartitionSpec as P

PB = 256
TILE = 128
CHUNKS = 2

bucket_edges = (19, 21, 24, 27, 31, 35, 40, 46, 52, 59, 67, 77, 87, 99, 113)
norm_eps = 1e-06
masked_score = -1e30
gelu_scale = 0.7978845608
gelu_cube = 0.044715

bf16 = jnp.bfloat16
f32 = jnp.float32
VMEM_LIMIT = 121 * 512 * 1024


def dot_nn(a, b):
    return jnp.dot(a, b, preferred_element_type=f32)


def dot_nt(a, b):
    return lax.dot_general(a, b, (((1,), (1,)), ((), ())), preferred_element_type=f32)


def dot_tn(a, b):
    return lax.dot_general(a, b, (((0,), (0,)), ((), ())), preferred_element_type=f32)


def two_parts(a):
    high = a.astype(bf16)
    return high, (a - high.astype(f32)).astype(bf16)


def vmem():
    return pl.BlockSpec(memory_space=pltpu.VMEM)


def smem():
    return pl.BlockSpec(memory_space=pltpu.SMEM)


def params():
    return pltpu.CompilerParams(vmem_limit_bytes=VMEM_LIMIT)


def remote_params(number):
    return pltpu.CompilerParams(
        vmem_limit_bytes=VMEM_LIMIT, collective_id=number, has_side_effects=True
    )


def cost(flops, nbytes):
    return pl.CostEstimate(flops=int(flops), bytes_accessed=int(nbytes), transcendentals=0)


def shape(dims, kind):
    return jax.ShapeDtypeStruct(dims, kind)


def inverse_rms(x):
    return lax.rsqrt(jnp.mean(x * x, axis=-1, keepdims=True) + norm_eps)


def bucket_onehot(buckets):
    distance = jnp.arange(TILE, dtype=jnp.int32)
    ids = jnp.minimum(distance, 16)
    for edge in bucket_edges:
        ids = ids + (distance >= edge).astype(jnp.int32)
    return (ids[:, None] == jnp.arange(buckets, dtype=jnp.int32)[None, :]).astype(f32)


def near_index(first):
    rows = lax.broadcasted_iota(jnp.int32, (TILE, TILE), 0)
    lanes = lax.broadcasted_iota(jnp.int32, (TILE, TILE), 1)
    return first + lanes - rows


def near_tiles(ctx_at, plen):
    start = ctx_at * PB
    return (
        (start, 0, 0, False),
        (start, TILE, TILE, False),
        (start + TILE, TILE, 0, False),
        (plen, PB, 0, False),
        (plen, PB + TILE, TILE, False),
        (plen + TILE, PB + TILE, 0, False),
        (plen + PB, PB, TILE, False),
        (start - TILE, 0, TILE, True),
    )


def add_near(s_ref, bias_row, ctx_at, plen):
    source = jnp.broadcast_to(bias_row, (TILE, TILE))
    add_tiles(s_ref, source, ctx_at, near_tiles(ctx_at, plen))


def add_tiles(s_ref, source, ctx_at, tiles):
    for first_row, first_lane, gap, guarded in tiles:
        def work(first_row=first_row, first_lane=first_lane, gap=gap):
            rows = pl.ds(first_row if isinstance(first_row, int) else pl.multiple_of(first_row, 16), TILE)
            lanes = slice(first_lane, first_lane + TILE)
            index = jnp.clip(near_index(gap), 0, TILE - 1)
            s_ref[rows, lanes] = s_ref[rows, lanes] + jnp.take_along_axis(source, index, axis=1)

        if guarded:
            pl.when(ctx_at > 0)(work)
        else:
            work()


def scores_to(s_ref, keys, queries, plen):
    s_ref[:plen, :] = dot_nt(keys[:plen], queries)
    s_ref[plen:, PB:] = dot_nt(keys[plen:], queries[PB:])


def limits(ctx_at, branch, tokens):
    lane = lax.broadcasted_iota(jnp.int32, (1, tokens), 1)
    return jnp.where(lane < PB, ctx_at * PB + lane + 1, branch - TILE)


def window_rows(first, count, branch):
    rows = lax.broadcasted_iota(jnp.int32, (TILE, count), 0)
    places = lax.broadcasted_iota(jnp.int32, (TILE, count), 1) + first
    return (places == rows + (branch - TILE)).astype(bf16)


def row_steps(first, count, lanes):
    return first + lax.broadcasted_iota(jnp.int32, (count, lanes), 0)


def own_allowed(first, count, lanes):
    return row_steps(first, count, lanes) <= lax.broadcasted_iota(jnp.int32, (count, lanes), 1)


def head_lanes(half):
    return lax.broadcasted_iota(jnp.int32, (1, TILE), 1) // (TILE // 2) == half


def pick_rows(pieces, lanes):
    row = lax.broadcasted_iota(jnp.int32, (8, lanes), 0)
    return jnp.where(row == 0, pieces[0], jnp.where(row == 1, pieces[1], 0.0))


def fold8(x, op):
    return op(x.reshape(x.shape[0] // 8, 8, x.shape[1]), axis=0)


def owner_device(index):
    cores = lax.axis_size("expert")
    return {"ctx": index // cores, "expert": lax.rem(index, cores)}


def owners():
    cores = lax.axis_size("expert")
    count = cores * lax.axis_size("ctx")
    return count, lax.axis_index("ctx") * cores + lax.axis_index("expert")


def greet_owners():
    count, me = owners()
    barrier = pltpu.get_barrier_semaphore()

    def greet(ahead, _):
        pl.semaphore_signal(
            barrier, inc=1, device_id=owner_device(lax.rem(me + ahead, count)),
            device_id_type=pl.DeviceIdType.MESH,
        )
        return 0

    lax.fori_loop(1, count, greet, 0)
    pl.semaphore_wait(barrier, count - 1)


def block_copy(source, target, sems, ahead):
    count, me = owners()
    peer = lax.rem(me + ahead, count)
    return pltpu.make_async_remote_copy(
        src_ref=source.at[peer], dst_ref=target.at[me],
        send_sem=sems.at[0, ahead - 1], recv_sem=sems.at[1, ahead - 1],
        device_id=owner_device(peer), device_id_type=pl.DeviceIdType.MESH,
    )


def await_blocks(source, target, sems, sent, received):
    def one(ahead, _):
        copy = block_copy(source, target, sems, ahead)
        if received:
            copy.wait_recv()
        if sent:
            copy.wait_send()
        return 0

    lax.fori_loop(1, owners()[0], one, 0)


def place_rows(slot_row, index, block_rows, tokens):
    rows = lax.broadcasted_iota(jnp.int32, (block_rows, tokens), 0) + index * block_rows
    return (rows == slot_row).astype(bf16)


def front_kernel(
    capacity,
    branch_ref, bias_ref, x_ref, cot_ref, gain_ref, route_row, arrive_row,
    wq_ref, wk_ref, wv_ref,
    slot_out, cot_out, normed_own_out, normed_out, q_ref, k_out, v_out, att_out, lse_out,
    prompt_ref, send_ref, s_ref, p_ref, prompt_sems, cot_sems,
):
    branch = branch_ref[0, 0]
    ctx_at, ctx_count = lax.axis_index("ctx"), lax.axis_size("ctx")
    plen = PB * ctx_count
    tokens, width = x_ref.shape
    own = tokens - PB
    gain = gain_ref[...].astype(f32)
    count, me = owners()
    block_rows = send_ref.shape[1]
    greet_owners()

    chunk = PB // CHUNKS

    def pass_on(step, up, c):
        block = ctx_at - step if up else ctx_at + step
        ahead = ctx_at + 1 if up else ctx_at - 1
        fits = (block >= 0) & (ahead < ctx_count) if up else (block < ctx_count) & (ahead >= 0)
        piece = pl.ds(c * chunk, chunk)
        source = x_ref.at[piece] if step == 0 else prompt_ref.at[block, piece]
        copy = pltpu.make_async_remote_copy(
            src_ref=source, dst_ref=prompt_ref.at[block, piece],
            send_sem=prompt_sems.at[0, int(up), step, c], recv_sem=prompt_sems.at[1, int(up), step, c],
            device_id={"ctx": ahead}, device_id_type=pl.DeviceIdType.MESH,
        )
        return fits, copy

    def arrival(step, up, c):
        block = ctx_at - step - 1 if up else ctx_at + step + 1
        fits = block >= 0 if up else block < ctx_count
        place = prompt_ref.at[block, pl.ds(c * chunk, chunk)]
        copy = pltpu.make_async_remote_copy(
            src_ref=place, dst_ref=place,
            send_sem=prompt_sems.at[0, int(up), step, c], recv_sem=prompt_sems.at[1, int(up), step, c],
            device_id={"ctx": ctx_at}, device_id_type=pl.DeviceIdType.MESH,
        )
        return fits, block, copy

    for c in range(CHUNKS):
        for up in (True, False):
            fits, copy = pass_on(0, up, c)
            pl.when(fits)(copy.start)

    x = x_ref[...].astype(f32)
    normed_own_out[...] = (x * inverse_rms(x) * gain).astype(bf16)

    def column(i, _):
        cols = pl.ds(pl.multiple_of(i * 256, 256), 256)
        q_ref[:, cols] = dot_nn(normed_own_out[...], wq_ref[:, cols]).astype(bf16)
        k_out[plen : plen + own, cols] = dot_nn(normed_own_out[PB:, :], wk_ref[:, cols]).astype(bf16)
        v_out[plen : plen + own, cols] = dot_nn(normed_own_out[PB:, :], wv_ref[:, cols]).astype(bf16)
        return 0

    lax.fori_loop(0, width // 256, column, 0)

    def project(block):
        rows = pl.ds(pl.multiple_of(block * PB, PB), PB)

        def prompt_column(i, _):
            cols = pl.ds(pl.multiple_of(i * 256, 256), 256)
            k_out[rows, cols] = dot_nn(normed_out[rows, :], wk_ref[:, cols]).astype(bf16)
            v_out[rows, cols] = dot_nn(normed_out[rows, :], wv_ref[:, cols]).astype(bf16)
            return 0

        lax.fori_loop(0, width // 256, prompt_column, 0)

    def take(block):
        x = prompt_ref[block].astype(f32)
        rows = pl.ds(pl.multiple_of(block * PB, PB), PB)
        normed_out[rows, :] = (x * inverse_rms(x) * gain).astype(bf16)
        project(block)

    for step in range(ctx_count - 1):
        for c in range(CHUNKS):
            for up in (True, False):
                fits, block, copy = arrival(step, up, c)
                pl.when(fits)(copy.wait_recv)
                if step < ctx_count - 2:
                    fits, copy = pass_on(step + 1, up, c)
                    pl.when(fits)(copy.start)
        if step == 0:
            normed_out[pl.ds(pl.multiple_of(ctx_at * PB, PB), PB), :] = normed_own_out[:PB, :]
            project(ctx_at)
        for up in (True, False):
            fits, block, copy = arrival(step, up, 0)
            pl.when(fits)(functools.partial(take, block))

    def down(row):
        column = jnp.broadcast_to(row[...].astype(f32), (TILE, tokens)).T
        return jnp.concatenate([column] * (tokens // TILE), axis=1)

    same = down(route_row) == route_row[...].astype(f32)
    earlier = down(arrive_row) < arrive_row[...].astype(f32)
    rank = jnp.sum(jnp.where(same & earlier, 1.0, 0.0), axis=0, keepdims=True).astype(jnp.int32)
    slot = jnp.where(rank < capacity, route_row[...] * block_rows + rank, count * block_rows)
    slot_out[...] = slot

    def send_cot(ahead, _):
        peer = lax.rem(me + ahead, count)
        place = place_rows(slot_out[...], peer, block_rows, tokens)
        send_ref[peer] = dot_nn(place, cot_ref[...]).astype(bf16)
        block_copy(send_ref, cot_out, cot_sems, ahead).start()
        return 0

    def send_cots():
        lax.fori_loop(1, count, send_cot, 0)
        cot_out[me] = dot_nn(place_rows(slot_out[...], me, block_rows, tokens), cot_ref[...]).astype(bf16)

    def window_column(i, _):
        cols = pl.ds(pl.multiple_of(i * 256, 256), 256)
        window = window_rows(0, plen, branch)
        k_out[plen + own :, cols] = dot_nn(window, k_out[:plen, cols]).astype(bf16)
        v_out[plen + own :, cols] = dot_nn(window, v_out[:plen, cols]).astype(bf16)
        return 0

    lax.fori_loop(0, width // 256, window_column, 0)
    p_ref[plen:, :PB] = jnp.zeros((own + TILE, PB), bf16)
    limit = limits(ctx_at, branch, tokens)

    def pair(g, _):
        pl.when(g == 1)(send_cots)
        lanes = pl.ds(pl.multiple_of(g * TILE, TILE), TILE)
        queries = q_ref[:, lanes]
        keys = k_out[:, lanes]
        values_t = v_out[:, lanes].T
        bias = bias_ref[g]
        lse_rows, att_rows = [], []
        for half in range(2):
            scores_to(s_ref, jnp.where(head_lanes(half), keys, jnp.zeros_like(keys)), queries, plen)
            add_near(s_ref, bias[half : half + 1, :], ctx_at, plen)

            def top_of(i, top):
                for part in range(0, TILE, 32):
                    first = pl.multiple_of(i * TILE + part, 32)
                    rows = pl.ds(first, 32)
                    s = jnp.where(row_steps(first, 32, tokens) < limit, s_ref[rows, :], masked_score)
                    s_ref[rows, :] = s
                    top = jnp.maximum(top, fold8(s, jnp.max))
                return top

            top = lax.fori_loop(0, plen // TILE, top_of, jnp.full((8, tokens), masked_score, f32))
            own_top = jnp.full((8, own), masked_score, f32)
            for i in range(own // TILE + 1):
                rows = slice(plen + i * TILE, plen + (i + 1) * TILE)
                s = s_ref[rows, PB:]
                if i < own // TILE:
                    s = jnp.where(own_allowed(i * TILE, TILE, own), s, masked_score)
                    s_ref[rows, PB:] = s
                own_top = jnp.maximum(own_top, fold8(s, jnp.max))
            top = jnp.concatenate([top[:, :PB], jnp.maximum(top[:, PB:], own_top)], axis=1)
            top = jnp.max(top, axis=0, keepdims=True)

            def weigh(i, total):
                for part in range(0, TILE, 32):
                    rows = pl.ds(pl.multiple_of(i * TILE + part, 32), 32)
                    p = jnp.exp(s_ref[rows, :] - top)
                    p_ref[rows, :] = p.astype(bf16)
                    total = total + fold8(p, jnp.sum)
                return total

            total = lax.fori_loop(0, plen // TILE, weigh, jnp.zeros((8, tokens), f32))
            own_total = jnp.zeros((8, own), f32)
            for i in range(own // TILE + 1):
                rows = slice(plen + i * TILE, plen + (i + 1) * TILE)
                p = jnp.exp(s_ref[rows, PB:] - top[:, PB:])
                p_ref[rows, PB:] = p.astype(bf16)
                own_total = own_total + fold8(p, jnp.sum)
            total = jnp.concatenate([total[:, :PB], total[:, PB:] + own_total], axis=1)
            total = jnp.sum(total, axis=0, keepdims=True)
            rows = slice(half * 64, half * 64 + 64)
            att_rows.append((dot_nn(values_t[rows, :], p_ref[...]) / total).astype(bf16))
            lse_rows.append(top + jnp.log(total))
        att_out[lanes, :] = jnp.concatenate(att_rows, axis=0)
        lse_out[g] = pick_rows(lse_rows, tokens)
        return 0

    lax.fori_loop(0, width // TILE, pair, 0)
    await_blocks(send_ref, cot_out, cot_sems, True, True)
    for step in range(ctx_count - 1):
        for c in range(CHUNKS):
            for up in (True, False):
                fits, copy = pass_on(step, up, c)
                pl.when(fits)(copy.wait_send)


def router_probs(logits, lane, experts):
    logits = jnp.where(lane < experts, logits, masked_score)
    logits = jnp.exp(logits - jnp.max(logits, axis=1, keepdims=True))
    return logits / jnp.sum(logits, axis=1, keepdims=True)


def gelu_parts(v):
    t = jnp.tanh(gelu_scale * (v + gelu_cube * (v * v * v)))
    half = 0.5 * (1.0 + t)
    slope = half + 0.5 * v * (1.0 - t * t) * (gelu_scale + (3.0 * gelu_scale * gelu_cube) * (v * v))
    return v * half, slope


def expert_kernel(
    experts,
    att_ref, x_ref, wo_ref, gain_ref, router_ref, slot_row, cot_ref, cot_rows, win_hbm, wout_hbm,
    rows_out, router_out, hidden_grad_out, wo_grad_out, att_grad_out, delta_out, gain_grad_out,
    result_out, hidden_ref,
    moe_ref, send_ref, win_ref, wout_ref, group_rows, sent_ref, result_acc, grad_acc,
    grad_send, grad_recv, low_ref, att_t_ref, rows_sems, grad_sems, load_sems,
):
    tokens, width = x_ref.shape
    count, me = owners()
    block_rows = send_ref.shape[1]
    hidden_units = win_ref.shape[1]
    loads = [
        pltpu.make_async_copy(win_hbm, win_ref, load_sems.at[0]),
        pltpu.make_async_copy(wout_hbm, wout_ref, load_sems.at[1]),
    ]
    for copy in loads:
        copy.start()
    greet_owners()

    def column(i, _):
        cols = pl.ds(pl.multiple_of(i * 256, 256), 256)
        hidden_ref[:, cols] = x_ref[:, cols].astype(f32) + dot_tn(att_ref[...], wo_ref[:, cols])
        return 0

    lax.fori_loop(0, width // 256, column, 0)
    hidden = hidden_ref[...]
    moe_ref[...] = (hidden * inverse_rms(hidden) * gain_ref[...].astype(f32)).astype(bf16)

    members = 2 * lax.axis_size("expert") if lax.axis_size("ctx") % 2 == 0 else count
    groups = count // members
    my_group = me // members

    def send_rows(ahead, _):
        peer = lax.rem(me + ahead, count)
        place = place_rows(slot_row[...], peer, block_rows, tokens)
        send_ref[peer] = dot_nn(place, moe_ref[...]).astype(bf16)
        block_copy(send_ref, rows_out, rows_sems, ahead).start()
        return 0

    def send_group(g, _):
        base = lax.rem(my_group + g, groups) * members

        def member(i, _):
            ahead = lax.rem(base + i - me + count, count)
            pl.when(ahead > 0)(lambda: (send_rows(ahead, 0), None)[1])
            return 0

        return lax.fori_loop(0, members, member, 0)

    lax.fori_loop(0, groups, send_group, 0)
    rows_out[me] = dot_nn(place_rows(slot_row[...], me, block_rows, tokens), moe_ref[...]).astype(bf16)

    router_out[...] = jnp.zeros_like(router_out)
    for copy in loads:
        copy.wait()

    def group(g, _):
        base = lax.rem(my_group + g, groups) * members

        def arrive(i, _):
            behind = lax.rem(me - base - i + count, count)
            pl.when(behind > 0)(lambda: block_copy(send_ref, rows_out, rows_sems, behind).wait_recv())
            return 0

        lax.fori_loop(0, members, arrive, 0)
        blocks = pl.ds(base, members)
        size = members * block_rows
        group_rows[...] = rows_out[blocks].reshape(size, width)
        slot_lane = lax.broadcasted_iota(jnp.int32, (size, TILE), 1)
        mine = slot_lane == me
        probs = router_probs(dot_nn(group_rows[...], router_ref[...]), slot_lane, experts)
        gate = jnp.sum(jnp.where(mine, probs, 0.0), axis=1, keepdims=True)
        cot_group = cot_rows[blocks].reshape(size, width).astype(f32)
        sent_ref[...] = (gate * cot_group).astype(bf16)
        result_acc[...] = jnp.zeros_like(result_acc)
        grad_acc[...] = jnp.zeros_like(grad_acc)

        def units(i, _):
            cols = pl.ds(pl.multiple_of(i * width, width), width)
            act, slope = gelu_parts(dot_nn(group_rows[...], win_ref[:, cols]))
            result_acc[...] += dot_nn(act.astype(bf16), wout_ref[cols, :])
            pre_grad = (dot_nt(sent_ref[...], wout_ref[cols, :]) * slope).astype(bf16)
            grad_acc[...] += dot_nt(pre_grad, win_ref[:, cols])
            return 0

        lax.fori_loop(0, hidden_units // width, units, 0)
        result = result_acc[...].astype(bf16)
        gate_grad = jnp.sum(cot_group * result.astype(f32), axis=1, keepdims=True)
        logit_grad = (gate_grad * gate) * (jnp.where(mine, 1.0, 0.0) - probs)
        high, low = two_parts(logit_grad)
        grad = grad_acc[...] + (dot_nt(high, router_ref[...]) + dot_nt(low, router_ref[...]))
        grad_send[blocks] = grad.astype(bf16).reshape(members, block_rows, width)
        gated = (gate * result.astype(f32)).astype(bf16)
        result_out[blocks] = gated.reshape(members, block_rows, width)

        def give(i, _):
            ahead = lax.rem(base + i - me + count, count)

            @pl.when(ahead > 0)
            def _():
                block_copy(grad_send, grad_recv, grad_sems, ahead).start()

            return 0

        lax.fori_loop(0, members, give, 0)
        router_out[...] += dot_tn(high, group_rows[...]) + dot_tn(low, group_rows[...])
        return 0

    lax.fori_loop(0, groups, group, 0)
    grad_recv[me] = grad_send[me]

    slots = count * block_rows
    place = place_rows(slot_row[...], 0, slots, tokens)
    await_blocks(grad_send, grad_recv, grad_sems, False, True)
    moe_grad = dot_tn(place, grad_recv[...].reshape(slots, width))
    hidden = hidden_ref[...]
    inverse = inverse_rms(hidden)
    scaled = hidden * inverse
    gain_grad_out[...] = jnp.sum(moe_grad * scaled, axis=0, keepdims=True)
    through = moe_grad * gain_ref[...].astype(f32)
    shared = jnp.mean(through * scaled, axis=1, keepdims=True)
    hidden_grad = cot_ref[...].astype(f32) + inverse * (through - scaled * shared)
    hidden_grad_out[...] = hidden_grad
    low_ref[...] = hidden_grad.astype(bf16)

    def back_column(i, _):
        cols = pl.ds(pl.multiple_of(i * 256, 256), 256)
        wo_grad = dot_nn(att_ref[...], low_ref[:, cols]).astype(bf16)
        wo_grad_out[:, :, cols] = wo_grad.reshape(width // 16, 16, 256)
        att_grad_out[:, cols] = dot_nt(low_ref[...], wo_ref[cols, :]).astype(bf16)
        att_t_ref[cols, :] = dot_nt(wo_ref[cols, :], low_ref[...]).astype(bf16)
        return 0

    lax.fori_loop(0, width // 256, back_column, 0)

    def pair(g, _):
        rows = pl.ds(pl.multiple_of(g * TILE, TILE), TILE)
        both = att_ref[rows, :].astype(f32) * att_t_ref[rows, :].astype(f32)
        delta_out[g] = pick_rows(
            [jnp.sum(both[:64], axis=0, keepdims=True), jnp.sum(both[64:], axis=0, keepdims=True)],
            tokens,
        )
        return 0

    lax.fori_loop(0, width // TILE, pair, 0)
    await_blocks(send_ref, rows_out, rows_sems, True, False)
    await_blocks(grad_send, grad_recv, grad_sems, True, False)


class Axis:
    def __init__(self, name, size, step=1):
        place = lax.axis_index(name)
        self.name, self.size, self.step, self.place = name, size, step, place
        self.index = lax.rem(place // step, size)

    def at(self, ahead):
        return lax.rem(self.index + ahead, self.size)

    def peer(self, ahead):
        return {self.name: self.place + (self.at(ahead) - self.index) * self.step}


def mesh_axes():
    dp, ctx, expert = lax.axis_size("dp"), lax.axis_size("ctx"), lax.axis_size("expert")
    cores, lines = Axis("expert", expert), Axis("ctx", ctx)
    if dp == 4:
        near, far = Axis("dp", 2, 1), Axis("dp", 2, 2)
        return [[cores, near, far, lines], [cores, far, near, lines]]
    return [[cores, Axis("dp", dp), lines]] * 2


def push(source, target, sems, slot, device):
    copy = pltpu.make_async_remote_copy(
        src_ref=source, dst_ref=target, send_sem=sems.at[0, slot], recv_sem=sems.at[1, slot],
        device_id=device, device_id_type=pl.DeviceIdType.MESH,
    )
    copy.start()
    return copy


def back_kernel(
    experts, plan,
    branch_ref, bias_ref, q_ref, k_hbm, v_hbm, att_grad_ref, lse_ref, delta_ref, normed_hbm, normed_own_ref,
    gain_ref, wq_ref, wk_ref, wv_ref, wo_part_hbm, moe_gain_ref, router_part_hbm, x_hbm, hidden_grad_hbm,
    hidden_hbm, slot_row, result_hbm, rows_hbm, cot_hbm, win_hbm, wout_hbm, router_ref,
    full_ref, small_out, input_out, in_out, out_out, layer_out, rows_all,
    k_ref, v_ref, normed_ref, s_ref, dp_ref, p_ref, ds_ref, dq_ref, dk_ref, dv_ref, window_k, window_v, picked_ref,
    hist_ref, gain_sum,
    local_ref, shared_send, shared_recv, parts_ref, acc_refs, recv_refs, small_ref, small_recv,
    result_recv, win_ref, wout_ref, rows_ref, cot_ref, rows_t,
    block_sems, load_sems, sems, small_sems, shared_sems, result_sems, rows_sems,
):
    group, pieces, lengths = plan
    flows = mesh_axes()
    branch = branch_ref[0, 0]
    ctx_at = lax.axis_index("ctx")
    ctx_count, dp_count = lax.axis_size("ctx"), lax.axis_size("dp")
    tokens, width = q_ref.shape
    own = tokens - PB
    plen = PB * ctx_count
    count, me = owners()
    lines, columns_dp = Axis("ctx", ctx_count), Axis("dp", dp_count)
    whole_axes = [Axis("expert", lax.axis_size("expert")), columns_dp, lines]
    gain = gain_ref[...].astype(f32)
    limit = limits(ctx_at, branch, tokens)
    blocks = ctx_count + 2
    rows_16 = width // 16

    def block_loads(i):
        size = TILE if i == 1 else PB
        rows = (plen, plen + own)[i] if i < 2 else pl.multiple_of(lines.at(i - 1) * PB, PB)
        sources = [(k_hbm, k_ref, 0), (v_hbm, v_ref, 1)]
        if 2 <= i < blocks - 1:
            sources.append((normed_hbm, normed_ref, 2))
        return [
            pltpu.make_async_copy(
                source.at[pl.ds(rows, size)], target.at[i % 2, pl.ds(0, size)], block_sems.at[i, n]
            )
            for source, target, n in sources
        ]

    for copy in block_loads(0):
        copy.start()
    slice_width = win_ref.shape[1]
    part = pl.ds(pl.multiple_of(lax.axis_index("dp") * slice_width, slice_width), slice_width)
    weight_loads = [
        pltpu.make_async_copy(win_hbm.at[:, part], win_ref, load_sems.at[0]),
        pltpu.make_async_copy(wout_hbm.at[part], wout_ref, load_sems.at[1]),
    ]
    own_result = pltpu.make_async_copy(result_hbm.at[me], result_recv.at[me], load_sems.at[2])
    wo_load = pltpu.make_async_copy(wo_part_hbm, parts_ref.at[pl.ds(0, rows_16)], load_sems.at[5 + 2 * dp_count])
    router_load = pltpu.make_async_copy(
        router_part_hbm.at[pl.ds(0, experts)], small_ref.at[pl.ds(0, experts)], load_sems.at[7 + 2 * dp_count]
    )
    for copy in [wo_load, *weight_loads, own_result, router_load]:
        copy.start()

    barrier = pltpu.get_barrier_semaphore()

    def greet(ahead, _):
        pl.semaphore_signal(
            barrier, inc=1, device_id=owner_device(lax.rem(me + ahead, count)),
            device_id_type=pl.DeviceIdType.MESH,
        )
        return 0

    lax.fori_loop(1, count, greet, 0)
    for ahead in range(1, dp_count):
        pl.semaphore_signal(
            barrier, inc=1, device_id=columns_dp.peer(ahead), device_id_type=pl.DeviceIdType.MESH
        )
    pl.semaphore_wait(barrier, count - 1 + dp_count - 1)

    slots_of = {}

    def slot(*key):
        return slots_of.setdefault(key, len(slots_of))

    started = []

    def reduce_start(j, s):
        axis, length = flows[j % 2][s], lengths[s]
        copies = []
        for ahead in range(1, axis.size):
            target = axis.at(ahead)
            if s == 0:
                source = parts_ref.at[pl.ds(j * group + target * length, length)]
            else:
                source = acc_refs[s - 1].at[j, pl.ds(target * length, length)]
            there = recv_refs[s].at[j, ahead - 1]
            copies.append(push(source, there, sems, slot("r", j, s, ahead), axis.peer(ahead)))
        started.extend(copies)
        return copies

    def base_of(j, s):
        base = j * group
        for t in range(s + 1):
            base = base + flows[j % 2][t].index * lengths[t]
        return base

    def reduce_finish(j, s, copies):
        axis, length = flows[j % 2][s], lengths[s]
        for copy in copies:
            copy.wait_recv()
        last = s == len(lengths) - 1

        size = 4 if length % 4 == 0 else 1

        def some(u, _):
            if s == 0:
                total = parts_ref[pl.ds(base_of(j, 0) + u * size, size)].astype(f32)
            else:
                total = acc_refs[s - 1][j, pl.ds(axis.index * length + u * size, size)].astype(f32)
            for ahead in range(1, axis.size):
                total = total + recv_refs[s][j, ahead - 1, pl.ds(u * size, size)].astype(f32)
            if last:
                full_ref[pl.ds(base_of(j, s) + u * size, size)] = total.astype(bf16)
            else:
                acc_refs[s][j, pl.ds(u * size, size)] = total.astype(bf16)
            return 0

        lax.fori_loop(0, length // size, some, 0)

    def spread_start(j, s):
        axis, length = flows[j % 2][s], lengths[s]
        here = full_ref.at[pl.ds(base_of(j, s), length)]
        copies = [
            push(here, here, sems, slot("s", j, s, ahead), axis.peer(ahead))
            for ahead in range(1, axis.size)
        ]
        started.extend(copies)
        return copies

    def small_slot(s, ahead):
        return sum(axis.size - 1 for axis in whole_axes[:s]) + ahead - 1

    def small_start(s):
        axis = whole_axes[s]
        copies = [
            push(small_ref, small_recv[s].at[ahead - 1], small_sems, small_slot(s, ahead), axis.peer(ahead))
            for ahead in range(1, axis.size)
        ]
        return copies

    def small_finish(s, copies):
        axis = whole_axes[s]
        for copy in copies:
            copy.wait()
        mine = small_ref[...]
        total = jnp.zeros_like(mine)
        for index in range(axis.size):
            piece = mine
            for ahead in range(1, axis.size):
                piece = jnp.where(axis.at(axis.size - ahead) == index, small_recv[s][ahead - 1], piece)
            total = total + piece
        if s == len(whole_axes) - 1:
            small_out[...] = total
        else:
            small_ref[...] = total

    stages = len(lengths)
    early = pieces > 1 and group <= rows_16
    begin = [blocks + j // 2 for j in range(pieces)]
    if early:
        begin = [blocks - 1] + [blocks + (j - 1) // 2 for j in range(1, pieces)]
    pending = {}

    def advance(time):
        for j in sorted(range(pieces), key=lambda j: begin[j]):
            s = time - begin[j]
            if not 0 <= s < 2 * stages:
                continue
            if s < stages:
                reduce_finish(j, s, pending[j, s])
                if s + 1 < stages:
                    pending[j, s + 1] = reduce_start(j, s + 1)
                else:
                    pending[j, s + 1] = spread_start(j, s)
            else:
                for copy in pending[j, s]:
                    copy.wait_recv()
                if s + 1 < 2 * stages:
                    pending[j, s + 1] = spread_start(j, 2 * stages - 1 - (s + 1))

    def put(first, cols, value):
        rows = value.shape[0]
        parts_ref[first // 16 : (first + rows) // 16, :, cols] = value.astype(bf16).reshape(
            rows // 16, 16, value.shape[1]
        )

    def columns(work):
        def column(i, _):
            work(pl.ds(pl.multiple_of(i * 256, 256), 256))
            return 0

        lax.fori_loop(0, width // 256, column, 0)

    if parts_ref.shape[0] > 4 * rows_16:
        extra = parts_ref.shape[0] - 4 * rows_16
        parts_ref[4 * rows_16 :] = jnp.zeros((extra, 16, width), bf16)
    wo_load.wait()
    if early:
        pending[0, 0] = reduce_start(0, 0)

    def give_result(ahead, _):
        block_copy(result_hbm, result_recv, result_sems, ahead).start()
        return 0

    lax.fori_loop(1, count, give_result, 0)

    def rows_copy(ahead, e):
        return pltpu.make_async_remote_copy(
            src_ref=rows_hbm.at[e], dst_ref=rows_all.at[ahead - 1, e],
            send_sem=rows_sems.at[0, ahead - 1, e], recv_sem=rows_sems.at[1, ahead - 1, e],
            device_id=columns_dp.peer(ahead), device_id_type=pl.DeviceIdType.MESH,
        )

    def each_row_block(act):
        def one(e, _):
            for ahead in range(1, dp_count):
                act(rows_copy(ahead, e))
            return 0

        lax.fori_loop(0, count, one, 0)

    each_row_block(lambda copy: copy.start())

    shared_copies = []
    shared_slots = shared_send.shape[0]
    hist_ref[...] = jnp.zeros_like(hist_ref)
    gain_sum[...] = jnp.zeros_like(gain_sum)
    for i in range(blocks):
        cont, window, at_home = i == 0, i == 1, i == blocks - 1
        remote = i - 1
        size = TILE if window else PB
        for copy in block_loads(i):
            copy.wait()
        if i + 1 < blocks:
            for copy in block_loads(i + 1):
                copy.start()
        block = lines.at(max(remote, 0))
        lanes_from = PB if cont or window else 0
        lanes_used = slice(lanes_from, tokens)
        if cont or at_home:
            near = [
                (0, lanes_from, 0, None),
                (0, lanes_from + TILE, TILE, None),
                (TILE, lanes_from + TILE, 0, None),
            ]
        elif window:
            near = [(0, PB, TILE, None)]
        else:
            near = [(TILE, 0, TILE, block == ctx_at - 1)]

        if not (cont or window):
            places = lax.broadcasted_iota(jnp.int32, (PB, TILE), 0) + block * PB
            picks = lax.broadcasted_iota(jnp.int32, (PB, TILE), 1) + (branch - TILE)
            picked_ref[...] = (places == picks).astype(bf16)

        def pair(g, _, i=i, cont=cont, window=window, size=size, block=block, lanes_used=lanes_used, near=near):
            lanes = pl.ds(pl.multiple_of(g * TILE, TILE), TILE)
            queries = q_ref[lanes_used, lanes]
            grads = att_grad_ref[lanes_used, lanes]
            keys = k_ref[i % 2, :size, lanes]
            values = v_ref[i % 2, :size, lanes]
            keys_t = keys.T
            bias = bias_ref[g]
            dk_parts, dv_parts, dq_parts = [], [], []
            stacked = s_ref.shape[0] // PB
            for halves in [(0, 1)] if stacked == 2 else [(0,), (1,)]:
                total = len(halves) * size

                def masked(rows):
                    return jnp.concatenate([jnp.where(head_lanes(h), rows, jnp.zeros_like(rows)) for h in halves])

                s_ref[:total, lanes_used] = dot_nt(masked(keys), queries)
                dp_ref[:total, lanes_used] = dot_nt(masked(values), grads)
                for n, half in enumerate(halves):
                    offset = n * size
                    lse = lse_ref[g][half : half + 1, lanes_used]
                    delta = delta_ref[g][half : half + 1, lanes_used]
                    source = jnp.broadcast_to(bias[half : half + 1, :], (TILE, TILE))
                    for first, lane, gap, when in near:
                        def add(first=first + offset, lane=lane, gap=gap):
                            there = (slice(first, first + TILE), slice(lane, lane + TILE))
                            index = jnp.clip(near_index(gap), 0, TILE - 1)
                            s_ref[there] = s_ref[there] + jnp.take_along_axis(source, index, axis=1)

                        add() if when is None else pl.when(when)(add)
                    step = 32
                    for first in range(0, size, step):
                        rows = slice(offset + first, offset + first + step)
                        p = jnp.exp(s_ref[rows, lanes_used] - lse)
                        if cont:
                            p = jnp.where(own_allowed(first, step, own), p, 0.0)
                        elif not window:
                            p = jnp.where(row_steps(block * PB + first, step, tokens) < limit, p, 0.0)
                        p_ref[rows, lanes_used] = p.astype(bf16)
                        ds_ref[rows, lanes_used] = (p * (dp_ref[rows, lanes_used] - delta)).astype(bf16)
                    for first, lane, gap, when in near:
                        def collect(first=first + offset, lane=lane, gap=gap, half=half):
                            tile = ds_ref[first : first + TILE, lane : lane + TILE].astype(f32)
                            if gap > 0:
                                tile = jnp.where(near_index(gap) < TILE, tile, 0.0)
                            turn = lax.broadcasted_iota(jnp.int32, (TILE, TILE), 1) + lax.broadcasted_iota(
                                jnp.int32, (TILE, TILE), 0
                            )
                            tile = jnp.take_along_axis(tile, (turn - gap) & (TILE - 1), axis=1)
                            hist_ref[g * 2 + half] += fold8(tile, jnp.sum)

                        collect() if when is None else pl.when(when)(collect)
                dv_all = dot_nn(p_ref[:total, lanes_used], grads)
                dk_all = dot_nn(ds_ref[:total, lanes_used], queries)
                for n, half in enumerate(halves):
                    rows = slice(n * size, n * size + size)
                    dv_parts.append(dv_all[rows])
                    dk_parts.append(dk_all[rows])
                    dq_parts.append(dot_nn(keys_t[half * 64 : half * 64 + 64, :], ds_ref[rows, lanes_used]))
            dq = jnp.concatenate(dq_parts, axis=0)
            if cont:
                dq_ref[lanes, :PB] = jnp.zeros((TILE, PB), f32)
                dq_ref[lanes, PB:] = dq
            else:
                dq_ref[lanes, lanes_used] += dq
            mine = head_lanes(0)
            dv, dk = jnp.where(mine, dv_parts[0], dv_parts[1]), jnp.where(mine, dk_parts[0], dk_parts[1])
            if window:
                window_v[:, lanes], window_k[:, lanes] = dv.astype(bf16), dk.astype(bf16)
            else:
                if not cont:
                    dv = dv + dot_nn(picked_ref[...], window_v[:, lanes])
                    dk = dk + dot_nn(picked_ref[...], window_k[:, lanes])
                dv_ref[:, lanes], dk_ref[:, lanes] = dv.astype(bf16), dk.astype(bf16)
            return 0

        lax.fori_loop(0, width // TILE, pair, 0)

        def block_column(cols, i=i, cont=cont, at_home=at_home, remote=remote):
            if cont:
                normed = normed_own_ref[PB:, cols]
            elif at_home:
                normed = normed_own_ref[:PB, cols]
            else:
                normed = normed_ref[i % 2, :, cols]
            wk_part = dot_nn(rows_t[:, :PB], dk_ref[:, cols])
            wv_part = dot_nn(rows_t[:, :PB], dv_ref[:, cols])
            if cont:
                in_out[:, cols] = wk_part
                out_out[:, cols] = wv_part
            elif not at_home:
                in_out[:, cols] += wk_part
                out_out[:, cols] += wv_part
            else:
                put(width, cols, out_out[:, cols] + wv_part)
                put(2 * width, cols, in_out[:, cols] + wk_part)
            grad = dot_nt(dk_ref[...], wk_ref[cols, :]) + dot_nt(dv_ref[...], wv_ref[cols, :])
            gain_sum[:, cols] += jnp.sum(grad * normed.astype(f32), axis=0, keepdims=True)
            if cont:
                local_ref[PB:, cols] = grad
            elif at_home:
                local_ref[:PB, cols] = grad
            else:
                shared_send[(remote - 1) % shared_slots, :, cols] = grad.astype(bf16)

        if window:
            continue
        if shared_slots < remote < ctx_count:
            shared_copies[remote - 1 - shared_slots].wait_send()
        if cont:
            rows_t[:, :PB] = normed_own_ref[PB:, :].T
        elif at_home:
            rows_t[:, :PB] = normed_own_ref[:PB, :].T
        else:
            rows_t[:, :PB] = normed_ref[i % 2].T
        columns(block_column)
        if 1 <= remote < ctx_count:
            n = remote - 1
            shared_copies.append(
                push(shared_send.at[n % shared_slots], shared_recv.at[n], shared_sems, n, lines.peer(remote))
            )
    started.extend(shared_copies[-shared_slots:])

    def ready(j):
        if j > 0 or not early:
            pending[j, 0] = reduce_start(j, 0)

    done = 3 * rows_16
    for j in range(pieces):
        if (j + 1) * group <= done:
            ready(j)
    rows_ref[:tokens, :] = dq_ref[...].T.astype(bf16)
    rows_t[:, :tokens] = normed_own_ref[...].T

    def query_column(cols):
        put(3 * width, cols, dot_nn(rows_t[:, :tokens], rows_ref[:tokens, cols]))

    columns(query_column)
    for j in range(pieces):
        if (j + 1) * group > done:
            ready(j)

    def query_grad(cols):
        grad = dot_nt(rows_ref[:tokens, :], wq_ref[cols, :])
        gain_sum[:, cols] += jnp.sum(grad * normed_own_ref[:, cols].astype(f32), axis=0, keepdims=True)
        local_ref[:, cols] += grad

    columns(query_grad)
    small_ref[experts:, :] = jnp.zeros((small_ref.shape[0] - experts, width), f32)
    small_ref[experts : experts + 1, :] = gain_sum[...] / gain
    small_ref[experts + 1 : experts + 2, :] = moe_gain_ref[...]
    router_load.wait()
    per_row = width // TILE
    for head in range(hist_ref.shape[0]):
        row, lane = 2 + experts + head // per_row, head % per_row * TILE
        small_ref[row : row + 1, lane : lane + TILE] = jnp.sum(hist_ref[head], axis=0, keepdims=True)
    small_pending = small_start(0)

    slots = rows_ref.shape[0]

    def rows_load(n):
        source = rows_hbm if n == 0 else rows_all.at[n - 1]
        return pltpu.make_async_copy(source, result_recv, load_sems.at[3 + 2 * n])

    hidden_load = pltpu.make_async_copy(hidden_hbm, input_out, load_sems.at[4 + 2 * dp_count])
    hidden_load.start()
    grad_load = pltpu.make_async_copy(hidden_grad_hbm, input_out, load_sems.at[3 + 2 * dp_count])
    x_loads = [
        pltpu.make_async_copy(x_hbm.at[pl.ds(n * PB, PB)], normed_ref.at[n], load_sems.at[6 + 2 * dp_count + 2 * n])
        for n in range(2)
    ]
    for copy in x_loads:
        copy.start()

    def grads_of(n, c):
        if c == 0:
            if n == 0:
                for copy in weight_loads:
                    copy.wait()
            rows_load(n).wait()
            rows_ref[...] = result_recv[...].reshape(slots, width)
            cot_from = columns_dp.at(dp_count - n)
            load = pltpu.make_async_copy(cot_hbm.at[cot_from], result_recv, load_sems.at[4 + 2 * n])
            load.start()
            lane = lax.broadcasted_iota(jnp.int32, (slots, TILE), 1)
            probs = router_probs(dot_nn(rows_ref[...], router_ref[...]), lane, experts)
            gate = jnp.sum(jnp.where(lane == me, probs, 0.0), axis=1, keepdims=True)
            load.wait()
            cot = result_recv[...].reshape(slots, width)
            cot_ref[...] = (gate * cot.astype(f32)).astype(bf16)
            if n == 0:
                each_row_block(lambda copy: copy.wait_recv())
            if n + 1 < dp_count:
                rows_load(n + 1).start()
            rows_t[...] = rows_ref[...].T
        cols = slice(c * 256, c * 256 + 256)
        act, slope = gelu_parts(dot_nn(rows_ref[...], win_ref[:, cols]))
        pre_grad = (dot_nt(cot_ref[...], wout_ref[cols, :]) * slope).astype(bf16)
        out_part = dot_tn(act.astype(bf16), cot_ref[...])
        in_part = dot_nn(rows_t[...], pre_grad)
        if n == 0:
            out_out[cols, :] = out_part
            in_out[:, cols] = in_part
        else:
            out_out[cols, :] += out_part
            in_out[:, cols] += in_part

    def input_back():
        for copy in shared_copies:
            copy.wait_recv()
        for copy in x_loads:
            copy.wait()
        grad_load.wait()
        for first, shared_rows in ((0, True), (PB, False)):
            rows = slice(first, PB if shared_rows else tokens)
            x = normed_ref[0 if shared_rows else 1].astype(f32)
            inverse = inverse_rms(x)
            grad = local_ref[rows, :]
            if shared_rows:
                for n in range(ctx_count - 1):
                    grad = grad + shared_recv[n].astype(f32)
            through = grad * gain
            scaled = x * inverse
            shared = jnp.mean(through * scaled, axis=1, keepdims=True)
            input_out[rows, :] += inverse * (through - scaled * shared)

    def layer():
        own_result.wait()
        await_blocks(result_hbm, result_recv, result_sems, False, True)
        place = place_rows(slot_row[...], 0, slots, tokens)
        returned = dot_tn(place, result_recv[...].reshape(slots, width))
        hidden_load.wait()
        layer_out[...] = (input_out[...] + returned).astype(bf16)
        rows_load(0).start()
        grad_load.start()

    work = [layer]
    work += [functools.partial(grads_of, n, c) for n in range(dp_count) for c in range(slice_width // 256)]
    work += [input_back]
    for time in range(blocks - 1, max(begin) + 2 * stages):
        if time >= blocks:
            advance(time)
        elif early:
            advance(time)
        s = time - blocks
        if 0 <= s < len(whole_axes):
            small_finish(s, small_pending)
            if s + 1 < len(whole_axes):
                small_pending = small_start(s + 1)
        for _ in range(-(-len(work) // (max(begin) + 2 * stages - time))):
            work.pop(0)()
    for copy in started:
        copy.wait_send()
    await_blocks(result_hbm, result_recv, result_sems, True, False)
    each_row_block(lambda copy: copy.wait_send())


def finish_kernel(full_ref, in_ref, out_ref, input_ref, layer_ref, *results):
    weights, rest = results[:4], results[4:]
    for n, weight in enumerate(weights):
        weight[...] = full_ref[n].astype(f32).reshape(weight.shape)
    for source, target in zip((in_ref, out_ref, input_ref, layer_ref), rest):
        target[...] = source[...]


def tail_plan(sizes, width):
    group = 1
    for size in sizes:
        group *= size
    units = 4 * width // 16
    pieces = -(-units // group)
    lengths, left = [], group
    for size in sizes:
        left //= size
        lengths.append(left)
    return group, pieces, lengths


def body(
    inputs, cotangent, route, arrival, branch, attn_gain, query_weight, key_weight, value_weight,
    output_weight, rel_table, moe_gain, router_weight, expert_in, expert_out,
):
    x = inputs[0]
    cot = cotangent[0]
    tokens, width = x.shape
    own = tokens - PB
    buckets, heads = rel_table.shape
    experts = router_weight.shape[1]
    capacity = 9 * tokens // (8 * experts)
    block_rows = capacity if capacity % 8 == 0 else -(-capacity // 16) * 16
    slots = experts * block_rows
    ctx_count = lax.axis_size("ctx")
    dp_count = lax.axis_size("dp")
    plen = PB * ctx_count
    keys_total = plen + own + TILE
    hidden_units = expert_in.shape[2]
    pairs = width // TILE
    attn_gain_row = attn_gain.reshape(1, width)
    moe_gain_row = moe_gain.reshape(1, width)
    onehot = bucket_onehot(buckets)
    by_distance = jnp.dot(onehot, rel_table.astype(f32), precision=lax.Precision.HIGHEST).T
    by_distance = by_distance - by_distance[:, TILE - 1 :]
    bias = jnp.pad(by_distance.reshape(pairs, 2, TILE), ((0, 0), (0, 6), (0, 0)))
    router_wide = jnp.pad(router_weight, ((0, 0), (0, TILE - experts)))
    route_row = route.reshape(1, tokens)
    arrive_row = arrival[0]
    blocks = shape((experts, block_rows, width), bf16)
    block_space = pltpu.VMEM((experts, block_rows, width), bf16)
    block_sems = pltpu.SemaphoreType.DMA((2, experts - 1))
    any_space = pl.BlockSpec(memory_space=pl.ANY)

    slot_row, cot_sent, normed_own, normed_all, queries, keys, values, att, lse = pl.pallas_call(
        functools.partial(front_kernel, capacity),
        out_shape=[
            shape((1, tokens), jnp.int32),
            blocks,
            shape((tokens, width), bf16),
            shape((plen, width), bf16),
            shape((tokens, width), bf16),
            shape((keys_total, width), bf16),
            shape((keys_total, width), bf16),
            shape((width, tokens), bf16),
            shape((pairs, 8, tokens), f32),
        ],
        in_specs=[smem()] + [vmem()] * 9,
        out_specs=[vmem()] * 9,
        scratch_shapes=[
            pltpu.VMEM((ctx_count, PB, width), bf16),
            block_space,
            pltpu.VMEM((keys_total, tokens), f32),
            pltpu.VMEM((keys_total, tokens), bf16),
            pltpu.SemaphoreType.DMA((2, 2, ctx_count - 1, CHUNKS)),
            block_sems,
        ],
        compiler_params=remote_params(1),
        cost_estimate=cost(40 * keys_total * tokens * width, 20 * width * width),
        name="front",
    )(
        branch, bias, x, cot, attn_gain_row, route_row, arrive_row,
        query_weight, key_weight, value_weight,
    )
    cot_all = lax.all_gather(cot_sent, "dp", axis=0, tiled=False)

    members = 2 * lax.axis_size("expert") if ctx_count % 2 == 0 else experts
    group_rows = members * block_rows
    (
        rows_sent, router_part, hidden_grad, wo_part, att_grad, delta, moe_gain_part,
        result, hidden,
    ) = pl.pallas_call(
        functools.partial(expert_kernel, experts),
        out_shape=[
            blocks, shape((TILE, width), f32), shape((tokens, width), f32), shape((width // 16, 16, width), bf16),
            shape((tokens, width), bf16), shape((pairs, 8, tokens), f32), shape((1, width), f32),
            blocks, shape((tokens, width), f32),
        ],
        in_specs=[vmem()] * 8 + [any_space] * 2,
        out_specs=[vmem()] * 9,
        scratch_shapes=[
            pltpu.VMEM((tokens, width), bf16),
            block_space,
            pltpu.VMEM((width, hidden_units), bf16),
            pltpu.VMEM((hidden_units, width), bf16),
            pltpu.VMEM((group_rows, width), bf16),
            pltpu.VMEM((group_rows, width), bf16),
            pltpu.VMEM((group_rows, width), f32),
            pltpu.VMEM((group_rows, width), f32),
            block_space, block_space,
            pltpu.VMEM((tokens, width), bf16),
            pltpu.VMEM((width, tokens), bf16),
            block_sems, block_sems,
            pltpu.SemaphoreType.DMA((2,)),
        ],
        compiler_params=remote_params(2),
        cost_estimate=cost(8 * slots * width * hidden_units, 12 * width * hidden_units),
        name="expert",
    )(
        att, x, output_weight, moe_gain_row, router_wide, slot_row, cot, cot_sent,
        expert_in[0], expert_out[0],
    )
    att_grad, cot_all = lax.optimization_barrier((att_grad, cot_all))

    expert_count = lax.axis_size("expert")
    dp_sizes = [2, 2] if dp_count == 4 else [dp_count]
    sizes = [expert_count, *dp_sizes, ctx_count]
    plan = tail_plan(sizes, width)
    group, pieces, lengths = plan
    units = group * pieces

    stacked = 2 if ctx_count <= 4 else 1
    table_rows = heads * TILE // width
    small_rows = -(-(2 + experts + table_rows) // 8) * 8
    slice_width = hidden_units // dp_count
    weights, small, input_grad, in_grad, out_grad, layer_out, _ = pl.pallas_call(
        functools.partial(back_kernel, experts, plan),
        out_shape=[
            shape((units, 16, width), bf16), shape((small_rows, width), f32), shape((tokens, width), f32),
            shape((width, slice_width), f32), shape((slice_width, width), f32), shape((tokens, width), bf16),
            shape((dp_count - 1, experts, block_rows, width), bf16),
        ],
        in_specs=[
            smem(), vmem(), vmem(), any_space, any_space, vmem(), vmem(), vmem(), any_space, vmem(),
            vmem(), vmem(), vmem(), vmem(), any_space, vmem(), any_space, any_space, any_space,
            any_space, vmem(), any_space, any_space, any_space, any_space, any_space, vmem(),
        ],
        out_specs=[vmem()] * 6 + [any_space],
        scratch_shapes=[
            pltpu.VMEM((2, PB, width), bf16),
            pltpu.VMEM((2, PB, width), bf16),
            pltpu.VMEM((2, PB, width), bf16),
            pltpu.VMEM((stacked * PB, tokens), f32),
            pltpu.VMEM((stacked * PB, tokens), f32),
            pltpu.VMEM((stacked * PB, tokens), bf16),
            pltpu.VMEM((stacked * PB, tokens), bf16),
            pltpu.VMEM((width, tokens), f32),
            pltpu.VMEM((PB, width), bf16),
            pltpu.VMEM((PB, width), bf16),
            pltpu.VMEM((TILE, width), bf16),
            pltpu.VMEM((TILE, width), bf16),
            pltpu.VMEM((PB, TILE), bf16),
            pltpu.VMEM((heads, 8, TILE), f32),
            pltpu.VMEM((1, width), f32),
            pltpu.VMEM((tokens, width), f32),
            pltpu.VMEM((ctx_count - 1 if ctx_count <= 4 else 1, PB, width), bf16),
            pltpu.VMEM((ctx_count - 1, PB, width), bf16),
            pltpu.VMEM((units, 16, width), bf16),
            [pltpu.VMEM((pieces, length, 16, width), bf16) for length in lengths[:-1]],
            [
                pltpu.VMEM((pieces, size - 1, length, 16, width), bf16)
                for size, length in zip(sizes, lengths)
            ],
            pltpu.VMEM((small_rows, width), f32),
            [pltpu.VMEM((size - 1, small_rows, width), f32) for size in (expert_count, dp_count, ctx_count)],
            block_space,
            pltpu.VMEM((width, slice_width), bf16),
            pltpu.VMEM((slice_width, width), bf16),
            pltpu.VMEM((slots, width), bf16),
            pltpu.VMEM((slots, width), bf16),
            pltpu.VMEM((width, slots), bf16),
            pltpu.SemaphoreType.DMA((ctx_count + 2, 3)),
            pltpu.SemaphoreType.DMA((9 + 2 * dp_count,)),
            pltpu.SemaphoreType.DMA((2, 2 * pieces * sum(size - 1 for size in sizes))),
            pltpu.SemaphoreType.DMA((2, expert_count + dp_count + ctx_count - 3)),
            pltpu.SemaphoreType.DMA((2, ctx_count - 1)),
            block_sems,
            pltpu.SemaphoreType.DMA((2, dp_count - 1, experts)),
        ],
        compiler_params=remote_params(0),
        cost_estimate=cost(
            8 * dp_count * slots * width * slice_width + 80 * keys_total * tokens * width,
            60 * width * slice_width,
        ),
        name="back",
    )(
        branch, bias, queries, keys, values, att_grad, lse, delta, normed_all, normed_own,
        attn_gain_row, query_weight, key_weight, value_weight, wo_part, moe_gain_part, router_part, x,
        hidden_grad, hidden, slot_row, result,
        rows_sent, cot_all, expert_in[0], expert_out[0], router_wide,
    )

    matrix_units = width // 16
    steps = 8

    def part_rows(rows, columns=width):
        return pl.BlockSpec((rows // steps, columns), lambda i: (i, 0))

    weights = weights[: 4 * matrix_units].reshape(4, matrix_units, 16, width)
    *weights, in_grad, out_grad, input_grad, layer_out = pl.pallas_call(
        finish_kernel,
        grid=(steps,),
        out_shape=[shape((width, width), f32)] * 4
        + [
            shape((width, slice_width), f32), shape((slice_width, width), f32),
            shape((tokens, width), f32), shape((tokens, width), bf16),
        ],
        in_specs=[
            pl.BlockSpec((4, matrix_units // steps, 16, width), lambda i: (0, i, 0, 0)),
            part_rows(width, slice_width), part_rows(slice_width), part_rows(tokens), part_rows(tokens),
        ],
        out_specs=[part_rows(width)] * 4
        + [part_rows(width, slice_width), part_rows(slice_width), part_rows(tokens), part_rows(tokens)],
        compiler_params=params(),
        cost_estimate=cost(8 * width * width, 48 * width * width),
        name="finish",
    )(weights, in_grad, out_grad, input_grad, layer_out)
    router_grad = small[:experts].T
    hist_sum = small[2 + experts : 2 + experts + table_rows].reshape(heads, TILE)
    last = onehot[:, buckets - 1 :]
    spread = jnp.concatenate([onehot[:, : buckets - 1], last - 1.0], axis=1)
    table_grad = jnp.dot(spread.T, hist_sum.T, precision=lax.Precision.HIGHEST)
    return (
        layer_out[None],
        input_grad[None],
        small[experts],
        weights[3],
        weights[2],
        weights[1],
        weights[0],
        table_grad,
        small[experts + 1],
        router_grad,
        in_grad[None],
        out_grad[None],
    )


def solution(mesh):
    grouped = P(("dp", "expert"), "ctx", None)
    placed = (
        grouped, grouped, grouped, grouped, P(("dp", "expert"), "ctx"),
        P(), P(), P(), P(), P(), P(), P(), P(),
        P(("ctx", "expert"), None, None),
        P(("ctx", "expert"), None, None),
    )
    return jax.shard_map(
        body,
        mesh=mesh,
        in_specs=placed,
        out_specs=(
            grouped, grouped, P(), P(), P(), P(), P(), P(), P(), P(),
            P(("ctx", "expert"), None, "dp"),
            P(("ctx", "expert"), "dp", None),
        ),
        check_vma=False,
    )
```

```python
import functools

import jax
import jax.numpy as jnp
from jax import lax
from jax.experimental import pallas as pl
from jax.experimental.pallas import tpu as pltpu
from jax.sharding import PartitionSpec as P

PB = 256
TILE = 128
CHUNKS = 2

bucket_edges = (19, 21, 24, 27, 31, 35, 40, 46, 52, 59, 67, 77, 87, 99, 113)
norm_eps = 1e-06
masked_score = -1e30
gelu_scale = 0.7978845608
gelu_cube = 0.044715

bf16 = jnp.bfloat16
f32 = jnp.float32
VMEM_LIMIT = 121 * 512 * 1024


def dot_nn(a, b):
    return jnp.dot(a, b, preferred_element_type=f32)


def dot_nt(a, b):
    return lax.dot_general(a, b, (((1,), (1,)), ((), ())), preferred_element_type=f32)


def dot_tn(a, b):
    return lax.dot_general(a, b, (((0,), (0,)), ((), ())), preferred_element_type=f32)


def two_parts(a):
    high = a.astype(bf16)
    return high, (a - high.astype(f32)).astype(bf16)


def vmem():
    return pl.BlockSpec(memory_space=pltpu.VMEM)


def smem():
    return pl.BlockSpec(memory_space=pltpu.SMEM)


def params():
    return pltpu.CompilerParams(vmem_limit_bytes=VMEM_LIMIT)


def remote_params(number):
    return pltpu.CompilerParams(
        vmem_limit_bytes=VMEM_LIMIT, collective_id=number, has_side_effects=True
    )


def cost(flops, nbytes):
    return pl.CostEstimate(flops=int(flops), bytes_accessed=int(nbytes), transcendentals=0)


def shape(dims, kind):
    return jax.ShapeDtypeStruct(dims, kind)


def inverse_rms(x):
    return lax.rsqrt(jnp.mean(x * x, axis=-1, keepdims=True) + norm_eps)


def bucket_onehot(buckets):
    distance = jnp.arange(TILE, dtype=jnp.int32)
    ids = jnp.minimum(distance, 16)
    for edge in bucket_edges:
        ids = ids + (distance >= edge).astype(jnp.int32)
    return (ids[:, None] == jnp.arange(buckets, dtype=jnp.int32)[None, :]).astype(f32)


def near_index(first):
    rows = lax.broadcasted_iota(jnp.int32, (TILE, TILE), 0)
    lanes = lax.broadcasted_iota(jnp.int32, (TILE, TILE), 1)
    return first + lanes - rows


def near_tiles(ctx_at, plen):
    start = ctx_at * PB
    return (
        (start, 0, 0, False),
        (start, TILE, TILE, False),
        (start + TILE, TILE, 0, False),
        (plen, PB, 0, False),
        (plen, PB + TILE, TILE, False),
        (plen + TILE, PB + TILE, 0, False),
        (plen + PB, PB, TILE, False),
        (start - TILE, 0, TILE, True),
    )


def add_near(s_ref, bias_row, ctx_at, plen):
    source = jnp.broadcast_to(bias_row, (TILE, TILE))
    add_tiles(s_ref, source, ctx_at, near_tiles(ctx_at, plen))


def add_tiles(s_ref, source, ctx_at, tiles):
    for first_row, first_lane, gap, guarded in tiles:
        def work(first_row=first_row, first_lane=first_lane, gap=gap):
            rows = pl.ds(first_row if isinstance(first_row, int) else pl.multiple_of(first_row, 16), TILE)
            lanes = slice(first_lane, first_lane + TILE)
            index = jnp.clip(near_index(gap), 0, TILE - 1)
            s_ref[rows, lanes] = s_ref[rows, lanes] + jnp.take_along_axis(source, index, axis=1)

        if guarded:
            pl.when(ctx_at > 0)(work)
        else:
            work()


def scores_to(s_ref, keys, queries, plen):
    s_ref[:plen, :] = dot_nt(keys[:plen], queries)
    s_ref[plen:, PB:] = dot_nt(keys[plen:], queries[PB:])


def limits(ctx_at, branch, tokens):
    lane = lax.broadcasted_iota(jnp.int32, (1, tokens), 1)
    return jnp.where(lane < PB, ctx_at * PB + lane + 1, branch - TILE)


def window_rows(first, count, branch):
    rows = lax.broadcasted_iota(jnp.int32, (TILE, count), 0)
    places = lax.broadcasted_iota(jnp.int32, (TILE, count), 1) + first
    return (places == rows + (branch - TILE)).astype(bf16)


def row_steps(first, count, lanes):
    return first + lax.broadcasted_iota(jnp.int32, (count, lanes), 0)


def own_allowed(first, count, lanes):
    return row_steps(first, count, lanes) <= lax.broadcasted_iota(jnp.int32, (count, lanes), 1)


def head_lanes(half):
    return lax.broadcasted_iota(jnp.int32, (1, TILE), 1) // (TILE // 2) == half


def pick_rows(pieces, lanes):
    row = lax.broadcasted_iota(jnp.int32, (8, lanes), 0)
    return jnp.where(row == 0, pieces[0], jnp.where(row == 1, pieces[1], 0.0))


def fold8(x, op):
    return op(x.reshape(x.shape[0] // 8, 8, x.shape[1]), axis=0)


def owner_device(index):
    cores = lax.axis_size("expert")
    return {"ctx": index // cores, "expert": lax.rem(index, cores)}


def owners():
    cores = lax.axis_size("expert")
    count = cores * lax.axis_size("ctx")
    return count, lax.axis_index("ctx") * cores + lax.axis_index("expert")


def greet_owners():
    count, me = owners()
    barrier = pltpu.get_barrier_semaphore()

    def greet(ahead, _):
        pl.semaphore_signal(
            barrier, inc=1, device_id=owner_device(lax.rem(me + ahead, count)),
            device_id_type=pl.DeviceIdType.MESH,
        )
        return 0

    lax.fori_loop(1, count, greet, 0)
    pl.semaphore_wait(barrier, count - 1)


def block_copy(source, target, sems, ahead):
    count, me = owners()
    peer = lax.rem(me + ahead, count)
    return pltpu.make_async_remote_copy(
        src_ref=source.at[peer], dst_ref=target.at[me],
        send_sem=sems.at[0, ahead - 1], recv_sem=sems.at[1, ahead - 1],
        device_id=owner_device(peer), device_id_type=pl.DeviceIdType.MESH,
    )


def await_blocks(source, target, sems, sent, received):
    def one(ahead, _):
        copy = block_copy(source, target, sems, ahead)
        if received:
            copy.wait_recv()
        if sent:
            copy.wait_send()
        return 0

    lax.fori_loop(1, owners()[0], one, 0)


def place_rows(slot_row, index, block_rows, tokens):
    rows = lax.broadcasted_iota(jnp.int32, (block_rows, tokens), 0) + index * block_rows
    return (rows == slot_row).astype(bf16)


def front_kernel(
    capacity,
    branch_ref, bias_ref, x_ref, cot_ref, gain_ref, route_row, arrive_row,
    wq_ref, wk_ref, wv_ref,
    slot_out, cot_out, normed_own_out, normed_out, q_ref, k_out, v_out, att_out, lse_out,
    prompt_ref, send_ref, s_ref, p_ref, prompt_sems, cot_sems,
):
    branch = branch_ref[0, 0]
    ctx_at, ctx_count = lax.axis_index("ctx"), lax.axis_size("ctx")
    plen = PB * ctx_count
    tokens, width = x_ref.shape
    own = tokens - PB
    gain = gain_ref[...].astype(f32)
    count, me = owners()
    block_rows = send_ref.shape[1]
    greet_owners()

    chunk = PB // CHUNKS

    def pass_on(step, up, c):
        block = ctx_at - step if up else ctx_at + step
        ahead = ctx_at + 1 if up else ctx_at - 1
        fits = (block >= 0) & (ahead < ctx_count) if up else (block < ctx_count) & (ahead >= 0)
        piece = pl.ds(c * chunk, chunk)
        source = x_ref.at[piece] if step == 0 else prompt_ref.at[block, piece]
        copy = pltpu.make_async_remote_copy(
            src_ref=source, dst_ref=prompt_ref.at[block, piece],
            send_sem=prompt_sems.at[0, int(up), step, c], recv_sem=prompt_sems.at[1, int(up), step, c],
            device_id={"ctx": ahead}, device_id_type=pl.DeviceIdType.MESH,
        )
        return fits, copy

    def arrival(step, up, c):
        block = ctx_at - step - 1 if up else ctx_at + step + 1
        fits = block >= 0 if up else block < ctx_count
        place = prompt_ref.at[block, pl.ds(c * chunk, chunk)]
        copy = pltpu.make_async_remote_copy(
            src_ref=place, dst_ref=place,
            send_sem=prompt_sems.at[0, int(up), step, c], recv_sem=prompt_sems.at[1, int(up), step, c],
            device_id={"ctx": ctx_at}, device_id_type=pl.DeviceIdType.MESH,
        )
        return fits, block, copy

    for c in range(CHUNKS):
        for up in (True, False):
            fits, copy = pass_on(0, up, c)
            pl.when(fits)(copy.start)

    x = x_ref[...].astype(f32)
    normed_own_out[...] = (x * inverse_rms(x) * gain).astype(bf16)

    def column(i, _):
        cols = pl.ds(pl.multiple_of(i * 256, 256), 256)
        q_ref[:, cols] = dot_nn(normed_own_out[...], wq_ref[:, cols]).astype(bf16)
        k_out[plen : plen + own, cols] = dot_nn(normed_own_out[PB:, :], wk_ref[:, cols]).astype(bf16)
        v_out[plen : plen + own, cols] = dot_nn(normed_own_out[PB:, :], wv_ref[:, cols]).astype(bf16)
        return 0

    lax.fori_loop(0, width // 256, column, 0)

    def project(block):
        rows = pl.ds(pl.multiple_of(block * PB, PB), PB)

        def prompt_column(i, _):
            cols = pl.ds(pl.multiple_of(i * 256, 256), 256)
            k_out[rows, cols] = dot_nn(normed_out[rows, :], wk_ref[:, cols]).astype(bf16)
            v_out[rows, cols] = dot_nn(normed_out[rows, :], wv_ref[:, cols]).astype(bf16)
            return 0

        lax.fori_loop(0, width // 256, prompt_column, 0)

    def take(block):
        x = prompt_ref[block].astype(f32)
        rows = pl.ds(pl.multiple_of(block * PB, PB), PB)
        normed_out[rows, :] = (x * inverse_rms(x) * gain).astype(bf16)
        project(block)

    def down(row):
        column = jnp.broadcast_to(row[...].astype(f32), (TILE, tokens)).T
        return jnp.concatenate([column] * (tokens // TILE), axis=1)

    same = down(route_row) == route_row[...].astype(f32)
    earlier = down(arrive_row) < arrive_row[...].astype(f32)
    rank = jnp.sum(jnp.where(same & earlier, 1.0, 0.0), axis=0, keepdims=True).astype(jnp.int32)
    slot = jnp.where(rank < capacity, route_row[...] * block_rows + rank, count * block_rows)
    slot_out[...] = slot

    def lay_out(peer, _):
        rows = dot_nn(place_rows(slot_out[...], peer, block_rows, tokens), cot_ref[...]).astype(bf16)
        send_ref[peer] = rows
        return 0

    def lay_out_all():
        lax.fori_loop(0, count, lay_out, 0)
        cot_out[me] = send_ref[me]

    for step in range(ctx_count - 1):
        if step == ctx_count - 2:
            lay_out_all()
        for c in range(CHUNKS):
            for up in (True, False):
                fits, block, copy = arrival(step, up, c)
                pl.when(fits)(copy.wait_recv)
                if step < ctx_count - 2:
                    fits, copy = pass_on(step + 1, up, c)
                    pl.when(fits)(copy.start)
        if step == 0:
            normed_out[pl.ds(pl.multiple_of(ctx_at * PB, PB), PB), :] = normed_own_out[:PB, :]
            project(ctx_at)
        for up in (True, False):
            fits, block, copy = arrival(step, up, 0)
            pl.when(fits)(functools.partial(take, block))

    def send_cots():
        def send_cot(ahead, _):
            block_copy(send_ref, cot_out, cot_sems, ahead).start()
            return 0

        lax.fori_loop(1, count, send_cot, 0)

    def window_column(i, _):
        cols = pl.ds(pl.multiple_of(i * 256, 256), 256)
        window = window_rows(0, plen, branch)
        k_out[plen + own :, cols] = dot_nn(window, k_out[:plen, cols]).astype(bf16)
        v_out[plen + own :, cols] = dot_nn(window, v_out[:plen, cols]).astype(bf16)
        return 0

    lax.fori_loop(0, width // 256, window_column, 0)
    p_ref[plen:, :PB] = jnp.zeros((own + TILE, PB), bf16)
    limit = limits(ctx_at, branch, tokens)

    def pair(g, _):
        pl.when(g == 1)(send_cots)
        lanes = pl.ds(pl.multiple_of(g * TILE, TILE), TILE)
        queries = q_ref[:, lanes]
        keys = k_out[:, lanes]
        values_t = v_out[:, lanes].T
        bias = bias_ref[g]
        lse_rows, att_rows = [], []
        for half in range(2):
            scores_to(s_ref, jnp.where(head_lanes(half), keys, jnp.zeros_like(keys)), queries, plen)
            add_near(s_ref, bias[half : half + 1, :], ctx_at, plen)

            def top_of(i, top):
                for part in range(0, TILE, 32):
                    first = pl.multiple_of(i * TILE + part, 32)
                    rows = pl.ds(first, 32)
                    s = jnp.where(row_steps(first, 32, tokens) < limit, s_ref[rows, :], masked_score)
                    s_ref[rows, :] = s
                    top = jnp.maximum(top, fold8(s, jnp.max))
                return top

            top = lax.fori_loop(0, plen // TILE, top_of, jnp.full((8, tokens), masked_score, f32))
            own_top = jnp.full((8, own), masked_score, f32)
            for i in range(own // TILE + 1):
                rows = slice(plen + i * TILE, plen + (i + 1) * TILE)
                s = s_ref[rows, PB:]
                if i < own // TILE:
                    s = jnp.where(own_allowed(i * TILE, TILE, own), s, masked_score)
                    s_ref[rows, PB:] = s
                own_top = jnp.maximum(own_top, fold8(s, jnp.max))
            top = jnp.concatenate([top[:, :PB], jnp.maximum(top[:, PB:], own_top)], axis=1)
            top = jnp.max(top, axis=0, keepdims=True)

            def weigh(i, total):
                for part in range(0, TILE, 32):
                    rows = pl.ds(pl.multiple_of(i * TILE + part, 32), 32)
                    p = jnp.exp(s_ref[rows, :] - top)
                    p_ref[rows, :] = p.astype(bf16)
                    total = total + fold8(p, jnp.sum)
                return total

            total = lax.fori_loop(0, plen // TILE, weigh, jnp.zeros((8, tokens), f32))
            own_total = jnp.zeros((8, own), f32)
            for i in range(own // TILE + 1):
                rows = slice(plen + i * TILE, plen + (i + 1) * TILE)
                p = jnp.exp(s_ref[rows, PB:] - top[:, PB:])
                p_ref[rows, PB:] = p.astype(bf16)
                own_total = own_total + fold8(p, jnp.sum)
            total = jnp.concatenate([total[:, :PB], total[:, PB:] + own_total], axis=1)
            total = jnp.sum(total, axis=0, keepdims=True)
            rows = slice(half * 64, half * 64 + 64)
            att_rows.append((dot_nn(values_t[rows, :], p_ref[...]) / total).astype(bf16))
            lse_rows.append(top + jnp.log(total))
        att_out[lanes, :] = jnp.concatenate(att_rows, axis=0)
        lse_out[g] = pick_rows(lse_rows, tokens)
        return 0

    lax.fori_loop(0, width // TILE, pair, 0)
    await_blocks(send_ref, cot_out, cot_sems, True, True)
    for step in range(ctx_count - 1):
        for c in range(CHUNKS):
            for up in (True, False):
                fits, copy = pass_on(step, up, c)
                pl.when(fits)(copy.wait_send)


def router_probs(logits, lane, experts):
    logits = jnp.where(lane < experts, logits, masked_score)
    logits = jnp.exp(logits - jnp.max(logits, axis=1, keepdims=True))
    return logits / jnp.sum(logits, axis=1, keepdims=True)


def gelu_parts(v):
    t = jnp.tanh(gelu_scale * (v + gelu_cube * (v * v * v)))
    half = 0.5 * (1.0 + t)
    slope = half + 0.5 * v * (1.0 - t * t) * (gelu_scale + (3.0 * gelu_scale * gelu_cube) * (v * v))
    return v * half, slope


def expert_kernel(
    experts,
    att_ref, x_ref, wo_ref, gain_ref, router_ref, slot_row, cot_ref, cot_rows, win_hbm, wout_hbm,
    rows_out, router_out, hidden_grad_out, wo_grad_out, att_grad_out, delta_out, gain_grad_out,
    result_out, hidden_ref,
    moe_ref, send_ref, win_ref, wout_ref, group_rows, sent_ref, result_acc, grad_acc,
    grad_send, grad_recv, low_ref, att_t_ref, rows_sems, grad_sems, load_sems,
):
    tokens, width = x_ref.shape
    count, me = owners()
    block_rows = send_ref.shape[1]
    hidden_units = win_ref.shape[1]
    loads = [
        pltpu.make_async_copy(win_hbm, win_ref, load_sems.at[0]),
        pltpu.make_async_copy(wout_hbm, wout_ref, load_sems.at[1]),
    ]
    for copy in loads:
        copy.start()
    greet_owners()

    moe_ref[...] = att_ref[...].T

    def column(i, _):
        cols = pl.ds(pl.multiple_of(i * 256, 256), 256)
        hidden_ref[:, cols] = x_ref[:, cols].astype(f32) + dot_nn(moe_ref[...], wo_ref[:, cols])
        return 0

    lax.fori_loop(0, width // 256, column, 0)
    hidden = hidden_ref[...]
    moe_ref[...] = (hidden * inverse_rms(hidden) * gain_ref[...].astype(f32)).astype(bf16)

    members = 2 * lax.axis_size("expert") if lax.axis_size("ctx") % 2 == 0 else count
    groups = count // members
    my_group = me // members

    def send_rows(ahead, _):
        peer = lax.rem(me + ahead, count)
        place = place_rows(slot_row[...], peer, block_rows, tokens)
        send_ref[peer] = dot_nn(place, moe_ref[...]).astype(bf16)
        block_copy(send_ref, rows_out, rows_sems, ahead).start()
        return 0

    def send_group(g, _):
        base = lax.rem(my_group + g, groups) * members

        def member(i, _):
            ahead = lax.rem(base + i - me + count, count)
            pl.when(ahead > 0)(lambda: (send_rows(ahead, 0), None)[1])
            return 0

        return lax.fori_loop(0, members, member, 0)

    lax.fori_loop(0, groups, send_group, 0)
    rows_out[me] = dot_nn(place_rows(slot_row[...], me, block_rows, tokens), moe_ref[...]).astype(bf16)

    router_out[...] = jnp.zeros_like(router_out)
    for copy in loads:
        copy.wait()

    def group(g, _):
        base = lax.rem(my_group + g, groups) * members

        def arrive(i, _):
            behind = lax.rem(me - base - i + count, count)
            pl.when(behind > 0)(lambda: block_copy(send_ref, rows_out, rows_sems, behind).wait_recv())
            return 0

        lax.fori_loop(0, members, arrive, 0)
        blocks = pl.ds(base, members)
        size = members * block_rows
        group_rows[...] = rows_out[blocks].reshape(size, width)
        slot_lane = lax.broadcasted_iota(jnp.int32, (size, TILE), 1)
        mine = slot_lane == me
        probs = router_probs(dot_nn(group_rows[...], router_ref[...]), slot_lane, experts)
        gate = jnp.sum(jnp.where(mine, probs, 0.0), axis=1, keepdims=True)
        cot_group = cot_rows[blocks].reshape(size, width).astype(f32)
        sent_ref[...] = (gate * cot_group).astype(bf16)
        result_acc[...] = jnp.zeros_like(result_acc)
        grad_acc[...] = jnp.zeros_like(grad_acc)

        def units(i, _):
            cols = pl.ds(pl.multiple_of(i * width, width), width)
            act, slope = gelu_parts(dot_nn(group_rows[...], win_ref[:, cols]))
            result_acc[...] += dot_nn(act.astype(bf16), wout_ref[cols, :])
            pre_grad = (dot_nt(sent_ref[...], wout_ref[cols, :]) * slope).astype(bf16)
            grad_acc[...] += dot_nt(pre_grad, win_ref[:, cols])
            return 0

        lax.fori_loop(0, hidden_units // width, units, 0)
        result = result_acc[...].astype(bf16)
        gate_grad = jnp.sum(cot_group * result.astype(f32), axis=1, keepdims=True)
        logit_grad = (gate_grad * gate) * (jnp.where(mine, 1.0, 0.0) - probs)
        high, low = two_parts(logit_grad)
        grad = grad_acc[...] + (dot_nt(high, router_ref[...]) + dot_nt(low, router_ref[...]))
        grad_send[blocks] = grad.astype(bf16).reshape(members, block_rows, width)
        gated = (gate * result.astype(f32)).astype(bf16)
        result_out[blocks] = gated.reshape(members, block_rows, width)

        def give(i, _):
            ahead = lax.rem(base + i - me + count, count)

            @pl.when(ahead > 0)
            def _():
                block_copy(grad_send, grad_recv, grad_sems, ahead).start()

            return 0

        lax.fori_loop(0, members, give, 0)
        router_out[...] += dot_tn(high, group_rows[...]) + dot_tn(low, group_rows[...])
        return 0

    lax.fori_loop(0, groups, group, 0)
    grad_recv[me] = grad_send[me]

    slots = count * block_rows
    place = place_rows(slot_row[...], 0, slots, tokens)
    await_blocks(grad_send, grad_recv, grad_sems, False, True)
    moe_grad = dot_tn(place, grad_recv[...].reshape(slots, width))
    hidden = hidden_ref[...]
    inverse = inverse_rms(hidden)
    scaled = hidden * inverse
    gain_grad_out[...] = jnp.sum(moe_grad * scaled, axis=0, keepdims=True)
    through = moe_grad * gain_ref[...].astype(f32)
    shared = jnp.mean(through * scaled, axis=1, keepdims=True)
    hidden_grad = cot_ref[...].astype(f32) + inverse * (through - scaled * shared)
    hidden_grad_out[...] = hidden_grad
    low_ref[...] = hidden_grad.astype(bf16)

    def back_column(i, _):
        cols = pl.ds(pl.multiple_of(i * 256, 256), 256)
        wo_grad = dot_nn(att_ref[...], low_ref[:, cols]).astype(bf16)
        wo_grad_out[:, :, cols] = wo_grad.reshape(width // 16, 16, 256)
        att_grad_out[:, cols] = dot_nt(low_ref[...], wo_ref[cols, :]).astype(bf16)
        att_t_ref[cols, :] = dot_nt(wo_ref[cols, :], low_ref[...]).astype(bf16)
        return 0

    lax.fori_loop(0, width // 256, back_column, 0)

    def pair(g, _):
        rows = pl.ds(pl.multiple_of(g * TILE, TILE), TILE)
        both = att_ref[rows, :].astype(f32) * att_t_ref[rows, :].astype(f32)
        delta_out[g] = pick_rows(
            [jnp.sum(both[:64], axis=0, keepdims=True), jnp.sum(both[64:], axis=0, keepdims=True)],
            tokens,
        )
        return 0

    lax.fori_loop(0, width // TILE, pair, 0)
    await_blocks(send_ref, rows_out, rows_sems, True, False)
    await_blocks(grad_send, grad_recv, grad_sems, True, False)


class Axis:
    def __init__(self, name, size, step=1):
        place = lax.axis_index(name)
        self.name, self.size, self.step, self.place = name, size, step, place
        self.index = lax.rem(place // step, size)

    def at(self, ahead):
        return lax.rem(self.index + ahead, self.size)

    def peer(self, ahead):
        return {self.name: self.place + (self.at(ahead) - self.index) * self.step}


def mesh_axes():
    dp, ctx, expert = lax.axis_size("dp"), lax.axis_size("ctx"), lax.axis_size("expert")
    cores, lines = Axis("expert", expert), Axis("ctx", ctx)
    if dp == 4:
        near, far = Axis("dp", 2, 1), Axis("dp", 2, 2)
        return [[cores, near, far, lines], [cores, far, near, lines]]
    return [[cores, Axis("dp", dp), lines]] * 2


def push(source, target, sems, slot, device):
    copy = pltpu.make_async_remote_copy(
        src_ref=source, dst_ref=target, send_sem=sems.at[0, slot], recv_sem=sems.at[1, slot],
        device_id=device, device_id_type=pl.DeviceIdType.MESH,
    )
    copy.start()
    return copy


def back_kernel(
    experts, plan,
    branch_ref, bias_ref, q_ref, k_hbm, v_hbm, att_grad_ref, lse_ref, delta_ref, normed_hbm, normed_own_ref,
    gain_ref, wq_ref, wk_ref, wv_ref, wo_part_hbm, moe_gain_ref, router_part_hbm, x_hbm, hidden_grad_hbm,
    hidden_hbm, slot_row, result_hbm, rows_hbm, cot_hbm, win_hbm, wout_hbm, router_ref,
    full_ref, small_out, input_out, in_out, out_out, layer_out, rows_all,
    k_ref, v_ref, normed_ref, s_ref, dp_ref, p_ref, ds_ref, dq_ref, dk_ref, dv_ref, window_k, window_v, picked_ref,
    hist_ref, gain_sum,
    local_ref, shared_send, shared_recv, parts_ref, acc_refs, recv_refs, small_ref, small_recv,
    result_recv, win_ref, wout_ref, rows_ref, cot_ref, rows_t,
    block_sems, load_sems, sems, small_sems, shared_sems, result_sems, rows_sems,
):
    group, pieces, lengths = plan
    flows = mesh_axes()
    branch = branch_ref[0, 0]
    ctx_at = lax.axis_index("ctx")
    ctx_count, dp_count = lax.axis_size("ctx"), lax.axis_size("dp")
    tokens, width = q_ref.shape
    own = tokens - PB
    plen = PB * ctx_count
    count, me = owners()
    lines, columns_dp = Axis("ctx", ctx_count), Axis("dp", dp_count)
    whole_axes = [Axis("expert", lax.axis_size("expert")), columns_dp, lines]
    gain = gain_ref[...].astype(f32)
    limit = limits(ctx_at, branch, tokens)
    blocks = ctx_count + 2
    rows_16 = width // 16

    def block_loads(i):
        size = TILE if i == 1 else PB
        rows = (plen, plen + own)[i] if i < 2 else pl.multiple_of(lines.at(i - 1) * PB, PB)
        sources = [(k_hbm, k_ref, 0), (v_hbm, v_ref, 1)]
        if 2 <= i < blocks - 1:
            sources.append((normed_hbm, normed_ref, 2))
        return [
            pltpu.make_async_copy(
                source.at[pl.ds(rows, size)], target.at[i % 2, pl.ds(0, size)], block_sems.at[i, n]
            )
            for source, target, n in sources
        ]

    for copy in block_loads(0):
        copy.start()
    slice_width = win_ref.shape[1]
    part = pl.ds(pl.multiple_of(lax.axis_index("dp") * slice_width, slice_width), slice_width)
    weight_loads = [
        pltpu.make_async_copy(win_hbm.at[:, part], win_ref, load_sems.at[0]),
        pltpu.make_async_copy(wout_hbm.at[part], wout_ref, load_sems.at[1]),
    ]
    own_result = pltpu.make_async_copy(result_hbm.at[me], result_recv.at[me], load_sems.at[2])
    wo_load = pltpu.make_async_copy(wo_part_hbm, parts_ref.at[pl.ds(0, rows_16)], load_sems.at[5 + 2 * dp_count])
    router_load = pltpu.make_async_copy(
        router_part_hbm.at[pl.ds(0, experts)], small_ref.at[pl.ds(0, experts)], load_sems.at[7 + 2 * dp_count]
    )
    for copy in [wo_load, *weight_loads, own_result, router_load]:
        copy.start()

    barrier = pltpu.get_barrier_semaphore()

    def greet(ahead, _):
        pl.semaphore_signal(
            barrier, inc=1, device_id=owner_device(lax.rem(me + ahead, count)),
            device_id_type=pl.DeviceIdType.MESH,
        )
        return 0

    lax.fori_loop(1, count, greet, 0)
    for ahead in range(1, dp_count):
        pl.semaphore_signal(
            barrier, inc=1, device_id=columns_dp.peer(ahead), device_id_type=pl.DeviceIdType.MESH
        )
    pl.semaphore_wait(barrier, count - 1 + dp_count - 1)

    slots_of = {}

    def slot(*key):
        return slots_of.setdefault(key, len(slots_of))

    started = []

    def reduce_start(j, s):
        axis, length = flows[j % 2][s], lengths[s]
        copies = []
        for ahead in range(1, axis.size):
            target = axis.at(ahead)
            if s == 0:
                source = parts_ref.at[pl.ds(j * group + target * length, length)]
            else:
                source = acc_refs[s - 1].at[j, pl.ds(target * length, length)]
            there = recv_refs[s].at[j, ahead - 1]
            copies.append(push(source, there, sems, slot("r", j, s, ahead), axis.peer(ahead)))
        started.extend(copies)
        return copies

    def base_of(j, s):
        base = j * group
        for t in range(s + 1):
            base = base + flows[j % 2][t].index * lengths[t]
        return base

    def reduce_finish(j, s, copies):
        axis, length = flows[j % 2][s], lengths[s]
        for copy in copies:
            copy.wait_recv()
        last = s == len(lengths) - 1

        size = 4 if length % 4 == 0 else 1

        def some(u, _):
            if s == 0:
                total = parts_ref[pl.ds(base_of(j, 0) + u * size, size)].astype(f32)
            else:
                total = acc_refs[s - 1][j, pl.ds(axis.index * length + u * size, size)].astype(f32)
            for ahead in range(1, axis.size):
                total = total + recv_refs[s][j, ahead - 1, pl.ds(u * size, size)].astype(f32)
            if last:
                full_ref[pl.ds(base_of(j, s) + u * size, size)] = total.astype(bf16)
            else:
                acc_refs[s][j, pl.ds(u * size, size)] = total.astype(bf16)
            return 0

        lax.fori_loop(0, length // size, some, 0)

    def spread_start(j, s):
        axis, length = flows[j % 2][s], lengths[s]
        here = full_ref.at[pl.ds(base_of(j, s), length)]
        copies = [
            push(here, here, sems, slot("s", j, s, ahead), axis.peer(ahead))
            for ahead in range(1, axis.size)
        ]
        started.extend(copies)
        return copies

    def small_slot(s, ahead):
        return sum(axis.size - 1 for axis in whole_axes[:s]) + ahead - 1

    def small_start(s):
        axis = whole_axes[s]
        copies = [
            push(small_ref, small_recv[s].at[ahead - 1], small_sems, small_slot(s, ahead), axis.peer(ahead))
            for ahead in range(1, axis.size)
        ]
        return copies

    def small_finish(s, copies):
        axis = whole_axes[s]
        for copy in copies:
            copy.wait()
        mine = small_ref[...]
        total = jnp.zeros_like(mine)
        for index in range(axis.size):
            piece = mine
            for ahead in range(1, axis.size):
                piece = jnp.where(axis.at(axis.size - ahead) == index, small_recv[s][ahead - 1], piece)
            total = total + piece
        if s == len(whole_axes) - 1:
            small_out[...] = total
        else:
            small_ref[...] = total

    stages = len(lengths)
    early = pieces > 1 and group <= rows_16
    begin = [blocks + j // 2 for j in range(pieces)]
    if early:
        begin = [blocks - 1] + [blocks + (j - 1) // 3 for j in range(1, pieces)]
    pending = {}

    def advance(time):
        for j in sorted(range(pieces), key=lambda j: begin[j]):
            s = time - begin[j]
            if not 0 <= s < 2 * stages:
                continue
            if s < stages:
                reduce_finish(j, s, pending[j, s])
                if s + 1 < stages:
                    pending[j, s + 1] = reduce_start(j, s + 1)
                else:
                    pending[j, s + 1] = spread_start(j, s)
            else:
                for copy in pending[j, s]:
                    copy.wait_recv()
                if s + 1 < 2 * stages:
                    pending[j, s + 1] = spread_start(j, 2 * stages - 1 - (s + 1))

    def put(first, cols, value):
        rows = value.shape[0]
        parts_ref[first // 16 : (first + rows) // 16, :, cols] = value.astype(bf16).reshape(
            rows // 16, 16, value.shape[1]
        )

    def columns(work):
        def column(i, _):
            work(pl.ds(pl.multiple_of(i * 256, 256), 256))
            return 0

        lax.fori_loop(0, width // 256, column, 0)

    if parts_ref.shape[0] > 4 * rows_16:
        extra = parts_ref.shape[0] - 4 * rows_16
        parts_ref[4 * rows_16 :] = jnp.zeros((extra, 16, width), bf16)
    wo_load.wait()
    if early:
        pending[0, 0] = reduce_start(0, 0)

    def give_result(ahead, _):
        block_copy(result_hbm, result_recv, result_sems, ahead).start()
        return 0

    lax.fori_loop(1, count, give_result, 0)

    def rows_copy(ahead, e):
        return pltpu.make_async_remote_copy(
            src_ref=rows_hbm.at[e], dst_ref=rows_all.at[ahead - 1, e],
            send_sem=rows_sems.at[0, ahead - 1, e], recv_sem=rows_sems.at[1, ahead - 1, e],
            device_id=columns_dp.peer(ahead), device_id_type=pl.DeviceIdType.MESH,
        )

    def each_row_block(act):
        def one(e, _):
            for ahead in range(1, dp_count):
                act(rows_copy(ahead, e))
            return 0

        lax.fori_loop(0, count, one, 0)

    each_row_block(lambda copy: copy.start())

    shared_copies = []
    shared_slots = shared_send.shape[0]
    hist_ref[...] = jnp.zeros_like(hist_ref)
    gain_sum[...] = jnp.zeros_like(gain_sum)
    for i in range(blocks):
        cont, window, at_home = i == 0, i == 1, i == blocks - 1
        remote = i - 1
        size = TILE if window else PB
        for copy in block_loads(i):
            copy.wait()
        if i + 1 < blocks:
            for copy in block_loads(i + 1):
                copy.start()
        block = lines.at(max(remote, 0))
        lanes_from = PB if cont or window else 0
        lanes_used = slice(lanes_from, tokens)
        if cont or at_home:
            near = [
                (0, lanes_from, 0, None),
                (0, lanes_from + TILE, TILE, None),
                (TILE, lanes_from + TILE, 0, None),
            ]
        elif window:
            near = [(0, PB, TILE, None)]
        else:
            near = [(TILE, 0, TILE, block == ctx_at - 1)]

        if not (cont or window):
            places = lax.broadcasted_iota(jnp.int32, (PB, TILE), 0) + block * PB
            picks = lax.broadcasted_iota(jnp.int32, (PB, TILE), 1) + (branch - TILE)
            picked_ref[...] = (places == picks).astype(bf16)

        def pair(g, _, i=i, cont=cont, window=window, size=size, block=block, lanes_used=lanes_used, near=near):
            lanes = pl.ds(pl.multiple_of(g * TILE, TILE), TILE)
            queries = q_ref[lanes_used, lanes]
            grads = att_grad_ref[lanes_used, lanes]
            keys = k_ref[i % 2, :size, lanes]
            values = v_ref[i % 2, :size, lanes]
            keys_t = keys.T
            bias = bias_ref[g]
            dk_parts, dv_parts, dq_parts = [], [], []
            stacked = s_ref.shape[0] // PB
            for halves in [(0, 1)] if stacked == 2 else [(0,), (1,)]:
                total = len(halves) * size

                def masked(rows):
                    return jnp.concatenate([jnp.where(head_lanes(h), rows, jnp.zeros_like(rows)) for h in halves])

                s_ref[:total, lanes_used] = dot_nt(masked(keys), queries)
                dp_ref[:total, lanes_used] = dot_nt(masked(values), grads)
                for n, half in enumerate(halves):
                    offset = n * size
                    lse = lse_ref[g][half : half + 1, lanes_used]
                    delta = delta_ref[g][half : half + 1, lanes_used]
                    source = jnp.broadcast_to(bias[half : half + 1, :], (TILE, TILE))
                    for first, lane, gap, when in near:
                        def add(first=first + offset, lane=lane, gap=gap):
                            there = (slice(first, first + TILE), slice(lane, lane + TILE))
                            index = jnp.clip(near_index(gap), 0, TILE - 1)
                            s_ref[there] = s_ref[there] + jnp.take_along_axis(source, index, axis=1)

                        add() if when is None else pl.when(when)(add)
                    step = 32
                    for first in range(0, size, step):
                        rows = slice(offset + first, offset + first + step)
                        p = jnp.exp(s_ref[rows, lanes_used] - lse)
                        if cont:
                            p = jnp.where(own_allowed(first, step, own), p, 0.0)
                        elif not window:
                            p = jnp.where(row_steps(block * PB + first, step, tokens) < limit, p, 0.0)
                        p_ref[rows, lanes_used] = p.astype(bf16)
                        ds_ref[rows, lanes_used] = (p * (dp_ref[rows, lanes_used] - delta)).astype(bf16)
                    for first, lane, gap, when in near:
                        def collect(first=first + offset, lane=lane, gap=gap, half=half):
                            tile = ds_ref[first : first + TILE, lane : lane + TILE].astype(f32)
                            if gap > 0:
                                tile = jnp.where(near_index(gap) < TILE, tile, 0.0)
                            turn = lax.broadcasted_iota(jnp.int32, (TILE, TILE), 1) + lax.broadcasted_iota(
                                jnp.int32, (TILE, TILE), 0
                            )
                            tile = jnp.take_along_axis(tile, (turn - gap) & (TILE - 1), axis=1)
                            hist_ref[g * 2 + half] += fold8(tile, jnp.sum)

                        collect() if when is None else pl.when(when)(collect)
                dv_all = dot_nn(p_ref[:total, lanes_used], grads)
                dk_all = dot_nn(ds_ref[:total, lanes_used], queries)
                for n, half in enumerate(halves):
                    rows = slice(n * size, n * size + size)
                    dv_parts.append(dv_all[rows])
                    dk_parts.append(dk_all[rows])
                    dq_parts.append(dot_nn(keys_t[half * 64 : half * 64 + 64, :], ds_ref[rows, lanes_used]))
            dq = jnp.concatenate(dq_parts, axis=0)
            if cont:
                dq_ref[lanes, :PB] = jnp.zeros((TILE, PB), f32)
                dq_ref[lanes, PB:] = dq
            else:
                dq_ref[lanes, lanes_used] += dq
            mine = head_lanes(0)
            dv, dk = jnp.where(mine, dv_parts[0], dv_parts[1]), jnp.where(mine, dk_parts[0], dk_parts[1])
            if window:
                window_v[:, lanes], window_k[:, lanes] = dv.astype(bf16), dk.astype(bf16)
            else:
                if not cont:
                    dv = dv + dot_nn(picked_ref[...], window_v[:, lanes])
                    dk = dk + dot_nn(picked_ref[...], window_k[:, lanes])
                dv_ref[:, lanes], dk_ref[:, lanes] = dv.astype(bf16), dk.astype(bf16)
            return 0

        lax.fori_loop(0, width // TILE, pair, 0)

        def block_column(cols, i=i, cont=cont, at_home=at_home, remote=remote):
            if cont:
                normed = normed_own_ref[PB:, cols]
            elif at_home:
                normed = normed_own_ref[:PB, cols]
            else:
                normed = normed_ref[i % 2, :, cols]
            wk_part = dot_nn(rows_t[:, :PB], dk_ref[:, cols])
            wv_part = dot_nn(rows_t[:, :PB], dv_ref[:, cols])
            if cont:
                in_out[:, cols] = wk_part
                out_out[:, cols] = wv_part
            elif not at_home:
                in_out[:, cols] += wk_part
                out_out[:, cols] += wv_part
            else:
                put(width, cols, out_out[:, cols] + wv_part)
                put(2 * width, cols, in_out[:, cols] + wk_part)
            grad = dot_nt(dk_ref[...], wk_ref[cols, :]) + dot_nt(dv_ref[...], wv_ref[cols, :])
            gain_sum[:, cols] += jnp.sum(grad * normed.astype(f32), axis=0, keepdims=True)
            if cont:
                local_ref[PB:, cols] = grad
            elif at_home:
                local_ref[:PB, cols] = grad
            else:
                shared_send[(remote - 1) % shared_slots, :, cols] = grad.astype(bf16)

        if window:
            continue
        if shared_slots < remote < ctx_count:
            shared_copies[remote - 1 - shared_slots].wait_send()
        if cont:
            rows_t[:, :PB] = normed_own_ref[PB:, :].T
        elif at_home:
            rows_t[:, :PB] = normed_own_ref[:PB, :].T
        else:
            rows_t[:, :PB] = normed_ref[i % 2].T
        columns(block_column)
        if 1 <= remote < ctx_count:
            n = remote - 1
            shared_copies.append(
                push(shared_send.at[n % shared_slots], shared_recv.at[n], shared_sems, n, lines.peer(remote))
            )
    started.extend(shared_copies[-shared_slots:])

    def ready(j):
        if j > 0 or not early:
            pending[j, 0] = reduce_start(j, 0)

    done = 3 * rows_16
    for j in range(pieces):
        if (j + 1) * group <= done:
            ready(j)
    rows_ref[:tokens, :] = dq_ref[...].T.astype(bf16)
    rows_t[:, :tokens] = normed_own_ref[...].T

    def query_column(cols):
        put(3 * width, cols, dot_nn(rows_t[:, :tokens], rows_ref[:tokens, cols]))

    columns(query_column)
    for j in range(pieces):
        if (j + 1) * group > done:
            ready(j)

    def query_grad(cols):
        grad = dot_nt(rows_ref[:tokens, :], wq_ref[cols, :])
        gain_sum[:, cols] += jnp.sum(grad * normed_own_ref[:, cols].astype(f32), axis=0, keepdims=True)
        local_ref[:, cols] += grad

    columns(query_grad)
    small_ref[experts:, :] = jnp.zeros((small_ref.shape[0] - experts, width), f32)
    small_ref[experts : experts + 1, :] = gain_sum[...] / gain
    small_ref[experts + 1 : experts + 2, :] = moe_gain_ref[...]
    router_load.wait()
    per_row = width // TILE
    for head in range(hist_ref.shape[0]):
        row, lane = 2 + experts + head // per_row, head % per_row * TILE
        small_ref[row : row + 1, lane : lane + TILE] = jnp.sum(hist_ref[head], axis=0, keepdims=True)
    small_pending = small_start(0)

    slots = rows_ref.shape[0]

    def rows_load(n):
        source = rows_hbm if n == 0 else rows_all.at[n - 1]
        return pltpu.make_async_copy(source, result_recv, load_sems.at[3 + 2 * n])

    hidden_load = pltpu.make_async_copy(hidden_hbm, input_out, load_sems.at[4 + 2 * dp_count])
    hidden_load.start()
    grad_load = pltpu.make_async_copy(hidden_grad_hbm, input_out, load_sems.at[3 + 2 * dp_count])
    x_loads = [
        pltpu.make_async_copy(x_hbm.at[pl.ds(n * PB, PB)], normed_ref.at[n], load_sems.at[6 + 2 * dp_count + 2 * n])
        for n in range(2)
    ]
    for copy in x_loads:
        copy.start()

    def grads_of(n, c):
        if c == 0:
            if n == 0:
                for copy in weight_loads:
                    copy.wait()
            rows_load(n).wait()
            rows_ref[...] = result_recv[...].reshape(slots, width)
            cot_from = columns_dp.at(dp_count - n)
            load = pltpu.make_async_copy(cot_hbm.at[cot_from], result_recv, load_sems.at[4 + 2 * n])
            load.start()
            lane = lax.broadcasted_iota(jnp.int32, (slots, TILE), 1)
            probs = router_probs(dot_nn(rows_ref[...], router_ref[...]), lane, experts)
            gate = jnp.sum(jnp.where(lane == me, probs, 0.0), axis=1, keepdims=True)
            load.wait()
            cot = result_recv[...].reshape(slots, width)
            cot_ref[...] = (gate * cot.astype(f32)).astype(bf16)
            if n == 0:
                each_row_block(lambda copy: copy.wait_recv())
            if n + 1 < dp_count:
                rows_load(n + 1).start()
            rows_t[...] = rows_ref[...].T
        cols = slice(c * 256, c * 256 + 256)
        act, slope = gelu_parts(dot_nn(rows_ref[...], win_ref[:, cols]))
        pre_grad = (dot_nt(cot_ref[...], wout_ref[cols, :]) * slope).astype(bf16)
        out_part = dot_tn(act.astype(bf16), cot_ref[...])
        in_part = dot_nn(rows_t[...], pre_grad)
        if n == 0:
            out_out[cols, :] = out_part
            in_out[:, cols] = in_part
        else:
            out_out[cols, :] += out_part
            in_out[:, cols] += in_part

    def input_back():
        for copy in shared_copies:
            copy.wait_recv()
        for copy in x_loads:
            copy.wait()
        grad_load.wait()
        for first, shared_rows in ((0, True), (PB, False)):
            rows = slice(first, PB if shared_rows else tokens)
            x = normed_ref[0 if shared_rows else 1].astype(f32)
            inverse = inverse_rms(x)
            grad = local_ref[rows, :]
            if shared_rows:
                for n in range(ctx_count - 1):
                    grad = grad + shared_recv[n].astype(f32)
            through = grad * gain
            scaled = x * inverse
            shared = jnp.mean(through * scaled, axis=1, keepdims=True)
            input_out[rows, :] += inverse * (through - scaled * shared)

    def layer():
        own_result.wait()
        await_blocks(result_hbm, result_recv, result_sems, False, True)
        place = place_rows(slot_row[...], 0, slots, tokens)
        returned = dot_tn(place, result_recv[...].reshape(slots, width))
        hidden_load.wait()
        layer_out[...] = (input_out[...] + returned).astype(bf16)
        rows_load(0).start()
        grad_load.start()

    work = [layer]
    work += [functools.partial(grads_of, n, c) for n in range(dp_count) for c in range(slice_width // 256)]
    work += [input_back]
    for time in range(blocks - 1, max(begin) + 2 * stages):
        if time >= blocks:
            advance(time)
        elif early:
            advance(time)
        s = time - blocks
        if 0 <= s < len(whole_axes):
            small_finish(s, small_pending)
            if s + 1 < len(whole_axes):
                small_pending = small_start(s + 1)
        for _ in range(-(-len(work) // (max(begin) + 2 * stages - time))):
            work.pop(0)()
    for copy in started:
        copy.wait_send()
    await_blocks(result_hbm, result_recv, result_sems, True, False)
    each_row_block(lambda copy: copy.wait_send())


def finish_kernel(
    experts, full_ref, in_ref, out_ref, input_ref, layer_ref, small_ref, spread_ref, *results,
):
    weights, rest, (attn_out, moe_out, router_out, table_out) = results[:4], results[4:8], results[8:]
    for n, weight in enumerate(weights):
        weight[...] = full_ref[n].astype(f32).reshape(weight.shape)
    for source, target in zip((in_ref, out_ref, input_ref, layer_ref), rest):
        target[...] = source[...].astype(target.dtype)

    @pl.when(pl.program_id(0) == 0)
    def _():
        router_out[...] = small_ref[:experts, :]
        attn_out[...] = small_ref[experts : experts + 1, :]
        moe_out[...] = small_ref[experts + 1 : experts + 2, :]
        per_row = small_ref.shape[1] // TILE
        hist = []
        for head in range(table_out.shape[0]):
            row, lane = 2 + experts + head // per_row, head % per_row * TILE
            hist.append(small_ref[row : row + 1, lane : lane + TILE])
        table_out[...] = jnp.dot(
            jnp.concatenate(hist, axis=0), spread_ref[...],
            preferred_element_type=f32, precision=lax.Precision.HIGHEST,
        )


def tail_plan(sizes, width):
    group = 1
    for size in sizes:
        group *= size
    units = 4 * width // 16
    pieces = -(-units // group)
    lengths, left = [], group
    for size in sizes:
        left //= size
        lengths.append(left)
    return group, pieces, lengths


def body(
    inputs, cotangent, route, arrival, branch, attn_gain, query_weight, key_weight, value_weight,
    output_weight, rel_table, moe_gain, router_weight, expert_in, expert_out,
):
    x = inputs[0]
    cot = cotangent[0]
    tokens, width = x.shape
    own = tokens - PB
    buckets, heads = rel_table.shape
    experts = router_weight.shape[1]
    capacity = 9 * tokens // (8 * experts)
    block_rows = capacity if capacity % 8 == 0 else -(-capacity // 16) * 16
    slots = experts * block_rows
    ctx_count = lax.axis_size("ctx")
    dp_count = lax.axis_size("dp")
    plen = PB * ctx_count
    keys_total = plen + own + TILE
    hidden_units = expert_in.shape[2]
    pairs = width // TILE
    attn_gain_row = attn_gain.reshape(1, width)
    moe_gain_row = moe_gain.reshape(1, width)
    onehot = bucket_onehot(buckets)
    by_distance = jnp.dot(onehot, rel_table.astype(f32), precision=lax.Precision.HIGHEST).T
    by_distance = by_distance - by_distance[:, TILE - 1 :]
    bias = jnp.pad(by_distance.reshape(pairs, 2, TILE), ((0, 0), (0, 6), (0, 0)))
    router_wide = jnp.pad(router_weight, ((0, 0), (0, TILE - experts)))
    route_row = route.reshape(1, tokens)
    arrive_row = arrival[0]
    blocks = shape((experts, block_rows, width), bf16)
    block_space = pltpu.VMEM((experts, block_rows, width), bf16)
    block_sems = pltpu.SemaphoreType.DMA((2, experts - 1))
    any_space = pl.BlockSpec(memory_space=pl.ANY)

    slot_row, cot_sent, normed_own, normed_all, queries, keys, values, att, lse = pl.pallas_call(
        functools.partial(front_kernel, capacity),
        out_shape=[
            shape((1, tokens), jnp.int32),
            blocks,
            shape((tokens, width), bf16),
            shape((plen, width), bf16),
            shape((tokens, width), bf16),
            shape((keys_total, width), bf16),
            shape((keys_total, width), bf16),
            shape((width, tokens), bf16),
            shape((pairs, 8, tokens), f32),
        ],
        in_specs=[smem()] + [vmem()] * 9,
        out_specs=[vmem()] * 9,
        scratch_shapes=[
            pltpu.VMEM((ctx_count, PB, width), bf16),
            block_space,
            pltpu.VMEM((keys_total, tokens), f32),
            pltpu.VMEM((keys_total, tokens), bf16),
            pltpu.SemaphoreType.DMA((2, 2, ctx_count - 1, CHUNKS)),
            block_sems,
        ],
        compiler_params=remote_params(1),
        cost_estimate=cost(40 * keys_total * tokens * width, 20 * width * width),
        name="front",
    )(
        branch, bias, x, cot, attn_gain_row, route_row, arrive_row,
        query_weight, key_weight, value_weight,
    )
    cot_all = lax.all_gather(cot_sent, "dp", axis=0, tiled=False)

    members = 2 * lax.axis_size("expert") if ctx_count % 2 == 0 else experts
    group_rows = members * block_rows
    (
        rows_sent, router_part, hidden_grad, wo_part, att_grad, delta, moe_gain_part,
        result, hidden,
    ) = pl.pallas_call(
        functools.partial(expert_kernel, experts),
        out_shape=[
            blocks, shape((TILE, width), f32), shape((tokens, width), f32), shape((width // 16, 16, width), bf16),
            shape((tokens, width), bf16), shape((pairs, 8, tokens), f32), shape((1, width), f32),
            blocks, shape((tokens, width), f32),
        ],
        in_specs=[vmem()] * 8 + [any_space] * 2,
        out_specs=[vmem()] * 9,
        scratch_shapes=[
            pltpu.VMEM((tokens, width), bf16),
            block_space,
            pltpu.VMEM((width, hidden_units), bf16),
            pltpu.VMEM((hidden_units, width), bf16),
            pltpu.VMEM((group_rows, width), bf16),
            pltpu.VMEM((group_rows, width), bf16),
            pltpu.VMEM((group_rows, width), f32),
            pltpu.VMEM((group_rows, width), f32),
            block_space, block_space,
            pltpu.VMEM((tokens, width), bf16),
            pltpu.VMEM((width, tokens), bf16),
            block_sems, block_sems,
            pltpu.SemaphoreType.DMA((2,)),
        ],
        compiler_params=remote_params(2),
        cost_estimate=cost(8 * slots * width * hidden_units, 12 * width * hidden_units),
        name="expert",
    )(
        att, x, output_weight, moe_gain_row, router_wide, slot_row, cot, cot_sent,
        expert_in[0], expert_out[0],
    )
    att_grad, cot_all = lax.optimization_barrier((att_grad, cot_all))

    expert_count = lax.axis_size("expert")
    dp_sizes = [2, 2] if dp_count == 4 else [dp_count]
    sizes = [expert_count, *dp_sizes, ctx_count]
    plan = tail_plan(sizes, width)
    group, pieces, lengths = plan
    units = group * pieces

    stacked = 2 if ctx_count <= 4 else 1
    table_rows = heads * TILE // width
    small_rows = -(-(2 + experts + table_rows) // 8) * 8
    slice_width = hidden_units // dp_count
    weights, small, input_grad, in_grad, out_grad, layer_out, _ = pl.pallas_call(
        functools.partial(back_kernel, experts, plan),
        out_shape=[
            shape((units, 16, width), bf16), shape((small_rows, width), f32), shape((tokens, width), f32),
            shape((width, slice_width), f32), shape((slice_width, width), f32), shape((tokens, width), bf16),
            shape((dp_count - 1, experts, block_rows, width), bf16),
        ],
        in_specs=[
            smem(), vmem(), vmem(), any_space, any_space, vmem(), vmem(), vmem(), any_space, vmem(),
            vmem(), vmem(), vmem(), vmem(), any_space, vmem(), any_space, any_space, any_space,
            any_space, vmem(), any_space, any_space, any_space, any_space, any_space, vmem(),
        ],
        out_specs=[vmem()] * 6 + [any_space],
        scratch_shapes=[
            pltpu.VMEM((2, PB, width), bf16),
            pltpu.VMEM((2, PB, width), bf16),
            pltpu.VMEM((2, PB, width), bf16),
            pltpu.VMEM((stacked * PB, tokens), f32),
            pltpu.VMEM((stacked * PB, tokens), f32),
            pltpu.VMEM((stacked * PB, tokens), bf16),
            pltpu.VMEM((stacked * PB, tokens), bf16),
            pltpu.VMEM((width, tokens), f32),
            pltpu.VMEM((PB, width), bf16),
            pltpu.VMEM((PB, width), bf16),
            pltpu.VMEM((TILE, width), bf16),
            pltpu.VMEM((TILE, width), bf16),
            pltpu.VMEM((PB, TILE), bf16),
            pltpu.VMEM((heads, 8, TILE), f32),
            pltpu.VMEM((1, width), f32),
            pltpu.VMEM((tokens, width), f32),
            pltpu.VMEM((ctx_count - 1 if ctx_count <= 4 else 1, PB, width), bf16),
            pltpu.VMEM((ctx_count - 1, PB, width), bf16),
            pltpu.VMEM((units, 16, width), bf16),
            [pltpu.VMEM((pieces, length, 16, width), bf16) for length in lengths[:-1]],
            [
                pltpu.VMEM((pieces, size - 1, length, 16, width), bf16)
                for size, length in zip(sizes, lengths)
            ],
            pltpu.VMEM((small_rows, width), f32),
            [pltpu.VMEM((size - 1, small_rows, width), f32) for size in (expert_count, dp_count, ctx_count)],
            block_space,
            pltpu.VMEM((width, slice_width), bf16),
            pltpu.VMEM((slice_width, width), bf16),
            pltpu.VMEM((slots, width), bf16),
            pltpu.VMEM((slots, width), bf16),
            pltpu.VMEM((width, slots), bf16),
            pltpu.SemaphoreType.DMA((ctx_count + 2, 3)),
            pltpu.SemaphoreType.DMA((9 + 2 * dp_count,)),
            pltpu.SemaphoreType.DMA((2, 2 * pieces * sum(size - 1 for size in sizes))),
            pltpu.SemaphoreType.DMA((2, expert_count + dp_count + ctx_count - 3)),
            pltpu.SemaphoreType.DMA((2, ctx_count - 1)),
            block_sems,
            pltpu.SemaphoreType.DMA((2, dp_count - 1, experts)),
        ],
        compiler_params=remote_params(0),
        cost_estimate=cost(
            8 * dp_count * slots * width * slice_width + 80 * keys_total * tokens * width,
            60 * width * slice_width,
        ),
        name="back",
    )(
        branch, bias, queries, keys, values, att_grad, lse, delta, normed_all, normed_own,
        attn_gain_row, query_weight, key_weight, value_weight, wo_part, moe_gain_part, router_part, x,
        hidden_grad, hidden, slot_row, result,
        rows_sent, cot_all, expert_in[0], expert_out[0], router_wide,
    )

    matrix_units = width // 16
    steps = 4

    def part_rows(rows, columns=width):
        return pl.BlockSpec((rows // steps, columns), lambda i: (i, 0))

    weights = weights[: 4 * matrix_units].reshape(4, matrix_units, 16, width)
    last = onehot[:, buckets - 1 :]
    spread = jnp.concatenate([onehot[:, : buckets - 1], last - 1.0], axis=1)

    def same(rows, columns):
        return pl.BlockSpec((rows, columns), lambda i: (0, 0))

    (
        *weights, in_grad, out_grad, input_grad, layer_out, attn_gain_grad, moe_gain_grad, router_grad, table_grad,
    ) = pl.pallas_call(
        functools.partial(finish_kernel, experts),
        grid=(steps,),
        out_shape=[shape((width, width), f32)] * 4
        + [
            shape((width, slice_width), f32), shape((slice_width, width), f32),
            shape((tokens, width), f32), shape((tokens, width), bf16),
            shape((1, width), f32), shape((1, width), f32), shape((experts, width), f32), shape((heads, buckets), f32),
        ],
        in_specs=[
            pl.BlockSpec(
                (4, matrix_units // steps, 16, width), lambda i: (0, i, 0, 0)
            ),
            part_rows(width, slice_width), part_rows(slice_width), part_rows(tokens), part_rows(tokens),
            same(small_rows, width), same(TILE, buckets),
        ],
        out_specs=[part_rows(width)] * 4
        + [part_rows(width, slice_width), part_rows(slice_width), part_rows(tokens), part_rows(tokens)]
        + [same(1, width), same(1, width), same(experts, width), same(heads, buckets)],
        compiler_params=params(),
        cost_estimate=cost(8 * width * width, 48 * width * width),
        name="finish",
    )(weights, in_grad, out_grad, input_grad, layer_out, small, spread)
    return (
        layer_out[None],
        input_grad[None],
        attn_gain_grad.reshape(width),
        weights[3],
        weights[2],
        weights[1],
        weights[0],
        table_grad.T,
        moe_gain_grad.reshape(width),
        router_grad.T,
        in_grad[None],
        out_grad[None],
    )


def solution(mesh):
    grouped = P(("dp", "expert"), "ctx", None)
    placed = (
        grouped, grouped, grouped, grouped, P(("dp", "expert"), "ctx"),
        P(), P(), P(), P(), P(), P(), P(), P(),
        P(("ctx", "expert"), None, None),
        P(("ctx", "expert"), None, None),
    )
    return jax.shard_map(
        body,
        mesh=mesh,
        in_specs=placed,
        out_specs=(
            grouped, grouped, P(), P(), P(), P(), P(), P(), P(), P(),
            P(("ctx", "expert"), None, "dp"),
            P(("ctx", "expert"), "dp", None),
        ),
        check_vma=False,
    )
```

```python
import functools

import jax
import jax.numpy as jnp
from jax import lax
from jax.experimental import pallas as pl
from jax.experimental.pallas import tpu as pltpu
from jax.sharding import PartitionSpec as P

PB = 256
TILE = 128
CHUNKS = 2

bucket_edges = (19, 21, 24, 27, 31, 35, 40, 46, 52, 59, 67, 77, 87, 99, 113)
norm_eps = 1e-06
masked_score = -1e30
gelu_scale = 0.7978845608
gelu_cube = 0.044715

bf16 = jnp.bfloat16
f32 = jnp.float32
VMEM_LIMIT = 121 * 512 * 1024


def dot_nn(a, b):
    return jnp.dot(a, b, preferred_element_type=f32)


def dot_nt(a, b):
    return lax.dot_general(a, b, (((1,), (1,)), ((), ())), preferred_element_type=f32)


def dot_tn(a, b):
    return lax.dot_general(a, b, (((0,), (0,)), ((), ())), preferred_element_type=f32)


def two_parts(a):
    high = a.astype(bf16)
    return high, (a - high.astype(f32)).astype(bf16)


def vmem():
    return pl.BlockSpec(memory_space=pltpu.VMEM)


def smem():
    return pl.BlockSpec(memory_space=pltpu.SMEM)


def params():
    return pltpu.CompilerParams(vmem_limit_bytes=VMEM_LIMIT)


def remote_params(number):
    return pltpu.CompilerParams(
        vmem_limit_bytes=VMEM_LIMIT, collective_id=number, has_side_effects=True
    )


def cost(flops, nbytes):
    return pl.CostEstimate(flops=int(flops), bytes_accessed=int(nbytes), transcendentals=0)


def shape(dims, kind):
    return jax.ShapeDtypeStruct(dims, kind)


def inverse_rms(x):
    return lax.rsqrt(jnp.mean(x * x, axis=-1, keepdims=True) + norm_eps)


def bucket_onehot(buckets):
    distance = jnp.arange(TILE, dtype=jnp.int32)
    ids = jnp.minimum(distance, 16)
    for edge in bucket_edges:
        ids = ids + (distance >= edge).astype(jnp.int32)
    return (ids[:, None] == jnp.arange(buckets, dtype=jnp.int32)[None, :]).astype(f32)


def near_index(first):
    rows = lax.broadcasted_iota(jnp.int32, (TILE, TILE), 0)
    lanes = lax.broadcasted_iota(jnp.int32, (TILE, TILE), 1)
    return first + lanes - rows


def near_tiles(ctx_at, plen):
    start = ctx_at * PB
    return (
        (start, 0, 0, False),
        (start, TILE, TILE, False),
        (start + TILE, TILE, 0, False),
        (plen, PB, 0, False),
        (plen, PB + TILE, TILE, False),
        (plen + TILE, PB + TILE, 0, False),
        (plen + PB, PB, TILE, False),
        (start - TILE, 0, TILE, True),
    )


def add_near(s_ref, bias_row, ctx_at, plen):
    source = jnp.broadcast_to(bias_row, (TILE, TILE))
    add_tiles(s_ref, source, ctx_at, near_tiles(ctx_at, plen))


def add_tiles(s_ref, source, ctx_at, tiles):
    for first_row, first_lane, gap, guarded in tiles:
        def work(first_row=first_row, first_lane=first_lane, gap=gap):
            rows = pl.ds(first_row if isinstance(first_row, int) else pl.multiple_of(first_row, 16), TILE)
            lanes = slice(first_lane, first_lane + TILE)
            index = jnp.clip(near_index(gap), 0, TILE - 1)
            s_ref[rows, lanes] = s_ref[rows, lanes] + jnp.take_along_axis(source, index, axis=1)

        if guarded:
            pl.when(ctx_at > 0)(work)
        else:
            work()


def scores_to(s_ref, keys, queries, plen):
    s_ref[:plen, :] = dot_nt(keys[:plen], queries)
    s_ref[plen:, PB:] = dot_nt(keys[plen:], queries[PB:])


def limits(ctx_at, branch, tokens):
    lane = lax.broadcasted_iota(jnp.int32, (1, tokens), 1)
    return jnp.where(lane < PB, ctx_at * PB + lane + 1, branch - TILE)


def window_rows(first, count, branch):
    rows = lax.broadcasted_iota(jnp.int32, (TILE, count), 0)
    places = lax.broadcasted_iota(jnp.int32, (TILE, count), 1) + first
    return (places == rows + (branch - TILE)).astype(bf16)


def row_steps(first, count, lanes):
    return first + lax.broadcasted_iota(jnp.int32, (count, lanes), 0)


def own_allowed(first, count, lanes):
    return row_steps(first, count, lanes) <= lax.broadcasted_iota(jnp.int32, (count, lanes), 1)


def head_lanes(half):
    return lax.broadcasted_iota(jnp.int32, (1, TILE), 1) // (TILE // 2) == half


def pick_rows(pieces, lanes):
    row = lax.broadcasted_iota(jnp.int32, (8, lanes), 0)
    return jnp.where(row == 0, pieces[0], jnp.where(row == 1, pieces[1], 0.0))


def fold8(x, op):
    return op(x.reshape(x.shape[0] // 8, 8, x.shape[1]), axis=0)


def owner_device(index):
    cores = lax.axis_size("expert")
    return {"ctx": index // cores, "expert": lax.rem(index, cores)}


def owners():
    cores = lax.axis_size("expert")
    count = cores * lax.axis_size("ctx")
    return count, lax.axis_index("ctx") * cores + lax.axis_index("expert")


def greet_owners():
    count, me = owners()
    barrier = pltpu.get_barrier_semaphore()

    def greet(ahead, _):
        pl.semaphore_signal(
            barrier, inc=1, device_id=owner_device(lax.rem(me + ahead, count)),
            device_id_type=pl.DeviceIdType.MESH,
        )
        return 0

    lax.fori_loop(1, count, greet, 0)
    pl.semaphore_wait(barrier, count - 1)


def block_copy(source, target, sems, ahead):
    count, me = owners()
    peer = lax.rem(me + ahead, count)
    return pltpu.make_async_remote_copy(
        src_ref=source.at[peer], dst_ref=target.at[me],
        send_sem=sems.at[0, ahead - 1], recv_sem=sems.at[1, ahead - 1],
        device_id=owner_device(peer), device_id_type=pl.DeviceIdType.MESH,
    )


def await_blocks(source, target, sems, sent, received):
    def one(ahead, _):
        copy = block_copy(source, target, sems, ahead)
        if received:
            copy.wait_recv()
        if sent:
            copy.wait_send()
        return 0

    lax.fori_loop(1, owners()[0], one, 0)


def place_rows(slot_row, index, block_rows, tokens):
    rows = lax.broadcasted_iota(jnp.int32, (block_rows, tokens), 0) + index * block_rows
    return (rows == slot_row).astype(bf16)


def front_kernel(
    capacity,
    branch_ref, bias_ref, x_ref, cot_ref, gain_ref, route_row, arrive_row,
    wq_ref, wk_ref, wv_ref,
    slot_out, cot_out, normed_own_out, normed_out, q_ref, k_out, v_out, att_out, lse_out,
    prompt_ref, send_ref, s_ref, p_ref, prompt_sems, cot_sems,
):
    branch = branch_ref[0, 0]
    ctx_at, ctx_count = lax.axis_index("ctx"), lax.axis_size("ctx")
    plen = PB * ctx_count
    tokens, width = x_ref.shape
    own = tokens - PB
    gain = gain_ref[...].astype(f32)
    count, me = owners()
    block_rows = send_ref.shape[1]
    greet_owners()

    chunk = PB // CHUNKS

    def pass_on(step, up, c):
        block = ctx_at - step if up else ctx_at + step
        ahead = ctx_at + 1 if up else ctx_at - 1
        fits = (block >= 0) & (ahead < ctx_count) if up else (block < ctx_count) & (ahead >= 0)
        piece = pl.ds(c * chunk, chunk)
        source = x_ref.at[piece] if step == 0 else prompt_ref.at[block, piece]
        copy = pltpu.make_async_remote_copy(
            src_ref=source, dst_ref=prompt_ref.at[block, piece],
            send_sem=prompt_sems.at[0, int(up), step, c], recv_sem=prompt_sems.at[1, int(up), step, c],
            device_id={"ctx": ahead}, device_id_type=pl.DeviceIdType.MESH,
        )
        return fits, copy

    def arrival(step, up, c):
        block = ctx_at - step - 1 if up else ctx_at + step + 1
        fits = block >= 0 if up else block < ctx_count
        place = prompt_ref.at[block, pl.ds(c * chunk, chunk)]
        copy = pltpu.make_async_remote_copy(
            src_ref=place, dst_ref=place,
            send_sem=prompt_sems.at[0, int(up), step, c], recv_sem=prompt_sems.at[1, int(up), step, c],
            device_id={"ctx": ctx_at}, device_id_type=pl.DeviceIdType.MESH,
        )
        return fits, block, copy

    for c in range(CHUNKS):
        for up in (True, False):
            fits, copy = pass_on(0, up, c)
            pl.when(fits)(copy.start)

    x = x_ref[...].astype(f32)
    normed_own_out[...] = (x * inverse_rms(x) * gain).astype(bf16)

    def column(i, _):
        cols = pl.ds(pl.multiple_of(i * 256, 256), 256)
        q_ref[:, cols] = dot_nn(normed_own_out[...], wq_ref[:, cols]).astype(bf16)
        k_out[plen : plen + own, cols] = dot_nn(normed_own_out[PB:, :], wk_ref[:, cols]).astype(bf16)
        v_out[plen : plen + own, cols] = dot_nn(normed_own_out[PB:, :], wv_ref[:, cols]).astype(bf16)
        return 0

    lax.fori_loop(0, width // 256, column, 0)

    def project(block):
        rows = pl.ds(pl.multiple_of(block * PB, PB), PB)

        def prompt_column(i, _):
            cols = pl.ds(pl.multiple_of(i * 256, 256), 256)
            k_out[rows, cols] = dot_nn(normed_out[rows, :], wk_ref[:, cols]).astype(bf16)
            v_out[rows, cols] = dot_nn(normed_out[rows, :], wv_ref[:, cols]).astype(bf16)
            return 0

        lax.fori_loop(0, width // 256, prompt_column, 0)

    def take(block):
        x = prompt_ref[block].astype(f32)
        rows = pl.ds(pl.multiple_of(block * PB, PB), PB)
        normed_out[rows, :] = (x * inverse_rms(x) * gain).astype(bf16)
        project(block)

    def down(row):
        column = jnp.broadcast_to(row[...].astype(f32), (TILE, tokens)).T
        return jnp.concatenate([column] * (tokens // TILE), axis=1)

    same = down(route_row) == route_row[...].astype(f32)
    earlier = down(arrive_row) < arrive_row[...].astype(f32)
    rank = jnp.sum(jnp.where(same & earlier, 1.0, 0.0), axis=0, keepdims=True).astype(jnp.int32)
    slot = jnp.where(rank < capacity, route_row[...] * block_rows + rank, count * block_rows)
    slot_out[...] = slot

    def lay_out(peer, _):
        rows = dot_nn(place_rows(slot_out[...], peer, block_rows, tokens), cot_ref[...]).astype(bf16)
        send_ref[peer] = rows
        return 0

    def lay_out_all():
        lax.fori_loop(0, count, lay_out, 0)
        cot_out[me] = send_ref[me]

    for step in range(ctx_count - 1):
        if step == ctx_count - 2:
            lay_out_all()
        for c in range(CHUNKS):
            for up in (True, False):
                fits, block, copy = arrival(step, up, c)
                pl.when(fits)(copy.wait_recv)
                if step < ctx_count - 2:
                    fits, copy = pass_on(step + 1, up, c)
                    pl.when(fits)(copy.start)
        if step == 0:
            normed_out[pl.ds(pl.multiple_of(ctx_at * PB, PB), PB), :] = normed_own_out[:PB, :]
            project(ctx_at)
        for up in (True, False):
            fits, block, copy = arrival(step, up, 0)
            pl.when(fits)(functools.partial(take, block))

    def send_cots():
        def send_cot(ahead, _):
            block_copy(send_ref, cot_out, cot_sems, ahead).start()
            return 0

        lax.fori_loop(1, count, send_cot, 0)

    def window_column(i, _):
        cols = pl.ds(pl.multiple_of(i * 256, 256), 256)
        window = window_rows(0, plen, branch)
        k_out[plen + own :, cols] = dot_nn(window, k_out[:plen, cols]).astype(bf16)
        v_out[plen + own :, cols] = dot_nn(window, v_out[:plen, cols]).astype(bf16)
        return 0

    lax.fori_loop(0, width // 256, window_column, 0)
    p_ref[plen:, :PB] = jnp.zeros((own + TILE, PB), bf16)
    limit = limits(ctx_at, branch, tokens)

    def pair(g, _):
        pl.when(g == 1)(send_cots)
        lanes = pl.ds(pl.multiple_of(g * TILE, TILE), TILE)
        queries = q_ref[:, lanes]
        keys = k_out[:, lanes]
        values_t = v_out[:, lanes].T
        bias = bias_ref[g]
        lse_rows, att_rows = [], []
        for half in range(2):
            scores_to(s_ref, jnp.where(head_lanes(half), keys, jnp.zeros_like(keys)), queries, plen)
            add_near(s_ref, bias[half : half + 1, :], ctx_at, plen)

            def top_of(i, top):
                for part in range(0, TILE, 32):
                    first = pl.multiple_of(i * TILE + part, 32)
                    rows = pl.ds(first, 32)
                    s = jnp.where(row_steps(first, 32, tokens) < limit, s_ref[rows, :], masked_score)
                    s_ref[rows, :] = s
                    top = jnp.maximum(top, fold8(s, jnp.max))
                return top

            top = lax.fori_loop(0, plen // TILE, top_of, jnp.full((8, tokens), masked_score, f32))
            own_top = jnp.full((8, own), masked_score, f32)
            for i in range(own // TILE + 1):
                rows = slice(plen + i * TILE, plen + (i + 1) * TILE)
                s = s_ref[rows, PB:]
                if i < own // TILE:
                    s = jnp.where(own_allowed(i * TILE, TILE, own), s, masked_score)
                    s_ref[rows, PB:] = s
                own_top = jnp.maximum(own_top, fold8(s, jnp.max))
            top = jnp.concatenate([top[:, :PB], jnp.maximum(top[:, PB:], own_top)], axis=1)
            top = jnp.max(top, axis=0, keepdims=True)

            def weigh(i, total):
                for part in range(0, TILE, 32):
                    rows = pl.ds(pl.multiple_of(i * TILE + part, 32), 32)
                    p = jnp.exp(s_ref[rows, :] - top)
                    p_ref[rows, :] = p.astype(bf16)
                    total = total + fold8(p, jnp.sum)
                return total

            total = lax.fori_loop(0, plen // TILE, weigh, jnp.zeros((8, tokens), f32))
            own_total = jnp.zeros((8, own), f32)
            for i in range(own // TILE + 1):
                rows = slice(plen + i * TILE, plen + (i + 1) * TILE)
                p = jnp.exp(s_ref[rows, PB:] - top[:, PB:])
                p_ref[rows, PB:] = p.astype(bf16)
                own_total = own_total + fold8(p, jnp.sum)
            total = jnp.concatenate([total[:, :PB], total[:, PB:] + own_total], axis=1)
            total = jnp.sum(total, axis=0, keepdims=True)
            rows = slice(half * 64, half * 64 + 64)
            att_rows.append((dot_nn(values_t[rows, :], p_ref[...]) / total).astype(bf16))
            lse_rows.append(top + jnp.log(total))
        att_out[lanes, :] = jnp.concatenate(att_rows, axis=0)
        lse_out[g] = pick_rows(lse_rows, tokens)
        return 0

    lax.fori_loop(0, width // TILE, pair, 0)
    await_blocks(send_ref, cot_out, cot_sems, True, True)
    for step in range(ctx_count - 1):
        for c in range(CHUNKS):
            for up in (True, False):
                fits, copy = pass_on(step, up, c)
                pl.when(fits)(copy.wait_send)


def router_probs(logits, lane, experts):
    logits = jnp.where(lane < experts, logits, masked_score)
    logits = jnp.exp(logits - jnp.max(logits, axis=1, keepdims=True))
    return logits / jnp.sum(logits, axis=1, keepdims=True)


def gelu_parts(v):
    t = jnp.tanh(gelu_scale * (v + gelu_cube * (v * v * v)))
    half = 0.5 * (1.0 + t)
    slope = half + 0.5 * v * (1.0 - t * t) * (gelu_scale + (3.0 * gelu_scale * gelu_cube) * (v * v))
    return v * half, slope


def expert_kernel(
    experts,
    att_ref, x_ref, wo_ref, gain_ref, router_ref, slot_row, cot_ref, cot_rows, win_hbm, wout_hbm,
    rows_out, router_out, hidden_grad_out, wo_grad_out, att_grad_out, delta_out, gain_grad_out,
    result_out, hidden_ref,
    moe_ref, send_ref, win_ref, wout_ref, group_rows, sent_ref, result_acc, grad_acc,
    grad_send, grad_recv, low_ref, att_t_ref, rows_sems, grad_sems, load_sems,
):
    tokens, width = x_ref.shape
    count, me = owners()
    block_rows = send_ref.shape[1]
    hidden_units = win_ref.shape[1]
    loads = [
        pltpu.make_async_copy(win_hbm, win_ref, load_sems.at[0]),
        pltpu.make_async_copy(wout_hbm, wout_ref, load_sems.at[1]),
    ]
    for copy in loads:
        copy.start()
    greet_owners()

    moe_ref[...] = att_ref[...].T

    def column(i, _):
        cols = pl.ds(pl.multiple_of(i * 256, 256), 256)
        hidden_ref[:, cols] = x_ref[:, cols].astype(f32) + dot_nn(moe_ref[...], wo_ref[:, cols])
        return 0

    lax.fori_loop(0, width // 256, column, 0)
    hidden = hidden_ref[...]
    moe_ref[...] = (hidden * inverse_rms(hidden) * gain_ref[...].astype(f32)).astype(bf16)

    members = 2 * lax.axis_size("expert") if lax.axis_size("ctx") % 2 == 0 else count
    groups = count // members
    my_group = me // members

    def send_rows(ahead, _):
        peer = lax.rem(me + ahead, count)
        place = place_rows(slot_row[...], peer, block_rows, tokens)
        send_ref[peer] = dot_nn(place, moe_ref[...]).astype(bf16)
        block_copy(send_ref, rows_out, rows_sems, ahead).start()
        return 0

    def send_group(g, _):
        base = lax.rem(my_group + g, groups) * members

        def member(i, _):
            ahead = lax.rem(base + i - me + count, count)
            pl.when(ahead > 0)(lambda: (send_rows(ahead, 0), None)[1])
            return 0

        return lax.fori_loop(0, members, member, 0)

    lax.fori_loop(0, groups, send_group, 0)
    rows_out[me] = dot_nn(place_rows(slot_row[...], me, block_rows, tokens), moe_ref[...]).astype(bf16)

    router_out[...] = jnp.zeros_like(router_out)
    for copy in loads:
        copy.wait()

    def group(g, _):
        base = lax.rem(my_group + g, groups) * members

        def arrive(i, _):
            behind = lax.rem(me - base - i + count, count)
            pl.when(behind > 0)(lambda: block_copy(send_ref, rows_out, rows_sems, behind).wait_recv())
            return 0

        lax.fori_loop(0, members, arrive, 0)
        blocks = pl.ds(base, members)
        size = members * block_rows
        group_rows[...] = rows_out[blocks].reshape(size, width)
        slot_lane = lax.broadcasted_iota(jnp.int32, (size, TILE), 1)
        mine = slot_lane == me
        probs = router_probs(dot_nn(group_rows[...], router_ref[...]), slot_lane, experts)
        gate = jnp.sum(jnp.where(mine, probs, 0.0), axis=1, keepdims=True)
        cot_group = cot_rows[blocks].reshape(size, width).astype(f32)
        sent_ref[...] = (gate * cot_group).astype(bf16)
        result_acc[...] = jnp.zeros_like(result_acc)
        grad_acc[...] = jnp.zeros_like(grad_acc)

        def units(i, _):
            cols = pl.ds(pl.multiple_of(i * width, width), width)
            act, slope = gelu_parts(dot_nn(group_rows[...], win_ref[:, cols]))
            result_acc[...] += dot_nn(act.astype(bf16), wout_ref[cols, :])
            pre_grad = (dot_nt(sent_ref[...], wout_ref[cols, :]) * slope).astype(bf16)
            grad_acc[...] += dot_nt(pre_grad, win_ref[:, cols])
            return 0

        lax.fori_loop(0, hidden_units // width, units, 0)
        result = result_acc[...].astype(bf16)
        gate_grad = jnp.sum(cot_group * result.astype(f32), axis=1, keepdims=True)
        logit_grad = (gate_grad * gate) * (jnp.where(mine, 1.0, 0.0) - probs)
        high, low = two_parts(logit_grad)
        grad = grad_acc[...] + (dot_nt(high, router_ref[...]) + dot_nt(low, router_ref[...]))
        grad_send[blocks] = grad.astype(bf16).reshape(members, block_rows, width)
        gated = (gate * result.astype(f32)).astype(bf16)
        result_out[blocks] = gated.reshape(members, block_rows, width)

        def give(i, _):
            ahead = lax.rem(base + i - me + count, count)

            @pl.when(ahead > 0)
            def _():
                block_copy(grad_send, grad_recv, grad_sems, ahead).start()

            return 0

        lax.fori_loop(0, members, give, 0)
        router_out[...] += dot_tn(high, group_rows[...]) + dot_tn(low, group_rows[...])
        return 0

    lax.fori_loop(0, groups, group, 0)
    grad_recv[me] = grad_send[me]

    slots = count * block_rows
    place = place_rows(slot_row[...], 0, slots, tokens)
    await_blocks(grad_send, grad_recv, grad_sems, False, True)
    moe_grad = dot_tn(place, grad_recv[...].reshape(slots, width))
    hidden = hidden_ref[...]
    inverse = inverse_rms(hidden)
    scaled = hidden * inverse
    gain_grad_out[...] = jnp.sum(moe_grad * scaled, axis=0, keepdims=True)
    through = moe_grad * gain_ref[...].astype(f32)
    shared = jnp.mean(through * scaled, axis=1, keepdims=True)
    hidden_grad = cot_ref[...].astype(f32) + inverse * (through - scaled * shared)
    hidden_grad_out[...] = hidden_grad
    low_ref[...] = hidden_grad.astype(bf16)

    def back_column(i, _):
        cols = pl.ds(pl.multiple_of(i * 256, 256), 256)
        wo_grad = dot_nn(att_ref[...], low_ref[:, cols]).astype(bf16)
        wo_grad_out[:, :, cols] = wo_grad.reshape(width // 16, 16, 256)
        att_grad_out[:, cols] = dot_nt(low_ref[...], wo_ref[cols, :]).astype(bf16)
        att_t_ref[cols, :] = dot_nt(wo_ref[cols, :], low_ref[...]).astype(bf16)
        return 0

    lax.fori_loop(0, width // 256, back_column, 0)

    def pair(g, _):
        rows = pl.ds(pl.multiple_of(g * TILE, TILE), TILE)
        both = att_ref[rows, :].astype(f32) * att_t_ref[rows, :].astype(f32)
        delta_out[g] = pick_rows(
            [jnp.sum(both[:64], axis=0, keepdims=True), jnp.sum(both[64:], axis=0, keepdims=True)],
            tokens,
        )
        return 0

    lax.fori_loop(0, width // TILE, pair, 0)
    await_blocks(send_ref, rows_out, rows_sems, True, False)
    await_blocks(grad_send, grad_recv, grad_sems, True, False)


class Axis:
    def __init__(self, name, size, step=1):
        place = lax.axis_index(name)
        self.name, self.size, self.step, self.place = name, size, step, place
        self.index = lax.rem(place // step, size)

    def at(self, ahead):
        return lax.rem(self.index + ahead, self.size)

    def peer(self, ahead):
        return {self.name: self.place + (self.at(ahead) - self.index) * self.step}


def mesh_axes():
    dp, ctx, expert = lax.axis_size("dp"), lax.axis_size("ctx"), lax.axis_size("expert")
    cores, lines = Axis("expert", expert), Axis("ctx", ctx)
    if dp == 4:
        near, far = Axis("dp", 2, 1), Axis("dp", 2, 2)
        return [[cores, near, far, lines], [cores, far, near, lines]]
    return [[cores, Axis("dp", dp), lines]] * 2


def push(source, target, sems, slot, device):
    copy = pltpu.make_async_remote_copy(
        src_ref=source, dst_ref=target, send_sem=sems.at[0, slot], recv_sem=sems.at[1, slot],
        device_id=device, device_id_type=pl.DeviceIdType.MESH,
    )
    copy.start()
    return copy


def back_kernel(
    experts, plan,
    branch_ref, bias_ref, q_ref, k_hbm, v_hbm, att_grad_ref, lse_ref, delta_ref, normed_hbm, normed_own_ref,
    gain_ref, wq_ref, wk_ref, wv_ref, wo_part_hbm, moe_gain_ref, router_part_hbm, x_hbm, hidden_grad_hbm,
    hidden_hbm, slot_row, result_hbm, rows_hbm, cot_hbm, win_hbm, wout_hbm, router_ref,
    full_ref, small_out, input_out, in_out, out_out, layer_out, rows_all,
    k_ref, v_ref, normed_ref, s_ref, dp_ref, p_ref, ds_ref, dq_ref, dk_ref, dv_ref, window_k, window_v, picked_ref,
    hist_ref, gain_sum,
    local_ref, shared_send, shared_recv, parts_ref, acc_refs, recv_refs, small_ref, small_recv,
    result_recv, win_ref, wout_ref, rows_ref, cot_ref, rows_t,
    block_sems, load_sems, sems, small_sems, shared_sems, result_sems, rows_sems,
):
    group, pieces, lengths = plan
    flows = mesh_axes()
    branch = branch_ref[0, 0]
    ctx_at = lax.axis_index("ctx")
    ctx_count, dp_count = lax.axis_size("ctx"), lax.axis_size("dp")
    tokens, width = q_ref.shape
    own = tokens - PB
    plen = PB * ctx_count
    count, me = owners()
    lines, columns_dp = Axis("ctx", ctx_count), Axis("dp", dp_count)
    whole_axes = [Axis("expert", lax.axis_size("expert")), columns_dp, lines]
    gain = gain_ref[...].astype(f32)
    limit = limits(ctx_at, branch, tokens)
    blocks = ctx_count + 2
    rows_16 = width // 16

    def block_loads(i):
        size = TILE if i == 1 else PB
        rows = (plen, plen + own)[i] if i < 2 else pl.multiple_of(lines.at(i - 1) * PB, PB)
        sources = [(k_hbm, k_ref, 0), (v_hbm, v_ref, 1)]
        if 2 <= i < blocks - 1:
            sources.append((normed_hbm, normed_ref, 2))
        return [
            pltpu.make_async_copy(
                source.at[pl.ds(rows, size)], target.at[i % 2, pl.ds(0, size)], block_sems.at[i, n]
            )
            for source, target, n in sources
        ]

    for copy in block_loads(0):
        copy.start()
    slice_width = win_ref.shape[1]
    part = pl.ds(pl.multiple_of(lax.axis_index("dp") * slice_width, slice_width), slice_width)
    weight_loads = [
        pltpu.make_async_copy(win_hbm.at[:, part], win_ref, load_sems.at[0]),
        pltpu.make_async_copy(wout_hbm.at[part], wout_ref, load_sems.at[1]),
    ]
    own_result = pltpu.make_async_copy(result_hbm.at[me], result_recv.at[me], load_sems.at[2])
    wo_load = pltpu.make_async_copy(wo_part_hbm, parts_ref.at[pl.ds(0, rows_16)], load_sems.at[5 + 2 * dp_count])
    router_load = pltpu.make_async_copy(
        router_part_hbm.at[pl.ds(0, experts)], small_ref.at[pl.ds(0, experts)], load_sems.at[7 + 2 * dp_count]
    )
    for copy in [wo_load, *weight_loads, own_result, router_load]:
        copy.start()

    barrier = pltpu.get_barrier_semaphore()

    def greet(ahead, _):
        pl.semaphore_signal(
            barrier, inc=1, device_id=owner_device(lax.rem(me + ahead, count)),
            device_id_type=pl.DeviceIdType.MESH,
        )
        return 0

    lax.fori_loop(1, count, greet, 0)
    for ahead in range(1, dp_count):
        pl.semaphore_signal(
            barrier, inc=1, device_id=columns_dp.peer(ahead), device_id_type=pl.DeviceIdType.MESH
        )
    pl.semaphore_wait(barrier, count - 1 + dp_count - 1)

    slots_of = {}

    def slot(*key):
        return slots_of.setdefault(key, len(slots_of))

    started = []

    def reduce_start(j, s):
        axis, length = flows[j % 2][s], lengths[s]
        copies = []
        for ahead in range(1, axis.size):
            target = axis.at(ahead)
            if s == 0:
                source = parts_ref.at[pl.ds(j * group + target * length, length)]
            else:
                source = acc_refs[s - 1].at[j, pl.ds(target * length, length)]
            there = recv_refs[s].at[j, ahead - 1]
            copies.append(push(source, there, sems, slot("r", j, s, ahead), axis.peer(ahead)))
        started.extend(copies)
        return copies

    def base_of(j, s):
        base = j * group
        for t in range(s + 1):
            base = base + flows[j % 2][t].index * lengths[t]
        return base

    def reduce_finish(j, s, copies):
        axis, length = flows[j % 2][s], lengths[s]
        for copy in copies:
            copy.wait_recv()
        last = s == len(lengths) - 1

        size = 4 if length % 4 == 0 else 1

        def some(u, _):
            if s == 0:
                total = parts_ref[pl.ds(base_of(j, 0) + u * size, size)].astype(f32)
            else:
                total = acc_refs[s - 1][j, pl.ds(axis.index * length + u * size, size)].astype(f32)
            for ahead in range(1, axis.size):
                total = total + recv_refs[s][j, ahead - 1, pl.ds(u * size, size)].astype(f32)
            if last:
                full_ref[pl.ds(base_of(j, s) + u * size, size)] = total.astype(bf16)
            else:
                acc_refs[s][j, pl.ds(u * size, size)] = total.astype(bf16)
            return 0

        lax.fori_loop(0, length // size, some, 0)

    def spread_start(j, s):
        axis, length = flows[j % 2][s], lengths[s]
        here = full_ref.at[pl.ds(base_of(j, s), length)]
        copies = [
            push(here, here, sems, slot("s", j, s, ahead), axis.peer(ahead))
            for ahead in range(1, axis.size)
        ]
        started.extend(copies)
        return copies

    def small_slot(s, ahead):
        return sum(axis.size - 1 for axis in whole_axes[:s]) + ahead - 1

    def small_start(s):
        axis = whole_axes[s]
        copies = [
            push(small_ref, small_recv[s].at[ahead - 1], small_sems, small_slot(s, ahead), axis.peer(ahead))
            for ahead in range(1, axis.size)
        ]
        return copies

    def small_finish(s, copies):
        axis = whole_axes[s]
        for copy in copies:
            copy.wait()
        mine = small_ref[...]
        total = jnp.zeros_like(mine)
        for index in range(axis.size):
            piece = mine
            for ahead in range(1, axis.size):
                piece = jnp.where(axis.at(axis.size - ahead) == index, small_recv[s][ahead - 1], piece)
            total = total + piece
        if s == len(whole_axes) - 1:
            small_out[...] = total
        else:
            small_ref[...] = total

    stages = len(lengths)
    early = pieces > 1 and group <= rows_16
    begin = [blocks + j // 2 for j in range(pieces)]
    if early:
        begin = [blocks - 2] + [blocks - 1 + (j - 1) // 2 for j in range(1, pieces)]
    pending = {}

    def advance(time):
        for j in sorted(range(pieces), key=lambda j: begin[j]):
            s = time - begin[j]
            if not 0 <= s < 2 * stages:
                continue
            if s < stages:
                reduce_finish(j, s, pending[j, s])
                if s + 1 < stages:
                    pending[j, s + 1] = reduce_start(j, s + 1)
                else:
                    pending[j, s + 1] = spread_start(j, s)
            else:
                for copy in pending[j, s]:
                    copy.wait_recv()
                if s + 1 < 2 * stages:
                    pending[j, s + 1] = spread_start(j, 2 * stages - 1 - (s + 1))

    def put(first, cols, value):
        rows = value.shape[0]
        parts_ref[first // 16 : (first + rows) // 16, :, cols] = value.astype(bf16).reshape(
            rows // 16, 16, value.shape[1]
        )

    def columns(work):
        def column(i, _):
            work(pl.ds(pl.multiple_of(i * 256, 256), 256))
            return 0

        lax.fori_loop(0, width // 256, column, 0)

    if parts_ref.shape[0] > 4 * rows_16:
        extra = parts_ref.shape[0] - 4 * rows_16
        parts_ref[4 * rows_16 :] = jnp.zeros((extra, 16, width), bf16)
    wo_load.wait()
    if early:
        pending[0, 0] = reduce_start(0, 0)

    def give_result(ahead, _):
        block_copy(result_hbm, result_recv, result_sems, ahead).start()
        return 0

    lax.fori_loop(1, count, give_result, 0)

    def rows_copy(ahead, e):
        return pltpu.make_async_remote_copy(
            src_ref=rows_hbm.at[e], dst_ref=rows_all.at[ahead - 1, e],
            send_sem=rows_sems.at[0, ahead - 1, e], recv_sem=rows_sems.at[1, ahead - 1, e],
            device_id=columns_dp.peer(ahead), device_id_type=pl.DeviceIdType.MESH,
        )

    def each_row_block(act):
        def one(e, _):
            for ahead in range(1, dp_count):
                act(rows_copy(ahead, e))
            return 0

        lax.fori_loop(0, count, one, 0)

    each_row_block(lambda copy: copy.start())

    shared_copies = []
    shared_slots = shared_send.shape[0]
    hist_ref[...] = jnp.zeros_like(hist_ref)
    gain_sum[...] = jnp.zeros_like(gain_sum)
    for i in range(blocks):
        cont, window, at_home = i == 0, i == 1, i == blocks - 1
        remote = i - 1
        size = TILE if window else PB
        for copy in block_loads(i):
            copy.wait()
        if i + 1 < blocks:
            for copy in block_loads(i + 1):
                copy.start()
        block = lines.at(max(remote, 0))
        lanes_from = PB if cont or window else 0
        lanes_used = slice(lanes_from, tokens)
        if cont or at_home:
            near = [
                (0, lanes_from, 0, None),
                (0, lanes_from + TILE, TILE, None),
                (TILE, lanes_from + TILE, 0, None),
            ]
        elif window:
            near = [(0, PB, TILE, None)]
        else:
            near = [(TILE, 0, TILE, block == ctx_at - 1)]

        if not (cont or window):
            places = lax.broadcasted_iota(jnp.int32, (PB, TILE), 0) + block * PB
            picks = lax.broadcasted_iota(jnp.int32, (PB, TILE), 1) + (branch - TILE)
            picked_ref[...] = (places == picks).astype(bf16)

        def pair(g, _, i=i, cont=cont, window=window, size=size, block=block, lanes_used=lanes_used, near=near):
            lanes = pl.ds(pl.multiple_of(g * TILE, TILE), TILE)
            queries = q_ref[lanes_used, lanes]
            grads = att_grad_ref[lanes_used, lanes]
            keys = k_ref[i % 2, :size, lanes]
            values = v_ref[i % 2, :size, lanes]
            keys_t = keys.T
            bias = bias_ref[g]
            dk_parts, dv_parts, dq_parts = [], [], []
            stacked = s_ref.shape[0] // PB
            for halves in [(0, 1)] if stacked == 2 else [(0,), (1,)]:
                total = len(halves) * size

                def masked(rows):
                    return jnp.concatenate([jnp.where(head_lanes(h), rows, jnp.zeros_like(rows)) for h in halves])

                s_ref[:total, lanes_used] = dot_nt(masked(keys), queries)
                dp_ref[:total, lanes_used] = dot_nt(masked(values), grads)
                for n, half in enumerate(halves):
                    offset = n * size
                    lse = lse_ref[g][half : half + 1, lanes_used]
                    delta = delta_ref[g][half : half + 1, lanes_used]
                    source = jnp.broadcast_to(bias[half : half + 1, :], (TILE, TILE))
                    for first, lane, gap, when in near:
                        def add(first=first + offset, lane=lane, gap=gap):
                            there = (slice(first, first + TILE), slice(lane, lane + TILE))
                            index = jnp.clip(near_index(gap), 0, TILE - 1)
                            s_ref[there] = s_ref[there] + jnp.take_along_axis(source, index, axis=1)

                        add() if when is None else pl.when(when)(add)
                    step = 32
                    for first in range(0, size, step):
                        rows = slice(offset + first, offset + first + step)
                        p = jnp.exp(s_ref[rows, lanes_used] - lse)
                        if cont:
                            p = jnp.where(own_allowed(first, step, own), p, 0.0)
                        elif not window:
                            p = jnp.where(row_steps(block * PB + first, step, tokens) < limit, p, 0.0)
                        p_ref[rows, lanes_used] = p.astype(bf16)
                        ds_ref[rows, lanes_used] = (p * (dp_ref[rows, lanes_used] - delta)).astype(bf16)
                    for first, lane, gap, when in near:
                        def collect(first=first + offset, lane=lane, gap=gap, half=half):
                            tile = ds_ref[first : first + TILE, lane : lane + TILE].astype(f32)
                            if gap > 0:
                                tile = jnp.where(near_index(gap) < TILE, tile, 0.0)
                            turn = lax.broadcasted_iota(jnp.int32, (TILE, TILE), 1) + lax.broadcasted_iota(
                                jnp.int32, (TILE, TILE), 0
                            )
                            tile = jnp.take_along_axis(tile, (turn - gap) & (TILE - 1), axis=1)
                            hist_ref[g * 2 + half] += fold8(tile, jnp.sum)

                        collect() if when is None else pl.when(when)(collect)
                dv_all = dot_nn(p_ref[:total, lanes_used], grads)
                dk_all = dot_nn(ds_ref[:total, lanes_used], queries)
                for n, half in enumerate(halves):
                    rows = slice(n * size, n * size + size)
                    dv_parts.append(dv_all[rows])
                    dk_parts.append(dk_all[rows])
                    dq_parts.append(dot_nn(keys_t[half * 64 : half * 64 + 64, :], ds_ref[rows, lanes_used]))
            dq = jnp.concatenate(dq_parts, axis=0)
            if cont:
                dq_ref[lanes, :PB] = jnp.zeros((TILE, PB), f32)
                dq_ref[lanes, PB:] = dq
            else:
                dq_ref[lanes, lanes_used] += dq
            mine = head_lanes(0)
            dv, dk = jnp.where(mine, dv_parts[0], dv_parts[1]), jnp.where(mine, dk_parts[0], dk_parts[1])
            if window:
                window_v[:, lanes], window_k[:, lanes] = dv.astype(bf16), dk.astype(bf16)
            else:
                if not cont:
                    dv = dv + dot_nn(picked_ref[...], window_v[:, lanes])
                    dk = dk + dot_nn(picked_ref[...], window_k[:, lanes])
                dv_ref[:, lanes], dk_ref[:, lanes] = dv.astype(bf16), dk.astype(bf16)
            return 0

        lax.fori_loop(0, width // TILE, pair, 0)

        def block_column(cols, i=i, cont=cont, at_home=at_home, remote=remote):
            if cont:
                normed = normed_own_ref[PB:, cols]
            elif at_home:
                normed = normed_own_ref[:PB, cols]
            else:
                normed = normed_ref[i % 2, :, cols]
            wk_part = dot_nn(rows_t[:, :PB], dk_ref[:, cols])
            wv_part = dot_nn(rows_t[:, :PB], dv_ref[:, cols])
            if cont:
                in_out[:, cols] = wk_part
                out_out[:, cols] = wv_part
            elif not at_home:
                in_out[:, cols] += wk_part
                out_out[:, cols] += wv_part
            else:
                put(width, cols, out_out[:, cols] + wv_part)
                put(2 * width, cols, in_out[:, cols] + wk_part)
            grad = dot_nt(dk_ref[...], wk_ref[cols, :]) + dot_nt(dv_ref[...], wv_ref[cols, :])
            gain_sum[:, cols] += jnp.sum(grad * normed.astype(f32), axis=0, keepdims=True)
            if cont:
                local_ref[PB:, cols] = grad
            elif at_home:
                local_ref[:PB, cols] = grad
            else:
                shared_send[(remote - 1) % shared_slots, :, cols] = grad.astype(bf16)

        if window:
            continue
        if shared_slots < remote < ctx_count:
            shared_copies[remote - 1 - shared_slots].wait_send()
        if cont:
            rows_t[:, :PB] = normed_own_ref[PB:, :].T
        elif at_home:
            rows_t[:, :PB] = normed_own_ref[:PB, :].T
        else:
            rows_t[:, :PB] = normed_ref[i % 2].T
        columns(block_column)
        if 1 <= remote < ctx_count:
            n = remote - 1
            shared_copies.append(
                push(shared_send.at[n % shared_slots], shared_recv.at[n], shared_sems, n, lines.peer(remote))
            )
        if early and i == blocks - 2:
            advance(i)
    started.extend(shared_copies[-shared_slots:])

    def ready(j):
        if j > 0 or not early:
            pending[j, 0] = reduce_start(j, 0)

    done = 3 * rows_16
    for j in range(pieces):
        if (j + 1) * group <= done:
            ready(j)
    rows_ref[:tokens, :] = dq_ref[...].T.astype(bf16)
    rows_t[:, :tokens] = normed_own_ref[...].T

    def query_column(cols):
        put(3 * width, cols, dot_nn(rows_t[:, :tokens], rows_ref[:tokens, cols]))

    columns(query_column)
    for j in range(pieces):
        if (j + 1) * group > done:
            ready(j)

    def query_grad(cols):
        grad = dot_nt(rows_ref[:tokens, :], wq_ref[cols, :])
        gain_sum[:, cols] += jnp.sum(grad * normed_own_ref[:, cols].astype(f32), axis=0, keepdims=True)
        local_ref[:, cols] += grad

    columns(query_grad)
    small_ref[experts:, :] = jnp.zeros((small_ref.shape[0] - experts, width), f32)
    small_ref[experts : experts + 1, :] = gain_sum[...] / gain
    small_ref[experts + 1 : experts + 2, :] = moe_gain_ref[...]
    router_load.wait()
    per_row = width // TILE
    for head in range(hist_ref.shape[0]):
        row, lane = 2 + experts + head // per_row, head % per_row * TILE
        small_ref[row : row + 1, lane : lane + TILE] = jnp.sum(hist_ref[head], axis=0, keepdims=True)
    small_pending = small_start(0)

    slots = rows_ref.shape[0]

    def rows_load(n):
        source = rows_hbm if n == 0 else rows_all.at[n - 1]
        return pltpu.make_async_copy(source, result_recv, load_sems.at[3 + 2 * n])

    hidden_load = pltpu.make_async_copy(hidden_hbm, input_out, load_sems.at[4 + 2 * dp_count])
    hidden_load.start()
    grad_load = pltpu.make_async_copy(hidden_grad_hbm, input_out, load_sems.at[3 + 2 * dp_count])
    x_loads = [
        pltpu.make_async_copy(x_hbm.at[pl.ds(n * PB, PB)], normed_ref.at[n], load_sems.at[6 + 2 * dp_count + 2 * n])
        for n in range(2)
    ]
    for copy in x_loads:
        copy.start()

    def grads_of(n, c):
        if c == 0:
            if n == 0:
                for copy in weight_loads:
                    copy.wait()
            rows_load(n).wait()
            rows_ref[...] = result_recv[...].reshape(slots, width)
            cot_from = columns_dp.at(dp_count - n)
            load = pltpu.make_async_copy(cot_hbm.at[cot_from], result_recv, load_sems.at[4 + 2 * n])
            load.start()
            lane = lax.broadcasted_iota(jnp.int32, (slots, TILE), 1)
            probs = router_probs(dot_nn(rows_ref[...], router_ref[...]), lane, experts)
            gate = jnp.sum(jnp.where(lane == me, probs, 0.0), axis=1, keepdims=True)
            load.wait()
            cot = result_recv[...].reshape(slots, width)
            cot_ref[...] = (gate * cot.astype(f32)).astype(bf16)
            if n == 0:
                each_row_block(lambda copy: copy.wait_recv())
            if n + 1 < dp_count:
                rows_load(n + 1).start()
            rows_t[...] = rows_ref[...].T
        cols = slice(c * 256, c * 256 + 256)
        act, slope = gelu_parts(dot_nn(rows_ref[...], win_ref[:, cols]))
        pre_grad = (dot_nt(cot_ref[...], wout_ref[cols, :]) * slope).astype(bf16)
        out_part = dot_tn(act.astype(bf16), cot_ref[...])
        in_part = dot_nn(rows_t[...], pre_grad)
        if n == 0:
            out_out[cols, :] = out_part
            in_out[:, cols] = in_part
        else:
            out_out[cols, :] += out_part
            in_out[:, cols] += in_part

    def input_back():
        for copy in shared_copies:
            copy.wait_recv()
        for copy in x_loads:
            copy.wait()
        grad_load.wait()
        for first, shared_rows in ((0, True), (PB, False)):
            rows = slice(first, PB if shared_rows else tokens)
            x = normed_ref[0 if shared_rows else 1].astype(f32)
            inverse = inverse_rms(x)
            grad = local_ref[rows, :]
            if shared_rows:
                for n in range(ctx_count - 1):
                    grad = grad + shared_recv[n].astype(f32)
            through = grad * gain
            scaled = x * inverse
            shared = jnp.mean(through * scaled, axis=1, keepdims=True)
            input_out[rows, :] += inverse * (through - scaled * shared)

    def layer():
        own_result.wait()
        await_blocks(result_hbm, result_recv, result_sems, False, True)
        place = place_rows(slot_row[...], 0, slots, tokens)
        returned = dot_tn(place, result_recv[...].reshape(slots, width))
        hidden_load.wait()
        layer_out[...] = (input_out[...] + returned).astype(bf16)
        rows_load(0).start()
        grad_load.start()

    work = [layer]
    work += [functools.partial(grads_of, n, c) for n in range(dp_count) for c in range(slice_width // 256)]
    work += [input_back]
    for time in range(blocks - 1, max(begin) + 2 * stages):
        if time >= blocks:
            advance(time)
        elif early:
            advance(time)
        s = time - blocks
        if 0 <= s < len(whole_axes):
            small_finish(s, small_pending)
            if s + 1 < len(whole_axes):
                small_pending = small_start(s + 1)
        for _ in range(-(-len(work) // (max(begin) + 2 * stages - time))):
            work.pop(0)()
    for copy in started:
        copy.wait_send()
    await_blocks(result_hbm, result_recv, result_sems, True, False)
    each_row_block(lambda copy: copy.wait_send())


def finish_kernel(
    experts, full_ref, in_ref, out_ref, input_ref, layer_ref, small_ref, spread_ref, *results,
):
    weights, rest, (attn_out, moe_out, router_out, table_out) = results[:4], results[4:8], results[8:]
    for n, weight in enumerate(weights):
        weight[...] = full_ref[n].astype(f32).reshape(weight.shape)
    for source, target in zip((in_ref, out_ref, input_ref, layer_ref), rest):
        target[...] = source[...].astype(target.dtype)

    @pl.when(pl.program_id(0) == 0)
    def _():
        router_out[...] = small_ref[:experts, :]
        attn_out[...] = small_ref[experts : experts + 1, :]
        moe_out[...] = small_ref[experts + 1 : experts + 2, :]
        per_row = small_ref.shape[1] // TILE
        hist = []
        for head in range(table_out.shape[0]):
            row, lane = 2 + experts + head // per_row, head % per_row * TILE
            hist.append(small_ref[row : row + 1, lane : lane + TILE])
        table_out[...] = jnp.dot(
            jnp.concatenate(hist, axis=0), spread_ref[...],
            preferred_element_type=f32, precision=lax.Precision.HIGHEST,
        )


def tail_plan(sizes, width):
    group = 1
    for size in sizes:
        group *= size
    units = 4 * width // 16
    pieces = -(-units // group)
    lengths, left = [], group
    for size in sizes:
        left //= size
        lengths.append(left)
    return group, pieces, lengths


def body(
    inputs, cotangent, route, arrival, branch, attn_gain, query_weight, key_weight, value_weight,
    output_weight, rel_table, moe_gain, router_weight, expert_in, expert_out,
):
    x = inputs[0]
    cot = cotangent[0]
    tokens, width = x.shape
    own = tokens - PB
    buckets, heads = rel_table.shape
    experts = router_weight.shape[1]
    capacity = 9 * tokens // (8 * experts)
    block_rows = capacity if capacity % 8 == 0 else -(-capacity // 16) * 16
    slots = experts * block_rows
    ctx_count = lax.axis_size("ctx")
    dp_count = lax.axis_size("dp")
    plen = PB * ctx_count
    keys_total = plen + own + TILE
    hidden_units = expert_in.shape[2]
    pairs = width // TILE
    attn_gain_row = attn_gain.reshape(1, width)
    moe_gain_row = moe_gain.reshape(1, width)
    onehot = bucket_onehot(buckets)
    by_distance = jnp.dot(onehot, rel_table.astype(f32), precision=lax.Precision.HIGHEST).T
    by_distance = by_distance - by_distance[:, TILE - 1 :]
    bias = jnp.pad(by_distance.reshape(pairs, 2, TILE), ((0, 0), (0, 6), (0, 0)))
    router_wide = jnp.pad(router_weight, ((0, 0), (0, TILE - experts)))
    route_row = route.reshape(1, tokens)
    arrive_row = arrival[0]
    blocks = shape((experts, block_rows, width), bf16)
    block_space = pltpu.VMEM((experts, block_rows, width), bf16)
    block_sems = pltpu.SemaphoreType.DMA((2, experts - 1))
    any_space = pl.BlockSpec(memory_space=pl.ANY)

    slot_row, cot_sent, normed_own, normed_all, queries, keys, values, att, lse = pl.pallas_call(
        functools.partial(front_kernel, capacity),
        out_shape=[
            shape((1, tokens), jnp.int32),
            blocks,
            shape((tokens, width), bf16),
            shape((plen, width), bf16),
            shape((tokens, width), bf16),
            shape((keys_total, width), bf16),
            shape((keys_total, width), bf16),
            shape((width, tokens), bf16),
            shape((pairs, 8, tokens), f32),
        ],
        in_specs=[smem()] + [vmem()] * 9,
        out_specs=[vmem()] * 9,
        scratch_shapes=[
            pltpu.VMEM((ctx_count, PB, width), bf16),
            block_space,
            pltpu.VMEM((keys_total, tokens), f32),
            pltpu.VMEM((keys_total, tokens), bf16),
            pltpu.SemaphoreType.DMA((2, 2, ctx_count - 1, CHUNKS)),
            block_sems,
        ],
        compiler_params=remote_params(1),
        cost_estimate=cost(40 * keys_total * tokens * width, 20 * width * width),
        name="front",
    )(
        branch, bias, x, cot, attn_gain_row, route_row, arrive_row,
        query_weight, key_weight, value_weight,
    )
    cot_all = lax.all_gather(cot_sent, "dp", axis=0, tiled=False)

    members = 2 * lax.axis_size("expert") if ctx_count % 2 == 0 else experts
    group_rows = members * block_rows
    (
        rows_sent, router_part, hidden_grad, wo_part, att_grad, delta, moe_gain_part,
        result, hidden,
    ) = pl.pallas_call(
        functools.partial(expert_kernel, experts),
        out_shape=[
            blocks, shape((TILE, width), f32), shape((tokens, width), f32), shape((width // 16, 16, width), bf16),
            shape((tokens, width), bf16), shape((pairs, 8, tokens), f32), shape((1, width), f32),
            blocks, shape((tokens, width), f32),
        ],
        in_specs=[vmem()] * 8 + [any_space] * 2,
        out_specs=[vmem()] * 9,
        scratch_shapes=[
            pltpu.VMEM((tokens, width), bf16),
            block_space,
            pltpu.VMEM((width, hidden_units), bf16),
            pltpu.VMEM((hidden_units, width), bf16),
            pltpu.VMEM((group_rows, width), bf16),
            pltpu.VMEM((group_rows, width), bf16),
            pltpu.VMEM((group_rows, width), f32),
            pltpu.VMEM((group_rows, width), f32),
            block_space, block_space,
            pltpu.VMEM((tokens, width), bf16),
            pltpu.VMEM((width, tokens), bf16),
            block_sems, block_sems,
            pltpu.SemaphoreType.DMA((2,)),
        ],
        compiler_params=remote_params(2),
        cost_estimate=cost(8 * slots * width * hidden_units, 12 * width * hidden_units),
        name="expert",
    )(
        att, x, output_weight, moe_gain_row, router_wide, slot_row, cot, cot_sent,
        expert_in[0], expert_out[0],
    )
    att_grad, cot_all = lax.optimization_barrier((att_grad, cot_all))

    expert_count = lax.axis_size("expert")
    dp_sizes = [2, 2] if dp_count == 4 else [dp_count]
    sizes = [expert_count, *dp_sizes, ctx_count]
    plan = tail_plan(sizes, width)
    group, pieces, lengths = plan
    units = group * pieces

    stacked = 2 if ctx_count <= 4 else 1
    table_rows = heads * TILE // width
    small_rows = -(-(2 + experts + table_rows) // 8) * 8
    slice_width = hidden_units // dp_count
    weights, small, input_grad, in_grad, out_grad, layer_out, _ = pl.pallas_call(
        functools.partial(back_kernel, experts, plan),
        out_shape=[
            shape((units, 16, width), bf16), shape((small_rows, width), f32), shape((tokens, width), f32),
            shape((width, slice_width), f32), shape((slice_width, width), f32), shape((tokens, width), bf16),
            shape((dp_count - 1, experts, block_rows, width), bf16),
        ],
        in_specs=[
            smem(), vmem(), vmem(), any_space, any_space, vmem(), vmem(), vmem(), any_space, vmem(),
            vmem(), vmem(), vmem(), vmem(), any_space, vmem(), any_space, any_space, any_space,
            any_space, vmem(), any_space, any_space, any_space, any_space, any_space, vmem(),
        ],
        out_specs=[vmem()] * 6 + [any_space],
        scratch_shapes=[
            pltpu.VMEM((2, PB, width), bf16),
            pltpu.VMEM((2, PB, width), bf16),
            pltpu.VMEM((2, PB, width), bf16),
            pltpu.VMEM((stacked * PB, tokens), f32),
            pltpu.VMEM((stacked * PB, tokens), f32),
            pltpu.VMEM((stacked * PB, tokens), bf16),
            pltpu.VMEM((stacked * PB, tokens), bf16),
            pltpu.VMEM((width, tokens), f32),
            pltpu.VMEM((PB, width), bf16),
            pltpu.VMEM((PB, width), bf16),
            pltpu.VMEM((TILE, width), bf16),
            pltpu.VMEM((TILE, width), bf16),
            pltpu.VMEM((PB, TILE), bf16),
            pltpu.VMEM((heads, 8, TILE), f32),
            pltpu.VMEM((1, width), f32),
            pltpu.VMEM((tokens, width), f32),
            pltpu.VMEM((ctx_count - 1 if ctx_count <= 4 else 1, PB, width), bf16),
            pltpu.VMEM((ctx_count - 1, PB, width), bf16),
            pltpu.VMEM((units, 16, width), bf16),
            [pltpu.VMEM((pieces, length, 16, width), bf16) for length in lengths[:-1]],
            [
                pltpu.VMEM((pieces, size - 1, length, 16, width), bf16)
                for size, length in zip(sizes, lengths)
            ],
            pltpu.VMEM((small_rows, width), f32),
            [pltpu.VMEM((size - 1, small_rows, width), f32) for size in (expert_count, dp_count, ctx_count)],
            block_space,
            pltpu.VMEM((width, slice_width), bf16),
            pltpu.VMEM((slice_width, width), bf16),
            pltpu.VMEM((slots, width), bf16),
            pltpu.VMEM((slots, width), bf16),
            pltpu.VMEM((width, slots), bf16),
            pltpu.SemaphoreType.DMA((ctx_count + 2, 3)),
            pltpu.SemaphoreType.DMA((9 + 2 * dp_count,)),
            pltpu.SemaphoreType.DMA((2, 2 * pieces * sum(size - 1 for size in sizes))),
            pltpu.SemaphoreType.DMA((2, expert_count + dp_count + ctx_count - 3)),
            pltpu.SemaphoreType.DMA((2, ctx_count - 1)),
            block_sems,
            pltpu.SemaphoreType.DMA((2, dp_count - 1, experts)),
        ],
        compiler_params=remote_params(0),
        cost_estimate=cost(
            8 * dp_count * slots * width * slice_width + 80 * keys_total * tokens * width,
            60 * width * slice_width,
        ),
        name="back",
    )(
        branch, bias, queries, keys, values, att_grad, lse, delta, normed_all, normed_own,
        attn_gain_row, query_weight, key_weight, value_weight, wo_part, moe_gain_part, router_part, x,
        hidden_grad, hidden, slot_row, result,
        rows_sent, cot_all, expert_in[0], expert_out[0], router_wide,
    )

    matrix_units = width // 16
    steps = 4

    def part_rows(rows, columns=width):
        return pl.BlockSpec((rows // steps, columns), lambda i: (i, 0))

    weights = weights[: 4 * matrix_units].reshape(4, matrix_units, 16, width)
    last = onehot[:, buckets - 1 :]
    spread = jnp.concatenate([onehot[:, : buckets - 1], last - 1.0], axis=1)

    def same(rows, columns):
        return pl.BlockSpec((rows, columns), lambda i: (0, 0))

    (
        *weights, in_grad, out_grad, input_grad, layer_out, attn_gain_grad, moe_gain_grad, router_grad, table_grad,
    ) = pl.pallas_call(
        functools.partial(finish_kernel, experts),
        grid=(steps,),
        out_shape=[shape((width, width), f32)] * 4
        + [
            shape((width, slice_width), f32), shape((slice_width, width), f32),
            shape((tokens, width), f32), shape((tokens, width), bf16),
            shape((1, width), f32), shape((1, width), f32), shape((experts, width), f32), shape((heads, buckets), f32),
        ],
        in_specs=[
            pl.BlockSpec(
                (4, matrix_units // steps, 16, width), lambda i: (0, i, 0, 0)
            ),
            part_rows(width, slice_width), part_rows(slice_width), part_rows(tokens), part_rows(tokens),
            same(small_rows, width), same(TILE, buckets),
        ],
        out_specs=[part_rows(width)] * 4
        + [part_rows(width, slice_width), part_rows(slice_width), part_rows(tokens), part_rows(tokens)]
        + [same(1, width), same(1, width), same(experts, width), same(heads, buckets)],
        compiler_params=params(),
        cost_estimate=cost(8 * width * width, 48 * width * width),
        name="finish",
    )(weights, in_grad, out_grad, input_grad, layer_out, small, spread)
    return (
        layer_out[None],
        input_grad[None],
        attn_gain_grad.reshape(width),
        weights[3],
        weights[2],
        weights[1],
        weights[0],
        table_grad.T,
        moe_gain_grad.reshape(width),
        router_grad.T,
        in_grad[None],
        out_grad[None],
    )


def solution(mesh):
    grouped = P(("dp", "expert"), "ctx", None)
    placed = (
        grouped, grouped, grouped, grouped, P(("dp", "expert"), "ctx"),
        P(), P(), P(), P(), P(), P(), P(), P(),
        P(("ctx", "expert"), None, None),
        P(("ctx", "expert"), None, None),
    )
    return jax.shard_map(
        body,
        mesh=mesh,
        in_specs=placed,
        out_specs=(
            grouped, grouped, P(), P(), P(), P(), P(), P(), P(), P(),
            P(("ctx", "expert"), None, "dp"),
            P(("ctx", "expert"), "dp", None),
        ),
        check_vma=False,
    )
```
